32 devices in a mesh: grp: 2 (over x), gx: 16 (over z, y, core).
Axes of the slice: x: 2, y: 2, z: 4, core: 2. Of those that a mesh axis runs over, the one named last changes fastest.
Arguments:
- cell_offsets: float32 [3, 81920], P(None, ('grp', 'gx')), parts along dimension 1, may hold values from 0 to 1
- electronegativity: float32 [81920], P(('grp', 'gx')), parts along dimension 0, may hold values from -44 to 80
- hardness: float32 [81920], P(('grp', 'gx')), parts along dimension 0, may hold values from 5 to 12
- charge_widths: float32 [81920], P(('grp', 'gx')), parts along dimension 0, may hold values from 0.9 to 1.4
- cell_counts: int32 [1024], P(('grp', 'gx')), parts along dimension 0, may hold values from 72 to 88, as said below
- cell_atoms: int32 [1024, 128], P(('grp', 'gx')), parts along dimension 0, may hold values from -1 to 2559, as said below
Outputs:
- charges: float32 [81920], P(('grp', 'gx')), parts along dimension 0
The draws below stay inside these ranges and needn't reach their ends.
There are 2 independent parts, one for each index of `grp`. The reference program is written for one: setup_inputs(seed, part) draws one part's arguments, and reference() takes and returns one part's arrays. A program takes and returns all parts, laid end to end along the dimension named above; each array names one. Nothing has to cross between parts.
Inputs may be any that keep to these rules, and one draw needn't show every extreme that they name: `cell_counts`: within each device's 32 cells the counts add up to 2560; on every device some cell holds 88 atoms and some cell 5 * 16 - 128 / 16. `cell_atoms`: row c lists the indices of cell c's atoms in its first cell_counts[c] slots and -1 in the others; each of a device's 2560 atoms appears exactly once in that device's rows.
All inputs are finite; a program needn't handle non-finite values.
Results may differ from the reference program's by a relative error of at most 0.0003.
Values sent between devices are 32-bit elements; how exact they have to be, the bound alone decides.
No kernel may reach another device: no remote copies, remote signals or barrier semaphores. Data moves between devices by JAX's collectives and lax.ppermute only.
A program may use at most 192 MiB of HBM per device.

```python
import math
import jax
import jax.numpy as jnp
from jax import lax

CX = 2
CY = 2
CZ = 8
TILE = 128
ITERS = 3
CELLS_DEV = 32
ATOMS_DEV = 2560
CELLS = 512
ATOMS = 40960
N_GX = 16


def cell_tables(key):
    devices = CELLS // CELLS_DEV
    half_cells = CELLS_DEV // 2
    middle = 5 * TILE // 8
    spread = TILE // 16

    def per_device(device_index):
        device_key = jax.random.fold_in(key, device_index)
        draw_keys = jax.random.split(device_key, 4)
        excess = jax.random.randint(draw_keys[0], (half_cells,), 0, spread + 1)
        forced = jax.random.randint(draw_keys[1], (), 0, half_cells)
        excess = jnp.where(jnp.arange(half_cells) == forced, spread, excess)
        paired = jnp.stack([middle + excess, middle - excess], axis=1).reshape(CELLS_DEV)
        counts = paired[jax.random.permutation(draw_keys[2], CELLS_DEV)]
        shuffle = jax.random.permutation(draw_keys[3], ATOMS_DEV)
        starts = jnp.cumsum(counts) - counts
        slot_index = jnp.arange(TILE)
        position = starts[:, None] + slot_index[None, :]
        filled = slot_index[None, :] < counts[:, None]
        members = jnp.where(filled, shuffle[jnp.minimum(position, ATOMS_DEV - 1)], -1)
        return (counts, members)
    counts, members = jax.vmap(per_device)(jnp.arange(devices))
    return (counts.reshape(CELLS).astype(jnp.int32), members.reshape(CELLS, TILE).astype(jnp.int32))


def draw_cell_counts(key, part):
    tables = cell_tables(key)
    return tables[0]


def draw_cell_atoms(key, part):
    tables = cell_tables(key)
    return tables[1]


def draw_electronegativity(key, part):
    key = jax.random.fold_in(key, 3)
    key_normal, key_rough = jax.random.split(key)
    position = jnp.arange(ATOMS, dtype=jnp.float32) / ATOMS
    rising = jnp.exp(jnp.log(3.0) * position)
    roughness = jnp.exp(jax.random.uniform(key_rough, (ATOMS,), jnp.float32, 0.0, jnp.log(3.4)))
    fluctuation = jnp.clip(jax.random.normal(key_normal, (ATOMS,), jnp.float32), -4.0, 4.0)
    center = 6.0
    return (rising * (center + 1.5 * roughness * fluctuation)).astype(jnp.float32)


def steps_of(rng, dims, cuts, least, top_value):
    def one(axis_at, blocks):
        heights = jax.random.uniform(jax.random.fold_in(jax.random.fold_in(rng, 6), axis_at), (blocks,), jnp.float32, least / len(cuts), top_value / len(cuts))
        return jnp.repeat(jnp.exp(heights), dims[axis_at] // blocks).reshape((-1,) + (1,) * (len(dims) - axis_at - 1))

    factor_of = one(*cuts[0])
    for cut in cuts[1:]:
        factor_of = factor_of * one(*cut)
    return factor_of


def setup_inputs(seed: int = 0, part: int = 0) -> dict:
    splits = jax.random.split(jax.random.key(seed), 7)
    part_splits = jax.random.split(jax.random.fold_in(splits[6], part), 7)
    return {
        "cell_offsets": jnp.clip(1.0 * jax.random.uniform(part_splits[0], (3, ATOMS), jnp.float32) ** steps_of(part_splits[0], (3, ATOMS), ((1, 16),), -0.2, 0.2), 0.0, 1.0),
        "electronegativity": draw_electronegativity(jax.random.fold_in(jax.random.fold_in(splits[6], part), 71), part),
        "hardness": jnp.clip(jnp.exp(math.log(12.0) - 0.87546874 * jax.random.uniform(part_splits[2], (ATOMS,), jnp.float32) ** steps_of(part_splits[2], (ATOMS,), ((0, 16),), -0.2, 0.2)), 5.0, 12.0),
        "charge_widths": jnp.clip(jnp.exp(math.log(1.4) - 0.44183276 * jax.random.uniform(part_splits[3], (ATOMS,), jnp.float32) ** steps_of(part_splits[3], (ATOMS,), ((0, 16),), -0.2, 0.2)), 0.9, 1.4),
        "cell_counts": draw_cell_counts(jax.random.fold_in(jax.random.fold_in(splits[6], part), 71), part),
        "cell_atoms": draw_cell_atoms(jax.random.fold_in(jax.random.fold_in(splits[6], part), 71), part),
    }


COULOMB = 14.399645
CELL_SIDE = 12.0
CUTOFF = 12.0
CLOSEST = 0.5
ROOT_TWO = math.sqrt(2.0)
ROOT_PI = math.sqrt(math.pi)
SCREEN = 1.0 / (math.sqrt(2.0) * 3.0)
EWALD_SELF = math.sqrt(2.0 / math.pi) / 3.0

def build_tiles(cell_offsets, electronegativity, hardness, charge_widths, cell_counts, cell_atoms):
    slot_count = cell_atoms.shape[1]
    occupied = jnp.arange(slot_count, dtype=jnp.int32)[None, :] < cell_counts[:, None]
    pointer = jnp.where(occupied, cell_atoms, 0).astype(jnp.int32)
    placed = jnp.take(cell_offsets, pointer, axis=1)
    widths = jnp.where(occupied, jnp.take(charge_widths, pointer), 1.0)
    diagonal = jnp.where(occupied, jnp.take(hardness, pointer) + COULOMB * (1.0 / (widths * ROOT_PI) - EWALD_SELF), 1.0)
    negativity = jnp.where(occupied, jnp.take(electronegativity, pointer), 0.0)
    weights = occupied.astype(diagonal.dtype)
    fields = jnp.concatenate([placed, widths[None]], axis=0)
    targets = jnp.stack([-negativity, weights])
    return (fields, diagonal, targets, weights)

def couple(window, moving):
    count_y = window.shape[2] - 2
    count_z = window.shape[3] - 2
    slot_count = window.shape[4]
    inside = window[:, 1, 1:1 + count_y, 1:1 + count_z]
    same_slot = jnp.arange(slot_count)[:, None] == jnp.arange(slot_count)[None, :]
    result = jnp.zeros((moving.shape[0], count_y, count_z, slot_count), window.dtype)
    for step_x in (-1, 0, 1):
        for step_y in (-1, 0, 1):
            for step_z in (-1, 0, 1):
                beside = window[:, 1 + step_x, 1 + step_y:1 + step_y + count_y, 1 + step_z:1 + step_z + count_z]
                carried = moving[:, 1 + step_x, 1 + step_y:1 + step_y + count_y, 1 + step_z:1 + step_z + count_z]
                delta_x = (beside[0][:, :, None, :] - inside[0][:, :, :, None] + step_x) * CELL_SIDE
                delta_y = (beside[1][:, :, None, :] - inside[1][:, :, :, None] + step_y) * CELL_SIDE
                delta_z = (beside[2][:, :, None, :] - inside[2][:, :, :, None] + step_z) * CELL_SIDE
                distance = jnp.sqrt(delta_x * delta_x + delta_y * delta_y + delta_z * delta_z)
                safe_distance = jnp.maximum(distance, CLOSEST)
                gamma_pair = jnp.sqrt(inside[3][:, :, :, None] * inside[3][:, :, :, None] + beside[3][:, :, None, :] * beside[3][:, :, None, :])
                kernel = COULOMB * (lax.erfc(safe_distance * SCREEN) - lax.erfc(safe_distance / (ROOT_TWO * gamma_pair))) / safe_distance
                within = distance < CUTOFF
                if step_x == 0 and step_y == 0 and (step_z == 0):
                    within = jnp.logical_and(within, jnp.logical_not(same_slot))
                kernel = jnp.where(within, kernel, 0.0)
                result = result + jnp.einsum('yzij,nyzj->nyzi', kernel, carried, precision=lax.Precision.HIGHEST)
    return result

def apply_operator(extended, moving_ext):
    count_x = extended.shape[1] - 2

    def one_slab(slab_index):
        window = lax.dynamic_slice_in_dim(extended, slab_index, 3, 1)
        moving = lax.dynamic_slice_in_dim(moving_ext, slab_index, 3, 1)
        return couple(window, moving)
    stacked = lax.map(one_slab, jnp.arange(count_x, dtype=jnp.int32))
    return jnp.moveaxis(stacked, 0, 1)

def to_grid(tiles):
    leading = tiles.shape[:-3]
    leading_count = len(leading)
    tiles = tiles.reshape(leading + (N_GX // 4, 2, 2, CX, CY, CZ, TILE))
    axes_order = tuple(range(leading_count)) + tuple((leading_count + a for a in (0, 3, 1, 4, 2, 5, 6)))
    return jnp.transpose(tiles, axes_order).reshape(leading + (N_GX // 4 * CX, 2 * CY, 2 * CZ, TILE))

def from_grid(values):
    values = values.reshape((N_GX // 4, CX, 2, CY, 2, CZ, TILE))
    return jnp.transpose(values, (0, 2, 4, 1, 3, 5, 6)).reshape((N_GX, CELLS_DEV, TILE))

def wrap_pad(values):
    return jnp.pad(values, ((0, 0), (1, 1), (1, 1), (1, 1), (0, 0)), mode='wrap')

def scatter_back(values, cell_counts, cell_atoms):
    slot_count = cell_atoms.shape[1]
    occupied = jnp.arange(slot_count, dtype=jnp.int32)[None, :] < cell_counts[:, None]
    target = jnp.where(occupied, cell_atoms, ATOMS_DEV).astype(jnp.int32)
    return jnp.zeros((ATOMS_DEV,), values.dtype).at[target.reshape(-1)].set(values.reshape(-1), mode='drop')

def summed_product(left, right):
    return lax.optimization_barrier(jnp.sum(left * right, axis=(1, 2, 3, 4)))

def expand_scalar(values):
    return values[:, None, None, None, None]

def reference(cell_offsets, electronegativity, hardness, charge_widths, cell_counts, cell_atoms):
    offsets_dev = jnp.moveaxis(cell_offsets.reshape(3, N_GX, ATOMS_DEV), 1, 0)
    counts_dev = cell_counts.reshape(N_GX, CELLS_DEV)
    atoms_dev = cell_atoms.reshape(N_GX, CELLS_DEV, TILE)
    fields, diagonal, targets, weights = jax.vmap(build_tiles)(offsets_dev, electronegativity.reshape(N_GX, ATOMS_DEV), hardness.reshape(N_GX, ATOMS_DEV), charge_widths.reshape(N_GX, ATOMS_DEV), counts_dev, atoms_dev)
    fields = to_grid(jnp.moveaxis(fields, 0, 1))
    diagonal = to_grid(diagonal)
    targets = to_grid(jnp.moveaxis(targets, 0, 1))
    weights = to_grid(weights)
    extended = wrap_pad(fields)

    def apply_matrix(direction):
        return weights * (diagonal * direction + apply_operator(extended, wrap_pad(direction)))
    solution = jnp.zeros_like(targets)
    residual = targets
    precond = residual / diagonal
    direction = precond
    current = summed_product(residual, precond)
    for iteration in range(ITERS):
        mapped = apply_matrix(direction)
        step_size = current / summed_product(direction, mapped)
        solution = solution + expand_scalar(step_size) * direction
        residual = residual - expand_scalar(step_size) * mapped
        if iteration + 1 < ITERS:
            precond = residual / diagonal
            following = summed_product(residual, precond)
            direction = precond + expand_scalar(following / current) * direction
            current = following
    balance = jnp.sum(solution[0]) / jnp.sum(solution[1])
    charge_grid = solution[0] - balance * solution[1]
    charges = jax.vmap(scatter_back)(from_grid(charge_grid), counts_dev, atoms_dev)
    return charges.reshape(ATOMS)
```

```python
import functools
import math

import jax
import jax.numpy as jnp
from jax import lax
from jax.experimental import pallas as pl
from jax.experimental.pallas import tpu as pltpu
from jax.sharding import PartitionSpec as P

CX = 2
CY = 2
CZ = 8
EX = CX + 2
EY = CY + 2
EZ = CZ + 2
CELLS = CX * CY * CZ
COLUMNS = EX * EY
LANES = 128
BLOCKS = 11
TILES = 18

COULOMB = 14.399645
ROOT_PI = math.sqrt(math.pi)
SCREEN = 1.0 / (math.sqrt(2.0) * 3.0)
EWALD_SELF = math.sqrt(2.0 / math.pi) / 3.0
SIDE = 12.0 * SCREEN
CUT_SQUARED = (12.0 * SCREEN) ** 2
CLOSEST_SQUARED = (0.5 * SCREEN) ** 2
PAIR_SCALE = COULOMB * SCREEN

VMEM = pltpu.VMEM
SMEM = pltpu.SMEM


def params(mib):
    return pltpu.CompilerParams(vmem_limit_bytes=mib * 2**20)


def lane_index(shape):
    return lax.broadcasted_iota(jnp.int32, shape, len(shape) - 1)


def row_index(shape):
    return lax.broadcasted_iota(jnp.int32, shape, len(shape) - 2)


def prepare_kernel(counts, offsets, negativity, hardness, widths, atoms, slots, diagonal, table):
    table[0:3, :] = offsets[...]
    table[3:4, :] = widths[...]
    table[4:5, :] = negativity[...]
    table[5:6, :] = hardness[...]
    table[6:8, :] = jnp.zeros((2, table.shape[1]), jnp.float32)
    chunks = table.shape[1] // LANES

    def one_cell(cell, _):
        count = counts[cell]
        occupied = lane_index((1, LANES)) < count
        pointer = jnp.where(occupied, atoms[pl.ds(cell, 1), :], 0)
        high = jnp.broadcast_to(pointer >> 7, (8, LANES))
        low = jnp.broadcast_to(pointer & 127, (8, LANES))
        picked = jnp.zeros((8, LANES), jnp.float32)
        for chunk in range(chunks):
            part = table[:, chunk * LANES : (chunk + 1) * LANES]
            picked = jnp.where(high == chunk, jnp.take_along_axis(part, low, axis=1), picked)
        width = jnp.where(occupied, picked[3:4], 1.0)
        diag = jnp.where(
            occupied, picked[5:6] + COULOMB * (1.0 / (width * ROOT_PI) - EWALD_SELF), 1.0
        )
        negative = jnp.where(occupied, picked[4:5], 0.0)
        slots[cell, 0:3, :] = picked[0:3] * SIDE
        slots[cell, 3:4, :] = (2.0 * SCREEN * SCREEN) * width * width
        slots[cell, 4:5, :] = -negative / diag
        slots[cell, 5:6, :] = jnp.where(occupied, 1.0 / diag, 0.0)
        slots[cell, 6:7, :] = jnp.zeros((1, LANES), jnp.float32)
        slots[cell, 7:8, :] = jnp.full((1, LANES), count.astype(jnp.float32))
        diagonal[pl.ds(cell, 1), :] = diag
        return 0

    lax.fori_loop(0, CELLS, one_cell, 0)


def prepare(counts, offsets, negativity, hardness, widths, atoms):
    return pl.pallas_call(
        prepare_kernel,
        out_shape=(
            jax.ShapeDtypeStruct((CELLS, 8, LANES), jnp.float32),
            jax.ShapeDtypeStruct((CELLS, LANES), jnp.float32),
        ),
        in_specs=[pl.BlockSpec(memory_space=SMEM)] + [pl.BlockSpec(memory_space=VMEM)] * 5,
        out_specs=(pl.BlockSpec(memory_space=VMEM), pl.BlockSpec(memory_space=VMEM)),
        scratch_shapes=[VMEM((8, offsets.shape[1]), jnp.float32)],
        compiler_params=params(8),
    )(counts, offsets, negativity[None], hardness[None], widths[None], atoms)


def triple_counts(counts, triple):
    base = (triple >> 3) * EZ + (triple & 7)
    return base, counts[base], counts[base + 1], counts[base + 2]


def pack_triples(counts, cells, packed, z_row):
    rows = cells.shape[1]
    lane = lane_index((rows, LANES))
    shift = None
    if z_row is not None:
        shift = jnp.where(row_index((rows, LANES)) == z_row, SIDE, 0.0)

    def one(triple, _):
        base, low, mid, top = triple_counts(counts, triple)
        first = cells[base]
        last = cells[base + 2]
        if shift is not None:
            first = first - shift
            last = last + shift
        second = pltpu.roll(cells[base + 1], low, 1)
        end = low + mid - LANES
        third = pltpu.roll(last, end, 1)
        packed[triple, 0] = jnp.where(lane < low, first, second)
        packed[triple, 1] = jnp.where(lane < end, second, third)
        packed[triple, 2] = jnp.where(lane < end + top - LANES, third, 0.0)
        return 0

    lax.fori_loop(0, COLUMNS * CZ, one, 0)


def cell_place(cell):
    z = cell % CZ
    column = (cell // (CY * CZ)) * EY + (cell // CZ) % CY
    return z, column


def neighbour_columns():
    return [(a, b) for a in range(3) for b in range(3)]


def overflow_of(counts, z, column):
    found = jnp.int32(0)
    for a, b in neighbour_columns():
        base = (column + a * EY + b) * EZ + z
        total = counts[base] + counts[base + 1] + counts[base + 2]
        found = jnp.where(total > 2 * LANES, 1, found)
    return found


def gather_overflow(packed, overflow, z, column, shifts):
    rows = overflow.shape[0]
    lane = lane_index((rows, LANES))
    row = row_index((rows, LANES))
    total = jnp.zeros((rows, LANES), jnp.float32)
    for index, (a, b) in enumerate(neighbour_columns()):
        tile = packed[(column + a * EY + b) * CZ + z, 2]
        if shifts:
            tile = tile + jnp.where(row == 0, (a - 1) * SIDE, 0.0)
            tile = tile + jnp.where(row == 1, (b - 1) * SIDE, 0.0)
        moved = pltpu.roll(tile, 8 * index, 1) if index else tile
        total = jnp.where((lane >= 8 * index) & (lane < 8 * index + 8), moved, total)
    overflow[...] = total


def couple(x_i, y_i, z_i, w_i, x_j, y_j, z_j, w_j):
    delta_x = x_j - x_i
    delta_y = y_j - y_i
    delta_z = z_j - z_i
    squared = delta_x * delta_x + delta_y * delta_y + delta_z * delta_z
    held = jnp.maximum(squared, CLOSEST_SQUARED)
    inverse = lax.rsqrt(held)
    distance = held * inverse
    scaled = distance * lax.rsqrt(w_i + w_j)
    value = (lax.erf(scaled) - lax.erf(distance)) * inverse
    return squared, value


def to_rows(sums, block):
    here = lane_index((8, LANES)) - row_index((8, LANES)) == 8 * block
    return jnp.where(here, jnp.sum(sums, axis=1, keepdims=True), 0.0)


def finish_cell(counts, cell, z, column, rows_s, rows_t, diagonal, out):
    count = counts[(column + EY + 1) * EZ + z + 1]
    scale = PAIR_SCALE / diagonal[pl.ds(cell, 1), :]
    live = lane_index((1, LANES)) < count
    out[cell, 0:1, :] = jnp.where(live, jnp.sum(rows_s, axis=0, keepdims=True) * scale, 0.0)
    out[cell, 1:2, :] = jnp.where(live, jnp.sum(rows_t, axis=0, keepdims=True) * scale, 0.0)


def build_kernel(counts, cells, diagonal, kernels, out, packed, overflow, turned):
    pack_triples(counts, cells, packed, 2)
    zero = jnp.zeros((8, LANES), jnp.float32)

    def one_cell(cell, _):
        z, column = cell_place(cell)
        here = (column + EY + 1) * EZ + z + 1
        below = counts[here - 1]
        blocks = (counts[here] + 7) >> 3
        spills = overflow_of(counts, z, column)

        @pl.when(spills > 0)
        def _():
            gather_overflow(packed, overflow, z, column, True)

        turned[...] = cells[here].T

        def one_block(block, carry):
            rows_s, rows_t = carry
            columns = turned[pl.ds(pl.multiple_of(8 * block, 8), 8), :]
            x_0 = jnp.broadcast_to(columns[:, 0:1], (8, LANES))
            y_0 = jnp.broadcast_to(columns[:, 1:2], (8, LANES))
            z_0 = jnp.broadcast_to(columns[:, 2:3], (8, LANES))
            w_0 = jnp.broadcast_to(columns[:, 3:4], (8, LANES))
            x_all = [x_0 + SIDE, x_0, x_0 - SIDE]
            y_all = [y_0 + SIDE, y_0, y_0 - SIDE]
            own = lane_index((8, LANES)) - row_index((8, LANES)) - (below + 8 * block)
            sum_s = zero
            sum_t = zero
            for index, (a, b) in enumerate(neighbour_columns()):
                triple = (column + a * EY + b) * CZ + z
                for half in range(2):
                    tile = packed.at[triple, half]
                    squared, value = couple(
                        x_all[a], y_all[b], z_0, w_0, tile[0:1], tile[1:2], tile[2:3], tile[3:4]
                    )
                    value = jnp.where(squared < CUT_SQUARED, value, 0.0)
                    if a == 1 and b == 1:
                        value = jnp.where(own == -LANES * half, 0.0, value)
                    kernels[cell, block, 2 * index + half] = value
                    sum_s = sum_s + value * tile[4:5]
                    sum_t = sum_t + value * tile[5:6]

            def spilled(_, sums):
                squared, value = couple(
                    x_0, y_0, z_0, w_0, overflow[0:1], overflow[1:2], overflow[2:3], overflow[3:4]
                )
                value = jnp.where(squared < CUT_SQUARED, value, 0.0)
                kernels[cell, block, TILES] = value
                return sums[0] + value * overflow[4:5], sums[1] + value * overflow[5:6]

            sum_s, sum_t = lax.fori_loop(0, spills, spilled, (sum_s, sum_t))
            return rows_s + to_rows(sum_s, block), rows_t + to_rows(sum_t, block)

        rows_s, rows_t = lax.fori_loop(0, blocks, one_block, (zero, zero))
        finish_cell(counts, cell, z, column, rows_s, rows_t, diagonal, out)
        return 0

    lax.fori_loop(0, CELLS, one_cell, 0)


KERNELS_SHAPE = (CELLS, BLOCKS, TILES + 1, 8, LANES)


def build(counts, cells, diagonal):
    return pl.pallas_call(
        build_kernel,
        out_shape=(
            VMEM(KERNELS_SHAPE, jnp.float32),
            jax.ShapeDtypeStruct((CELLS, 2, LANES), jnp.float32),
        ),
        in_specs=[pl.BlockSpec(memory_space=SMEM)] + [pl.BlockSpec(memory_space=VMEM)] * 2,
        out_specs=(pl.BlockSpec(memory_space=VMEM), pl.BlockSpec(memory_space=VMEM)),
        scratch_shapes=[
            VMEM((COLUMNS * CZ, 3, 8, LANES), jnp.float32),
            VMEM((8, LANES), jnp.float32),
            VMEM((LANES, 8), jnp.float32),
        ],
        compiler_params=params(16),
    )(counts, cells, diagonal)


def apply_tiles(counts, kernels, moving, diagonal, out, packed, overflow):
    pack_triples(counts, moving, packed, None)
    zero = jnp.zeros((8, LANES), jnp.float32)

    def one_cell(cell, _):
        z, column = cell_place(cell)
        here = (column + EY + 1) * EZ + z + 1
        blocks = (counts[here] + 7) >> 3
        spills = overflow_of(counts, z, column)

        @pl.when(spills > 0)
        def _():
            gather_overflow(packed, overflow, z, column, False)

        def one_block(block, carry):
            rows_s, rows_t = carry
            sum_s = zero
            sum_t = zero
            for index, (a, b) in enumerate(neighbour_columns()):
                triple = (column + a * EY + b) * CZ + z
                for half in range(2):
                    value = kernels[cell, block, 2 * index + half]
                    sum_s = sum_s + value * packed[triple, half, 0:1]
                    sum_t = sum_t + value * packed[triple, half, 1:2]

            def spilled(_, sums):
                value = kernels[cell, block, TILES]
                return sums[0] + value * overflow[0:1], sums[1] + value * overflow[1:2]

            sum_s, sum_t = lax.fori_loop(0, spills, spilled, (sum_s, sum_t))
            return rows_s + to_rows(sum_s, block), rows_t + to_rows(sum_t, block)

        rows_s, rows_t = lax.fori_loop(0, blocks, one_block, (zero, zero))
        finish_cell(counts, cell, z, column, rows_s, rows_t, diagonal, out)
        return 0

    lax.fori_loop(0, CELLS, one_cell, 0)


def apply_kernel(counts, kernels, moving, diagonal, out, packed, overflow):
    apply_tiles(counts, kernels, moving, diagonal, out, packed, overflow)


def last_kernel(
    counts, kernels, moving, diagonal, slots, first, second, moments, third, packed, overflow
):
    apply_tiles(counts, kernels, moving, diagonal, third, packed, overflow)
    d = diagonal[...][:, None, :]
    v_0 = slots[:, 4:6, :]
    v_1 = first[...]
    v_2 = second[...]
    d_0 = d * v_0
    d_2 = d * v_2
    parts = [d_0 * v_0, d_0 * v_1, d * v_1 * v_1, d_2 * v_1, d_2 * v_2, d_2 * third[...]]
    for index, part in enumerate(parts + [v_0, v_1, v_2]):
        moments[2 * index : 2 * index + 2, :] = jnp.sum(part, axis=0)
    moments[18:24, :] = jnp.zeros((6, LANES), jnp.float32)


PACK_SCRATCH = [VMEM((COLUMNS * CZ, 3, 2, LANES), jnp.float32), VMEM((2, LANES), jnp.float32)]


def apply_stored(counts, kernels, moving, diagonal):
    return pl.pallas_call(
        apply_kernel,
        out_shape=jax.ShapeDtypeStruct((CELLS, 2, LANES), jnp.float32),
        in_specs=[pl.BlockSpec(memory_space=SMEM)] + [pl.BlockSpec(memory_space=VMEM)] * 3,
        out_specs=pl.BlockSpec(memory_space=VMEM),
        scratch_shapes=PACK_SCRATCH,
        compiler_params=params(16),
    )(counts, pltpu.with_memory_space_constraint(kernels, VMEM), moving, diagonal)


def apply_last(counts, kernels, moving, diagonal, slots, first, second):
    return pl.pallas_call(
        last_kernel,
        out_shape=jax.ShapeDtypeStruct((24, LANES), jnp.float32),
        in_specs=[pl.BlockSpec(memory_space=SMEM)] + [pl.BlockSpec(memory_space=VMEM)] * 6,
        out_specs=pl.BlockSpec(memory_space=VMEM),
        scratch_shapes=[VMEM((CELLS, 2, LANES), jnp.float32)] + PACK_SCRATCH,
        compiler_params=params(16),
    )(
        counts,
        pltpu.with_memory_space_constraint(kernels, VMEM),
        moving,
        diagonal,
        slots,
        first,
        second,
    )


def solve(g):
    tiny = 1e-6
    h = [g[k] + g[k + 1] for k in range(5)]
    ratio_1 = h[1] / h[0]
    ratio_2 = h[2] / h[0]
    pivot_1 = h[2] - ratio_1 * h[1]
    mixed = h[3] - ratio_1 * h[2]
    rest_1 = g[1] - ratio_1 * g[0]
    live_1 = pivot_1 > tiny * h[2]
    safe_1 = jnp.where(live_1, pivot_1, 1.0)
    ratio_3 = jnp.where(live_1, mixed / safe_1, 0.0)
    pivot_2 = h[4] - ratio_2 * h[2] - ratio_3 * mixed
    rest_2 = g[2] - ratio_2 * g[0] - ratio_3 * rest_1
    live_2 = live_1 & (pivot_2 > tiny * h[4])
    c_2 = jnp.where(live_2, rest_2 / jnp.where(live_2, pivot_2, 1.0), 0.0)
    c_1 = jnp.where(live_1, (rest_1 - mixed * c_2) / safe_1, 0.0)
    c_0 = (g[0] - h[1] * c_1 - h[2] * c_2) / h[0]
    return c_0, c_1, c_2


def finish_kernel(counts, moments, slots, first, second, atoms, out):
    summed = jnp.broadcast_to(jnp.sum(moments[...], axis=1, keepdims=True), (24, LANES))
    rows = [summed[2 * k : 2 * k + 2] for k in range(9)]
    c_0, c_1, c_2 = solve(rows[:6])
    totals = c_0 * rows[6] + c_1 * rows[7] + c_2 * rows[8]
    balance = totals[0:1] / totals[1:2]
    sign = jnp.concatenate([jnp.ones((1, LANES), jnp.float32), -balance], axis=0)
    c_0, c_1, c_2 = c_0 * sign, c_1 * sign, c_2 * sign
    high_rows = out.shape[0]
    padded = (high_rows + 7) // 8 * 8
    row_low = row_index((LANES, LANES))
    row_high = row_index((padded, LANES))

    def one_cell(cell, total):
        mixed = c_0 * slots[cell, 4:6, :] + c_1 * first[cell] + c_2 * second[cell]
        charge = jnp.sum(mixed, axis=0, keepdims=True)
        live = lane_index((1, LANES)) < counts[cell]
        pointer = jnp.where(live, atoms[pl.ds(cell, 1), :], -1)
        placed = jnp.where((pointer >> 7) == row_high, charge, 0.0)
        part_0 = placed.astype(jnp.bfloat16)
        left = placed - part_0.astype(jnp.float32)
        part_1 = left.astype(jnp.bfloat16)
        part_2 = (left - part_1.astype(jnp.float32)).astype(jnp.bfloat16)
        lows = jnp.where((pointer & 127) == row_low, 1.0, 0.0).astype(jnp.bfloat16)
        for part in (part_2, part_1, part_0):
            total = total + lax.dot_general(
                part, lows, (((1,), (1,)), ((), ())), preferred_element_type=jnp.float32
            )
        return total

    total = lax.fori_loop(0, CELLS, one_cell, jnp.zeros((padded, LANES), jnp.float32))
    out[...] = total[:high_rows]


def finish(counts, moments, slots, first, second, atoms, atoms_local):
    return pl.pallas_call(
        finish_kernel,
        out_shape=jax.ShapeDtypeStruct((atoms_local // LANES, LANES), jnp.float32),
        in_specs=[pl.BlockSpec(memory_space=SMEM)] + [pl.BlockSpec(memory_space=VMEM)] * 5,
        out_specs=pl.BlockSpec(memory_space=VMEM),
        compiler_params=params(8),
    )(counts, moments, slots, first, second, atoms)


def partner(block, axis, apart):
    count = lax.axis_size(axis)
    route = [(low, low ^ (1 << apart)) for low in range(count)]
    return lax.ppermute(block, axis, route)


def from_behind(x, axis, by):
    peers = lax.axis_size(axis)
    return lax.ppermute(x, axis, [(i, (i + by) % peers) for i in range(peers)])


def extend_rims(cells):
    cells = cells.reshape((CX, CY, CZ) + cells.shape[1:])
    faces = jnp.concatenate([cells[:, :, -1:], cells[:, :, :1]], axis=2)
    other = partner(faces, "gx", 0)
    cells = jnp.concatenate([other[:, :, 0:1], cells, other[:, :, 1:2]], axis=2)
    faces = jnp.concatenate([cells[:, -1:], cells[:, :1]], axis=1)
    other = partner(faces, "gx", 1)
    cells = jnp.concatenate([other[:, 0:1], cells, other[:, 1:2]], axis=1)
    below = from_behind(cells[-1:], "gx", 4)
    above = from_behind(cells[:1], "gx", -4)
    cells = jnp.concatenate([below, cells, above], axis=0)
    return cells.reshape((EX * EY * EZ,) + cells.shape[3:])


def global_sum(values):
    count = lax.axis_size("gx")
    if count & (count - 1):
        return lax.psum(values, "gx")
    for bit in range(count.bit_length() - 1):
        values = values + partner(values, "gx", bit)
    return values


def local(cell_offsets, electronegativity, hardness, charge_widths, cell_counts, cell_atoms):
    slots, diagonal = prepare(
        cell_counts, cell_offsets, electronegativity, hardness, charge_widths, cell_atoms
    )
    cells = extend_rims(slots)
    counts = cells[:, 7, 0].astype(jnp.int32)
    kernels, first = build(counts, cells, diagonal)
    second = apply_stored(counts, kernels, extend_rims(first), diagonal)
    moments = apply_last(counts, kernels, extend_rims(second), diagonal, slots, first, second)
    moments = global_sum(moments)
    charges = finish(
        cell_counts, moments, slots, first, second, cell_atoms, cell_offsets.shape[1]
    )
    return charges.reshape(-1)


def solution(mesh):
    placed = (
        P(None, ("grp", "gx")),
        P(("grp", "gx")),
        P(("grp", "gx")),
        P(("grp", "gx")),
        P(("grp", "gx")),
        P(("grp", "gx"), None),
    )
    return jax.shard_map(
        local, mesh=mesh, in_specs=placed, out_specs=P(("grp", "gx")), check_vma=False
    )
```

```python
import functools
import math

import jax
import jax.numpy as jnp
from jax import lax
from jax.experimental import pallas as pl
from jax.experimental.pallas import tpu as pltpu
from jax.sharding import PartitionSpec as P

CX = 2
CY = 2
CZ = 8
EX = CX + 2
EY = CY + 2
EZ = CZ + 2
CELLS = CX * CY * CZ
COLUMNS = EX * EY
LANES = 128
BLOCKS = 11
TILES = 19
SELF_TILES = (8, 9)

COULOMB = 14.399645
ROOT_PI = math.sqrt(math.pi)
SCREEN = 1.0 / (math.sqrt(2.0) * 3.0)
EWALD_SELF = math.sqrt(2.0 / math.pi) / 3.0
SIDE = 12.0 * SCREEN
CUT_SQUARED = (12.0 * SCREEN) ** 2
CLOSEST_SQUARED = (0.5 * SCREEN) ** 2
PAIR_SCALE = COULOMB * SCREEN

VMEM = pltpu.VMEM
SMEM = pltpu.SMEM


def params(mib):
    return pltpu.CompilerParams(vmem_limit_bytes=mib * 2**20)


def lane_index(shape):
    return lax.broadcasted_iota(jnp.int32, shape, len(shape) - 1)


def row_index(shape):
    return lax.broadcasted_iota(jnp.int32, shape, len(shape) - 2)


def prepare_kernel(
    counts, offsets, negativity, hardness, widths, atoms, slots, diagonal,
    raw_offsets, raw_negativity, raw_hardness, raw_widths, raw_atoms, table, sems,
):
    copies = [
        pltpu.make_async_copy(source, target, sems.at[index])
        for index, (source, target) in enumerate(
            [
                (offsets, raw_offsets),
                (negativity, raw_negativity),
                (hardness, raw_hardness),
                (widths, raw_widths),
                (atoms, raw_atoms),
            ]
        )
    ]
    for copy in copies:
        copy.start()
    for copy in copies:
        copy.wait()
    chunks = table.shape[0]
    for chunk in range(chunks):
        here = slice(chunk * LANES, (chunk + 1) * LANES)
        table[chunk, 0:3, :] = raw_offsets[:, here]
        table[chunk, 3:4, :] = raw_widths[chunk : chunk + 1, :]
        table[chunk, 4:5, :] = raw_negativity[chunk : chunk + 1, :]
        table[chunk, 5:6, :] = raw_hardness[chunk : chunk + 1, :]
        table[chunk, 6:8, :] = jnp.zeros((2, LANES), jnp.float32)

    def one_cell(cell, _):
        count = counts[cell]
        occupied = lane_index((1, LANES)) < count
        pointer = jnp.where(occupied, raw_atoms[pl.ds(cell, 1), :], 0)
        high = jnp.broadcast_to(pointer >> 7, (8, LANES))
        low = jnp.broadcast_to(pointer & 127, (8, LANES))
        picked = jnp.zeros((8, LANES), jnp.float32)
        for chunk in range(chunks):
            part = jnp.take_along_axis(table[chunk], low, axis=1)
            picked = jnp.where(high == chunk, part, picked)
        width = jnp.where(occupied, picked[3:4], 1.0)
        diag = jnp.where(
            occupied, picked[5:6] + COULOMB * (1.0 / (width * ROOT_PI) - EWALD_SELF), 1.0
        )
        negative = jnp.where(occupied, picked[4:5], 0.0)
        slots[cell, 0:3, :] = picked[0:3] * SIDE
        slots[cell, 3:4, :] = (2.0 * SCREEN * SCREEN) * width * width
        slots[cell, 4:5, :] = -negative / diag
        slots[cell, 5:6, :] = jnp.where(occupied, 1.0 / diag, 0.0)
        slots[cell, 6:7, :] = jnp.zeros((1, LANES), jnp.float32)
        slots[cell, 7:8, :] = jnp.full((1, LANES), count.astype(jnp.float32))
        diagonal[pl.ds(cell, 1), :] = diag
        return 0

    lax.fori_loop(0, CELLS, one_cell, 0, unroll=4)


def prepare(counts, offsets, negativity, hardness, widths, atoms):
    chunks = offsets.shape[1] // LANES
    plane = (chunks, LANES)
    return pl.pallas_call(
        prepare_kernel,
        out_shape=(
            jax.ShapeDtypeStruct((CELLS, 8, LANES), jnp.float32),
            jax.ShapeDtypeStruct((CELLS, LANES), jnp.float32),
        ),
        in_specs=[pl.BlockSpec(memory_space=SMEM)] + [pl.BlockSpec(memory_space=pltpu.HBM)] * 5,
        out_specs=(pl.BlockSpec(memory_space=VMEM), pl.BlockSpec(memory_space=VMEM)),
        scratch_shapes=[
            VMEM(offsets.shape, jnp.float32),
            VMEM(plane, jnp.float32),
            VMEM(plane, jnp.float32),
            VMEM(plane, jnp.float32),
            VMEM(atoms.shape, jnp.int32),
            VMEM((chunks, 8, LANES), jnp.float32),
            pltpu.SemaphoreType.DMA((5,)),
        ],
        compiler_params=params(8),
    )(
        counts,
        offsets,
        negativity.reshape(plane),
        hardness.reshape(plane),
        widths.reshape(plane),
        atoms,
    )


def pack_triples(counts, cells, packed, z_row):
    lane = lane_index((8, LANES))
    if z_row is not None:
        shift = jnp.where(row_index((8, LANES)) == z_row, SIDE, 0.0)

    def one(triple, _):
        base = (triple >> 3) * EZ + (triple & 7)
        low = jnp.broadcast_to(counts[pl.ds(base, 1), :], (8, LANES))
        mid = jnp.broadcast_to(counts[pl.ds(base + 1, 1), :], (8, LANES))
        top = jnp.broadcast_to(counts[pl.ds(base + 2, 1), :], (8, LANES))
        end = low + mid - LANES
        first = cells[base]
        last = cells[base + 2]
        if z_row is not None:
            first = first - shift
            last = last + shift
        second = jnp.take_along_axis(cells[base + 1], (lane - low) & 127, axis=1)
        third = jnp.take_along_axis(last, (lane - end) & 127, axis=1)
        packed[triple, 0] = jnp.where(lane < low, first, second)
        packed[triple, 1] = jnp.where(lane < end, second, third)
        packed[triple, 2] = jnp.where(lane < end + top - LANES, third, 0.0)
        return 0

    lax.fori_loop(0, COLUMNS * CZ, one, 0, unroll=8)


def cell_place(cell):
    z = cell % CZ
    column = (cell // (CY * CZ)) * EY + (cell // CZ) % CY
    return z, column, (column + EY + 1) * EZ + z + 1


def neighbour_columns():
    return [(a, b) for a in range(3) for b in range(3)]


def gathered_overflow(packed, z, column, shifts):
    lane = lane_index((8, LANES))
    row = row_index((8, LANES))
    total = jnp.zeros((8, LANES), jnp.float32)
    for index, (a, b) in enumerate(neighbour_columns()):
        tile = packed[(column + a * EY + b) * CZ + z, 2]
        if shifts:
            offset = jnp.where(row == 0, (a - 1) * SIDE, jnp.where(row == 1, (b - 1) * SIDE, 0.0))
            tile = tile + offset
        moved = pltpu.roll(tile, 8 * index, 1) if index else tile
        total = jnp.where((lane >= 8 * index) & (lane < 8 * index + 8), moved, total)
    return total


def spread(row):
    return jnp.broadcast_to(row, (8, LANES))


def couple(x_i, y_i, z_i, w_i, x_j, y_j, z_j, w_j):
    delta_x = x_j - x_i
    delta_y = y_j - y_i
    delta_z = z_j - z_i
    squared = delta_x * delta_x + delta_y * delta_y + delta_z * delta_z
    held = jnp.maximum(squared, CLOSEST_SQUARED)
    inverse = lax.rsqrt(held)
    distance = held * inverse
    scaled = distance * lax.rsqrt(w_i + w_j)
    value = (lax.erf(scaled) - lax.erf(distance)) * inverse
    return jnp.where(squared < CUT_SQUARED, value, 0.0)


def to_rows(sums, block):
    here = lane_index((8, LANES)) - row_index((8, LANES)) == 8 * block
    return jnp.where(here, jnp.sum(sums, axis=1, keepdims=True), 0.0)


def finish_cell(counts, cell, here, rows_s, rows_t, diagonal, out):
    scale = PAIR_SCALE / diagonal[pl.ds(cell, 1), :]
    live = lane_index((1, LANES)) < counts[pl.ds(here, 1), :]
    out[cell, 0:1, :] = jnp.where(live, jnp.sum(rows_s, axis=0, keepdims=True) * scale, 0.0)
    out[cell, 1:2, :] = jnp.where(live, jnp.sum(rows_t, axis=0, keepdims=True) * scale, 0.0)


def build_kernel(cells, diagonal, kernels, out, counts, packed, turned, beside):
    counts[...] = cells[:, 7, :].astype(jnp.int32)
    pack_triples(counts, cells, packed, 2)

    def turn(cell, _):
        turned[cell] = cells[cell_place(cell)[2]].T[: 8 * BLOCKS]
        return 0

    lax.fori_loop(0, CELLS, turn, 0, unroll=4)

    def one_cell(cell, _):
        z, column, here = cell_place(cell)
        for index, (a, b) in enumerate(neighbour_columns()):
            for half in range(2):
                tile = packed[(column + a * EY + b) * CZ + z, half]
                shifts = ((a - 1) * SIDE, (b - 1) * SIDE)
                for row in range(6):
                    line = tile[row : row + 1]
                    if row < 2 and shifts[row]:
                        line = line + shifts[row]
                    beside[2 * index + half, row] = spread(line)
        tile = gathered_overflow(packed, z, column, True)
        for row in range(6):
            beside[TILES - 1, row] = spread(tile[row : row + 1])
        below = spread(counts[pl.ds(here - 1, 1), :])
        own = lane_index((8, LANES)) - row_index((8, LANES)) - below
        rows_s = jnp.zeros((8, LANES), jnp.float32)
        rows_t = rows_s
        for block in range(BLOCKS):
            columns = turned[cell, 8 * block : 8 * block + 8, :]
            mine = [jnp.broadcast_to(columns[:, k : k + 1], (8, LANES)) for k in range(4)]
            sum_s = jnp.zeros((8, LANES), jnp.float32)
            sum_t = sum_s
            for tile in range(TILES):
                value = couple(*mine, *[beside[tile, k] for k in range(4)])
                if tile in SELF_TILES:
                    half = tile - SELF_TILES[0]
                    value = jnp.where(own == 8 * block - LANES * half, 0.0, value)
                kernels[cell, block, tile] = value
                sum_s = sum_s + value * beside[tile, 4]
                sum_t = sum_t + value * beside[tile, 5]
            rows_s = rows_s + to_rows(sum_s, block)
            rows_t = rows_t + to_rows(sum_t, block)
        finish_cell(counts, cell, here, rows_s, rows_t, diagonal, out)
        return 0

    lax.fori_loop(0, CELLS, one_cell, 0)


KERNELS_SHAPE = (CELLS, BLOCKS, TILES, 8, LANES)
ANYWHERE = pl.BlockSpec(memory_space=VMEM)


def build(cells, diagonal):
    return pl.pallas_call(
        build_kernel,
        out_shape=(
            VMEM(KERNELS_SHAPE, jnp.float32),
            jax.ShapeDtypeStruct((CELLS, 2, LANES), jnp.float32),
            jax.ShapeDtypeStruct((EX * EY * EZ, LANES), jnp.int32),
        ),
        in_specs=[ANYWHERE] * 2,
        out_specs=(ANYWHERE,) * 3,
        scratch_shapes=[
            VMEM((COLUMNS * CZ, 3, 8, LANES), jnp.float32),
            VMEM((CELLS, 8 * BLOCKS, 8), jnp.float32),
            VMEM((TILES, 6, 8, LANES), jnp.float32),
        ],
        compiler_params=params(8),
    )(cells, diagonal)


def apply_tiles(counts, kernels, moving, diagonal, out, wide, packed):
    wide[:, 0:2, :] = moving[...]
    wide[:, 2:8, :] = jnp.zeros((wide.shape[0], 6, LANES), jnp.float32)
    pack_triples(counts, wide, packed, None)

    def one_cell(cell, _):
        z, column, here = cell_place(cell)
        beside_s = []
        beside_t = []
        for a, b in neighbour_columns():
            for half in range(2):
                tile = packed[(column + a * EY + b) * CZ + z, half]
                beside_s.append(spread(tile[0:1]))
                beside_t.append(spread(tile[1:2]))
        tile = gathered_overflow(packed, z, column, False)
        beside_s.append(spread(tile[0:1]))
        beside_t.append(spread(tile[1:2]))
        rows_s = jnp.zeros((8, LANES), jnp.float32)
        rows_t = rows_s
        for block in range(BLOCKS):
            sum_s = jnp.zeros((8, LANES), jnp.float32)
            sum_t = sum_s
            for tile in range(TILES):
                value = kernels[cell, block, tile]
                sum_s = sum_s + value * beside_s[tile]
                sum_t = sum_t + value * beside_t[tile]
            rows_s = rows_s + to_rows(sum_s, block)
            rows_t = rows_t + to_rows(sum_t, block)
        finish_cell(counts, cell, here, rows_s, rows_t, diagonal, out)
        return 0

    lax.fori_loop(0, CELLS, one_cell, 0)


def apply_kernel(counts, kernels, moving, diagonal, out, wide, packed):
    apply_tiles(counts, kernels, moving, diagonal, out, wide, packed)


def last_kernel(
    counts, kernels, moving, diagonal, slots, first, second, moments, third, wide, packed
):
    apply_tiles(counts, kernels, moving, diagonal, third, wide, packed)
    d = diagonal[...][:, None, :]
    v_0 = slots[:, 4:6, :]
    v_1 = first[...]
    v_2 = second[...]
    d_0 = d * v_0
    d_2 = d * v_2
    parts = [d_0 * v_0, d_0 * v_1, d * v_1 * v_1, d_2 * v_1, d_2 * v_2, d_2 * third[...]]
    for index, part in enumerate(parts + [v_0, v_1, v_2]):
        moments[2 * index : 2 * index + 2, :] = jnp.sum(part, axis=0)
    moments[18:24, :] = jnp.zeros((6, LANES), jnp.float32)


PACK_SCRATCH = [
    VMEM((EX * EY * EZ, 8, LANES), jnp.float32),
    VMEM((COLUMNS * CZ, 3, 8, LANES), jnp.float32),
]


def apply_stored(counts, kernels, moving, diagonal):
    return pl.pallas_call(
        apply_kernel,
        out_shape=jax.ShapeDtypeStruct((CELLS, 2, LANES), jnp.float32),
        in_specs=[ANYWHERE] * 4,
        out_specs=ANYWHERE,
        scratch_shapes=PACK_SCRATCH,
        compiler_params=params(8),
    )(counts, pltpu.with_memory_space_constraint(kernels, VMEM), moving, diagonal)


def apply_last(counts, kernels, moving, diagonal, slots, first, second):
    return pl.pallas_call(
        last_kernel,
        out_shape=jax.ShapeDtypeStruct((24, LANES), jnp.float32),
        in_specs=[ANYWHERE] * 7,
        out_specs=ANYWHERE,
        scratch_shapes=[VMEM((CELLS, 2, LANES), jnp.float32)] + PACK_SCRATCH,
        compiler_params=params(8),
    )(
        counts,
        pltpu.with_memory_space_constraint(kernels, VMEM),
        moving,
        diagonal,
        slots,
        first,
        second,
    )


def solve(g):
    tiny = 1e-6
    h = [g[k] + g[k + 1] for k in range(5)]
    ratio_1 = h[1] / h[0]
    ratio_2 = h[2] / h[0]
    pivot_1 = h[2] - ratio_1 * h[1]
    mixed = h[3] - ratio_1 * h[2]
    rest_1 = g[1] - ratio_1 * g[0]
    live_1 = pivot_1 > tiny * h[2]
    safe_1 = jnp.where(live_1, pivot_1, 1.0)
    ratio_3 = jnp.where(live_1, mixed / safe_1, 0.0)
    pivot_2 = h[4] - ratio_2 * h[2] - ratio_3 * mixed
    rest_2 = g[2] - ratio_2 * g[0] - ratio_3 * rest_1
    live_2 = live_1 & (pivot_2 > tiny * h[4])
    c_2 = jnp.where(live_2, rest_2 / jnp.where(live_2, pivot_2, 1.0), 0.0)
    c_1 = jnp.where(live_1, (rest_1 - mixed * c_2) / safe_1, 0.0)
    c_0 = (g[0] - h[1] * c_1 - h[2] * c_2) / h[0]
    return c_0, c_1, c_2


def finish_kernel(counts, moments, slots, first, second, atoms, out):
    summed = jnp.broadcast_to(jnp.sum(moments[...], axis=1, keepdims=True), (24, LANES))
    rows = [summed[2 * k : 2 * k + 2] for k in range(9)]
    c_0, c_1, c_2 = solve(rows[:6])
    totals = c_0 * rows[6] + c_1 * rows[7] + c_2 * rows[8]
    balance = totals[0:1] / totals[1:2]
    sign = jnp.concatenate([jnp.ones((1, LANES), jnp.float32), -balance], axis=0)
    c_0, c_1, c_2 = c_0 * sign, c_1 * sign, c_2 * sign
    high_rows = out.shape[0]
    padded = (high_rows + 15) // 16 * 16
    row_low = row_index((LANES, LANES))
    row_high = row_index((padded, LANES))

    def one_cell(cell, total):
        mixed = c_0 * slots[cell, 4:6, :] + c_1 * first[cell] + c_2 * second[cell]
        charge = jnp.sum(mixed, axis=0, keepdims=True)
        live = lane_index((1, LANES)) < counts[cell]
        pointer = jnp.where(live, atoms[pl.ds(cell, 1), :], -1)
        placed = jnp.where((pointer >> 7) == row_high, charge, 0.0)
        part_0 = placed.astype(jnp.bfloat16)
        left = placed - part_0.astype(jnp.float32)
        part_1 = left.astype(jnp.bfloat16)
        part_2 = (left - part_1.astype(jnp.float32)).astype(jnp.bfloat16)
        lows = jnp.where((pointer & 127) == row_low, 1.0, 0.0).astype(jnp.bfloat16)
        parts = jnp.concatenate([part_0, part_1, part_2], axis=0)
        return total + lax.dot_general(
            parts, lows, (((1,), (1,)), ((), ())), preferred_element_type=jnp.float32
        )

    total = jnp.zeros((3 * padded, LANES), jnp.float32)
    total = lax.fori_loop(0, CELLS, one_cell, total, unroll=8)
    total = total[2 * padded :] + total[padded : 2 * padded] + total[:padded]
    out[...] = total[:high_rows]


def finish(counts, moments, slots, first, second, atoms, atoms_local):
    return pl.pallas_call(
        finish_kernel,
        out_shape=jax.ShapeDtypeStruct((atoms_local // LANES, LANES), jnp.float32),
        in_specs=[pl.BlockSpec(memory_space=SMEM)] + [pl.BlockSpec(memory_space=VMEM)] * 5,
        out_specs=pl.BlockSpec(memory_space=VMEM),
        compiler_params=params(8),
    )(counts, moments, slots, first, second, atoms)


def partner(block, axis, apart):
    count = lax.axis_size(axis)
    route = [(low, low ^ (1 << apart)) for low in range(count)]
    return lax.ppermute(block, axis, route)


def from_behind(x, axis, by):
    peers = lax.axis_size(axis)
    return lax.ppermute(x, axis, [(i, (i + by) % peers) for i in range(peers)])


def extend_rims(cells):
    cells = cells.reshape((CX, CY, CZ) + cells.shape[1:])
    faces = jnp.concatenate([cells[:, :, -1:], cells[:, :, :1]], axis=2)
    other = partner(faces, "gx", 0)
    cells = jnp.concatenate([other[:, :, 0:1], cells, other[:, :, 1:2]], axis=2)
    faces = jnp.concatenate([cells[:, -1:], cells[:, :1]], axis=1)
    other = partner(faces, "gx", 1)
    cells = jnp.concatenate([other[:, 0:1], cells, other[:, 1:2]], axis=1)
    below = from_behind(cells[-1:], "gx", 4)
    above = from_behind(cells[:1], "gx", -4)
    cells = jnp.concatenate([below, cells, above], axis=0)
    return cells.reshape((EX * EY * EZ,) + cells.shape[3:])


def global_sum(values):
    count = lax.axis_size("gx")
    if count & (count - 1):
        return lax.psum(values, "gx")
    for bit in range(count.bit_length() - 1):
        values = values + partner(values, "gx", bit)
    return values


def local(cell_offsets, electronegativity, hardness, charge_widths, cell_counts, cell_atoms):
    slots, diagonal = prepare(
        cell_counts, cell_offsets, electronegativity, hardness, charge_widths, cell_atoms
    )
    cells = extend_rims(slots)
    kernels, first, counts = build(cells, diagonal)
    second = apply_stored(counts, kernels, extend_rims(first), diagonal)
    moments = apply_last(counts, kernels, extend_rims(second), diagonal, slots, first, second)
    moments = global_sum(moments)
    charges = finish(
        cell_counts, moments, slots, first, second, cell_atoms, cell_offsets.shape[1]
    )
    return charges.reshape(-1)


def solution(mesh):
    placed = (
        P(None, ("grp", "gx")),
        P(("grp", "gx")),
        P(("grp", "gx")),
        P(("grp", "gx")),
        P(("grp", "gx")),
        P(("grp", "gx"), None),
    )
    return jax.shard_map(
        local, mesh=mesh, in_specs=placed, out_specs=P(("grp", "gx")), check_vma=False
    )
```

```python
import functools
import math

import jax
import jax.numpy as jnp
from jax import lax
from jax.experimental import pallas as pl
from jax.experimental.pallas import tpu as pltpu
from jax.sharding import PartitionSpec as P

CX = 2
CY = 2
CZ = 8
EZ = CZ + 2
CELLS = CX * CY * CZ
QUADS = CX * CY
LANES = 128
BLOCKS = 11
GROUPS = ((0, 1, 2, 3), (4, 5, 6, 7), (8, 9, 10))

COULOMB = 14.399645
ROOT_PI = math.sqrt(math.pi)
SCREEN = 1.0 / (math.sqrt(2.0) * 3.0)
EWALD_SELF = math.sqrt(2.0 / math.pi) / 3.0
SIDE = 12.0 * SCREEN
CUT_SQUARED = (12.0 * SCREEN) ** 2
CLOSEST_SQUARED = (0.5 * SCREEN) ** 2
PAIR_SCALE = COULOMB * SCREEN

VMEM = pltpu.VMEM
SMEM = pltpu.SMEM


def params(mib):
    return pltpu.CompilerParams(vmem_limit_bytes=mib * 2**20)


def lane_index(shape):
    return lax.broadcasted_iota(jnp.int32, shape, len(shape) - 1)


def row_index(shape):
    return lax.broadcasted_iota(jnp.int32, shape, len(shape) - 2)


def prepare_kernel(
    counts_hbm, offsets, negativity, hardness, widths, atoms, slots, diagonal,
    counts, raw_offsets, raw_negativity, raw_hardness, raw_widths, raw_atoms, table, sems,
):
    copies = [
        pltpu.make_async_copy(source, target, sems.at[index])
        for index, (source, target) in enumerate(
            [
                (counts_hbm, counts),
                (offsets, raw_offsets),
                (negativity, raw_negativity),
                (hardness, raw_hardness),
                (widths, raw_widths),
                (atoms, raw_atoms),
            ]
        )
    ]
    for copy in copies:
        copy.start()
    for copy in copies:
        copy.wait()
    chunks = table.shape[0]
    for chunk in range(chunks):
        here = slice(chunk * LANES, (chunk + 1) * LANES)
        table[chunk, 0:3, :] = raw_offsets[:, here]
        table[chunk, 3:4, :] = raw_widths[chunk : chunk + 1, :]
        table[chunk, 4:5, :] = raw_negativity[chunk : chunk + 1, :]
        table[chunk, 5:6, :] = raw_hardness[chunk : chunk + 1, :]
        table[chunk, 6:8, :] = jnp.zeros((2, LANES), jnp.float32)

    def one_cell(cell, _):
        count = counts[cell]
        occupied = lane_index((1, LANES)) < count
        pointer = jnp.where(occupied, raw_atoms[pl.ds(cell, 1), :], 0)
        high = jnp.broadcast_to(pointer >> 7, (8, LANES))
        low = jnp.broadcast_to(pointer & 127, (8, LANES))
        picked = jnp.zeros((8, LANES), jnp.float32)
        for chunk in range(chunks):
            part = jnp.take_along_axis(table[chunk], low, axis=1)
            picked = jnp.where(high == chunk, part, picked)
        width = jnp.where(occupied, picked[3:4], 1.0)
        diag = jnp.where(
            occupied, picked[5:6] + COULOMB * (1.0 / (width * ROOT_PI) - EWALD_SELF), 1.0
        )
        negative = jnp.where(occupied, picked[4:5], 0.0)
        place = jnp.where(
            row_index((8, LANES)) == 0, cell // (CY * CZ), (cell // CZ) % CY
        ).astype(jnp.float32)
        place = jnp.where(row_index((8, LANES)) < 2, place, 0.0)
        slots[cell, 0:3, :] = ((picked + place) * SIDE)[0:3]
        slots[cell, 3:4, :] = (2.0 * SCREEN * SCREEN) * width * width
        slots[cell, 4:5, :] = -negative / diag
        slots[cell, 5:6, :] = jnp.where(occupied, 1.0 / diag, 0.0)
        slots[cell, 6:7, :] = jnp.zeros((1, LANES), jnp.float32)
        slots[cell, 7:8, :] = jnp.full((1, LANES), count.astype(jnp.float32))
        diagonal[pl.ds(cell, 1), :] = diag
        return 0

    lax.fori_loop(0, CELLS, one_cell, 0, unroll=4)


def prepare(counts, offsets, negativity, hardness, widths, atoms):
    chunks = offsets.shape[1] // LANES
    plane = (chunks, LANES)
    return pl.pallas_call(
        prepare_kernel,
        out_shape=(
            jax.ShapeDtypeStruct((CELLS, 8, LANES), jnp.float32),
            jax.ShapeDtypeStruct((CELLS, LANES), jnp.float32),
        ),
        in_specs=[pl.BlockSpec(memory_space=pltpu.HBM)] * 6,
        out_specs=(pl.BlockSpec(memory_space=VMEM), pl.BlockSpec(memory_space=VMEM)),
        scratch_shapes=[
            SMEM(counts.shape, jnp.int32),
            VMEM(offsets.shape, jnp.float32),
            VMEM(plane, jnp.float32),
            VMEM(plane, jnp.float32),
            VMEM(plane, jnp.float32),
            VMEM(atoms.shape, jnp.int32),
            VMEM((chunks, 8, LANES), jnp.float32),
            pltpu.SemaphoreType.DMA((6,)),
        ],
        compiler_params=params(8),
    )(
        *[
            pltpu.with_memory_space_constraint(array, pltpu.HBM)
            for array in (
                counts,
                offsets,
                negativity.reshape(plane),
                hardness.reshape(plane),
                widths.reshape(plane),
                atoms,
            )
        ]
    )


def pack_column(info, cells, source, packed, target, shift):
    lane = lane_index((8, LANES))
    row = row_index((8, LANES))
    for z in range(CZ):
        base = source * EZ + z
        low, mid, top = [spread(info[base + k, 7:8, :]).astype(jnp.int32) for k in range(3)]
        end = low + mid - LANES
        tiles = [cells[base + k] for k in range(3)]
        if shift is not None:
            for k in range(3):
                offset = jnp.where(row == 2, (k - 1) * SIDE, 0.0)
                for axis in range(2):
                    offset = jnp.where(row == axis, shift[axis] * SIDE, offset)
                tiles[k] = tiles[k] + offset
        second = jnp.take_along_axis(tiles[1], (lane - low) & 127, axis=1)
        third = jnp.take_along_axis(tiles[2], (lane - end) & 127, axis=1)
        packed[target * CZ + z, 0] = jnp.where(lane < low, tiles[0], second)
        packed[target * CZ + z, 1] = jnp.where(lane < end, second, third)
        packed[target * CZ + z, 2] = jnp.where(lane < end + top - LANES, third, 0.0)


def pack_core(info, cells, packed, start, build):
    for q in range(QUADS):
        pack_column(info, cells, q, packed, start + q, (0, 0) if build else None)


def pack_faces(infos, pieces, packed, start, build):
    for side in range(2):
        sign = 2 * side - 1
        for y in range(CY):
            shift = (sign * CX, 0) if build else None
            pack_column(infos[side], pieces[side], y, packed, start + 2 * side + y, shift)
        for x in range(CX):
            shift = (0, sign * CY) if build else None
            source = 2 * x + 1 - side
            pack_column(infos[2], pieces[2], source, packed, start + 4 + 2 * x + side, shift)


def pack_corners(info, cells, packed, start, build):
    for side_x in range(2):
        for side_y in range(2):
            shift = ((2 * side_x - 1) * CX, (2 * side_y - 1) * CY) if build else None
            source = 2 * side_x + 1 - side_y
            pack_column(info, cells, source, packed, start + 2 * side_x + side_y, shift)


def core_columns(q):
    return [q ^ k for k in range(4)]


def face_columns(q):
    x, y = q >> 1, q & 1
    return [2 * x, 2 * x + 1, 4 + y, 6 + y]


def overflow_of(packed, columns, z, first):
    lane = lane_index((8, LANES))
    total = jnp.zeros((8, LANES), jnp.float32)
    for index, column in enumerate(columns):
        tile = packed[column * CZ + z, 2]
        at = 8 * (first + index)
        moved = pltpu.roll(tile, at, 1) if at else tile
        total = jnp.where((lane >= at) & (lane < at + 8), moved, total)
    return total


def spread(row):
    return jnp.broadcast_to(row, (8, LANES))


def couple(x_i, y_i, z_i, w_i, x_j, y_j, z_j, w_j):
    delta_x = x_j - x_i
    delta_y = y_j - y_i
    delta_z = z_j - z_i
    squared = delta_x * delta_x + delta_y * delta_y + delta_z * delta_z
    held = jnp.maximum(squared, CLOSEST_SQUARED)
    inverse = lax.rsqrt(held)
    distance = held * inverse
    scaled = distance * lax.rsqrt(w_i + w_j)
    value = (lax.erf(scaled) - lax.erf(distance)) * inverse
    return jnp.where(squared < CUT_SQUARED, value, 0.0)


def to_rows(sums, block):
    here = lane_index((8, LANES)) - row_index((8, LANES)) == 8 * block
    return jnp.where(here, jnp.sum(sums, axis=1, keepdims=True), 0.0)


def build_cell(cell, tiles, turned, beside, kernels, below):
    for index, tile in enumerate(tiles):
        for row in range(6):
            beside[index, row] = spread(tile[row : row + 1])
    own = None
    if below is not None:
        own = lane_index((8, LANES)) - row_index((8, LANES)) - below
    rows_s = jnp.zeros((8, LANES), jnp.float32)
    rows_t = rows_s
    for group in GROUPS:
        mine = []
        for block in group:
            columns = turned[cell, 8 * block : 8 * block + 8, :]
            mine.append([jnp.broadcast_to(columns[:, k : k + 1], (8, LANES)) for k in range(4)])
        sums_s = [jnp.zeros((8, LANES), jnp.float32) for _ in group]
        sums_t = list(sums_s)
        for index in range(len(tiles)):
            line = [beside[index, k] for k in range(6)]
            for at, block in enumerate(group):
                value = couple(*mine[at], *line[:4])
                if own is not None and index < 2:
                    value = jnp.where(own == 8 * block - LANES * index, 0.0, value)
                kernels[cell, block, index] = value
                sums_s[at] = sums_s[at] + value * line[4]
                sums_t[at] = sums_t[at] + value * line[5]
        for at, block in enumerate(group):
            rows_s = rows_s + to_rows(sums_s[at], block)
            rows_t = rows_t + to_rows(sums_t[at], block)
    return jnp.sum(rows_s, axis=0, keepdims=True), jnp.sum(rows_t, axis=0, keepdims=True)


def core_kernel(core, kernels, out, spill, turned, packed, beside):
    pack_core(core, core, packed, 0, True)
    for cell in range(CELLS):
        here = (cell // CZ) * EZ + cell % CZ + 1
        turned[cell] = core[here].T[: 8 * BLOCKS]

    def one_cell(cell, _):
        q, z = cell // CZ, cell % CZ
        columns = core_columns(q)
        tiles = [packed[c * CZ + z, half] for c in columns for half in range(2)]
        below = spread(core[q * EZ + z, 7:8, :]).astype(jnp.int32)
        row_s, row_t = build_cell(cell, tiles, turned, beside, kernels, below)
        out[cell, 0:1, :] = row_s
        out[cell, 1:2, :] = row_t
        spill[cell] = overflow_of(packed, columns, z, 0)
        return 0

    lax.fori_loop(0, CELLS, one_cell, 0)


def face_kernel(x_low, x_high, beyond, turned, before, spill_before, kernels, out, spill, packed, beside):
    pieces = [x_low, x_high, beyond]
    pack_faces(pieces, pieces, packed, 0, True)

    def one_cell(cell, _):
        q, z = cell // CZ, cell % CZ
        columns = face_columns(q)
        tiles = [packed[c * CZ + z, half] for c in columns for half in range(2)]
        row_s, row_t = build_cell(cell, tiles, turned, beside, kernels, None)
        out[cell, 0:1, :] = row_s + before[cell, 0:1, :]
        out[cell, 1:2, :] = row_t + before[cell, 1:2, :]
        spill[cell] = spill_before[cell] + overflow_of(packed, columns, z, 4)
        return 0

    lax.fori_loop(0, CELLS, one_cell, 0)


def finish_cell(info, cell, here, row_s, row_t, diagonal, out):
    scale = PAIR_SCALE / diagonal[pl.ds(cell, 1), :]
    live = lane_index((1, LANES)) < info[here, 7:8, :].astype(jnp.int32)
    out[cell, 0:1, :] = jnp.where(live, row_s * scale, 0.0)
    out[cell, 1:2, :] = jnp.where(live, row_t * scale, 0.0)


def corner_kernel(corners, turned, before, spill_before, core, diagonal, kernels, out, packed, beside):
    pack_corners(corners, corners, packed, 0, True)

    def one_cell(cell, _):
        q, z = cell // CZ, cell % CZ
        tiles = [packed[q * CZ + z, half] for half in range(2)]
        tiles.append(spill_before[cell] + overflow_of(packed, [q], z, 8))
        row_s, row_t = build_cell(cell, tiles, turned, beside, kernels, None)
        row_s = row_s + before[cell, 0:1, :]
        row_t = row_t + before[cell, 1:2, :]
        finish_cell(core, cell, q * EZ + z + 1, row_s, row_t, diagonal, out)
        return 0

    lax.fori_loop(0, CELLS, one_cell, 0, unroll=2)


IN_VMEM = pl.BlockSpec(memory_space=VMEM)
PAIR = jax.ShapeDtypeStruct((CELLS, 2, LANES), jnp.float32)
SPILL = jax.ShapeDtypeStruct((CELLS, 8, LANES), jnp.float32)
TURNED = jax.ShapeDtypeStruct((CELLS, 8 * BLOCKS, 8), jnp.float32)
CORE_TILES, FACE_TILES, CORNER_TILES = 8, 8, 3


def held(tiles):
    return VMEM((CELLS, BLOCKS, tiles, 8, LANES), jnp.float32)


def call(kernel, outs, scratch, tiles, *arrays):
    work = CELLS * BLOCKS * tiles * 8 * LANES
    return pl.pallas_call(
        kernel,
        out_shape=outs,
        in_specs=[IN_VMEM] * len(arrays),
        out_specs=jax.tree.map(lambda _: IN_VMEM, outs),
        scratch_shapes=scratch,
        compiler_params=params(8),
        cost_estimate=pl.CostEstimate(
            flops=30 * work, bytes_accessed=8 * work, transcendentals=4 * work
        ),
    )(*arrays)


def packs(columns):
    return VMEM((columns * CZ, 3, 8, LANES), jnp.float32)


def besides(tiles):
    return VMEM((tiles, 6, 8, LANES), jnp.float32)


def build_core(core):
    return call(
        core_kernel,
        (held(CORE_TILES), PAIR, SPILL, TURNED),
        [packs(4), besides(CORE_TILES)],
        CORE_TILES,
        core,
    )


def build_faces(pieces, turned, before, spill):
    return call(
        face_kernel,
        (held(FACE_TILES), PAIR, SPILL),
        [packs(8), besides(FACE_TILES)],
        FACE_TILES,
        *pieces,
        turned,
        before,
        spill,
    )


def build_corners(corners, turned, before, spill, core, diagonal):
    return call(
        corner_kernel,
        (held(CORNER_TILES), PAIR),
        [packs(4), besides(CORNER_TILES)],
        CORNER_TILES,
        corners,
        turned,
        before,
        spill,
        core,
        diagonal,
    )


def apply_tiles(infos, pieces, stored, diagonal, out, wides, packed):
    for piece, wide in zip(pieces, wides):
        wide[:, 0:2, :] = piece[...]
        wide[:, 2:8, :] = jnp.zeros((wide.shape[0], 6, LANES), jnp.float32)
    pack_core(infos[0], wides[0], packed, 0, False)
    pack_faces(infos[1:4], wides[1:4], packed, 4, False)
    pack_corners(infos[4], wides[4], packed, 12, False)

    def one_cell(cell, _):
        q, z = cell // CZ, cell % CZ
        columns = core_columns(q) + [4 + c for c in face_columns(q)] + [12 + q]
        tiles = [packed[c * CZ + z, half] for c in columns for half in range(2)]
        tiles.append(overflow_of(packed, columns, z, 0))
        sums_s = [jnp.zeros((8, LANES), jnp.float32) for _ in range(BLOCKS)]
        sums_t = list(sums_s)
        where = [(ref, index) for ref in stored for index in range(ref.shape[2])]
        for tile, (ref, index) in zip(tiles, where):
            line_s = spread(tile[0:1])
            line_t = spread(tile[1:2])
            for block in range(BLOCKS):
                value = ref[cell, block, index]
                sums_s[block] = sums_s[block] + value * line_s
                sums_t[block] = sums_t[block] + value * line_t
        rows_s = jnp.zeros((8, LANES), jnp.float32)
        rows_t = rows_s
        for block in range(BLOCKS):
            rows_s = rows_s + to_rows(sums_s[block], block)
            rows_t = rows_t + to_rows(sums_t[block], block)
        row_s = jnp.sum(rows_s, axis=0, keepdims=True)
        row_t = jnp.sum(rows_t, axis=0, keepdims=True)
        finish_cell(infos[0], cell, q * EZ + z + 1, row_s, row_t, diagonal, out)
        return 0

    lax.fori_loop(0, CELLS, one_cell, 0)


def apply_kernel(*refs):
    infos, pieces, stored, (diagonal, out), wides, (packed,) = split(refs, 5, 5, 3, 2, 5, 1)
    apply_tiles(infos, pieces, stored, diagonal, out, wides, packed)


def split(refs, *sizes):
    parts = []
    for size in sizes:
        parts.append(refs[:size])
        refs = refs[size:]
    return parts


def last_kernel(*refs):
    infos, pieces, stored, rest, wides, (packed,) = split(refs, 5, 5, 3, 6, 5, 1)
    diagonal, slots, first, second, moments, third = rest
    apply_tiles(infos, pieces, stored, diagonal, third, wides, packed)
    d = diagonal[...][:, None, :]
    v_0 = slots[:, 4:6, :]
    v_1 = first[...]
    v_2 = second[...]
    d_0 = d * v_0
    d_2 = d * v_2
    parts = [d_0 * v_0, d_0 * v_1, d * v_1 * v_1, d_2 * v_1, d_2 * v_2, d_2 * third[...]]
    for index, part in enumerate(parts + [v_0, v_1, v_2]):
        moments[2 * index : 2 * index + 2, :] = jnp.sum(part, axis=0)
    moments[18:24, :] = jnp.zeros((6, LANES), jnp.float32)


def apply_scratch(pieces):
    return [VMEM((piece.shape[0], 8, LANES), jnp.float32) for piece in pieces] + [packs(16)]


def apply_stored(infos, pieces, stored, diagonal):
    stored = [pltpu.with_memory_space_constraint(tiles, VMEM) for tiles in stored]
    return call(
        apply_kernel, PAIR, apply_scratch(pieces), 2, *infos, *pieces, *stored, diagonal
    )


def apply_last(infos, pieces, stored, diagonal, slots, first, second):
    stored = [pltpu.with_memory_space_constraint(tiles, VMEM) for tiles in stored]
    third = VMEM((CELLS, 2, LANES), jnp.float32)
    return call(
        last_kernel,
        jax.ShapeDtypeStruct((24, LANES), jnp.float32),
        [third] + apply_scratch(pieces),
        2,
        *infos,
        *pieces,
        *stored,
        diagonal,
        slots,
        first,
        second,
    )


def solve(g):
    tiny = 1e-6
    h = [g[k] + g[k + 1] for k in range(5)]
    ratio_1 = h[1] / h[0]
    ratio_2 = h[2] / h[0]
    pivot_1 = h[2] - ratio_1 * h[1]
    mixed = h[3] - ratio_1 * h[2]
    rest_1 = g[1] - ratio_1 * g[0]
    live_1 = pivot_1 > tiny * h[2]
    safe_1 = jnp.where(live_1, pivot_1, 1.0)
    ratio_3 = jnp.where(live_1, mixed / safe_1, 0.0)
    pivot_2 = h[4] - ratio_2 * h[2] - ratio_3 * mixed
    rest_2 = g[2] - ratio_2 * g[0] - ratio_3 * rest_1
    live_2 = live_1 & (pivot_2 > tiny * h[4])
    c_2 = jnp.where(live_2, rest_2 / jnp.where(live_2, pivot_2, 1.0), 0.0)
    c_1 = jnp.where(live_1, (rest_1 - mixed * c_2) / safe_1, 0.0)
    c_0 = (g[0] - h[1] * c_1 - h[2] * c_2) / h[0]
    return c_0, c_1, c_2


def finish_kernel(counts, moments, slots, first, second, atoms, out):
    summed = jnp.broadcast_to(jnp.sum(moments[...], axis=1, keepdims=True), (24, LANES))
    rows = [summed[2 * k : 2 * k + 2] for k in range(9)]
    c_0, c_1, c_2 = solve(rows[:6])
    totals = c_0 * rows[6] + c_1 * rows[7] + c_2 * rows[8]
    balance = totals[0:1] / totals[1:2]
    sign = jnp.concatenate([jnp.ones((1, LANES), jnp.float32), -balance], axis=0)
    c_0, c_1, c_2 = c_0 * sign, c_1 * sign, c_2 * sign
    high_rows = out.shape[0]
    padded = (high_rows + 15) // 16 * 16
    row_low = row_index((LANES, LANES))
    row_high = row_index((padded, LANES))

    def one_cell(cell, total):
        mixed = c_0 * slots[cell, 4:6, :] + c_1 * first[cell] + c_2 * second[cell]
        charge = jnp.sum(mixed, axis=0, keepdims=True)
        live = lane_index((1, LANES)) < counts[cell]
        pointer = jnp.where(live, atoms[pl.ds(cell, 1), :], -1)
        placed = jnp.where((pointer >> 7) == row_high, charge, 0.0)
        part_0 = placed.astype(jnp.bfloat16)
        left = placed - part_0.astype(jnp.float32)
        part_1 = left.astype(jnp.bfloat16)
        part_2 = (left - part_1.astype(jnp.float32)).astype(jnp.bfloat16)
        lows = jnp.where((pointer & 127) == row_low, 1.0, 0.0).astype(jnp.bfloat16)
        parts = jnp.concatenate([part_0, part_1, part_2], axis=0)
        return total + lax.dot_general(
            parts, lows, (((1,), (1,)), ((), ())), preferred_element_type=jnp.float32
        )

    total = jnp.zeros((3 * padded, LANES), jnp.float32)
    total = lax.fori_loop(0, CELLS, one_cell, total, unroll=8)
    total = total[2 * padded :] + total[padded : 2 * padded] + total[:padded]
    out[...] = total[:high_rows]


def finish(counts, moments, slots, first, second, atoms, atoms_local):
    return pl.pallas_call(
        finish_kernel,
        out_shape=jax.ShapeDtypeStruct((atoms_local // LANES, LANES), jnp.float32),
        in_specs=[pl.BlockSpec(memory_space=SMEM)] + [pl.BlockSpec(memory_space=VMEM)] * 5,
        out_specs=pl.BlockSpec(memory_space=VMEM),
        compiler_params=params(8),
    )(counts, moments, slots, first, second, atoms)


def partner(block, axis, apart):
    count = lax.axis_size(axis)
    route = [(low, low ^ (1 << apart)) for low in range(count)]
    return lax.ppermute(block, axis, route)


def from_behind(x, axis, by):
    peers = lax.axis_size(axis)
    return lax.ppermute(x, axis, [(i, (i + by) % peers) for i in range(peers)])


def with_z_faces(cells):
    cells = cells.reshape((QUADS, CZ) + cells.shape[1:])
    faces = jnp.concatenate([cells[:, -1:], cells[:, :1]], axis=1)
    other = partner(faces, "gx", 0)
    return jnp.concatenate([other[:, 0:1], cells, other[:, 1:2]], axis=1)


def flat(columns):
    return columns.reshape((-1,) + columns.shape[-2:])


def extended(cells):
    core = with_z_faces(cells)
    beyond = partner(core, "gx", 1)
    low = from_behind(jnp.concatenate([core[2:], beyond[2:]], axis=0), "gx", 4)
    high = from_behind(jnp.concatenate([core[:2], beyond[:2]], axis=0), "gx", -4)
    corners = jnp.concatenate([low[2:], high[2:]], axis=0)
    return [flat(part) for part in (core, low[:2], high[:2], beyond, corners)]


def global_sum(values):
    count = lax.axis_size("gx")
    if count & (count - 1):
        return lax.psum(values, "gx")
    for bit in range(count.bit_length() - 1):
        values = values + partner(values, "gx", bit)
    return values


def local(cell_offsets, electronegativity, hardness, charge_widths, cell_counts, cell_atoms):
    slots, diagonal = prepare(
        cell_counts, cell_offsets, electronegativity, hardness, charge_widths, cell_atoms
    )
    core = with_z_faces(slots)
    low = from_behind(core[2:], "gx", 4)
    high = from_behind(core[:2], "gx", -4)
    beyond = partner(core, "gx", 1)
    core_tiles, sums, spill, turned = build_core(flat(core))
    low, high, sums = lax.optimization_barrier((low, high, sums))
    corners = partner(jnp.concatenate([low, high], axis=0), "gx", 1)
    pieces = [flat(part) for part in (low, high, beyond)]
    face_tiles, sums, spill = build_faces(pieces, turned, sums, spill)
    infos = [flat(core)] + pieces + [flat(corners)]
    corner_tiles, first = build_corners(flat(corners), turned, sums, spill, flat(core), diagonal)
    stored = [core_tiles, face_tiles, corner_tiles]
    second = apply_stored(infos, extended(first), stored, diagonal)
    moments = apply_last(infos, extended(second), stored, diagonal, slots, first, second)
    moments = global_sum(moments)
    charges = finish(
        cell_counts, moments, slots, first, second, cell_atoms, cell_offsets.shape[1]
    )
    return charges.reshape(-1)


def solution(mesh):
    placed = (
        P(None, ("grp", "gx")),
        P(("grp", "gx")),
        P(("grp", "gx")),
        P(("grp", "gx")),
        P(("grp", "gx")),
        P(("grp", "gx"), None),
    )
    return jax.shard_map(
        local, mesh=mesh, in_specs=placed, out_specs=P(("grp", "gx")), check_vma=False
    )
```

```python
import functools
import math

import jax
import jax.numpy as jnp
from jax import lax
from jax.experimental import pallas as pl
from jax.experimental.pallas import tpu as pltpu
from jax.sharding import PartitionSpec as P

CX = 2
CY = 2
CZ = 8
EZ = CZ + 2
CELLS = CX * CY * CZ
QUADS = CX * CY
LANES = 128
BLOCKS = 11
GROUPS = ((0, 1, 2, 3), (4, 5, 6, 7), (8, 9, 10))

COULOMB = 14.399645
ROOT_PI = math.sqrt(math.pi)
SCREEN = 1.0 / (math.sqrt(2.0) * 3.0)
EWALD_SELF = math.sqrt(2.0 / math.pi) / 3.0
SIDE = 12.0 * SCREEN
CUT_SQUARED = (12.0 * SCREEN) ** 2
CLOSEST_SQUARED = (0.5 * SCREEN) ** 2
PAIR_SCALE = COULOMB * SCREEN

VMEM = pltpu.VMEM
SMEM = pltpu.SMEM


def params(mib):
    return pltpu.CompilerParams(vmem_limit_bytes=mib * 2**20)


def lane_index(shape):
    return lax.broadcasted_iota(jnp.int32, shape, len(shape) - 1)


def row_index(shape):
    return lax.broadcasted_iota(jnp.int32, shape, len(shape) - 2)


def prepare_kernel(
    counts_hbm, offsets, negativity, hardness, widths, atoms, slots, diagonal,
    counts, raw_offsets, raw_negativity, raw_hardness, raw_widths, raw_atoms, table, sems,
):
    copies = [
        pltpu.make_async_copy(source, target, sems.at[index])
        for index, (source, target) in enumerate(
            [
                (counts_hbm, counts),
                (offsets, raw_offsets),
                (negativity, raw_negativity),
                (hardness, raw_hardness),
                (widths, raw_widths),
                (atoms, raw_atoms),
            ]
        )
    ]
    for copy in copies:
        copy.start()
    for copy in copies:
        copy.wait()
    chunks = table.shape[0]
    for chunk in range(chunks):
        here = slice(chunk * LANES, (chunk + 1) * LANES)
        table[chunk, 0:3, :] = raw_offsets[:, here]
        table[chunk, 3:4, :] = raw_widths[chunk : chunk + 1, :]
        table[chunk, 4:5, :] = raw_negativity[chunk : chunk + 1, :]
        table[chunk, 5:6, :] = raw_hardness[chunk : chunk + 1, :]
        table[chunk, 6:8, :] = jnp.zeros((2, LANES), jnp.float32)

    def one_cell(cell, _):
        count = counts[cell]
        occupied = lane_index((1, LANES)) < count
        pointer = jnp.where(occupied, raw_atoms[pl.ds(cell, 1), :], 0)
        high = jnp.broadcast_to(pointer >> 7, (8, LANES))
        low = jnp.broadcast_to(pointer & 127, (8, LANES))
        picked = jnp.zeros((8, LANES), jnp.float32)
        for chunk in range(chunks):
            part = jnp.take_along_axis(table[chunk], low, axis=1)
            picked = jnp.where(high == chunk, part, picked)
        width = jnp.where(occupied, picked[3:4], 1.0)
        diag = jnp.where(
            occupied, picked[5:6] + COULOMB * (1.0 / (width * ROOT_PI) - EWALD_SELF), 1.0
        )
        negative = jnp.where(occupied, picked[4:5], 0.0)
        place = jnp.where(
            row_index((8, LANES)) == 0, cell // (CY * CZ), (cell // CZ) % CY
        ).astype(jnp.float32)
        place = jnp.where(row_index((8, LANES)) < 2, place, 0.0)
        slots[cell, 0:3, :] = ((picked + place) * SIDE)[0:3]
        slots[cell, 3:4, :] = (2.0 * SCREEN * SCREEN) * width * width
        slots[cell, 4:5, :] = -negative / diag
        slots[cell, 5:6, :] = jnp.where(occupied, 1.0 / diag, 0.0)
        slots[cell, 6:7, :] = jnp.zeros((1, LANES), jnp.float32)
        slots[cell, 7:8, :] = jnp.full((1, LANES), count.astype(jnp.float32))
        diagonal[pl.ds(cell, 1), :] = diag
        return 0

    lax.fori_loop(0, CELLS, one_cell, 0, unroll=4)


def prepare(counts, offsets, negativity, hardness, widths, atoms):
    chunks = offsets.shape[1] // LANES
    plane = (chunks, LANES)
    return pl.pallas_call(
        prepare_kernel,
        out_shape=(
            jax.ShapeDtypeStruct((CELLS, 8, LANES), jnp.float32),
            jax.ShapeDtypeStruct((CELLS, LANES), jnp.float32),
        ),
        in_specs=[pl.BlockSpec(memory_space=pltpu.HBM)] * 6,
        out_specs=(pl.BlockSpec(memory_space=VMEM), pl.BlockSpec(memory_space=VMEM)),
        scratch_shapes=[
            SMEM(counts.shape, jnp.int32),
            VMEM(offsets.shape, jnp.float32),
            VMEM(plane, jnp.float32),
            VMEM(plane, jnp.float32),
            VMEM(plane, jnp.float32),
            VMEM(atoms.shape, jnp.int32),
            VMEM((chunks, 8, LANES), jnp.float32),
            pltpu.SemaphoreType.DMA((6,)),
        ],
        compiler_params=params(8),
    )(
        *[
            pltpu.with_memory_space_constraint(array, pltpu.HBM)
            for array in (
                counts,
                offsets,
                negativity.reshape(plane),
                hardness.reshape(plane),
                widths.reshape(plane),
                atoms,
            )
        ]
    )


def pack_column(info, cells, source, spreads, spills, target, shift):
    lane = lane_index((8, LANES))
    row = row_index((8, LANES))
    for z in range(CZ):
        base = source * EZ + z
        low, mid, top = [spread(info[base + k, 7:8, :]).astype(jnp.int32) for k in range(3)]
        end = low + mid - LANES
        tiles = [cells[base + k] for k in range(3)]
        if shift is not None:
            for k in range(3):
                offset = jnp.where(row == 2, (k - 1) * SIDE, 0.0)
                for axis in range(2):
                    offset = jnp.where(row == axis, shift[axis] * SIDE, offset)
                tiles[k] = tiles[k] + offset
        second = jnp.take_along_axis(tiles[1], (lane - low) & 127, axis=1)
        third = jnp.take_along_axis(tiles[2], (lane - end) & 127, axis=1)
        halves = [jnp.where(lane < low, tiles[0], second), jnp.where(lane < end, second, third)]
        for half, tile in enumerate(halves):
            for index in range(spreads.shape[2]):
                spreads[target * CZ + z, half, index] = spread(tile[index : index + 1])
        spills[target * CZ + z] = jnp.where(lane < end + top - LANES, third, 0.0)


def pack_core(info, cells, spreads, spills, start, build):
    for q in range(QUADS):
        pack_column(info, cells, q, spreads, spills, start + q, (0, 0) if build else None)


def pack_faces(infos, pieces, spreads, spills, start, build):
    for side in range(2):
        sign = 2 * side - 1
        for y in range(CY):
            shift = (sign * CX, 0) if build else None
            pack_column(infos[side], pieces[side], y, spreads, spills, start + 2 * side + y, shift)
        for x in range(CX):
            shift = (0, sign * CY) if build else None
            source = 2 * x + 1 - side
            pack_column(infos[2], pieces[2], source, spreads, spills, start + 4 + 2 * x + side, shift)


def pack_corners(info, cells, spreads, spills, start, build):
    for side_x in range(2):
        for side_y in range(2):
            shift = ((2 * side_x - 1) * CX, (2 * side_y - 1) * CY) if build else None
            source = 2 * side_x + 1 - side_y
            pack_column(info, cells, source, spreads, spills, start + 2 * side_x + side_y, shift)


def core_columns(q):
    return [q ^ k for k in range(4)]


def face_columns(q):
    x, y = q >> 1, q & 1
    return [2 * x, 2 * x + 1, 4 + y, 6 + y]


def overflow_of(spills, columns, z, first):
    lane = lane_index((8, LANES))
    total = jnp.zeros((8, LANES), jnp.float32)
    for index, column in enumerate(columns):
        tile = spills[column * CZ + z]
        at = 8 * (first + index)
        moved = pltpu.roll(tile, at, 1) if at else tile
        total = jnp.where((lane >= at) & (lane < at + 8), moved, total)
    return total


def spread(row):
    return jnp.broadcast_to(row, (8, LANES))


def couple(x_i, y_i, z_i, w_i, x_j, y_j, z_j, w_j):
    delta_x = x_j - x_i
    delta_y = y_j - y_i
    delta_z = z_j - z_i
    squared = delta_x * delta_x + delta_y * delta_y + delta_z * delta_z
    held = jnp.maximum(squared, CLOSEST_SQUARED)
    inverse = lax.rsqrt(held)
    distance = held * inverse
    scaled = distance * lax.rsqrt(w_i + w_j)
    value = (lax.erf(scaled) - lax.erf(distance)) * inverse
    return jnp.where(squared < CUT_SQUARED, value, 0.0)


def to_rows(sums, block):
    here = lane_index((8, LANES)) - row_index((8, LANES)) == 8 * block
    return jnp.where(here, jnp.sum(sums, axis=1, keepdims=True), 0.0)


def add_rows(cell, sums, rows):
    for index in range(2):
        total = jnp.zeros((8, LANES), jnp.float32)
        for block in range(BLOCKS):
            total = total + to_rows(sums[cell, block, index], block)
        rows.append(jnp.sum(total, axis=0, keepdims=True))


def finish_cells(info, sums, diagonal, out):
    def one_cell(cell, _):
        rows = []
        add_rows(cell, sums, rows)
        here = (cell // CZ) * EZ + cell % CZ + 1
        scale = PAIR_SCALE / diagonal[pl.ds(cell, 1), :]
        live = lane_index((1, LANES)) < info[here, 7:8, :].astype(jnp.int32)
        out[cell, 0:1, :] = jnp.where(live, rows[0] * scale, 0.0)
        out[cell, 1:2, :] = jnp.where(live, rows[1] * scale, 0.0)
        return 0

    lax.fori_loop(0, CELLS, one_cell, 0, unroll=4)


def build_cell(cell, lines, turned, kernels, before, sums, below):
    own = None
    if below is not None:
        own = lane_index((8, LANES)) - row_index((8, LANES)) - below
    for group in GROUPS:
        mine = [[turned[cell, block, k] for k in range(4)] for block in group]
        if before is None:
            sums_s = [jnp.zeros((8, LANES), jnp.float32) for _ in group]
            sums_t = list(sums_s)
        else:
            sums_s = [before[cell, block, 0] for block in group]
            sums_t = [before[cell, block, 1] for block in group]
        for index, line_of in enumerate(lines):
            line = [line_of(k) for k in range(6)]
            for at, block in enumerate(group):
                value = couple(*mine[at], *line[:4])
                if own is not None and index < 2:
                    value = jnp.where(own == 8 * block - LANES * index, 0.0, value)
                kernels[cell, block, index] = value
                sums_s[at] = sums_s[at] + value * line[4]
                sums_t[at] = sums_t[at] + value * line[5]
        for at, block in enumerate(group):
            sums[cell, block, 0] = sums_s[at]
            sums[cell, block, 1] = sums_t[at]


def lines_of(spreads, columns, z):
    def line(column, half):
        return lambda k: spreads[column * CZ + z, half, k]

    return [line(column, half) for column in columns for half in range(2)]


def core_kernel(core, kernels, sums, spill, turned, spreads, spills):
    for cell in range(CELLS):
        columns = core[(cell // CZ) * EZ + cell % CZ + 1].T
        for block in range(BLOCKS):
            for k in range(4):
                column = columns[8 * block : 8 * block + 8, k : k + 1]
                turned[cell, block, k] = jnp.broadcast_to(column, (8, LANES))
    pack_core(core, core, spreads, spills, 0, True)

    def one_spill(cell, _):
        spill[cell] = overflow_of(spills, core_columns(cell // CZ), cell % CZ, 0)
        return 0

    lax.fori_loop(0, CELLS, one_spill, 0, unroll=4)

    def one_cell(cell, _):
        q, z = cell // CZ, cell % CZ
        below = spread(core[q * EZ + z, 7:8, :]).astype(jnp.int32)
        build_cell(cell, lines_of(spreads, core_columns(q), z), turned, kernels, None, sums, below)
        return 0

    lax.fori_loop(0, CELLS, one_cell, 0)


def face_kernel(x_low, x_high, beyond, turned, before, spill_before, kernels, sums, spill, spreads, spills):
    pieces = [x_low, x_high, beyond]
    pack_faces(pieces, pieces, spreads, spills, 0, True)

    def one_spill(cell, _):
        found = overflow_of(spills, face_columns(cell // CZ), cell % CZ, 4)
        spill[cell] = spill_before[cell] + found
        return 0

    lax.fori_loop(0, CELLS, one_spill, 0, unroll=4)

    def one_cell(cell, _):
        lines = lines_of(spreads, face_columns(cell // CZ), cell % CZ)
        build_cell(cell, lines, turned, kernels, before, sums, None)
        return 0

    lax.fori_loop(0, CELLS, one_cell, 0)


def corner_kernel(
    corners, turned, before, spill_before, core, diagonal, kernels, out, spreads, spills, rest, sums
):
    pack_corners(corners, corners, spreads, spills, 0, True)

    def one_spill(cell, _):
        tile = spill_before[cell] + overflow_of(spills, [cell // CZ], cell % CZ, 8)
        for k in range(6):
            rest[cell, k] = spread(tile[k : k + 1])
        return 0

    lax.fori_loop(0, CELLS, one_spill, 0, unroll=4)

    def one_cell(cell, _):
        lines = lines_of(spreads, [cell // CZ], cell % CZ) + [lambda k: rest[cell, k]]
        build_cell(cell, lines, turned, kernels, before, sums, None)
        return 0

    lax.fori_loop(0, CELLS, one_cell, 0, unroll=2)
    finish_cells(core, sums, diagonal, out)


IN_VMEM = pl.BlockSpec(memory_space=VMEM)
PAIR = jax.ShapeDtypeStruct((CELLS, 2, LANES), jnp.float32)
SPILL = jax.ShapeDtypeStruct((CELLS, 8, LANES), jnp.float32)
SUMS = jax.ShapeDtypeStruct((CELLS, BLOCKS, 2, 8, LANES), jnp.float32)
TURNED = jax.ShapeDtypeStruct((CELLS, BLOCKS, 4, 8, LANES), jnp.float32)
CORE_TILES, FACE_TILES, CORNER_TILES = 8, 8, 3


def held(tiles):
    return VMEM((CELLS, BLOCKS, tiles, 8, LANES), jnp.float32)


def call(kernel, outs, scratch, tiles, *arrays):
    work = CELLS * BLOCKS * tiles * 8 * LANES
    return pl.pallas_call(
        kernel,
        out_shape=outs,
        in_specs=[IN_VMEM] * len(arrays),
        out_specs=jax.tree.map(lambda _: IN_VMEM, outs),
        scratch_shapes=scratch,
        compiler_params=params(8),
        cost_estimate=pl.CostEstimate(
            flops=30 * work, bytes_accessed=8 * work, transcendentals=4 * work
        ),
    )(*arrays)


def packs(columns, rows):
    return [
        VMEM((columns * CZ, 2, rows, 8, LANES), jnp.float32),
        VMEM((columns * CZ, 8, LANES), jnp.float32),
    ]


def build_core(core):
    return call(
        core_kernel, (held(CORE_TILES), SUMS, SPILL, TURNED), packs(4, 6), CORE_TILES, core
    )


def build_faces(pieces, turned, before, spill):
    return call(
        face_kernel,
        (held(FACE_TILES), SUMS, SPILL),
        packs(8, 6),
        FACE_TILES,
        *pieces,
        turned,
        before,
        spill,
    )


def build_corners(corners, turned, before, spill, core, diagonal):
    scratch = packs(4, 6) + [
        VMEM((CELLS, 6, 8, LANES), jnp.float32),
        VMEM(SUMS.shape, jnp.float32),
    ]
    return call(
        corner_kernel,
        (held(CORNER_TILES), PAIR),
        scratch,
        CORNER_TILES,
        corners,
        turned,
        before,
        spill,
        core,
        diagonal,
    )


def apply_tiles(infos, pieces, stored, diagonal, out, wides, spreads, spills, rest, sums):
    for piece, wide in zip(pieces, wides):
        wide[:, 0:2, :] = piece[...]
    pack_core(infos[0], wides[0], spreads, spills, 0, False)
    pack_faces(infos[1:4], wides[1:4], spreads, spills, 4, False)
    pack_corners(infos[4], wides[4], spreads, spills, 12, False)

    def columns_of(q):
        return core_columns(q) + [4 + c for c in face_columns(q)] + [12 + q]

    def one_spill(cell, _):
        tile = overflow_of(spills, columns_of(cell // CZ), cell % CZ, 0)
        for k in range(2):
            rest[cell, k] = spread(tile[k : k + 1])
        return 0

    lax.fori_loop(0, CELLS, one_spill, 0, unroll=4)

    def one_cell(cell, _):
        lines = lines_of(spreads, columns_of(cell // CZ), cell % CZ) + [lambda k: rest[cell, k]]
        sums_s = [jnp.zeros((8, LANES), jnp.float32) for _ in range(BLOCKS)]
        sums_t = list(sums_s)
        where = [(ref, index) for ref in stored for index in range(ref.shape[2])]
        for line, (ref, index) in zip(lines, where):
            line_s, line_t = line(0), line(1)
            for block in range(BLOCKS):
                value = ref[cell, block, index]
                sums_s[block] = sums_s[block] + value * line_s
                sums_t[block] = sums_t[block] + value * line_t
        for block in range(BLOCKS):
            sums[cell, block, 0] = sums_s[block]
            sums[cell, block, 1] = sums_t[block]
        return 0

    lax.fori_loop(0, CELLS, one_cell, 0, unroll=2)
    finish_cells(infos[0], sums, diagonal, out)


def split(refs, *sizes):
    parts = []
    for size in sizes:
        parts.append(refs[:size])
        refs = refs[size:]
    return parts


def apply_kernel(*refs):
    infos, pieces, stored, (diagonal, out), wides, work = split(refs, 5, 5, 3, 2, 5, 4)
    apply_tiles(infos, pieces, stored, diagonal, out, wides, *work)


def last_kernel(*refs):
    infos, pieces, stored, rest, wides, work = split(refs, 5, 5, 3, 6, 5, 4)
    diagonal, slots, first, second, moments, third = rest
    apply_tiles(infos, pieces, stored, diagonal, third, wides, *work)
    d = diagonal[...][:, None, :]
    v_0 = slots[:, 4:6, :]
    v_1 = first[...]
    v_2 = second[...]
    d_0 = d * v_0
    d_2 = d * v_2
    parts = [d_0 * v_0, d_0 * v_1, d * v_1 * v_1, d_2 * v_1, d_2 * v_2, d_2 * third[...]]
    for index, part in enumerate(parts + [v_0, v_1, v_2]):
        moments[2 * index : 2 * index + 2, :] = jnp.sum(part, axis=0)
    moments[18:24, :] = jnp.zeros((6, LANES), jnp.float32)


def apply_scratch(pieces):
    wides = [VMEM((piece.shape[0], 8, LANES), jnp.float32) for piece in pieces]
    rest = VMEM((CELLS, 2, 8, LANES), jnp.float32)
    return wides + packs(16, 2) + [rest, VMEM(SUMS.shape, jnp.float32)]


def apply_stored(infos, pieces, stored, diagonal):
    stored = [pltpu.with_memory_space_constraint(tiles, VMEM) for tiles in stored]
    return call(
        apply_kernel, PAIR, apply_scratch(pieces), 2, *infos, *pieces, *stored, diagonal
    )


def apply_last(infos, pieces, stored, diagonal, slots, first, second):
    stored = [pltpu.with_memory_space_constraint(tiles, VMEM) for tiles in stored]
    third = VMEM((CELLS, 2, LANES), jnp.float32)
    return call(
        last_kernel,
        jax.ShapeDtypeStruct((24, LANES), jnp.float32),
        [third] + apply_scratch(pieces),
        2,
        *infos,
        *pieces,
        *stored,
        diagonal,
        slots,
        first,
        second,
    )


def solve(g):
    tiny = 1e-6
    h = [g[k] + g[k + 1] for k in range(5)]
    ratio_1 = h[1] / h[0]
    ratio_2 = h[2] / h[0]
    pivot_1 = h[2] - ratio_1 * h[1]
    mixed = h[3] - ratio_1 * h[2]
    rest_1 = g[1] - ratio_1 * g[0]
    live_1 = pivot_1 > tiny * h[2]
    safe_1 = jnp.where(live_1, pivot_1, 1.0)
    ratio_3 = jnp.where(live_1, mixed / safe_1, 0.0)
    pivot_2 = h[4] - ratio_2 * h[2] - ratio_3 * mixed
    rest_2 = g[2] - ratio_2 * g[0] - ratio_3 * rest_1
    live_2 = live_1 & (pivot_2 > tiny * h[4])
    c_2 = jnp.where(live_2, rest_2 / jnp.where(live_2, pivot_2, 1.0), 0.0)
    c_1 = jnp.where(live_1, (rest_1 - mixed * c_2) / safe_1, 0.0)
    c_0 = (g[0] - h[1] * c_1 - h[2] * c_2) / h[0]
    return c_0, c_1, c_2


def finish_kernel(counts, moments, slots, first, second, atoms, out):
    summed = jnp.sum(jnp.sum(moments[...], axis=0), axis=1, keepdims=True)
    summed = jnp.broadcast_to(summed, (24, LANES))
    rows = [summed[2 * k : 2 * k + 2] for k in range(9)]
    c_0, c_1, c_2 = solve(rows[:6])
    totals = c_0 * rows[6] + c_1 * rows[7] + c_2 * rows[8]
    balance = totals[0:1] / totals[1:2]
    sign = jnp.concatenate([jnp.ones((1, LANES), jnp.float32), -balance], axis=0)
    c_0, c_1, c_2 = c_0 * sign, c_1 * sign, c_2 * sign
    high_rows = out.shape[0]
    padded = (high_rows + 15) // 16 * 16
    row_low = row_index((LANES, LANES))
    row_high = row_index((padded, LANES))

    def one_cell(cell, total):
        mixed = c_0 * slots[cell, 4:6, :] + c_1 * first[cell] + c_2 * second[cell]
        charge = jnp.sum(mixed, axis=0, keepdims=True)
        live = lane_index((1, LANES)) < counts[cell]
        pointer = jnp.where(live, atoms[pl.ds(cell, 1), :], -1)
        placed = jnp.where((pointer >> 7) == row_high, charge, 0.0)
        part_0 = placed.astype(jnp.bfloat16)
        left = placed - part_0.astype(jnp.float32)
        part_1 = left.astype(jnp.bfloat16)
        part_2 = (left - part_1.astype(jnp.float32)).astype(jnp.bfloat16)
        lows = jnp.where((pointer & 127) == row_low, 1.0, 0.0).astype(jnp.bfloat16)
        parts = jnp.concatenate([part_0, part_1, part_2], axis=0)
        return total + lax.dot_general(
            parts, lows, (((1,), (1,)), ((), ())), preferred_element_type=jnp.float32
        )

    total = jnp.zeros((3 * padded, LANES), jnp.float32)
    total = lax.fori_loop(0, CELLS, one_cell, total, unroll=8)
    total = total[2 * padded :] + total[padded : 2 * padded] + total[:padded]
    out[...] = total[:high_rows]


def finish(counts, moments, slots, first, second, atoms, atoms_local):
    return pl.pallas_call(
        finish_kernel,
        out_shape=jax.ShapeDtypeStruct((atoms_local // LANES, LANES), jnp.float32),
        in_specs=[pl.BlockSpec(memory_space=SMEM)] + [pl.BlockSpec(memory_space=VMEM)] * 5,
        out_specs=pl.BlockSpec(memory_space=VMEM),
        compiler_params=params(8),
    )(counts, moments, slots, first, second, atoms)


def partner(block, axis, apart):
    count = lax.axis_size(axis)
    route = [(low, low ^ (1 << apart)) for low in range(count)]
    return lax.ppermute(block, axis, route)


def from_behind(x, axis, by):
    peers = lax.axis_size(axis)
    return lax.ppermute(x, axis, [(i, (i + by) % peers) for i in range(peers)])


def with_z_faces(cells):
    cells = cells.reshape((QUADS, CZ) + cells.shape[1:])
    faces = jnp.concatenate([cells[:, -1:], cells[:, :1]], axis=1)
    other = partner(faces, "gx", 0)
    return jnp.concatenate([other[:, 0:1], cells, other[:, 1:2]], axis=1)


def flat(columns):
    return columns.reshape((-1,) + columns.shape[-2:])


def extended(cells):
    core = with_z_faces(cells)
    beyond = partner(core, "gx", 1)
    low = from_behind(jnp.concatenate([core[2:], beyond[2:]], axis=0), "gx", 4)
    high = from_behind(jnp.concatenate([core[:2], beyond[:2]], axis=0), "gx", -4)
    corners = jnp.concatenate([low[2:], high[2:]], axis=0)
    return [flat(part) for part in (core, low[:2], high[:2], beyond, corners)]


def local(cell_offsets, electronegativity, hardness, charge_widths, cell_counts, cell_atoms):
    slots, diagonal = prepare(
        cell_counts, cell_offsets, electronegativity, hardness, charge_widths, cell_atoms
    )
    core = with_z_faces(slots)
    low = from_behind(core[2:], "gx", 4)
    high = from_behind(core[:2], "gx", -4)
    beyond = partner(core, "gx", 1)
    core_tiles, sums, spill, turned = build_core(flat(core))
    low, high, sums = lax.optimization_barrier((low, high, sums))
    corners = partner(jnp.concatenate([low, high], axis=0), "gx", 1)
    pieces = [flat(part) for part in (low, high, beyond)]
    face_tiles, sums, spill = build_faces(pieces, turned, sums, spill)
    infos = [flat(core)] + pieces + [flat(corners)]
    corner_tiles, first = build_corners(flat(corners), turned, sums, spill, flat(core), diagonal)
    stored = [core_tiles, face_tiles, corner_tiles]
    second = apply_stored(infos, extended(first), stored, diagonal)
    moments = apply_last(infos, extended(second), stored, diagonal, slots, first, second)
    moments = lax.all_gather(moments, "gx")
    charges = finish(
        cell_counts, moments, slots, first, second, cell_atoms, cell_offsets.shape[1]
    )
    return charges.reshape(-1)


def solution(mesh):
    placed = (
        P(None, ("grp", "gx")),
        P(("grp", "gx")),
        P(("grp", "gx")),
        P(("grp", "gx")),
        P(("grp", "gx")),
        P(("grp", "gx"), None),
    )
    return jax.shard_map(
        local, mesh=mesh, in_specs=placed, out_specs=P(("grp", "gx")), check_vma=False
    )
```

```python
import functools
import math

import jax
import jax.numpy as jnp
from jax import lax
from jax.experimental import pallas as pl
from jax.experimental.pallas import tpu as pltpu
from jax.sharding import PartitionSpec as P

CX = 2
CY = 2
CZ = 8
EZ = CZ + 2
CELLS = CX * CY * CZ
QUADS = CX * CY
LANES = 128
BLOCKS = 11
GROUPS = ((0, 1, 2, 3), (4, 5, 6, 7), (8, 9, 10))

COULOMB = 14.399645
ROOT_PI = math.sqrt(math.pi)
SCREEN = 1.0 / (math.sqrt(2.0) * 3.0)
EWALD_SELF = math.sqrt(2.0 / math.pi) / 3.0
SIDE = 12.0 * SCREEN
CUT_SQUARED = (12.0 * SCREEN) ** 2
CLOSEST_SQUARED = (0.5 * SCREEN) ** 2
PAIR_SCALE = COULOMB * SCREEN

VMEM = pltpu.VMEM
SMEM = pltpu.SMEM


def params(mib):
    return pltpu.CompilerParams(vmem_limit_bytes=mib * 2**20)


def lane_index(shape):
    return lax.broadcasted_iota(jnp.int32, shape, len(shape) - 1)


def row_index(shape):
    return lax.broadcasted_iota(jnp.int32, shape, len(shape) - 2)


def prepare_kernel(
    counts_hbm, offsets, negativity, hardness, widths, atoms, slots, diagonal,
    counts, raw_offsets, raw_negativity, raw_hardness, raw_widths, raw_atoms, table, sems,
):
    copies = [
        pltpu.make_async_copy(source, target, sems.at[index])
        for index, (source, target) in enumerate(
            [
                (counts_hbm, counts),
                (offsets, raw_offsets),
                (negativity, raw_negativity),
                (hardness, raw_hardness),
                (widths, raw_widths),
                (atoms, raw_atoms),
            ]
        )
    ]
    for copy in copies:
        copy.start()
    for copy in copies:
        copy.wait()
    chunks = table.shape[0]
    for chunk in range(chunks):
        here = slice(chunk * LANES, (chunk + 1) * LANES)
        table[chunk, 0:3, :] = raw_offsets[:, here]
        table[chunk, 3:4, :] = raw_widths[chunk : chunk + 1, :]
        table[chunk, 4:5, :] = raw_negativity[chunk : chunk + 1, :]
        table[chunk, 5:6, :] = raw_hardness[chunk : chunk + 1, :]
        table[chunk, 6:8, :] = jnp.zeros((2, LANES), jnp.float32)

    def one_cell(cell, _):
        count = counts[cell]
        occupied = lane_index((1, LANES)) < count
        pointer = jnp.where(occupied, raw_atoms[pl.ds(cell, 1), :], 0)
        high = jnp.broadcast_to(pointer >> 7, (8, LANES))
        low = jnp.broadcast_to(pointer & 127, (8, LANES))
        picked = jnp.zeros((8, LANES), jnp.float32)
        for chunk in range(chunks):
            part = jnp.take_along_axis(table[chunk], low, axis=1)
            picked = jnp.where(high == chunk, part, picked)
        width = jnp.where(occupied, picked[3:4], 1.0)
        diag = jnp.where(
            occupied, picked[5:6] + COULOMB * (1.0 / (width * ROOT_PI) - EWALD_SELF), 1.0
        )
        negative = jnp.where(occupied, picked[4:5], 0.0)
        place = jnp.where(
            row_index((8, LANES)) == 0, cell // (CY * CZ), (cell // CZ) % CY
        ).astype(jnp.float32)
        place = jnp.where(row_index((8, LANES)) < 2, place, 0.0)
        slots[cell, 0:3, :] = ((picked + place) * SIDE)[0:3]
        slots[cell, 3:4, :] = (2.0 * SCREEN * SCREEN) * width * width
        slots[cell, 4:5, :] = -negative / diag
        slots[cell, 5:6, :] = jnp.where(occupied, 1.0 / diag, 0.0)
        slots[cell, 6:7, :] = jnp.zeros((1, LANES), jnp.float32)
        slots[cell, 7:8, :] = jnp.full((1, LANES), count.astype(jnp.float32))
        diagonal[pl.ds(cell, 1), :] = diag
        return 0

    lax.fori_loop(0, CELLS, one_cell, 0, unroll=4)


def prepare(counts, offsets, negativity, hardness, widths, atoms):
    chunks = offsets.shape[1] // LANES
    plane = (chunks, LANES)
    return pl.pallas_call(
        prepare_kernel,
        out_shape=(
            jax.ShapeDtypeStruct((CELLS, 8, LANES), jnp.float32),
            jax.ShapeDtypeStruct((CELLS, LANES), jnp.float32),
        ),
        in_specs=[pl.BlockSpec(memory_space=pltpu.HBM)] * 6,
        out_specs=(pl.BlockSpec(memory_space=VMEM), pl.BlockSpec(memory_space=VMEM)),
        scratch_shapes=[
            SMEM(counts.shape, jnp.int32),
            VMEM(offsets.shape, jnp.float32),
            VMEM(plane, jnp.float32),
            VMEM(plane, jnp.float32),
            VMEM(plane, jnp.float32),
            VMEM(atoms.shape, jnp.int32),
            VMEM((chunks, 8, LANES), jnp.float32),
            pltpu.SemaphoreType.DMA((6,)),
        ],
        compiler_params=params(8),
    )(
        *[
            pltpu.with_memory_space_constraint(array, pltpu.HBM)
            for array in (
                counts,
                offsets,
                negativity.reshape(plane),
                hardness.reshape(plane),
                widths.reshape(plane),
                atoms,
            )
        ]
    )


def pack_column(info, cells, source, spreads, spills, target, shift):
    lane = lane_index((8, LANES))
    row = row_index((8, LANES))
    for z in range(CZ):
        base = source * EZ + z
        low, mid, top = [spread(info[base + k, 7:8, :]).astype(jnp.int32) for k in range(3)]
        end = low + mid - LANES
        tiles = [cells[base + k] for k in range(3)]
        if shift is not None:
            for k in range(3):
                offset = jnp.where(row == 2, (k - 1) * SIDE, 0.0)
                for axis in range(2):
                    offset = jnp.where(row == axis, shift[axis] * SIDE, offset)
                tiles[k] = tiles[k] + offset
        second = jnp.take_along_axis(tiles[1], (lane - low) & 127, axis=1)
        third = jnp.take_along_axis(tiles[2], (lane - end) & 127, axis=1)
        halves = [jnp.where(lane < low, tiles[0], second), jnp.where(lane < end, second, third)]
        for half, tile in enumerate(halves):
            for index in range(spreads.shape[2]):
                spreads[target * CZ + z, half, index] = spread(tile[index : index + 1])
        spills[target * CZ + z] = jnp.where(lane < end + top - LANES, third, 0.0)


def pack_core(info, cells, spreads, spills, start, build):
    for q in range(QUADS):
        pack_column(info, cells, q, spreads, spills, start + q, (0, 0) if build else None)


def pack_faces(infos, pieces, spreads, spills, start, build):
    for side in range(2):
        sign = 2 * side - 1
        for y in range(CY):
            shift = (sign * CX, 0) if build else None
            pack_column(infos[side], pieces[side], y, spreads, spills, start + 2 * side + y, shift)
        for x in range(CX):
            shift = (0, sign * CY) if build else None
            source = 2 * x + 1 - side
            pack_column(infos[2], pieces[2], source, spreads, spills, start + 4 + 2 * x + side, shift)


def pack_corners(info, cells, spreads, spills, start, build):
    for side_x in range(2):
        for side_y in range(2):
            shift = ((2 * side_x - 1) * CX, (2 * side_y - 1) * CY) if build else None
            source = 2 * side_x + 1 - side_y
            pack_column(info, cells, source, spreads, spills, start + 2 * side_x + side_y, shift)


def core_columns(q):
    return [q ^ k for k in range(4)]


def face_columns(q):
    x, y = q >> 1, q & 1
    return [2 * x, 2 * x + 1, 4 + y, 6 + y]


def overflow_of(spills, columns, z, first):
    lane = lane_index((8, LANES))
    total = jnp.zeros((8, LANES), jnp.float32)
    for index, column in enumerate(columns):
        tile = spills[column * CZ + z]
        at = 8 * (first + index)
        moved = pltpu.roll(tile, at, 1) if at else tile
        total = jnp.where((lane >= at) & (lane < at + 8), moved, total)
    return total


def spread(row):
    return jnp.broadcast_to(row, (8, LANES))


def couple(x_i, y_i, z_i, w_i, x_j, y_j, z_j, w_j):
    delta_x = x_j - x_i
    delta_y = y_j - y_i
    delta_z = z_j - z_i
    squared = delta_x * delta_x + delta_y * delta_y + delta_z * delta_z
    held = jnp.maximum(squared, CLOSEST_SQUARED)
    inverse = lax.rsqrt(held)
    distance = held * inverse
    scaled = distance * lax.rsqrt(w_i + w_j)
    value = (lax.erf(scaled) - lax.erf(distance)) * inverse
    return jnp.where(squared < CUT_SQUARED, value, 0.0)


def to_rows(sums, block):
    here = lane_index((8, LANES)) - row_index((8, LANES)) == 8 * block
    return jnp.where(here, jnp.sum(sums, axis=1, keepdims=True), 0.0)


def add_rows(cell, sums, rows):
    for index in range(2):
        total = jnp.zeros((8, LANES), jnp.float32)
        for block in range(BLOCKS):
            total = total + to_rows(sums[cell, block, index], block)
        rows.append(jnp.sum(total, axis=0, keepdims=True))


def finish_cells(info, sums, diagonal, out):
    def one_cell(cell, _):
        rows = []
        add_rows(cell, sums, rows)
        here = (cell // CZ) * EZ + cell % CZ + 1
        scale = PAIR_SCALE / diagonal[pl.ds(cell, 1), :]
        live = lane_index((1, LANES)) < info[here, 7:8, :].astype(jnp.int32)
        out[cell, 0:1, :] = jnp.where(live, rows[0] * scale, 0.0)
        out[cell, 1:2, :] = jnp.where(live, rows[1] * scale, 0.0)
        return 0

    lax.fori_loop(0, CELLS, one_cell, 0, unroll=4)


def build_cell(cell, lines, turned, kernels, before, sums, below):
    own = None
    if below is not None:
        own = lane_index((8, LANES)) - row_index((8, LANES)) - below
    for group in GROUPS:
        mine = [[turned[cell, block, k] for k in range(4)] for block in group]
        if before is None:
            sums_s = [jnp.zeros((8, LANES), jnp.float32) for _ in group]
            sums_t = list(sums_s)
        else:
            sums_s = [before[cell, block, 0] for block in group]
            sums_t = [before[cell, block, 1] for block in group]
        for index, line_of in enumerate(lines):
            line = [line_of(k) for k in range(6)]
            for at, block in enumerate(group):
                value = couple(*mine[at], *line[:4])
                if own is not None and index < 2:
                    value = jnp.where(own == 8 * block - LANES * index, 0.0, value)
                kernels[cell, block, index] = value
                sums_s[at] = sums_s[at] + value * line[4]
                sums_t[at] = sums_t[at] + value * line[5]
        for at, block in enumerate(group):
            sums[cell, block, 0] = sums_s[at]
            sums[cell, block, 1] = sums_t[at]


def lines_of(spreads, columns, z):
    def line(column, half):
        return lambda k: spreads[column * CZ + z, half, k]

    return [line(column, half) for column in columns for half in range(2)]


def core_kernel(core, kernels, sums, spill, turned, spreads, spills):
    for cell in range(CELLS):
        columns = core[(cell // CZ) * EZ + cell % CZ + 1].T
        for block in range(BLOCKS):
            for k in range(4):
                column = columns[8 * block : 8 * block + 8, k : k + 1]
                turned[cell, block, k] = jnp.broadcast_to(column, (8, LANES))
    pack_core(core, core, spreads, spills, 0, True)

    def one_spill(cell, _):
        spill[cell] = overflow_of(spills, core_columns(cell // CZ), cell % CZ, 0)
        return 0

    lax.fori_loop(0, CELLS, one_spill, 0, unroll=4)

    def one_cell(cell, _):
        q, z = cell // CZ, cell % CZ
        below = spread(core[q * EZ + z, 7:8, :]).astype(jnp.int32)
        build_cell(cell, lines_of(spreads, core_columns(q), z), turned, kernels, None, sums, below)
        return 0

    lax.fori_loop(0, CELLS, one_cell, 0)


def face_kernel(x_low, x_high, beyond, turned, before, spill_before, kernels, sums, spill, spreads, spills):
    pieces = [x_low, x_high, beyond]
    pack_faces(pieces, pieces, spreads, spills, 0, True)

    def one_spill(cell, _):
        found = overflow_of(spills, face_columns(cell // CZ), cell % CZ, 4)
        spill[cell] = spill_before[cell] + found
        return 0

    lax.fori_loop(0, CELLS, one_spill, 0, unroll=4)

    def one_cell(cell, _):
        lines = lines_of(spreads, face_columns(cell // CZ), cell % CZ)
        build_cell(cell, lines, turned, kernels, before, sums, None)
        return 0

    lax.fori_loop(0, CELLS, one_cell, 0)


def corner_kernel(
    corners, turned, before, spill_before, core, diagonal, kernels, out, spreads, spills, rest, sums
):
    pack_corners(corners, corners, spreads, spills, 0, True)

    def one_spill(cell, _):
        tile = spill_before[cell] + overflow_of(spills, [cell // CZ], cell % CZ, 8)
        for k in range(6):
            rest[cell, k] = spread(tile[k : k + 1])
        return 0

    lax.fori_loop(0, CELLS, one_spill, 0, unroll=4)

    def one_cell(cell, _):
        lines = lines_of(spreads, [cell // CZ], cell % CZ) + [lambda k: rest[cell, k]]
        build_cell(cell, lines, turned, kernels, before, sums, None)
        return 0

    lax.fori_loop(0, CELLS, one_cell, 0, unroll=2)
    finish_cells(core, sums, diagonal, out)


IN_VMEM = pl.BlockSpec(memory_space=VMEM)
PAIR = jax.ShapeDtypeStruct((CELLS, 2, LANES), jnp.float32)
SPILL = jax.ShapeDtypeStruct((CELLS, 8, LANES), jnp.float32)
SUMS = jax.ShapeDtypeStruct((CELLS, BLOCKS, 2, 8, LANES), jnp.float32)
TURNED = jax.ShapeDtypeStruct((CELLS, BLOCKS, 4, 8, LANES), jnp.float32)
CORE_TILES, FACE_TILES, CORNER_TILES = 8, 8, 3


def held(tiles):
    return VMEM((CELLS, BLOCKS, tiles, 8, LANES), jnp.float32)


def call(kernel, outs, scratch, tiles, *arrays):
    work = CELLS * BLOCKS * tiles * 8 * LANES
    return pl.pallas_call(
        kernel,
        out_shape=outs,
        in_specs=[IN_VMEM] * len(arrays),
        out_specs=jax.tree.map(lambda _: IN_VMEM, outs),
        scratch_shapes=scratch,
        compiler_params=params(8),
        cost_estimate=pl.CostEstimate(
            flops=30 * work, bytes_accessed=8 * work, transcendentals=4 * work
        ),
    )(*arrays)


def packs(columns, rows):
    return [
        VMEM((columns * CZ, 2, rows, 8, LANES), jnp.float32),
        VMEM((columns * CZ, 8, LANES), jnp.float32),
    ]


def build_core(core):
    return call(
        core_kernel, (held(CORE_TILES), SUMS, SPILL, TURNED), packs(4, 6), CORE_TILES, core
    )


def build_faces(pieces, turned, before, spill):
    return call(
        face_kernel,
        (held(FACE_TILES), SUMS, SPILL),
        packs(8, 6),
        FACE_TILES,
        *pieces,
        turned,
        before,
        spill,
    )


def build_corners(corners, turned, before, spill, core, diagonal):
    scratch = packs(4, 6) + [
        VMEM((CELLS, 6, 8, LANES), jnp.float32),
        VMEM(SUMS.shape, jnp.float32),
    ]
    return call(
        corner_kernel,
        (held(CORNER_TILES), PAIR),
        scratch,
        CORNER_TILES,
        corners,
        turned,
        before,
        spill,
        core,
        diagonal,
    )


def apply_cells(stored, lines_for, before, sums):
    def one_cell(cell, _):
        if before is None:
            sums_s = [jnp.zeros((8, LANES), jnp.float32) for _ in range(BLOCKS)]
            sums_t = list(sums_s)
        else:
            sums_s = [before[cell, block, 0] for block in range(BLOCKS)]
            sums_t = [before[cell, block, 1] for block in range(BLOCKS)]
        for index, line in enumerate(lines_for(cell)):
            line_s, line_t = line(0), line(1)
            for block in range(BLOCKS):
                value = stored[cell, block, index]
                sums_s[block] = sums_s[block] + value * line_s
                sums_t[block] = sums_t[block] + value * line_t
        for block in range(BLOCKS):
            sums[cell, block, 0] = sums_s[block]
            sums[cell, block, 1] = sums_t[block]
        return 0

    lax.fori_loop(0, CELLS, one_cell, 0, unroll=2)


def widen(pieces, wides):
    for piece, wide in zip(pieces, wides):
        wide[:, 0:2, :] = piece[...]


def apply_core_kernel(info, core, stored, sums, spill, wide, spreads, spills):
    widen([core], [wide])
    pack_core(info, wide, spreads, spills, 0, False)

    def one_spill(cell, _):
        spill[cell] = overflow_of(spills, core_columns(cell // CZ), cell % CZ, 0)
        return 0

    lax.fori_loop(0, CELLS, one_spill, 0, unroll=4)
    apply_cells(
        stored, lambda cell: lines_of(spreads, core_columns(cell // CZ), cell % CZ), None, sums
    )


def apply_face_kernel(*refs):
    infos, pieces, (stored, before, spill_before, sums, spill), wides, (spreads, spills) = split(
        refs, 3, 3, 5, 3, 2
    )
    widen(pieces, wides)
    pack_faces(infos, wides, spreads, spills, 0, False)

    def one_spill(cell, _):
        found = overflow_of(spills, face_columns(cell // CZ), cell % CZ, 4)
        spill[cell] = spill_before[cell] + found
        return 0

    lax.fori_loop(0, CELLS, one_spill, 0, unroll=4)
    apply_cells(
        stored, lambda cell: lines_of(spreads, face_columns(cell // CZ), cell % CZ), before, sums
    )


def apply_corner_tiles(
    info, corners, stored, before, spill_before, core, diagonal, out, wide, spreads, spills, rest, sums
):
    widen([corners], [wide])
    pack_corners(info, wide, spreads, spills, 0, False)

    def one_spill(cell, _):
        tile = spill_before[cell] + overflow_of(spills, [cell // CZ], cell % CZ, 8)
        for k in range(2):
            rest[cell, k] = spread(tile[k : k + 1])
        return 0

    lax.fori_loop(0, CELLS, one_spill, 0, unroll=4)

    def lines_for(cell):
        return lines_of(spreads, [cell // CZ], cell % CZ) + [lambda k: rest[cell, k]]

    apply_cells(stored, lines_for, before, sums)
    finish_cells(core, sums, diagonal, out)


def split(refs, *sizes):
    parts = []
    for size in sizes:
        parts.append(refs[:size])
        refs = refs[size:]
    return parts


def apply_last_kernel(*refs):
    ins, (slots, first, second, moments, third), work = split(refs, 7, 5, 5)
    diagonal = ins[6]
    apply_corner_tiles(*ins, third, *work)
    d = diagonal[...][:, None, :]
    v_0 = slots[:, 4:6, :]
    v_1 = first[...]
    v_2 = second[...]
    d_0 = d * v_0
    d_2 = d * v_2
    parts = [d_0 * v_0, d_0 * v_1, d * v_1 * v_1, d_2 * v_1, d_2 * v_2, d_2 * third[...]]
    for index, part in enumerate(parts + [v_0, v_1, v_2]):
        moments[2 * index : 2 * index + 2, :] = jnp.sum(part, axis=0)
    moments[18:24, :] = jnp.zeros((6, LANES), jnp.float32)


def wide(piece):
    return VMEM((piece.shape[0], 8, LANES), jnp.float32)


def apply_core(info, core, stored):
    stored = pltpu.with_memory_space_constraint(stored, VMEM)
    scratch = [wide(core)] + packs(4, 2)
    return call(apply_core_kernel, (SUMS, SPILL), scratch, 2, info, core, stored)


def apply_faces(infos, pieces, stored, before, spill):
    stored = pltpu.with_memory_space_constraint(stored, VMEM)
    scratch = [wide(piece) for piece in pieces] + packs(8, 2)
    return call(
        apply_face_kernel, (SUMS, SPILL), scratch, 2, *infos, *pieces, stored, before, spill
    )


def apply_corners(info, corners, stored, before, spill, core, diagonal, last):
    stored = pltpu.with_memory_space_constraint(stored, VMEM)
    rest = VMEM((CELLS, 2, 8, LANES), jnp.float32)
    scratch = [wide(corners)] + packs(4, 2) + [rest, VMEM(SUMS.shape, jnp.float32)]
    arrays = [info, corners, stored, before, spill, core, diagonal]
    if last is None:
        return call(apply_corner_tiles, PAIR, scratch, 2, *arrays)
    third = VMEM((CELLS, 2, LANES), jnp.float32)
    out = jax.ShapeDtypeStruct((24, LANES), jnp.float32)
    return call(apply_last_kernel, out, [third] + scratch, 2, *arrays, *last)


def solve(g):
    tiny = 1e-6
    h = [g[k] + g[k + 1] for k in range(5)]
    ratio_1 = h[1] / h[0]
    ratio_2 = h[2] / h[0]
    pivot_1 = h[2] - ratio_1 * h[1]
    mixed = h[3] - ratio_1 * h[2]
    rest_1 = g[1] - ratio_1 * g[0]
    live_1 = pivot_1 > tiny * h[2]
    safe_1 = jnp.where(live_1, pivot_1, 1.0)
    ratio_3 = jnp.where(live_1, mixed / safe_1, 0.0)
    pivot_2 = h[4] - ratio_2 * h[2] - ratio_3 * mixed
    rest_2 = g[2] - ratio_2 * g[0] - ratio_3 * rest_1
    live_2 = live_1 & (pivot_2 > tiny * h[4])
    c_2 = jnp.where(live_2, rest_2 / jnp.where(live_2, pivot_2, 1.0), 0.0)
    c_1 = jnp.where(live_1, (rest_1 - mixed * c_2) / safe_1, 0.0)
    c_0 = (g[0] - h[1] * c_1 - h[2] * c_2) / h[0]
    return c_0, c_1, c_2


def finish_kernel(counts, moments, slots, first, second, atoms, out):
    summed = jnp.broadcast_to(jnp.sum(moments[...], axis=1, keepdims=True), (24, LANES))
    rows = [summed[2 * k : 2 * k + 2] for k in range(9)]
    c_0, c_1, c_2 = solve(rows[:6])
    totals = c_0 * rows[6] + c_1 * rows[7] + c_2 * rows[8]
    balance = totals[0:1] / totals[1:2]
    sign = jnp.concatenate([jnp.ones((1, LANES), jnp.float32), -balance], axis=0)
    c_0, c_1, c_2 = c_0 * sign, c_1 * sign, c_2 * sign
    high_rows = out.shape[0]
    padded = (high_rows + 15) // 16 * 16
    row_low = row_index((LANES, LANES))
    row_high = row_index((padded, LANES))

    def one_cell(cell, total):
        mixed = c_0 * slots[cell, 4:6, :] + c_1 * first[cell] + c_2 * second[cell]
        charge = jnp.sum(mixed, axis=0, keepdims=True)
        live = lane_index((1, LANES)) < counts[cell]
        pointer = jnp.where(live, atoms[pl.ds(cell, 1), :], -1)
        placed = jnp.where((pointer >> 7) == row_high, charge, 0.0)
        part_0 = placed.astype(jnp.bfloat16)
        left = placed - part_0.astype(jnp.float32)
        part_1 = left.astype(jnp.bfloat16)
        part_2 = (left - part_1.astype(jnp.float32)).astype(jnp.bfloat16)
        lows = jnp.where((pointer & 127) == row_low, 1.0, 0.0).astype(jnp.bfloat16)
        parts = jnp.concatenate([part_0, part_1, part_2], axis=0)
        return total + lax.dot_general(
            parts, lows, (((1,), (1,)), ((), ())), preferred_element_type=jnp.float32
        )

    total = jnp.zeros((3 * padded, LANES), jnp.float32)
    total = lax.fori_loop(0, CELLS, one_cell, total, unroll=8)
    total = total[2 * padded :] + total[padded : 2 * padded] + total[:padded]
    out[...] = total[:high_rows]


def finish(counts, moments, slots, first, second, atoms, atoms_local):
    return pl.pallas_call(
        finish_kernel,
        out_shape=jax.ShapeDtypeStruct((atoms_local // LANES, LANES), jnp.float32),
        in_specs=[pl.BlockSpec(memory_space=SMEM)] + [pl.BlockSpec(memory_space=VMEM)] * 5,
        out_specs=pl.BlockSpec(memory_space=VMEM),
        compiler_params=params(8),
    )(counts, moments, slots, first, second, atoms)


def partner(block, axis, mask):
    count = lax.axis_size(axis)
    return lax.ppermute(block, axis, [(low, low ^ mask) for low in range(count)])


def from_behind(x, axis, by):
    peers = lax.axis_size(axis)
    return lax.ppermute(x, axis, [(i, (i + by) % peers) for i in range(peers)])


def with_z_faces(cells):
    cells = cells.reshape((QUADS, CZ) + cells.shape[1:])
    faces = jnp.concatenate([cells[:, -1:], cells[:, :1]], axis=1)
    other = partner(faces, "gx", 1)
    return jnp.concatenate([other[:, 0:1], cells, other[:, 1:2]], axis=1)


def flat(columns):
    return columns.reshape((-1,) + columns.shape[-2:])


def exchange(cells, on_core, on_faces, on_corners):
    core = with_z_faces(cells)
    low = from_behind(core[2:], "gx", 4)
    high = from_behind(core[:2], "gx", -4)
    beyond = partner(core, "gx", 2)
    sums, spill, *more = on_core(flat(core))
    low, high, sums = lax.optimization_barrier((low, high, sums))
    corners = partner(jnp.concatenate([low, high], axis=0), "gx", 2)
    pieces = [flat(part) for part in (low, high, beyond)]
    sums, spill, *more = on_faces(pieces, sums, spill, *more)
    corners = flat(corners)
    return flat(core), pieces, corners, on_corners(corners, sums, spill, flat(core), *more)


def global_sum(values):
    count = lax.axis_size("gx")
    if count & (count - 1):
        return lax.psum(values, "gx")
    step = 1
    while step < count:
        if step >= 4 and 4 * step <= count:
            others = [partner(values, "gx", k * step) for k in (1, 2, 3)]
            values = (values + others[0]) + (others[1] + others[2])
            step *= 4
        else:
            values = values + partner(values, "gx", step)
            step *= 2
    return values


def local(cell_offsets, electronegativity, hardness, charge_widths, cell_counts, cell_atoms):
    slots, diagonal = prepare(
        cell_counts, cell_offsets, electronegativity, hardness, charge_widths, cell_atoms
    )
    stored = []

    def keep(tiles, *others):
        stored.append(tiles)
        return others

    core, pieces, corners, (first,) = exchange(
        slots,
        lambda core: keep(*build_core(core)),
        lambda faces, sums, spill, turned: keep(*build_faces(faces, turned, sums, spill)) + (turned,),
        lambda corners, sums, spill, core, turned: keep(
            *build_corners(corners, turned, sums, spill, core, diagonal)
        ),
    )

    def apply(cells, last):
        return exchange(
            cells,
            lambda own: apply_core(core, own, stored[0]),
            lambda faces, sums, spill: apply_faces(pieces, faces, stored[1], sums, spill),
            lambda others, sums, spill, _: apply_corners(
                corners, others, stored[2], sums, spill, core, diagonal, last
            ),
        )[3]

    second = apply(first, None)
    moments = global_sum(apply(second, (slots, first, second)))
    charges = finish(
        cell_counts, moments, slots, first, second, cell_atoms, cell_offsets.shape[1]
    )
    return charges.reshape(-1)


def solution(mesh):
    placed = (
        P(None, ("grp", "gx")),
        P(("grp", "gx")),
        P(("grp", "gx")),
        P(("grp", "gx")),
        P(("grp", "gx")),
        P(("grp", "gx"), None),
    )
    return jax.shard_map(
        local, mesh=mesh, in_specs=placed, out_specs=P(("grp", "gx")), check_vma=False
    )
```

```python
import functools
import math

import jax
import jax.numpy as jnp
from jax import lax
from jax.experimental import pallas as pl
from jax.experimental.pallas import tpu as pltpu
from jax.sharding import PartitionSpec as P

CX = 2
CY = 2
CZ = 8
EZ = CZ + 2
CELLS = CX * CY * CZ
QUADS = CX * CY
LANES = 128
BLOCKS = 11

COULOMB = 14.399645
ROOT_PI = math.sqrt(math.pi)
SCREEN = 1.0 / (math.sqrt(2.0) * 3.0)
EWALD_SELF = math.sqrt(2.0 / math.pi) / 3.0
SIDE = 12.0 * SCREEN
CUT_SQUARED = (12.0 * SCREEN) ** 2
CLOSEST_SQUARED = (0.5 * SCREEN) ** 2
PAIR_SCALE = COULOMB * SCREEN

VMEM = pltpu.VMEM
SMEM = pltpu.SMEM


def params(mib):
    return pltpu.CompilerParams(vmem_limit_bytes=mib * 2**20)


def lane_index(shape):
    return lax.broadcasted_iota(jnp.int32, shape, len(shape) - 1)


def row_index(shape):
    return lax.broadcasted_iota(jnp.int32, shape, len(shape) - 2)


def prepare_kernel(
    counts_hbm, offsets, negativity, hardness, widths, atoms, slots, diagonal,
    counts, raw_offsets, raw_negativity, raw_hardness, raw_widths, raw_atoms, table, sems,
):
    copies = [
        pltpu.make_async_copy(source, target, sems.at[index])
        for index, (source, target) in enumerate(
            [
                (counts_hbm, counts),
                (offsets, raw_offsets),
                (negativity, raw_negativity),
                (hardness, raw_hardness),
                (widths, raw_widths),
                (atoms, raw_atoms),
            ]
        )
    ]
    for copy in copies:
        copy.start()
    for copy in copies:
        copy.wait()
    chunks = table.shape[0]
    for chunk in range(chunks):
        here = slice(chunk * LANES, (chunk + 1) * LANES)
        table[chunk, 0:3, :] = raw_offsets[:, here]
        table[chunk, 3:4, :] = raw_widths[chunk : chunk + 1, :]
        table[chunk, 4:5, :] = raw_negativity[chunk : chunk + 1, :]
        table[chunk, 5:6, :] = raw_hardness[chunk : chunk + 1, :]
        table[chunk, 6:8, :] = jnp.zeros((2, LANES), jnp.float32)

    def one_cell(cell, _):
        count = counts[cell]
        occupied = lane_index((1, LANES)) < count
        pointer = jnp.where(occupied, raw_atoms[pl.ds(cell, 1), :], 0)
        high = jnp.broadcast_to(pointer >> 7, (8, LANES))
        low = jnp.broadcast_to(pointer & 127, (8, LANES))
        picked = jnp.zeros((8, LANES), jnp.float32)
        for chunk in range(chunks):
            part = jnp.take_along_axis(table[chunk], low, axis=1)
            picked = jnp.where(high == chunk, part, picked)
        width = jnp.where(occupied, picked[3:4], 1.0)
        diag = jnp.where(
            occupied, picked[5:6] + COULOMB * (1.0 / (width * ROOT_PI) - EWALD_SELF), 1.0
        )
        negative = jnp.where(occupied, picked[4:5], 0.0)
        place = jnp.where(
            row_index((8, LANES)) == 0, cell // (CY * CZ), (cell // CZ) % CY
        ).astype(jnp.float32)
        place = jnp.where(row_index((8, LANES)) < 2, place, 0.0)
        slots[cell, 0:3, :] = ((picked + place) * SIDE)[0:3]
        slots[cell, 3:4, :] = (2.0 * SCREEN * SCREEN) * width * width
        slots[cell, 4:5, :] = -negative / diag
        slots[cell, 5:6, :] = jnp.where(occupied, 1.0 / diag, 0.0)
        slots[cell, 6:7, :] = jnp.zeros((1, LANES), jnp.float32)
        slots[cell, 7:8, :] = jnp.full((1, LANES), count.astype(jnp.float32))
        diagonal[pl.ds(cell, 1), :] = diag
        return 0

    lax.fori_loop(0, CELLS, one_cell, 0, unroll=4)


def prepare(counts, offsets, negativity, hardness, widths, atoms):
    chunks = offsets.shape[1] // LANES
    plane = (chunks, LANES)
    return pl.pallas_call(
        prepare_kernel,
        out_shape=(
            jax.ShapeDtypeStruct((CELLS, 8, LANES), jnp.float32),
            jax.ShapeDtypeStruct((CELLS, LANES), jnp.float32),
        ),
        in_specs=[pl.BlockSpec(memory_space=pltpu.HBM)] * 6,
        out_specs=(pl.BlockSpec(memory_space=VMEM), pl.BlockSpec(memory_space=VMEM)),
        scratch_shapes=[
            SMEM(counts.shape, jnp.int32),
            VMEM(offsets.shape, jnp.float32),
            VMEM(plane, jnp.float32),
            VMEM(plane, jnp.float32),
            VMEM(plane, jnp.float32),
            VMEM(atoms.shape, jnp.int32),
            VMEM((chunks, 8, LANES), jnp.float32),
            pltpu.SemaphoreType.DMA((6,)),
        ],
        compiler_params=params(8),
    )(
        *[
            pltpu.with_memory_space_constraint(array, pltpu.HBM)
            for array in (
                counts,
                offsets,
                negativity.reshape(plane),
                hardness.reshape(plane),
                widths.reshape(plane),
                atoms,
            )
        ]
    )


def centred(axis, cells):
    return (cells - (CX / 2, CY / 2, 1 / 2)[axis]) * SIDE


def operand(tile, scale, one_row, norm_row):
    row = row_index((8, LANES))
    place = jnp.where(row < 3, tile, 0.0)
    norm = jnp.sum(place * place, axis=0, keepdims=True)
    rows = jnp.where(row == one_row, 1.0, jnp.where(row == norm_row, norm, scale * place))
    high = rows.astype(jnp.bfloat16).astype(jnp.float32)
    rest = rows - high
    middle = rest.astype(jnp.bfloat16).astype(jnp.float32)
    return high, middle, rest - middle


def own_operand(tile):
    high, middle, low = operand(tile, 1.0, 4, 3)
    return jnp.concatenate([high, high, middle, high, low, middle], axis=0)


def beside_operand(tile):
    high, middle, low = operand(tile, -2.0, 3, 4)
    return jnp.concatenate([high, middle, high, low, high, middle], axis=0).astype(jnp.bfloat16)


def pack_column(info, cells, source, operands, spreads, spills, target, shift):
    lane = lane_index((8, LANES))
    row = row_index((8, LANES))
    first = 3 if operands is not None else 0
    for z in range(CZ):
        base = source * EZ + z
        here = target * CZ + z
        low, mid, top = [spread(info[base + k, 7:8, :]).astype(jnp.int32) for k in range(3)]
        end = low + mid - LANES
        tiles = [cells[base + k] for k in range(3)]
        if operands is not None:
            for k in range(3):
                offset = jnp.where(row == 2, centred(2, k - 1), 0.0)
                for axis in range(2):
                    offset = jnp.where(row == axis, centred(axis, shift[axis]), offset)
                tiles[k] = tiles[k] + offset
        second = jnp.take_along_axis(tiles[1], (lane - low) & 127, axis=1)
        third = jnp.take_along_axis(tiles[2], (lane - end) & 127, axis=1)
        halves = [jnp.where(lane < low, tiles[0], second), jnp.where(lane < end, second, third)]
        for half, tile in enumerate(halves):
            for index in range(spreads.shape[2]):
                spreads[here, half, index] = spread(tile[first + index : first + index + 1])
            if operands is not None:
                operands[here, :, half * LANES : (half + 1) * LANES] = beside_operand(tile)
        spills[here] = jnp.where(lane < end + top - LANES, third, 0.0)


def pack_core(info, cells, operands, spreads, spills, start):
    for q in range(QUADS):
        pack_column(info, cells, q, operands, spreads, spills, start + q, (0, 0))


def pack_faces(infos, pieces, operands, spreads, spills, start):
    for side in range(2):
        sign = 2 * side - 1
        for y in range(CY):
            shift = (sign * CX, 0)
            pack_column(infos[side], pieces[side], y, operands, spreads, spills, start + 2 * side + y, shift)
        for x in range(CX):
            shift = (0, sign * CY)
            source = 2 * x + 1 - side
            pack_column(infos[2], pieces[2], source, operands, spreads, spills, start + 4 + 2 * x + side, shift)


def pack_corners(info, cells, operands, spreads, spills, start):
    for side_x in range(2):
        for side_y in range(2):
            shift = ((2 * side_x - 1) * CX, (2 * side_y - 1) * CY)
            source = 2 * side_x + 1 - side_y
            pack_column(info, cells, source, operands, spreads, spills, start + 2 * side_x + side_y, shift)


def core_columns(q):
    return [q ^ k for k in range(4)]


def face_columns(q):
    x, y = q >> 1, q & 1
    return [2 * x, 2 * x + 1, 4 + y, 6 + y]


def overflow_of(spills, columns, z, first):
    lane = lane_index((8, LANES))
    total = jnp.zeros((8, LANES), jnp.float32)
    for index, column in enumerate(columns):
        tile = spills[column * CZ + z]
        at = 8 * (first + index)
        moved = pltpu.roll(tile, at, 1) if at else tile
        total = jnp.where((lane >= at) & (lane < at + 8), moved, total)
    return total


def spread(row):
    return jnp.broadcast_to(row, (8, LANES))


def couple(squared, widths):
    held = jnp.maximum(squared, CLOSEST_SQUARED)
    inverse = lax.rsqrt(held)
    distance = held * inverse
    scaled = distance * lax.rsqrt(widths)
    value = (lax.erf(scaled) - lax.erf(distance)) * inverse
    return jnp.where(squared < CUT_SQUARED, value, 0.0)


def to_rows(sums, block):
    here = lane_index((8, LANES)) - row_index((8, LANES)) == 8 * block
    return jnp.where(here, jnp.sum(sums, axis=1, keepdims=True), 0.0)


def add_rows(cell, sums, rows):
    for index in range(2):
        total = jnp.zeros((8, LANES), jnp.float32)
        for block in range(BLOCKS):
            total = total + to_rows(sums[cell, block, index], block)
        rows.append(jnp.sum(total, axis=0, keepdims=True))


def finish_cells(info, sums, diagonal, out):
    def one_cell(cell, _):
        rows = []
        add_rows(cell, sums, rows)
        here = (cell // CZ) * EZ + cell % CZ + 1
        scale = PAIR_SCALE / diagonal[pl.ds(cell, 1), :]
        live = lane_index((1, LANES)) < info[here, 7:8, :].astype(jnp.int32)
        out[cell, 0:1, :] = jnp.where(live, rows[0] * scale, 0.0)
        out[cell, 1:2, :] = jnp.where(live, rows[1] * scale, 0.0)
        return 0

    lax.fori_loop(0, CELLS, one_cell, 0, unroll=4)


def build_cell(cell, lines, mine, turned, kernels, before, sums, below):
    own = None
    if below is not None:
        own = lane_index((8, LANES)) - row_index((8, LANES)) - below
    sums_s, sums_t = start_sums(cell, before)
    index = 0
    for other, line in lines:
        squares = lax.dot_general(
            mine[cell], other, (((1,), (0,)), ((), ())), preferred_element_type=jnp.float32
        )
        for half in range(other.shape[1] // LANES):
            width, line_s, line_t = [line(half, k) for k in range(3)]
            for block in range(BLOCKS):
                square = squares[8 * block : 8 * block + 8, half * LANES : (half + 1) * LANES]
                value = couple(square, turned[cell, block] + width)
                if own is not None and index < 2:
                    value = jnp.where(own == 8 * block - LANES * index, 0.0, value)
                kernels[cell, block, index] = value
                sums_s[block] = sums_s[block] + value * line_s
                sums_t[block] = sums_t[block] + value * line_t
            index += 1
    for block in range(BLOCKS):
        sums[cell, block, 0] = sums_s[block]
        sums[cell, block, 1] = sums_t[block]


def start_sums(cell, before):
    if before is None:
        zeros = [jnp.zeros((8, LANES), jnp.float32) for _ in range(BLOCKS)]
        return zeros, list(zeros)
    sums_s = [before[cell, block, 0] for block in range(BLOCKS)]
    return sums_s, [before[cell, block, 1] for block in range(BLOCKS)]


def groups_of(operands, spreads, columns, z):
    def group(column):
        here = column * CZ + z
        return operands[here], lambda half, k: spreads[here, half, k]

    return [group(column) for column in columns]


def lines_of(spreads, columns, z):
    def line(column, half):
        return lambda k: spreads[column * CZ + z, half, k]

    return [line(column, half) for column in columns for half in range(2)]


def core_kernel(core, kernels, sums, spill, mine, turned, operands, spreads, spills):
    row = row_index((8, LANES))
    middle = jnp.where(row == 2, centred(2, 0), jnp.where(row < 2, centred(0, 0), 0.0))
    for cell in range(CELLS):
        here = core[(cell // CZ) * EZ + cell % CZ + 1]
        mine[cell] = own_operand(here + middle).T[: 8 * BLOCKS + 8].astype(jnp.bfloat16)
        columns = here.T
        for block in range(BLOCKS):
            width = columns[8 * block : 8 * block + 8, 3:4]
            turned[cell, block] = jnp.broadcast_to(width, (8, LANES))
    pack_core(core, core, operands, spreads, spills, 0)

    def one_spill(cell, _):
        spill[cell] = overflow_of(spills, core_columns(cell // CZ), cell % CZ, 0)
        return 0

    lax.fori_loop(0, CELLS, one_spill, 0, unroll=4)

    def one_cell(cell, _):
        q, z = cell // CZ, cell % CZ
        below = spread(core[q * EZ + z, 7:8, :]).astype(jnp.int32)
        groups = groups_of(operands, spreads, core_columns(q), z)
        build_cell(cell, groups, mine, turned, kernels, None, sums, below)
        return 0

    lax.fori_loop(0, CELLS, one_cell, 0)


def face_kernel(
    x_low, x_high, beyond, mine, turned, before, spill_before, kernels, sums, spill,
    operands, spreads, spills,
):
    pieces = [x_low, x_high, beyond]
    pack_faces(pieces, pieces, operands, spreads, spills, 0)

    def one_spill(cell, _):
        found = overflow_of(spills, face_columns(cell // CZ), cell % CZ, 4)
        spill[cell] = spill_before[cell] + found
        return 0

    lax.fori_loop(0, CELLS, one_spill, 0, unroll=4)

    def one_cell(cell, _):
        groups = groups_of(operands, spreads, face_columns(cell // CZ), cell % CZ)
        build_cell(cell, groups, mine, turned, kernels, before, sums, None)
        return 0

    lax.fori_loop(0, CELLS, one_cell, 0)


def corner_kernel(
    corners, mine, turned, before, spill_before, core, diagonal, kernels, out,
    operands, spreads, spills, rest_operand, rest, sums,
):
    pack_corners(corners, corners, operands, spreads, spills, 0)

    def one_spill(cell, _):
        tile = spill_before[cell] + overflow_of(spills, [cell // CZ], cell % CZ, 8)
        for k in range(3):
            rest[cell, k] = spread(tile[3 + k : 4 + k])
        rest_operand[cell] = beside_operand(tile)
        return 0

    lax.fori_loop(0, CELLS, one_spill, 0, unroll=4)

    def one_cell(cell, _):
        groups = groups_of(operands, spreads, [cell // CZ], cell % CZ)
        groups.append((rest_operand[cell], lambda _, k: rest[cell, k]))
        build_cell(cell, groups, mine, turned, kernels, before, sums, None)
        return 0

    lax.fori_loop(0, CELLS, one_cell, 0, unroll=2)
    finish_cells(core, sums, diagonal, out)


IN_VMEM = pl.BlockSpec(memory_space=VMEM)
PAIR = jax.ShapeDtypeStruct((CELLS, 2, LANES), jnp.float32)
SPILL = jax.ShapeDtypeStruct((CELLS, 8, LANES), jnp.float32)
SUMS = jax.ShapeDtypeStruct((CELLS, BLOCKS, 2, 8, LANES), jnp.float32)
TURNED = jax.ShapeDtypeStruct((CELLS, BLOCKS, 8, LANES), jnp.float32)
PARTS = 48
MINE = jax.ShapeDtypeStruct((CELLS, 8 * BLOCKS + 8, PARTS), jnp.bfloat16)
CORE_TILES, FACE_TILES, CORNER_TILES = 8, 8, 3


def held(tiles):
    return VMEM((CELLS, BLOCKS, tiles, 8, LANES), jnp.float32)


def call(kernel, outs, scratch, tiles, *arrays):
    work = CELLS * BLOCKS * tiles * 8 * LANES
    return pl.pallas_call(
        kernel,
        out_shape=outs,
        in_specs=[IN_VMEM] * len(arrays),
        out_specs=jax.tree.map(lambda _: IN_VMEM, outs),
        scratch_shapes=scratch,
        compiler_params=params(8),
        cost_estimate=pl.CostEstimate(
            flops=30 * work, bytes_accessed=8 * work, transcendentals=4 * work
        ),
    )(*arrays)


def packs(columns, rows):
    return [
        VMEM((columns * CZ, 2, rows, 8, LANES), jnp.float32),
        VMEM((columns * CZ, 8, LANES), jnp.float32),
    ]


def operand_packs(columns):
    operands = VMEM((columns * CZ, PARTS, 2 * LANES), jnp.bfloat16)
    return [operands] + packs(columns, 3)


def build_core(core):
    outs = (held(CORE_TILES), SUMS, SPILL, MINE, TURNED)
    return call(core_kernel, outs, operand_packs(4), CORE_TILES, core)


def build_faces(pieces, mine, turned, before, spill):
    return call(
        face_kernel,
        (held(FACE_TILES), SUMS, SPILL),
        operand_packs(8),
        FACE_TILES,
        *pieces,
        mine,
        turned,
        before,
        spill,
    )


def build_corners(corners, mine, turned, before, spill, core, diagonal):
    scratch = operand_packs(4) + [
        VMEM((CELLS, PARTS, LANES), jnp.bfloat16),
        VMEM((CELLS, 3, 8, LANES), jnp.float32),
        VMEM(SUMS.shape, jnp.float32),
    ]
    return call(
        corner_kernel,
        (held(CORNER_TILES), PAIR),
        scratch,
        CORNER_TILES,
        corners,
        mine,
        turned,
        before,
        spill,
        core,
        diagonal,
    )


def apply_cells(stored, lines_for, before, sums):
    def one_cell(cell, _):
        sums_s, sums_t = start_sums(cell, before)
        for index, line in enumerate(lines_for(cell)):
            line_s, line_t = line(0), line(1)
            for block in range(BLOCKS):
                value = stored[cell, block, index]
                sums_s[block] = sums_s[block] + value * line_s
                sums_t[block] = sums_t[block] + value * line_t
        for block in range(BLOCKS):
            sums[cell, block, 0] = sums_s[block]
            sums[cell, block, 1] = sums_t[block]
        return 0

    lax.fori_loop(0, CELLS, one_cell, 0, unroll=2)


def widen(pieces, wides):
    for piece, wide in zip(pieces, wides):
        wide[:, 0:2, :] = piece[...]


def apply_core_kernel(info, core, stored, sums, spill, wide, spreads, spills):
    widen([core], [wide])
    pack_core(info, wide, None, spreads, spills, 0)

    def one_spill(cell, _):
        spill[cell] = overflow_of(spills, core_columns(cell // CZ), cell % CZ, 0)
        return 0

    lax.fori_loop(0, CELLS, one_spill, 0, unroll=4)
    apply_cells(
        stored, lambda cell: lines_of(spreads, core_columns(cell // CZ), cell % CZ), None, sums
    )


def apply_face_kernel(*refs):
    infos, pieces, (stored, before, spill_before, sums, spill), wides, (spreads, spills) = split(
        refs, 3, 3, 5, 3, 2
    )
    widen(pieces, wides)
    pack_faces(infos, wides, None, spreads, spills, 0)

    def one_spill(cell, _):
        found = overflow_of(spills, face_columns(cell // CZ), cell % CZ, 4)
        spill[cell] = spill_before[cell] + found
        return 0

    lax.fori_loop(0, CELLS, one_spill, 0, unroll=4)
    apply_cells(
        stored, lambda cell: lines_of(spreads, face_columns(cell // CZ), cell % CZ), before, sums
    )


def apply_corner_tiles(
    info, corners, stored, before, spill_before, core, diagonal, out, wide, spreads, spills, rest, sums
):
    widen([corners], [wide])
    pack_corners(info, wide, None, spreads, spills, 0)

    def one_spill(cell, _):
        tile = spill_before[cell] + overflow_of(spills, [cell // CZ], cell % CZ, 8)
        for k in range(2):
            rest[cell, k] = spread(tile[k : k + 1])
        return 0

    lax.fori_loop(0, CELLS, one_spill, 0, unroll=4)

    def lines_for(cell):
        return lines_of(spreads, [cell // CZ], cell % CZ) + [lambda k: rest[cell, k]]

    apply_cells(stored, lines_for, before, sums)
    finish_cells(core, sums, diagonal, out)


def split(refs, *sizes):
    parts = []
    for size in sizes:
        parts.append(refs[:size])
        refs = refs[size:]
    return parts


def apply_last_kernel(*refs):
    ins, (slots, first, second, moments, third), work = split(refs, 7, 5, 5)
    diagonal = ins[6]
    apply_corner_tiles(*ins, third, *work)
    d = diagonal[...][:, None, :]
    v_0 = slots[:, 4:6, :]
    v_1 = first[...]
    v_2 = second[...]
    d_0 = d * v_0
    d_2 = d * v_2
    parts = [d_0 * v_0, d_0 * v_1, d * v_1 * v_1, d_2 * v_1, d_2 * v_2, d_2 * third[...]]
    for index, part in enumerate(parts + [v_0, v_1, v_2]):
        moments[2 * index : 2 * index + 2, :] = jnp.sum(part, axis=0)
    moments[18:24, :] = jnp.zeros((6, LANES), jnp.float32)


def wide(piece):
    return VMEM((piece.shape[0], 8, LANES), jnp.float32)


def apply_core(info, core, stored):
    stored = pltpu.with_memory_space_constraint(stored, VMEM)
    scratch = [wide(core)] + packs(4, 2)
    return call(apply_core_kernel, (SUMS, SPILL), scratch, 2, info, core, stored)


def apply_faces(infos, pieces, stored, before, spill):
    stored = pltpu.with_memory_space_constraint(stored, VMEM)
    scratch = [wide(piece) for piece in pieces] + packs(8, 2)
    return call(
        apply_face_kernel, (SUMS, SPILL), scratch, 2, *infos, *pieces, stored, before, spill
    )


def apply_corners(info, corners, stored, before, spill, core, diagonal, last):
    stored = pltpu.with_memory_space_constraint(stored, VMEM)
    rest = VMEM((CELLS, 2, 8, LANES), jnp.float32)
    scratch = [wide(corners)] + packs(4, 2) + [rest, VMEM(SUMS.shape, jnp.float32)]
    arrays = [info, corners, stored, before, spill, core, diagonal]
    if last is None:
        return call(apply_corner_tiles, PAIR, scratch, 2, *arrays)
    third = VMEM((CELLS, 2, LANES), jnp.float32)
    out = jax.ShapeDtypeStruct((24, LANES), jnp.float32)
    return call(apply_last_kernel, out, [third] + scratch, 2, *arrays, *last)


def solve(g):
    tiny = 1e-6
    h = [g[k] + g[k + 1] for k in range(5)]
    ratio_1 = h[1] / h[0]
    ratio_2 = h[2] / h[0]
    pivot_1 = h[2] - ratio_1 * h[1]
    mixed = h[3] - ratio_1 * h[2]
    rest_1 = g[1] - ratio_1 * g[0]
    live_1 = pivot_1 > tiny * h[2]
    safe_1 = jnp.where(live_1, pivot_1, 1.0)
    ratio_3 = jnp.where(live_1, mixed / safe_1, 0.0)
    pivot_2 = h[4] - ratio_2 * h[2] - ratio_3 * mixed
    rest_2 = g[2] - ratio_2 * g[0] - ratio_3 * rest_1
    live_2 = live_1 & (pivot_2 > tiny * h[4])
    c_2 = jnp.where(live_2, rest_2 / jnp.where(live_2, pivot_2, 1.0), 0.0)
    c_1 = jnp.where(live_1, (rest_1 - mixed * c_2) / safe_1, 0.0)
    c_0 = (g[0] - h[1] * c_1 - h[2] * c_2) / h[0]
    return c_0, c_1, c_2


def finish_kernel(counts, moments, slots, first, second, atoms, out):
    summed = jnp.broadcast_to(jnp.sum(moments[...], axis=1, keepdims=True), (24, LANES))
    rows = [summed[2 * k : 2 * k + 2] for k in range(9)]
    c_0, c_1, c_2 = solve(rows[:6])
    totals = c_0 * rows[6] + c_1 * rows[7] + c_2 * rows[8]
    balance = totals[0:1] / totals[1:2]
    sign = jnp.concatenate([jnp.ones((1, LANES), jnp.float32), -balance], axis=0)
    c_0, c_1, c_2 = c_0 * sign, c_1 * sign, c_2 * sign
    high_rows = out.shape[0]
    padded = (high_rows + 15) // 16 * 16
    row_low = row_index((LANES, LANES))
    row_high = row_index((padded, LANES))

    def one_cell(cell, total):
        mixed = c_0 * slots[cell, 4:6, :] + c_1 * first[cell] + c_2 * second[cell]
        charge = jnp.sum(mixed, axis=0, keepdims=True)
        live = lane_index((1, LANES)) < counts[cell]
        pointer = jnp.where(live, atoms[pl.ds(cell, 1), :], -1)
        placed = jnp.where((pointer >> 7) == row_high, charge, 0.0)
        part_0 = placed.astype(jnp.bfloat16)
        left = placed - part_0.astype(jnp.float32)
        part_1 = left.astype(jnp.bfloat16)
        part_2 = (left - part_1.astype(jnp.float32)).astype(jnp.bfloat16)
        lows = jnp.where((pointer & 127) == row_low, 1.0, 0.0).astype(jnp.bfloat16)
        parts = jnp.concatenate([part_0, part_1, part_2], axis=0)
        return total + lax.dot_general(
            parts, lows, (((1,), (1,)), ((), ())), preferred_element_type=jnp.float32
        )

    total = jnp.zeros((3 * padded, LANES), jnp.float32)
    total = lax.fori_loop(0, CELLS, one_cell, total, unroll=8)
    total = total[2 * padded :] + total[padded : 2 * padded] + total[:padded]
    out[...] = total[:high_rows]


def finish(counts, moments, slots, first, second, atoms, atoms_local):
    return pl.pallas_call(
        finish_kernel,
        out_shape=jax.ShapeDtypeStruct((atoms_local // LANES, LANES), jnp.float32),
        in_specs=[pl.BlockSpec(memory_space=SMEM)] + [pl.BlockSpec(memory_space=VMEM)] * 5,
        out_specs=pl.BlockSpec(memory_space=VMEM),
        compiler_params=params(8),
    )(counts, moments, slots, first, second, atoms)


def partner(block, axis, mask):
    count = lax.axis_size(axis)
    return lax.ppermute(block, axis, [(low, low ^ mask) for low in range(count)])


def from_behind(x, axis, by):
    peers = lax.axis_size(axis)
    return lax.ppermute(x, axis, [(i, (i + by) % peers) for i in range(peers)])


def with_z_faces(cells):
    cells = cells.reshape((QUADS, CZ) + cells.shape[1:])
    faces = jnp.concatenate([cells[:, -1:], cells[:, :1]], axis=1)
    other = partner(faces, "gx", 1)
    return jnp.concatenate([other[:, 0:1], cells, other[:, 1:2]], axis=1)


def flat(columns):
    return columns.reshape((-1,) + columns.shape[-2:])


def exchange(cells, on_core, on_faces, on_corners):
    core = with_z_faces(cells)
    low = from_behind(core[2:], "gx", 4)
    high = from_behind(core[:2], "gx", -4)
    beyond = partner(core, "gx", 2)
    sums, spill, *more = on_core(flat(core))
    low, high, sums = lax.optimization_barrier((low, high, sums))
    corners = partner(jnp.concatenate([low, high], axis=0), "gx", 2)
    pieces = [flat(part) for part in (low, high, beyond)]
    sums, spill, *more = on_faces(pieces, sums, spill, *more)
    corners = flat(corners)
    return flat(core), pieces, corners, on_corners(corners, sums, spill, flat(core), *more)


def global_sum(values):
    count = lax.axis_size("gx")
    if count & (count - 1):
        return lax.psum(values, "gx")
    step = 1
    while step < count:
        if step >= 4 and 4 * step <= count:
            others = [partner(values, "gx", k * step) for k in (1, 2, 3)]
            values = (values + others[0]) + (others[1] + others[2])
            step *= 4
        else:
            values = values + partner(values, "gx", step)
            step *= 2
    return values


def local(cell_offsets, electronegativity, hardness, charge_widths, cell_counts, cell_atoms):
    slots, diagonal = prepare(
        cell_counts, cell_offsets, electronegativity, hardness, charge_widths, cell_atoms
    )
    stored = []

    def keep(tiles, *others):
        stored.append(tiles)
        return others

    core, pieces, corners, (first,) = exchange(
        slots,
        lambda core: keep(*build_core(core)),
        lambda faces, sums, spill, *own: keep(*build_faces(faces, *own, sums, spill)) + own,
        lambda corners, sums, spill, core, *own: keep(
            *build_corners(corners, *own, sums, spill, core, diagonal)
        ),
    )

    def apply(cells, last):
        return exchange(
            cells,
            lambda own: apply_core(core, own, stored[0]),
            lambda faces, sums, spill: apply_faces(pieces, faces, stored[1], sums, spill),
            lambda others, sums, spill, _: apply_corners(
                corners, others, stored[2], sums, spill, core, diagonal, last
            ),
        )[3]

    second = apply(first, None)
    moments = global_sum(apply(second, (slots, first, second)))
    charges = finish(
        cell_counts, moments, slots, first, second, cell_atoms, cell_offsets.shape[1]
    )
    return charges.reshape(-1)


def solution(mesh):
    placed = (
        P(None, ("grp", "gx")),
        P(("grp", "gx")),
        P(("grp", "gx")),
        P(("grp", "gx")),
        P(("grp", "gx")),
        P(("grp", "gx"), None),
    )
    return jax.shard_map(
        local, mesh=mesh, in_specs=placed, out_specs=P(("grp", "gx")), check_vma=False
    )
```

```python
import functools
import math

import jax
import jax.numpy as jnp
from jax import lax
from jax.experimental import pallas as pl
from jax.experimental.pallas import tpu as pltpu
from jax.sharding import PartitionSpec as P

CX = 2
CY = 2
CZ = 8
EZ = CZ + 2
CELLS = CX * CY * CZ
QUADS = CX * CY
LANES = 128
BLOCKS = 11

COULOMB = 14.399645
ROOT_PI = math.sqrt(math.pi)
SCREEN = 1.0 / (math.sqrt(2.0) * 3.0)
EWALD_SELF = math.sqrt(2.0 / math.pi) / 3.0
SIDE = 12.0 * SCREEN
CUT_SQUARED = (12.0 * SCREEN) ** 2
CLOSEST_SQUARED = (0.5 * SCREEN) ** 2
PAIR_SCALE = COULOMB * SCREEN

VMEM = pltpu.VMEM
SMEM = pltpu.SMEM


def params(mib):
    return pltpu.CompilerParams(vmem_limit_bytes=mib * 2**20)


def lane_index(shape):
    return lax.broadcasted_iota(jnp.int32, shape, len(shape) - 1)


def row_index(shape):
    return lax.broadcasted_iota(jnp.int32, shape, len(shape) - 2)


def prepare_kernel(
    counts_hbm, offsets, negativity, hardness, widths, atoms, slots, diagonal,
    counts, raw_offsets, raw_negativity, raw_hardness, raw_widths, raw_atoms, table, sems,
):
    copies = [
        pltpu.make_async_copy(source, target, sems.at[index])
        for index, (source, target) in enumerate(
            [
                (counts_hbm, counts),
                (offsets, raw_offsets),
                (negativity, raw_negativity),
                (hardness, raw_hardness),
                (widths, raw_widths),
                (atoms, raw_atoms),
            ]
        )
    ]
    for copy in copies:
        copy.start()
    for copy in copies:
        copy.wait()
    chunks = table.shape[0]
    for chunk in range(chunks):
        here = slice(chunk * LANES, (chunk + 1) * LANES)
        table[chunk, 0:3, :] = raw_offsets[:, here]
        table[chunk, 3:4, :] = raw_widths[chunk : chunk + 1, :]
        table[chunk, 4:5, :] = raw_negativity[chunk : chunk + 1, :]
        table[chunk, 5:6, :] = raw_hardness[chunk : chunk + 1, :]
        table[chunk, 6:8, :] = jnp.zeros((2, LANES), jnp.float32)

    def one_cell(cell, _):
        count = counts[cell]
        occupied = lane_index((1, LANES)) < count
        pointer = jnp.where(occupied, raw_atoms[pl.ds(cell, 1), :], 0)
        high = jnp.broadcast_to(pointer >> 7, (8, LANES))
        low = jnp.broadcast_to(pointer & 127, (8, LANES))
        picked = jnp.zeros((8, LANES), jnp.float32)
        for chunk in range(chunks):
            part = jnp.take_along_axis(table[chunk], low, axis=1)
            picked = jnp.where(high == chunk, part, picked)
        width = jnp.where(occupied, picked[3:4], 1.0)
        diag = jnp.where(
            occupied, picked[5:6] + COULOMB * (1.0 / (width * ROOT_PI) - EWALD_SELF), 1.0
        )
        negative = jnp.where(occupied, picked[4:5], 0.0)
        place = jnp.where(
            row_index((8, LANES)) == 0, cell // (CY * CZ), (cell // CZ) % CY
        ).astype(jnp.float32)
        place = jnp.where(row_index((8, LANES)) < 2, place, 0.0)
        slots[cell, 0:3, :] = ((picked + place) * SIDE)[0:3]
        slots[cell, 3:4, :] = (2.0 * SCREEN * SCREEN) * width * width
        slots[cell, 4:5, :] = -negative / diag
        slots[cell, 5:6, :] = jnp.where(occupied, 1.0 / diag, 0.0)
        slots[cell, 6:7, :] = jnp.zeros((1, LANES), jnp.float32)
        slots[cell, 7:8, :] = jnp.full((1, LANES), count.astype(jnp.float32))
        diagonal[pl.ds(cell, 1), :] = diag
        return 0

    lax.fori_loop(0, CELLS, one_cell, 0, unroll=4)


def prepare(counts, offsets, negativity, hardness, widths, atoms):
    chunks = offsets.shape[1] // LANES
    plane = (chunks, LANES)
    return pl.pallas_call(
        prepare_kernel,
        out_shape=(
            jax.ShapeDtypeStruct((CELLS, 8, LANES), jnp.float32),
            jax.ShapeDtypeStruct((CELLS, LANES), jnp.float32),
        ),
        in_specs=[pl.BlockSpec(memory_space=pltpu.HBM)] * 6,
        out_specs=(pl.BlockSpec(memory_space=VMEM), pl.BlockSpec(memory_space=VMEM)),
        scratch_shapes=[
            SMEM(counts.shape, jnp.int32),
            VMEM(offsets.shape, jnp.float32),
            VMEM(plane, jnp.float32),
            VMEM(plane, jnp.float32),
            VMEM(plane, jnp.float32),
            VMEM(atoms.shape, jnp.int32),
            VMEM((chunks, 8, LANES), jnp.float32),
            pltpu.SemaphoreType.DMA((6,)),
        ],
        compiler_params=params(8),
    )(
        *[
            pltpu.with_memory_space_constraint(array, pltpu.HBM)
            for array in (
                counts,
                offsets,
                negativity.reshape(plane),
                hardness.reshape(plane),
                widths.reshape(plane),
                atoms,
            )
        ]
    )


def centred(axis, cells):
    return (cells - (CX / 2, CY / 2, 1 / 2)[axis]) * SIDE


def operand(tile, scale, one_row, norm_row):
    row = row_index((8, LANES))
    place = jnp.where(row < 3, tile, 0.0)
    norm = jnp.sum(place * place, axis=0, keepdims=True)
    rows = jnp.where(row == one_row, 1.0, jnp.where(row == norm_row, norm, scale * place))
    high = rows.astype(jnp.bfloat16).astype(jnp.float32)
    rest = rows - high
    middle = rest.astype(jnp.bfloat16).astype(jnp.float32)
    return high, middle, rest - middle


def own_operand(tile):
    high, middle, low = operand(tile, 1.0, 4, 3)
    return jnp.concatenate([high, high, middle, high, low, middle], axis=0)


def beside_operand(tile):
    high, middle, low = operand(tile, -2.0, 3, 4)
    return jnp.concatenate([high, middle, high, low, high, middle], axis=0).astype(jnp.bfloat16)


def pack_column(info, cells, source, operands, spreads, spills, target, shift):
    lane = lane_index((8, LANES))
    row = row_index((8, LANES))
    first = 3 if operands is not None else 0
    for z in range(CZ):
        base = source * EZ + z
        here = target * CZ + z
        low, mid, top = [spread(info[base + k, 7:8, :]).astype(jnp.int32) for k in range(3)]
        end = low + mid - LANES
        tiles = [cells[base + k] for k in range(3)]
        if operands is not None:
            for k in range(3):
                offset = jnp.where(row == 2, centred(2, k - 1), 0.0)
                for axis in range(2):
                    offset = jnp.where(row == axis, centred(axis, shift[axis]), offset)
                tiles[k] = tiles[k] + offset
        second = jnp.take_along_axis(tiles[1], (lane - low) & 127, axis=1)
        third = jnp.take_along_axis(tiles[2], (lane - end) & 127, axis=1)
        halves = [jnp.where(lane < low, tiles[0], second), jnp.where(lane < end, second, third)]
        for half, tile in enumerate(halves):
            for index in range(spreads.shape[2]):
                spreads[here, half, index] = spread(tile[first + index : first + index + 1])
            if operands is not None:
                operands[here, :, half * LANES : (half + 1) * LANES] = beside_operand(tile)
        spills[here] = jnp.where(lane < end + top - LANES, third, 0.0)


def pack_core(info, cells, operands, spreads, spills, start):
    for q in range(QUADS):
        pack_column(info, cells, q, operands, spreads, spills, start + q, (0, 0))


def pack_faces(infos, pieces, operands, spreads, spills, start):
    for side in range(2):
        sign = 2 * side - 1
        for y in range(CY):
            shift = (sign * CX, 0)
            pack_column(infos[side], pieces[side], y, operands, spreads, spills, start + 2 * side + y, shift)
        for x in range(CX):
            shift = (0, sign * CY)
            source = 2 * x + 1 - side
            pack_column(infos[2], pieces[2], source, operands, spreads, spills, start + 4 + 2 * x + side, shift)


def pack_corners(info, cells, operands, spreads, spills, start):
    for side_x in range(2):
        for side_y in range(2):
            shift = ((2 * side_x - 1) * CX, (2 * side_y - 1) * CY)
            source = 2 * side_x + 1 - side_y
            pack_column(info, cells, source, operands, spreads, spills, start + 2 * side_x + side_y, shift)


def core_columns(q):
    return [q ^ k for k in range(4)]


def face_columns(q):
    x, y = q >> 1, q & 1
    return [2 * x, 2 * x + 1, 4 + y, 6 + y]


def overflow_of(spills, columns, z, first):
    lane = lane_index((8, LANES))
    total = jnp.zeros((8, LANES), jnp.float32)
    for index, column in enumerate(columns):
        tile = spills[column * CZ + z]
        at = 8 * (first + index)
        moved = pltpu.roll(tile, at, 1) if at else tile
        total = jnp.where((lane >= at) & (lane < at + 8), moved, total)
    return total


def spread(row):
    return jnp.broadcast_to(row, (8, LANES))


def couple(squared, widths):
    held = jnp.maximum(squared, CLOSEST_SQUARED)
    inverse = lax.rsqrt(held)
    distance = held * inverse
    scaled = distance * lax.rsqrt(widths)
    value = (lax.erf(scaled) - lax.erf(distance)) * inverse
    return jnp.where(squared < CUT_SQUARED, value, 0.0)


def to_rows(sums, block):
    here = lane_index((8, LANES)) - row_index((8, LANES)) == 8 * block
    return jnp.where(here, jnp.sum(sums, axis=1, keepdims=True), 0.0)


def add_rows(cell, sums, rows):
    for index in range(2):
        total = jnp.zeros((8, LANES), jnp.float32)
        for block in range(BLOCKS):
            total = total + to_rows(sums[cell, block, index], block)
        rows.append(jnp.sum(total, axis=0, keepdims=True))


def finish_cells(info, sums, diagonal, out):
    def one_cell(cell, _):
        rows = []
        add_rows(cell, sums, rows)
        here = (cell // CZ) * EZ + cell % CZ + 1
        scale = PAIR_SCALE / diagonal[pl.ds(cell, 1), :]
        live = lane_index((1, LANES)) < info[here, 7:8, :].astype(jnp.int32)
        out[cell, 0:1, :] = jnp.where(live, rows[0] * scale, 0.0)
        out[cell, 1:2, :] = jnp.where(live, rows[1] * scale, 0.0)
        return 0

    lax.fori_loop(0, CELLS, one_cell, 0, unroll=4)


def square_up(cell, groups, mine, squares):
    for index, (other, _) in enumerate(groups):
        width = other.shape[1]
        squares[index, :, :width] = lax.dot_general(
            mine[cell], other, (((1,), (0,)), ((), ())), preferred_element_type=jnp.float32
        )


def build_cell(cell, groups, squares, turned, kernels, before, sums, below):
    own = None
    if below is not None:
        own = lane_index((8, LANES)) - row_index((8, LANES)) - below
    sums_s, sums_t = start_sums(cell, before)
    index = 0
    for at, (other, line) in enumerate(groups):
        for half in range(other.shape[1] // LANES):
            width, line_s, line_t = [line(half, k) for k in range(3)]
            for block in range(BLOCKS):
                square = squares[
                    at, 8 * block : 8 * block + 8, half * LANES : (half + 1) * LANES
                ]
                value = couple(square, turned[cell, block] + width)
                if own is not None and index < 2:
                    value = jnp.where(own == 8 * block - LANES * index, 0.0, value)
                kernels[cell, block, index] = value
                sums_s[block] = sums_s[block] + value * line_s
                sums_t[block] = sums_t[block] + value * line_t
            index += 1
    for block in range(BLOCKS):
        sums[cell, block, 0] = sums_s[block]
        sums[cell, block, 1] = sums_t[block]


def build_cells(groups_for, mine, even, odd, turned, kernels, before, sums, below_for):
    square_up(0, groups_for(0), mine, even)

    def build(cell, squares):
        below = None if below_for is None else below_for(cell)
        build_cell(cell, groups_for(cell), squares, turned, kernels, before, sums, below)

    def two_cells(pair, _):
        cell = 2 * pair
        square_up(cell + 1, groups_for(cell + 1), mine, odd)
        build(cell, even)
        after = jnp.minimum(cell + 2, CELLS - 1)
        square_up(after, groups_for(after), mine, even)
        build(cell + 1, odd)
        return 0

    lax.fori_loop(0, CELLS // 2, two_cells, 0)


def start_sums(cell, before):
    if before is None:
        zeros = [jnp.zeros((8, LANES), jnp.float32) for _ in range(BLOCKS)]
        return zeros, list(zeros)
    sums_s = [before[cell, block, 0] for block in range(BLOCKS)]
    return sums_s, [before[cell, block, 1] for block in range(BLOCKS)]


def groups_of(operands, spreads, columns, z):
    def group(column):
        here = column * CZ + z
        return operands[here], lambda half, k: spreads[here, half, k]

    return [group(column) for column in columns]


def lines_of(spreads, columns, z):
    def line(column, half):
        return lambda k: spreads[column * CZ + z, half, k]

    return [line(column, half) for column in columns for half in range(2)]


def core_kernel(
    core, kernels, sums, spill, mine, turned, operands, spreads, spills, even, odd
):
    row = row_index((8, LANES))
    middle = jnp.where(row == 2, centred(2, 0), jnp.where(row < 2, centred(0, 0), 0.0))
    for cell in range(CELLS):
        here = core[(cell // CZ) * EZ + cell % CZ + 1]
        mine[cell] = own_operand(here + middle).T[: 8 * BLOCKS + 8].astype(jnp.bfloat16)
        columns = here.T
        for block in range(BLOCKS):
            width = columns[8 * block : 8 * block + 8, 3:4]
            turned[cell, block] = jnp.broadcast_to(width, (8, LANES))
    pack_core(core, core, operands, spreads, spills, 0)

    def one_spill(cell, _):
        spill[cell] = overflow_of(spills, core_columns(cell // CZ), cell % CZ, 0)
        return 0

    lax.fori_loop(0, CELLS, one_spill, 0, unroll=4)

    def below_for(cell):
        return spread(core[(cell // CZ) * EZ + cell % CZ, 7:8, :]).astype(jnp.int32)

    def groups_for(cell):
        return groups_of(operands, spreads, core_columns(cell // CZ), cell % CZ)

    build_cells(groups_for, mine, even, odd, turned, kernels, None, sums, below_for)


def face_kernel(
    x_low, x_high, beyond, mine, turned, before, spill_before, kernels, sums, spill,
    operands, spreads, spills, even, odd,
):
    pieces = [x_low, x_high, beyond]
    pack_faces(pieces, pieces, operands, spreads, spills, 0)

    def one_spill(cell, _):
        found = overflow_of(spills, face_columns(cell // CZ), cell % CZ, 4)
        spill[cell] = spill_before[cell] + found
        return 0

    lax.fori_loop(0, CELLS, one_spill, 0, unroll=4)

    def groups_for(cell):
        return groups_of(operands, spreads, face_columns(cell // CZ), cell % CZ)

    build_cells(groups_for, mine, even, odd, turned, kernels, before, sums, None)


def corner_kernel(
    corners, mine, turned, before, spill_before, core, diagonal, kernels, out,
    operands, spreads, spills, even, odd, rest_operand, rest, sums,
):
    pack_corners(corners, corners, operands, spreads, spills, 0)

    def one_spill(cell, _):
        tile = spill_before[cell] + overflow_of(spills, [cell // CZ], cell % CZ, 8)
        for k in range(3):
            rest[cell, k] = spread(tile[3 + k : 4 + k])
        rest_operand[cell] = beside_operand(tile)
        return 0

    lax.fori_loop(0, CELLS, one_spill, 0, unroll=4)

    def groups_for(cell):
        groups = groups_of(operands, spreads, [cell // CZ], cell % CZ)
        return groups + [(rest_operand[cell], lambda _, k: rest[cell, k])]

    build_cells(groups_for, mine, even, odd, turned, kernels, before, sums, None)
    finish_cells(core, sums, diagonal, out)


IN_VMEM = pl.BlockSpec(memory_space=VMEM)
PAIR = jax.ShapeDtypeStruct((CELLS, 2, LANES), jnp.float32)
SPILL = jax.ShapeDtypeStruct((CELLS, 8, LANES), jnp.float32)
SUMS = jax.ShapeDtypeStruct((CELLS, BLOCKS, 2, 8, LANES), jnp.float32)
TURNED = jax.ShapeDtypeStruct((CELLS, BLOCKS, 8, LANES), jnp.float32)
PARTS = 48
MINE = jax.ShapeDtypeStruct((CELLS, 8 * BLOCKS + 8, PARTS), jnp.bfloat16)
CORE_TILES, FACE_TILES, CORNER_TILES = 8, 8, 3


def held(tiles):
    return VMEM((CELLS, BLOCKS, tiles, 8, LANES), jnp.float32)


def call(kernel, outs, scratch, tiles, *arrays):
    work = CELLS * BLOCKS * tiles * 8 * LANES
    return pl.pallas_call(
        kernel,
        out_shape=outs,
        in_specs=[IN_VMEM] * len(arrays),
        out_specs=jax.tree.map(lambda _: IN_VMEM, outs),
        scratch_shapes=scratch,
        compiler_params=params(8),
        cost_estimate=pl.CostEstimate(
            flops=30 * work, bytes_accessed=8 * work, transcendentals=4 * work
        ),
    )(*arrays)


def packs(columns, rows):
    return [
        VMEM((columns * CZ, 2, rows, 8, LANES), jnp.float32),
        VMEM((columns * CZ, 8, LANES), jnp.float32),
    ]


def operand_packs(columns, groups):
    operands = VMEM((columns * CZ, PARTS, 2 * LANES), jnp.bfloat16)
    squares = VMEM((groups, 8 * BLOCKS + 8, 2 * LANES), jnp.float32)
    return [operands] + packs(columns, 3) + [squares, squares]


def build_core(core):
    outs = (held(CORE_TILES), SUMS, SPILL, MINE, TURNED)
    return call(core_kernel, outs, operand_packs(4, 4), CORE_TILES, core)


def build_faces(pieces, mine, turned, before, spill):
    return call(
        face_kernel,
        (held(FACE_TILES), SUMS, SPILL),
        operand_packs(8, 4),
        FACE_TILES,
        *pieces,
        mine,
        turned,
        before,
        spill,
    )


def build_corners(corners, mine, turned, before, spill, core, diagonal):
    scratch = operand_packs(4, 2) + [
        VMEM((CELLS, PARTS, LANES), jnp.bfloat16),
        VMEM((CELLS, 3, 8, LANES), jnp.float32),
        VMEM(SUMS.shape, jnp.float32),
    ]
    return call(
        corner_kernel,
        (held(CORNER_TILES), PAIR),
        scratch,
        CORNER_TILES,
        corners,
        mine,
        turned,
        before,
        spill,
        core,
        diagonal,
    )


def apply_cells(stored, lines_for, before, sums):
    def one_cell(cell, _):
        sums_s, sums_t = start_sums(cell, before)
        for index, line in enumerate(lines_for(cell)):
            line_s, line_t = line(0), line(1)
            for block in range(BLOCKS):
                value = stored[cell, block, index]
                sums_s[block] = sums_s[block] + value * line_s
                sums_t[block] = sums_t[block] + value * line_t
        for block in range(BLOCKS):
            sums[cell, block, 0] = sums_s[block]
            sums[cell, block, 1] = sums_t[block]
        return 0

    lax.fori_loop(0, CELLS, one_cell, 0, unroll=2)


def widen(pieces, wides):
    for piece, wide in zip(pieces, wides):
        wide[:, 0:2, :] = piece[...]


def apply_core_kernel(info, core, stored, sums, spill, wide, spreads, spills):
    widen([core], [wide])
    pack_core(info, wide, None, spreads, spills, 0)

    def one_spill(cell, _):
        spill[cell] = overflow_of(spills, core_columns(cell // CZ), cell % CZ, 0)
        return 0

    lax.fori_loop(0, CELLS, one_spill, 0, unroll=4)
    apply_cells(
        stored, lambda cell: lines_of(spreads, core_columns(cell // CZ), cell % CZ), None, sums
    )


def apply_face_kernel(*refs):
    infos, pieces, (stored, before, spill_before, sums, spill), wides, (spreads, spills) = split(
        refs, 3, 3, 5, 3, 2
    )
    widen(pieces, wides)
    pack_faces(infos, wides, None, spreads, spills, 0)

    def one_spill(cell, _):
        found = overflow_of(spills, face_columns(cell // CZ), cell % CZ, 4)
        spill[cell] = spill_before[cell] + found
        return 0

    lax.fori_loop(0, CELLS, one_spill, 0, unroll=4)
    apply_cells(
        stored, lambda cell: lines_of(spreads, face_columns(cell // CZ), cell % CZ), before, sums
    )


def apply_corner_tiles(
    info, corners, stored, before, spill_before, core, diagonal, out, wide, spreads, spills, rest, sums
):
    widen([corners], [wide])
    pack_corners(info, wide, None, spreads, spills, 0)

    def one_spill(cell, _):
        tile = spill_before[cell] + overflow_of(spills, [cell // CZ], cell % CZ, 8)
        for k in range(2):
            rest[cell, k] = spread(tile[k : k + 1])
        return 0

    lax.fori_loop(0, CELLS, one_spill, 0, unroll=4)

    def lines_for(cell):
        return lines_of(spreads, [cell // CZ], cell % CZ) + [lambda k: rest[cell, k]]

    apply_cells(stored, lines_for, before, sums)
    finish_cells(core, sums, diagonal, out)


def split(refs, *sizes):
    parts = []
    for size in sizes:
        parts.append(refs[:size])
        refs = refs[size:]
    return parts


def apply_last_kernel(*refs):
    ins, (slots, first, second, moments, third), work = split(refs, 7, 5, 5)
    diagonal = ins[6]
    apply_corner_tiles(*ins, third, *work)
    d = diagonal[...][:, None, :]
    v_0 = slots[:, 4:6, :]
    v_1 = first[...]
    v_2 = second[...]
    d_0 = d * v_0
    d_2 = d * v_2
    parts = [d_0 * v_0, d_0 * v_1, d * v_1 * v_1, d_2 * v_1, d_2 * v_2, d_2 * third[...]]
    for index, part in enumerate(parts + [v_0, v_1, v_2]):
        moments[2 * index : 2 * index + 2, :] = jnp.sum(part, axis=0)
    moments[18:24, :] = jnp.zeros((6, LANES), jnp.float32)


def wide(piece):
    return VMEM((piece.shape[0], 8, LANES), jnp.float32)


def apply_core(info, core, stored):
    stored = pltpu.with_memory_space_constraint(stored, VMEM)
    scratch = [wide(core)] + packs(4, 2)
    return call(apply_core_kernel, (SUMS, SPILL), scratch, 2, info, core, stored)


def apply_faces(infos, pieces, stored, before, spill):
    stored = pltpu.with_memory_space_constraint(stored, VMEM)
    scratch = [wide(piece) for piece in pieces] + packs(8, 2)
    return call(
        apply_face_kernel, (SUMS, SPILL), scratch, 2, *infos, *pieces, stored, before, spill
    )


def apply_corners(info, corners, stored, before, spill, core, diagonal, last):
    stored = pltpu.with_memory_space_constraint(stored, VMEM)
    rest = VMEM((CELLS, 2, 8, LANES), jnp.float32)
    scratch = [wide(corners)] + packs(4, 2) + [rest, VMEM(SUMS.shape, jnp.float32)]
    arrays = [info, corners, stored, before, spill, core, diagonal]
    if last is None:
        return call(apply_corner_tiles, PAIR, scratch, 2, *arrays)
    third = VMEM((CELLS, 2, LANES), jnp.float32)
    out = jax.ShapeDtypeStruct((24, LANES), jnp.float32)
    return call(apply_last_kernel, out, [third] + scratch, 2, *arrays, *last)


def solve(g):
    tiny = 1e-6
    h = [g[k] + g[k + 1] for k in range(5)]
    ratio_1 = h[1] / h[0]
    ratio_2 = h[2] / h[0]
    pivot_1 = h[2] - ratio_1 * h[1]
    mixed = h[3] - ratio_1 * h[2]
    rest_1 = g[1] - ratio_1 * g[0]
    live_1 = pivot_1 > tiny * h[2]
    safe_1 = jnp.where(live_1, pivot_1, 1.0)
    ratio_3 = jnp.where(live_1, mixed / safe_1, 0.0)
    pivot_2 = h[4] - ratio_2 * h[2] - ratio_3 * mixed
    rest_2 = g[2] - ratio_2 * g[0] - ratio_3 * rest_1
    live_2 = live_1 & (pivot_2 > tiny * h[4])
    c_2 = jnp.where(live_2, rest_2 / jnp.where(live_2, pivot_2, 1.0), 0.0)
    c_1 = jnp.where(live_1, (rest_1 - mixed * c_2) / safe_1, 0.0)
    c_0 = (g[0] - h[1] * c_1 - h[2] * c_2) / h[0]
    return c_0, c_1, c_2


def finish_kernel(counts, moments, slots, first, second, atoms, out):
    summed = jnp.broadcast_to(jnp.sum(moments[...], axis=1, keepdims=True), (24, LANES))
    rows = [summed[2 * k : 2 * k + 2] for k in range(9)]
    c_0, c_1, c_2 = solve(rows[:6])
    totals = c_0 * rows[6] + c_1 * rows[7] + c_2 * rows[8]
    balance = totals[0:1] / totals[1:2]
    sign = jnp.concatenate([jnp.ones((1, LANES), jnp.float32), -balance], axis=0)
    c_0, c_1, c_2 = c_0 * sign, c_1 * sign, c_2 * sign
    high_rows = out.shape[0]
    padded = (high_rows + 15) // 16 * 16
    row_low = row_index((LANES, LANES))
    row_high = row_index((padded, LANES))

    def one_cell(cell, total):
        mixed = c_0 * slots[cell, 4:6, :] + c_1 * first[cell] + c_2 * second[cell]
        charge = jnp.sum(mixed, axis=0, keepdims=True)
        live = lane_index((1, LANES)) < counts[cell]
        pointer = jnp.where(live, atoms[pl.ds(cell, 1), :], -1)
        placed = jnp.where((pointer >> 7) == row_high, charge, 0.0)
        part_0 = placed.astype(jnp.bfloat16)
        left = placed - part_0.astype(jnp.float32)
        part_1 = left.astype(jnp.bfloat16)
        part_2 = (left - part_1.astype(jnp.float32)).astype(jnp.bfloat16)
        lows = jnp.where((pointer & 127) == row_low, 1.0, 0.0).astype(jnp.bfloat16)
        parts = jnp.concatenate([part_0, part_1, part_2], axis=0)
        return total + lax.dot_general(
            parts, lows, (((1,), (1,)), ((), ())), preferred_element_type=jnp.float32
        )

    total = jnp.zeros((3 * padded, LANES), jnp.float32)
    total = lax.fori_loop(0, CELLS, one_cell, total, unroll=8)
    total = total[2 * padded :] + total[padded : 2 * padded] + total[:padded]
    out[...] = total[:high_rows]


def finish(counts, moments, slots, first, second, atoms, atoms_local):
    return pl.pallas_call(
        finish_kernel,
        out_shape=jax.ShapeDtypeStruct((atoms_local // LANES, LANES), jnp.float32),
        in_specs=[pl.BlockSpec(memory_space=SMEM)] + [pl.BlockSpec(memory_space=VMEM)] * 5,
        out_specs=pl.BlockSpec(memory_space=VMEM),
        compiler_params=params(8),
    )(counts, moments, slots, first, second, atoms)


def partner(block, axis, mask):
    count = lax.axis_size(axis)
    return lax.ppermute(block, axis, [(low, low ^ mask) for low in range(count)])


def from_behind(x, axis, by):
    peers = lax.axis_size(axis)
    return lax.ppermute(x, axis, [(i, (i + by) % peers) for i in range(peers)])


def with_z_faces(cells):
    cells = cells.reshape((QUADS, CZ) + cells.shape[1:])
    faces = jnp.concatenate([cells[:, -1:], cells[:, :1]], axis=1)
    other = partner(faces, "gx", 1)
    return jnp.concatenate([other[:, 0:1], cells, other[:, 1:2]], axis=1)


def flat(columns):
    return columns.reshape((-1,) + columns.shape[-2:])


def exchange(cells, on_core, on_faces, on_corners):
    core = with_z_faces(cells)
    low = from_behind(core[2:], "gx", 4)
    high = from_behind(core[:2], "gx", -4)
    beyond = partner(core, "gx", 2)
    sums, spill, *more = on_core(flat(core))
    low, high, sums = lax.optimization_barrier((low, high, sums))
    corners = partner(jnp.concatenate([low, high], axis=0), "gx", 2)
    pieces = [flat(part) for part in (low, high, beyond)]
    sums, spill, *more = on_faces(pieces, sums, spill, *more)
    corners = flat(corners)
    return flat(core), pieces, corners, on_corners(corners, sums, spill, flat(core), *more)


def global_sum(values):
    count = lax.axis_size("gx")
    if count & (count - 1):
        return lax.psum(values, "gx")
    step = 1
    while step < count:
        if step >= 4 and 4 * step <= count:
            others = [partner(values, "gx", k * step) for k in (1, 2, 3)]
            values = (values + others[0]) + (others[1] + others[2])
            step *= 4
        else:
            values = values + partner(values, "gx", step)
            step *= 2
    return values


def local(cell_offsets, electronegativity, hardness, charge_widths, cell_counts, cell_atoms):
    slots, diagonal = prepare(
        cell_counts, cell_offsets, electronegativity, hardness, charge_widths, cell_atoms
    )
    stored = []

    def keep(tiles, *others):
        stored.append(tiles)
        return others

    core, pieces, corners, (first,) = exchange(
        slots,
        lambda core: keep(*build_core(core)),
        lambda faces, sums, spill, *own: keep(*build_faces(faces, *own, sums, spill)) + own,
        lambda corners, sums, spill, core, *own: keep(
            *build_corners(corners, *own, sums, spill, core, diagonal)
        ),
    )

    def apply(cells, last):
        return exchange(
            cells,
            lambda own: apply_core(core, own, stored[0]),
            lambda faces, sums, spill: apply_faces(pieces, faces, stored[1], sums, spill),
            lambda others, sums, spill, _: apply_corners(
                corners, others, stored[2], sums, spill, core, diagonal, last
            ),
        )[3]

    second = apply(first, None)
    moments = global_sum(apply(second, (slots, first, second)))
    charges = finish(
        cell_counts, moments, slots, first, second, cell_atoms, cell_offsets.shape[1]
    )
    return charges.reshape(-1)


def solution(mesh):
    placed = (
        P(None, ("grp", "gx")),
        P(("grp", "gx")),
        P(("grp", "gx")),
        P(("grp", "gx")),
        P(("grp", "gx")),
        P(("grp", "gx"), None),
    )
    return jax.shard_map(
        local, mesh=mesh, in_specs=placed, out_specs=P(("grp", "gx")), check_vma=False
    )
```

```python
import functools
import math

import jax
import jax.numpy as jnp
from jax import lax
from jax.experimental import pallas as pl
from jax.experimental.pallas import tpu as pltpu
from jax.sharding import PartitionSpec as P

CX = 2
CY = 2
CZ = 8
EZ = CZ + 2
CELLS = CX * CY * CZ
QUADS = CX * CY
LANES = 128
BLOCKS = 11

COULOMB = 14.399645
ROOT_PI = math.sqrt(math.pi)
SCREEN = 1.0 / (math.sqrt(2.0) * 3.0)
EWALD_SELF = math.sqrt(2.0 / math.pi) / 3.0
SIDE = 12.0 * SCREEN
CUT_SQUARED = (12.0 * SCREEN) ** 2
CLOSEST_SQUARED = (0.5 * SCREEN) ** 2
PAIR_SCALE = COULOMB * SCREEN

VMEM = pltpu.VMEM
SMEM = pltpu.SMEM


def params(mib):
    return pltpu.CompilerParams(vmem_limit_bytes=mib * 2**20)


def lane_index(shape):
    return lax.broadcasted_iota(jnp.int32, shape, len(shape) - 1)


def row_index(shape):
    return lax.broadcasted_iota(jnp.int32, shape, len(shape) - 2)


def prepare_kernel(
    counts_hbm, offsets, negativity, hardness, widths, atoms, slots, diagonal,
    counts, raw_offsets, raw_negativity, raw_hardness, raw_widths, raw_atoms, table, sems,
):
    copies = [
        pltpu.make_async_copy(source, target, sems.at[index])
        for index, (source, target) in enumerate(
            [
                (counts_hbm, counts),
                (offsets, raw_offsets),
                (negativity, raw_negativity),
                (hardness, raw_hardness),
                (widths, raw_widths),
                (atoms, raw_atoms),
            ]
        )
    ]
    for copy in copies:
        copy.start()
    for copy in copies:
        copy.wait()
    chunks = table.shape[0]
    for chunk in range(chunks):
        here = slice(chunk * LANES, (chunk + 1) * LANES)
        table[chunk, 0:3, :] = raw_offsets[:, here]
        table[chunk, 3:4, :] = raw_widths[chunk : chunk + 1, :]
        table[chunk, 4:5, :] = raw_negativity[chunk : chunk + 1, :]
        table[chunk, 5:6, :] = raw_hardness[chunk : chunk + 1, :]
        table[chunk, 6:8, :] = jnp.zeros((2, LANES), jnp.float32)

    def one_cell(cell, _):
        count = counts[cell]
        occupied = lane_index((1, LANES)) < count
        pointer = jnp.where(occupied, raw_atoms[pl.ds(cell, 1), :], 0)
        high = jnp.broadcast_to(pointer >> 7, (8, LANES))
        low = jnp.broadcast_to(pointer & 127, (8, LANES))
        picked = jnp.zeros((8, LANES), jnp.float32)
        for chunk in range(chunks):
            part = jnp.take_along_axis(table[chunk], low, axis=1)
            picked = jnp.where(high == chunk, part, picked)
        width = jnp.where(occupied, picked[3:4], 1.0)
        diag = jnp.where(
            occupied, picked[5:6] + COULOMB * (1.0 / (width * ROOT_PI) - EWALD_SELF), 1.0
        )
        negative = jnp.where(occupied, picked[4:5], 0.0)
        place = jnp.where(
            row_index((8, LANES)) == 0, cell // (CY * CZ), (cell // CZ) % CY
        ).astype(jnp.float32)
        place = jnp.where(row_index((8, LANES)) < 2, place, 0.0)
        slots[cell, 0:3, :] = ((picked + place) * SIDE)[0:3]
        slots[cell, 3:4, :] = (2.0 * SCREEN * SCREEN) * width * width
        slots[cell, 4:5, :] = -negative / diag
        slots[cell, 5:6, :] = jnp.where(occupied, 1.0 / diag, 0.0)
        slots[cell, 6:7, :] = jnp.zeros((1, LANES), jnp.float32)
        slots[cell, 7:8, :] = jnp.full((1, LANES), count.astype(jnp.float32))
        diagonal[pl.ds(cell, 1), :] = diag
        return 0

    lax.fori_loop(0, CELLS, one_cell, 0, unroll=4)


def prepare(counts, offsets, negativity, hardness, widths, atoms):
    chunks = offsets.shape[1] // LANES
    plane = (chunks, LANES)
    return pl.pallas_call(
        prepare_kernel,
        out_shape=(
            jax.ShapeDtypeStruct((CELLS, 8, LANES), jnp.float32),
            jax.ShapeDtypeStruct((CELLS, LANES), jnp.float32),
        ),
        in_specs=[pl.BlockSpec(memory_space=pltpu.HBM)] * 6,
        out_specs=(pl.BlockSpec(memory_space=VMEM), pl.BlockSpec(memory_space=VMEM)),
        scratch_shapes=[
            SMEM(counts.shape, jnp.int32),
            VMEM(offsets.shape, jnp.float32),
            VMEM(plane, jnp.float32),
            VMEM(plane, jnp.float32),
            VMEM(plane, jnp.float32),
            VMEM(atoms.shape, jnp.int32),
            VMEM((chunks, 8, LANES), jnp.float32),
            pltpu.SemaphoreType.DMA((6,)),
        ],
        compiler_params=params(8),
    )(
        *[
            pltpu.with_memory_space_constraint(array, pltpu.HBM)
            for array in (
                counts,
                offsets,
                negativity.reshape(plane),
                hardness.reshape(plane),
                widths.reshape(plane),
                atoms,
            )
        ]
    )


def pack_column(info, cells, source, packed, spills, target, at, shift):
    lane = lane_index((8, LANES))
    row = row_index((8, LANES))
    for z in range(CZ):
        base = source * EZ + z
        low, mid, top = [spread(info[base + k, 7:8, :]).astype(jnp.int32) for k in range(3)]
        end = low + mid - LANES
        tiles = [cells[base + k] for k in range(3)]
        if shift is not None:
            for k in range(3):
                offset = jnp.where(row == 2, (k - 1) * SIDE, 0.0)
                for axis in range(2):
                    offset = jnp.where(row == axis, shift[axis] * SIDE, offset)
                tiles[k] = tiles[k] + offset
        second = jnp.take_along_axis(tiles[1], (lane - low) & 127, axis=1)
        third = jnp.take_along_axis(tiles[2], (lane - end) & 127, axis=1)
        packed[target * CZ + z, 0] = jnp.where(lane < low, tiles[0], second)
        packed[target * CZ + z, 1] = jnp.where(lane < end, second, third)
        spill = jnp.where(lane < end + top - LANES, third, 0.0)
        spills[target * CZ + z] = pltpu.roll(spill, at, 1) if at else spill


def pack_core(info, cells, packed, spills, build):
    for q in range(QUADS):
        pack_column(info, cells, q, packed, spills, q, 8 * q, (0, 0) if build else None)


def pack_faces(infos, pieces, packed, spills, build):
    for side in range(2):
        sign = 2 * side - 1
        for y in range(CY):
            shift = (sign * CX, 0) if build else None
            at = 32 + 8 * y
            pack_column(infos[side], pieces[side], y, packed, spills, 2 * side + y, at, shift)
        for x in range(CX):
            shift = (0, sign * CY) if build else None
            source = 2 * x + 1 - side
            target = 4 + 2 * x + side
            at = 48 + 8 * x
            pack_column(infos[2], pieces[2], source, packed, spills, target, at, shift)


def pack_corners(info, cells, packed, spills, build):
    for side_x in range(2):
        for side_y in range(2):
            shift = ((2 * side_x - 1) * CX, (2 * side_y - 1) * CY) if build else None
            source = 2 * side_x + 1 - side_y
            pack_column(info, cells, source, packed, spills, 2 * side_x + side_y, 64, shift)


def core_columns(q):
    return [q ^ k for k in range(4)]


def face_columns(q):
    x, y = q >> 1, q & 1
    return [2 * x, 2 * x + 1, 4 + y, 6 + y]


def overflow_of(spills, columns, z):
    return sum(spills[column * CZ + z] for column in columns)


def spread(row):
    return jnp.broadcast_to(row, (8, LANES))


def couple(x_i, y_i, z_i, w_i, x_j, y_j, z_j, w_j):
    delta_x = x_j - x_i
    delta_y = y_j - y_i
    delta_z = z_j - z_i
    squared = delta_x * delta_x + delta_y * delta_y + delta_z * delta_z
    held = jnp.maximum(squared, CLOSEST_SQUARED)
    inverse = lax.rsqrt(held)
    distance = held * inverse
    scaled = distance * lax.rsqrt(w_i + w_j)
    value = (lax.erf(scaled) - lax.erf(distance)) * inverse
    return jnp.where(squared < CUT_SQUARED, value, 0.0)


def to_rows(sums, block):
    here = lane_index((8, LANES)) - row_index((8, LANES)) == 8 * block
    return jnp.where(here, jnp.sum(sums, axis=1, keepdims=True), 0.0)


def add_rows(cell, sums, rows):
    for index in range(2):
        total = jnp.zeros((8, LANES), jnp.float32)
        for block in range(BLOCKS):
            total = total + to_rows(sums[cell, block, index], block)
        rows.append(jnp.sum(total, axis=0, keepdims=True))


def finish_cell(cell, info, sums, diagonal, out):
    rows = []
    add_rows(cell, sums, rows)
    here = (cell // CZ) * EZ + cell % CZ + 1
    scale = PAIR_SCALE / diagonal[pl.ds(cell, 1), :]
    live = lane_index((1, LANES)) < info[here, 7:8, :].astype(jnp.int32)
    out[cell, 0:1, :] = jnp.where(live, rows[0] * scale, 0.0)
    out[cell, 1:2, :] = jnp.where(live, rows[1] * scale, 0.0)


def build_cell(cell, lines, turned, kernels, before, sums, below):
    own = None
    if below is not None:
        own = lane_index((8, LANES)) - row_index((8, LANES)) - below
    sums_s, sums_t = start_sums(cell, before)
    for index, line in enumerate(lines):
        beside = [line(k) for k in range(6)]
        for block in range(BLOCKS):
            value = couple(*[turned[cell, block, k] for k in range(4)], *beside[:4])
            if own is not None and index < 2:
                value = jnp.where(own == 8 * block - LANES * index, 0.0, value)
            kernels[cell, block, index] = value
            sums_s[block] = sums_s[block] + value * beside[4]
            sums_t[block] = sums_t[block] + value * beside[5]
    for block in range(BLOCKS):
        sums[cell, block, 0] = sums_s[block]
        sums[cell, block, 1] = sums_t[block]


def start_sums(cell, before):
    if before is None:
        zeros = [jnp.zeros((8, LANES), jnp.float32) for _ in range(BLOCKS)]
        return zeros, list(zeros)
    sums_s = [before[cell, block, 0] for block in range(BLOCKS)]
    return sums_s, [before[cell, block, 1] for block in range(BLOCKS)]


def lines_of(packed, columns, z):
    def line(column, half):
        return lambda k: spread(packed[column * CZ + z, half, k : k + 1, :])

    return [line(column, half) for column in columns for half in range(2)]


def rest_line(rest, cell):
    return lambda k: spread(rest[cell, k : k + 1, :])


def parts_of(value):
    high = value.astype(jnp.bfloat16).astype(jnp.float32)
    rest = value - high
    middle = rest.astype(jnp.bfloat16).astype(jnp.float32)
    return high, middle, rest - middle


def turn_cells(core, turned):
    chosen = row_index((24, 4 * LANES)) & 7
    ones = jnp.where(chosen == lane_index((24, 4 * LANES)) >> 7, 1.0, 0.0).astype(jnp.bfloat16)
    for cell in range(CELLS):
        here = core[(cell // CZ) * EZ + cell % CZ + 1]
        left = jnp.concatenate(parts_of(here), axis=0).T[: 8 * BLOCKS + 8].astype(jnp.bfloat16)
        wide = lax.dot_general(
            left, ones, (((1,), (0,)), ((), ())), preferred_element_type=jnp.float32
        )
        for block in range(BLOCKS):
            for k in range(4):
                turned[cell, block, k] = wide[8 * block : 8 * block + 8, k * LANES : (k + 1) * LANES]


def core_spills(spills, spill):
    for z in range(CZ):
        spill[z] = overflow_of(spills, range(QUADS), z)


def face_spills(spills, before, spill):
    for cell in range(CELLS):
        q, z = cell // CZ, cell % CZ
        spill[cell] = before[z] + overflow_of(spills, face_columns(q), z)


def corner_spills(spills, before, rest):
    for cell in range(CELLS):
        rest[cell] = before[cell] + spills[cell]


def core_kernel(core, kernels, sums, spill, turned, packed, spills):
    turn_cells(core, turned)
    pack_core(core, core, packed, spills, True)
    core_spills(spills, spill)

    def one_cell(cell, _):
        q, z = cell // CZ, cell % CZ
        below = spread(core[q * EZ + z, 7:8, :]).astype(jnp.int32)
        build_cell(cell, lines_of(packed, core_columns(q), z), turned, kernels, None, sums, below)
        return 0

    lax.fori_loop(0, CELLS, one_cell, 0)


def face_kernel(
    x_low, x_high, beyond, turned, before, spill_before, kernels, sums, spill, packed, spills
):
    pieces = [x_low, x_high, beyond]
    pack_faces(pieces, pieces, packed, spills, True)
    face_spills(spills, spill_before, spill)

    def one_cell(cell, _):
        lines = lines_of(packed, face_columns(cell // CZ), cell % CZ)
        build_cell(cell, lines, turned, kernels, before, sums, None)
        return 0

    lax.fori_loop(0, CELLS, one_cell, 0)


def corner_kernel(
    corners, turned, before, spill_before, core, diagonal, kernels, out, packed, spills, rest, sums
):
    pack_corners(corners, corners, packed, spills, True)
    corner_spills(spills, spill_before, rest)

    def one_cell(cell, _):
        finish_cell(jnp.maximum(cell - 1, 0), core, sums, diagonal, out)
        lines = lines_of(packed, [cell // CZ], cell % CZ) + [rest_line(rest, cell)]
        build_cell(cell, lines, turned, kernels, before, sums, None)
        return 0

    sums[0] = jnp.zeros(SUMS.shape[1:], jnp.float32)
    lax.fori_loop(0, CELLS, one_cell, 0)
    finish_cell(CELLS - 1, core, sums, diagonal, out)


IN_VMEM = pl.BlockSpec(memory_space=VMEM)
PAIR = jax.ShapeDtypeStruct((CELLS, 2, LANES), jnp.float32)
SPILL = jax.ShapeDtypeStruct((CELLS, 8, LANES), jnp.float32)
SUMS = jax.ShapeDtypeStruct((CELLS, BLOCKS, 2, 8, LANES), jnp.float32)
TURNED = jax.ShapeDtypeStruct((CELLS, BLOCKS, 4, 8, LANES), jnp.float32)
CORE_SPILL = jax.ShapeDtypeStruct((CZ, 8, LANES), jnp.float32)
CORE_TILES, FACE_TILES, CORNER_TILES = 8, 8, 3


def held(tiles):
    return VMEM((CELLS, BLOCKS, tiles, 8, LANES), jnp.float32)


def call(kernel, outs, scratch, tiles, *arrays):
    work = CELLS * BLOCKS * tiles * 8 * LANES
    return pl.pallas_call(
        kernel,
        out_shape=outs,
        in_specs=[IN_VMEM] * len(arrays),
        out_specs=jax.tree.map(lambda _: IN_VMEM, outs),
        scratch_shapes=scratch,
        compiler_params=params(8),
        cost_estimate=pl.CostEstimate(
            flops=30 * work, bytes_accessed=8 * work, transcendentals=4 * work
        ),
    )(*arrays)


def packs(columns):
    return [
        VMEM((columns * CZ, 2, 8, LANES), jnp.float32),
        VMEM((columns * CZ, 8, LANES), jnp.float32),
    ]


def build_core(core):
    outs = (held(CORE_TILES), SUMS, CORE_SPILL, TURNED)
    return call(core_kernel, outs, packs(4), CORE_TILES, core)


def build_faces(pieces, turned, before, spill):
    outs = (held(FACE_TILES), SUMS, SPILL)
    return call(face_kernel, outs, packs(8), FACE_TILES, *pieces, turned, before, spill)


def corner_scratch():
    return packs(4) + [VMEM(SPILL.shape, jnp.float32), VMEM(SUMS.shape, jnp.float32)]


def build_corners(corners, turned, before, spill, core, diagonal):
    arrays = [corners, turned, before, spill, core, diagonal]
    return call(corner_kernel, (held(CORNER_TILES), PAIR), corner_scratch(), CORNER_TILES, *arrays)


def apply_cell(cell, lines, stored, before, sums):
    sums_s, sums_t = start_sums(cell, before)
    for index, line in enumerate(lines):
        line_s, line_t = line(0), line(1)
        for block in range(BLOCKS):
            value = stored[cell, block, index]
            sums_s[block] = sums_s[block] + value * line_s
            sums_t[block] = sums_t[block] + value * line_t
    for block in range(BLOCKS):
        sums[cell, block, 0] = sums_s[block]
        sums[cell, block, 1] = sums_t[block]


def widen(pieces, wides):
    for piece, wide in zip(pieces, wides):
        wide[:, 0:2, :] = piece[...]


def apply_core_kernel(info, core, stored, sums, spill, wide, packed, spills):
    widen([core], [wide])
    pack_core(info, wide, packed, spills, False)
    core_spills(spills, spill)

    def one_cell(cell, _):
        lines = lines_of(packed, core_columns(cell // CZ), cell % CZ)
        apply_cell(cell, lines, stored, None, sums)
        return 0

    lax.fori_loop(0, CELLS, one_cell, 0, unroll=2)


def apply_face_kernel(*refs):
    infos, pieces, (stored, before, spill_before, sums, spill), wides, (packed, spills) = split(
        refs, 3, 3, 5, 3, 2
    )
    widen(pieces, wides)
    pack_faces(infos, wides, packed, spills, False)
    face_spills(spills, spill_before, spill)

    def one_cell(cell, _):
        lines = lines_of(packed, face_columns(cell // CZ), cell % CZ)
        apply_cell(cell, lines, stored, before, sums)
        return 0

    lax.fori_loop(0, CELLS, one_cell, 0, unroll=2)


def apply_corner_tiles(
    info, corners, stored, before, spill_before, core, diagonal, out, wide, packed, spills, rest, sums
):
    widen([corners], [wide])
    pack_corners(info, wide, packed, spills, False)
    corner_spills(spills, spill_before, rest)

    def one_cell(cell, _):
        finish_cell(jnp.maximum(cell - 1, 0), core, sums, diagonal, out)
        lines = lines_of(packed, [cell // CZ], cell % CZ) + [rest_line(rest, cell)]
        apply_cell(cell, lines, stored, before, sums)
        return 0

    sums[0] = jnp.zeros(SUMS.shape[1:], jnp.float32)
    lax.fori_loop(0, CELLS, one_cell, 0, unroll=2)
    finish_cell(CELLS - 1, core, sums, diagonal, out)


def split(refs, *sizes):
    parts = []
    for size in sizes:
        parts.append(refs[:size])
        refs = refs[size:]
    return parts


def apply_last_kernel(*refs):
    ins, (slots, first, second, moments, third), work = split(refs, 7, 5, 5)
    diagonal = ins[6]
    apply_corner_tiles(*ins, third, *work)
    d = diagonal[...][:, None, :]
    v_0 = slots[:, 4:6, :]
    v_1 = first[...]
    v_2 = second[...]
    d_0 = d * v_0
    d_2 = d * v_2
    parts = [d_0 * v_0, d_0 * v_1, d * v_1 * v_1, d_2 * v_1, d_2 * v_2, d_2 * third[...]]
    for index, part in enumerate(parts + [v_0, v_1, v_2]):
        moments[2 * index : 2 * index + 2, :] = jnp.sum(part, axis=0)
    moments[18:24, :] = jnp.zeros((6, LANES), jnp.float32)


def wide(piece):
    return VMEM((piece.shape[0], 8, LANES), jnp.float32)


def apply_core(info, core, stored):
    stored = pltpu.with_memory_space_constraint(stored, VMEM)
    scratch = [wide(core)] + packs(4)
    return call(apply_core_kernel, (SUMS, CORE_SPILL), scratch, 2, info, core, stored)


def apply_faces(infos, pieces, stored, before, spill):
    stored = pltpu.with_memory_space_constraint(stored, VMEM)
    scratch = [wide(piece) for piece in pieces] + packs(8)
    return call(
        apply_face_kernel, (SUMS, SPILL), scratch, 2, *infos, *pieces, stored, before, spill
    )


def apply_corners(info, corners, stored, before, spill, core, diagonal, last):
    stored = pltpu.with_memory_space_constraint(stored, VMEM)
    scratch = [wide(corners)] + corner_scratch()
    arrays = [info, corners, stored, before, spill, core, diagonal]
    if last is None:
        return call(apply_corner_tiles, PAIR, scratch, 2, *arrays)
    third = VMEM((CELLS, 2, LANES), jnp.float32)
    out = jax.ShapeDtypeStruct((24, LANES), jnp.float32)
    return call(apply_last_kernel, out, [third] + scratch, 2, *arrays, *last)


def solve(g):
    tiny = 1e-6
    h = [g[k] + g[k + 1] for k in range(5)]
    ratio_1 = h[1] / h[0]
    ratio_2 = h[2] / h[0]
    pivot_1 = h[2] - ratio_1 * h[1]
    mixed = h[3] - ratio_1 * h[2]
    rest_1 = g[1] - ratio_1 * g[0]
    live_1 = pivot_1 > tiny * h[2]
    safe_1 = jnp.where(live_1, pivot_1, 1.0)
    ratio_3 = jnp.where(live_1, mixed / safe_1, 0.0)
    pivot_2 = h[4] - ratio_2 * h[2] - ratio_3 * mixed
    rest_2 = g[2] - ratio_2 * g[0] - ratio_3 * rest_1
    live_2 = live_1 & (pivot_2 > tiny * h[4])
    c_2 = jnp.where(live_2, rest_2 / jnp.where(live_2, pivot_2, 1.0), 0.0)
    c_1 = jnp.where(live_1, (rest_1 - mixed * c_2) / safe_1, 0.0)
    c_0 = (g[0] - h[1] * c_1 - h[2] * c_2) / h[0]
    return c_0, c_1, c_2


def finish_kernel(counts, moments, slots, first, second, atoms, out):
    summed = jnp.broadcast_to(jnp.sum(moments[...], axis=1, keepdims=True), (24, LANES))
    rows = [summed[2 * k : 2 * k + 2] for k in range(9)]
    c_0, c_1, c_2 = solve(rows[:6])
    totals = c_0 * rows[6] + c_1 * rows[7] + c_2 * rows[8]
    balance = totals[0:1] / totals[1:2]
    sign = jnp.concatenate([jnp.ones((1, LANES), jnp.float32), -balance], axis=0)
    c_0, c_1, c_2 = c_0 * sign, c_1 * sign, c_2 * sign
    high_rows = out.shape[0]
    padded = (high_rows + 15) // 16 * 16
    row_low = row_index((LANES, LANES))
    row_high = row_index((padded, LANES))

    def one_cell(cell, total):
        mixed = c_0 * slots[cell, 4:6, :] + c_1 * first[cell] + c_2 * second[cell]
        charge = jnp.sum(mixed, axis=0, keepdims=True)
        live = lane_index((1, LANES)) < counts[cell]
        pointer = jnp.where(live, atoms[pl.ds(cell, 1), :], -1)
        placed = jnp.where((pointer >> 7) == row_high, charge, 0.0)
        part_0 = placed.astype(jnp.bfloat16)
        left = placed - part_0.astype(jnp.float32)
        part_1 = left.astype(jnp.bfloat16)
        part_2 = (left - part_1.astype(jnp.float32)).astype(jnp.bfloat16)
        lows = jnp.where((pointer & 127) == row_low, 1.0, 0.0).astype(jnp.bfloat16)
        parts = jnp.concatenate([part_0, part_1, part_2], axis=0)
        return total + lax.dot_general(
            parts, lows, (((1,), (1,)), ((), ())), preferred_element_type=jnp.float32
        )

    total = jnp.zeros((3 * padded, LANES), jnp.float32)
    total = lax.fori_loop(0, CELLS, one_cell, total, unroll=8)
    total = total[2 * padded :] + total[padded : 2 * padded] + total[:padded]
    out[...] = total[:high_rows]


def finish(counts, moments, slots, first, second, atoms, atoms_local):
    return pl.pallas_call(
        finish_kernel,
        out_shape=jax.ShapeDtypeStruct((atoms_local // LANES, LANES), jnp.float32),
        in_specs=[pl.BlockSpec(memory_space=SMEM)] + [pl.BlockSpec(memory_space=VMEM)] * 5,
        out_specs=pl.BlockSpec(memory_space=VMEM),
        compiler_params=params(8),
    )(counts, moments, slots, first, second, atoms)


def partner(block, axis, mask):
    count = lax.axis_size(axis)
    return lax.ppermute(block, axis, [(low, low ^ mask) for low in range(count)])


def from_behind(x, axis, by):
    peers = lax.axis_size(axis)
    return lax.ppermute(x, axis, [(i, (i + by) % peers) for i in range(peers)])


def with_z_faces(cells):
    cells = cells.reshape((QUADS, CZ) + cells.shape[1:])
    faces = jnp.concatenate([cells[:, -1:], cells[:, :1]], axis=1)
    other = partner(faces, "gx", 1)
    return jnp.concatenate([other[:, 0:1], cells, other[:, 1:2]], axis=1)


def flat(columns):
    return columns.reshape((-1,) + columns.shape[-2:])


def exchange(cells, on_core, on_faces, on_corners):
    core = with_z_faces(cells)
    low = from_behind(core[2:], "gx", 4)
    high = from_behind(core[:2], "gx", -4)
    beyond = partner(core, "gx", 2)
    sums, spill, *more = on_core(flat(core))
    low, high, sums = lax.optimization_barrier((low, high, sums))
    corners = partner(jnp.concatenate([low, high], axis=0), "gx", 2)
    pieces = [flat(part) for part in (low, high, beyond)]
    sums, spill, *more = on_faces(pieces, sums, spill, *more)
    corners = flat(corners)
    return flat(core), pieces, corners, on_corners(corners, sums, spill, flat(core), *more)


def global_sum(values):
    count = lax.axis_size("gx")
    if count & (count - 1):
        return lax.psum(values, "gx")
    step = 1
    while step < count:
        if step >= 4 and 4 * step <= count:
            others = [partner(values, "gx", k * step) for k in (1, 2, 3)]
            values = (values + others[0]) + (others[1] + others[2])
            step *= 4
        else:
            values = values + partner(values, "gx", step)
            step *= 2
    return values


def local(cell_offsets, electronegativity, hardness, charge_widths, cell_counts, cell_atoms):
    slots, diagonal = prepare(
        cell_counts, cell_offsets, electronegativity, hardness, charge_widths, cell_atoms
    )
    stored = []

    def keep(tiles, *others):
        stored.append(tiles)
        return others

    core, pieces, corners, (first,) = exchange(
        slots,
        lambda core: keep(*build_core(core)),
        lambda faces, sums, spill, *own: keep(*build_faces(faces, *own, sums, spill)) + own,
        lambda corners, sums, spill, core, *own: keep(
            *build_corners(corners, *own, sums, spill, core, diagonal)
        ),
    )

    def apply(cells, last):
        return exchange(
            cells,
            lambda own: apply_core(core, own, stored[0]),
            lambda faces, sums, spill: apply_faces(pieces, faces, stored[1], sums, spill),
            lambda others, sums, spill, _: apply_corners(
                corners, others, stored[2], sums, spill, core, diagonal, last
            ),
        )[3]

    second = apply(first, None)
    moments = global_sum(apply(second, (slots, first, second)))
    charges = finish(
        cell_counts, moments, slots, first, second, cell_atoms, cell_offsets.shape[1]
    )
    return charges.reshape(-1)


def solution(mesh):
    placed = (
        P(None, ("grp", "gx")),
        P(("grp", "gx")),
        P(("grp", "gx")),
        P(("grp", "gx")),
        P(("grp", "gx")),
        P(("grp", "gx"), None),
    )
    return jax.shard_map(
        local, mesh=mesh, in_specs=placed, out_specs=P(("grp", "gx")), check_vma=False
    )
```

```python
import functools
import math

import jax
import jax.numpy as jnp
from jax import lax
from jax.experimental import pallas as pl
from jax.experimental.pallas import tpu as pltpu
from jax.sharding import PartitionSpec as P

CX = 2
CY = 2
CZ = 8
EZ = CZ + 2
CELLS = CX * CY * CZ
QUADS = CX * CY
LANES = 128
BLOCKS = 11

COULOMB = 14.399645
ROOT_PI = math.sqrt(math.pi)
SCREEN = 1.0 / (math.sqrt(2.0) * 3.0)
EWALD_SELF = math.sqrt(2.0 / math.pi) / 3.0
SIDE = 12.0 * SCREEN
CUT_SQUARED = (12.0 * SCREEN) ** 2
CLOSEST_SQUARED = (0.5 * SCREEN) ** 2
PAIR_SCALE = COULOMB * SCREEN

VMEM = pltpu.VMEM
SMEM = pltpu.SMEM


def params(mib):
    return pltpu.CompilerParams(vmem_limit_bytes=mib * 2**20)


def lane_index(shape):
    return lax.broadcasted_iota(jnp.int32, shape, len(shape) - 1)


def row_index(shape):
    return lax.broadcasted_iota(jnp.int32, shape, len(shape) - 2)


def prepare_kernel(
    counts_hbm, offsets, negativity, hardness, widths, atoms, slots, diagonal,
    counts, raw_offsets, raw_negativity, raw_hardness, raw_widths, raw_atoms, table, sems,
):
    copies = [
        pltpu.make_async_copy(source, target, sems.at[index])
        for index, (source, target) in enumerate(
            [
                (counts_hbm, counts),
                (offsets, raw_offsets),
                (negativity, raw_negativity),
                (hardness, raw_hardness),
                (widths, raw_widths),
                (atoms, raw_atoms),
            ]
        )
    ]
    for copy in copies:
        copy.start()
    for copy in copies:
        copy.wait()
    chunks = table.shape[0]
    for chunk in range(chunks):
        here = slice(chunk * LANES, (chunk + 1) * LANES)
        table[chunk, 0:3, :] = raw_offsets[:, here]
        table[chunk, 3:4, :] = raw_widths[chunk : chunk + 1, :]
        table[chunk, 4:5, :] = raw_negativity[chunk : chunk + 1, :]
        table[chunk, 5:6, :] = raw_hardness[chunk : chunk + 1, :]
        table[chunk, 6:8, :] = jnp.zeros((2, LANES), jnp.float32)

    def one_cell(cell, _):
        count = counts[cell]
        occupied = lane_index((1, LANES)) < count
        pointer = jnp.where(occupied, raw_atoms[pl.ds(cell, 1), :], 0)
        high = jnp.broadcast_to(pointer >> 7, (8, LANES))
        low = jnp.broadcast_to(pointer & 127, (8, LANES))
        picked = jnp.zeros((8, LANES), jnp.float32)
        for chunk in range(chunks):
            part = jnp.take_along_axis(table[chunk], low, axis=1)
            picked = jnp.where(high == chunk, part, picked)
        width = jnp.where(occupied, picked[3:4], 1.0)
        diag = jnp.where(
            occupied, picked[5:6] + COULOMB * (1.0 / (width * ROOT_PI) - EWALD_SELF), 1.0
        )
        negative = jnp.where(occupied, picked[4:5], 0.0)
        place = jnp.where(
            row_index((8, LANES)) == 0, cell // (CY * CZ), (cell // CZ) % CY
        ).astype(jnp.float32)
        place = jnp.where(row_index((8, LANES)) < 2, place, 0.0)
        slots[cell, 0:3, :] = ((picked + place) * SIDE)[0:3]
        slots[cell, 3:4, :] = (2.0 * SCREEN * SCREEN) * width * width
        slots[cell, 4:5, :] = -negative / diag
        slots[cell, 5:6, :] = jnp.where(occupied, 1.0 / diag, 0.0)
        slots[cell, 6:7, :] = jnp.zeros((1, LANES), jnp.float32)
        slots[cell, 7:8, :] = jnp.full((1, LANES), count.astype(jnp.float32))
        diagonal[pl.ds(cell, 1), :] = diag
        return 0

    lax.fori_loop(0, CELLS, one_cell, 0, unroll=4)


def prepare(counts, offsets, negativity, hardness, widths, atoms):
    chunks = offsets.shape[1] // LANES
    plane = (chunks, LANES)
    return pl.pallas_call(
        prepare_kernel,
        out_shape=(
            jax.ShapeDtypeStruct((CELLS, 8, LANES), jnp.float32),
            jax.ShapeDtypeStruct((CELLS, LANES), jnp.float32),
        ),
        in_specs=[pl.BlockSpec(memory_space=pltpu.HBM)] * 6,
        out_specs=(pl.BlockSpec(memory_space=VMEM), pl.BlockSpec(memory_space=VMEM)),
        scratch_shapes=[
            SMEM(counts.shape, jnp.int32),
            VMEM(offsets.shape, jnp.float32),
            VMEM(plane, jnp.float32),
            VMEM(plane, jnp.float32),
            VMEM(plane, jnp.float32),
            VMEM(atoms.shape, jnp.int32),
            VMEM((chunks, 8, LANES), jnp.float32),
            pltpu.SemaphoreType.DMA((6,)),
        ],
        compiler_params=params(8),
    )(
        *[
            pltpu.with_memory_space_constraint(array, pltpu.HBM)
            for array in (
                counts,
                offsets,
                negativity.reshape(plane),
                hardness.reshape(plane),
                widths.reshape(plane),
                atoms,
            )
        ]
    )


def pack_column(info, cells, source, packed, spills, target, at, shift):
    lane = lane_index((8, LANES))
    row = row_index((8, LANES))
    for z in range(CZ):
        base = source * EZ + z
        low, mid, top = [spread(info[base + k, 7:8, :]).astype(jnp.int32) for k in range(3)]
        end = low + mid - LANES
        tiles = [cells[base + k] for k in range(3)]
        if shift is not None:
            for k in range(3):
                offset = jnp.where(row == 2, (k - 1) * SIDE, 0.0)
                for axis in range(2):
                    offset = jnp.where(row == axis, shift[axis] * SIDE, offset)
                tiles[k] = tiles[k] + offset
        second = jnp.take_along_axis(tiles[1], (lane - low) & 127, axis=1)
        third = jnp.take_along_axis(tiles[2], (lane - end) & 127, axis=1)
        packed[target * CZ + z, 0] = jnp.where(lane < low, tiles[0], second)
        packed[target * CZ + z, 1] = jnp.where(lane < end, second, third)
        spill = jnp.where(lane < end + top - LANES, third, 0.0)
        spills[target * CZ + z] = pltpu.roll(spill, at, 1) if at else spill


def pack_core(info, cells, packed, spills, build):
    for q in range(QUADS):
        pack_column(info, cells, q, packed, spills, q, 8 * q, (0, 0) if build else None)


def pack_faces(infos, pieces, packed, spills, build):
    for side in range(2):
        sign = 2 * side - 1
        for y in range(CY):
            shift = (sign * CX, 0) if build else None
            at = 32 + 8 * y
            pack_column(infos[side], pieces[side], y, packed, spills, 2 * side + y, at, shift)
        for x in range(CX):
            shift = (0, sign * CY) if build else None
            source = 2 * x + 1 - side
            target = 4 + 2 * x + side
            at = 48 + 8 * x
            pack_column(infos[2], pieces[2], source, packed, spills, target, at, shift)


def pack_corners(infos, pieces, packed, spills, build):
    for side_x in range(2):
        for side_y in range(2):
            shift = ((2 * side_x - 1) * CX, (2 * side_y - 1) * CY) if build else None
            info, cells, target = infos[side_x], pieces[side_x], 2 * side_x + side_y
            pack_column(info, cells, 1 - side_y, packed, spills, target, 64, shift)


def core_columns(q):
    return [q ^ k for k in range(4)]


def face_columns(q):
    x, y = q >> 1, q & 1
    return [2 * x, 2 * x + 1, 4 + y, 6 + y]


def overflow_of(spills, columns, z):
    return sum(spills[column * CZ + z] for column in columns)


def spread(row):
    return jnp.broadcast_to(row, (8, LANES))


def couple(x_i, y_i, z_i, w_i, x_j, y_j, z_j, w_j):
    delta_x = x_j - x_i
    delta_y = y_j - y_i
    delta_z = z_j - z_i
    squared = delta_x * delta_x + delta_y * delta_y + delta_z * delta_z
    held = jnp.maximum(squared, CLOSEST_SQUARED)
    inverse = lax.rsqrt(held)
    distance = held * inverse
    scaled = distance * lax.rsqrt(w_i + w_j)
    value = (lax.erf(scaled) - lax.erf(distance)) * inverse
    return jnp.where(squared < CUT_SQUARED, value, 0.0)


def to_rows(sums, block):
    here = lane_index((8, LANES)) - row_index((8, LANES)) == 8 * block
    return jnp.where(here, jnp.sum(sums, axis=1, keepdims=True), 0.0)


def add_rows(cell, sums, rows):
    for index in range(2):
        total = jnp.zeros((8, LANES), jnp.float32)
        for block in range(BLOCKS):
            total = total + to_rows(sums[cell, block, index], block)
        rows.append(jnp.sum(total, axis=0, keepdims=True))


def finish_cell(cell, info, sums, diagonal, out):
    rows = []
    add_rows(cell, sums, rows)
    here = (cell // CZ) * EZ + cell % CZ + 1
    scale = PAIR_SCALE / diagonal[pl.ds(cell, 1), :]
    live = lane_index((1, LANES)) < info[here, 7:8, :].astype(jnp.int32)
    out[cell, 0:1, :] = jnp.where(live, rows[0] * scale, 0.0)
    out[cell, 1:2, :] = jnp.where(live, rows[1] * scale, 0.0)


def build_cell(cell, lines, turned, kernels, before, sums, below):
    own = None
    if below is not None:
        own = lane_index((8, LANES)) - row_index((8, LANES)) - below
    sums_s, sums_t = start_sums(cell, before)
    for index, line in enumerate(lines):
        beside = [line(k) for k in range(6)]
        for block in range(BLOCKS):
            value = couple(*[turned[cell, block, k] for k in range(4)], *beside[:4])
            if own is not None and index < 2:
                value = jnp.where(own == 8 * block - LANES * index, 0.0, value)
            kernels[cell, block, index] = value
            sums_s[block] = sums_s[block] + value * beside[4]
            sums_t[block] = sums_t[block] + value * beside[5]
    for block in range(BLOCKS):
        sums[cell, block, 0] = sums_s[block]
        sums[cell, block, 1] = sums_t[block]


def start_sums(cell, before):
    if before is None:
        zeros = [jnp.zeros((8, LANES), jnp.float32) for _ in range(BLOCKS)]
        return zeros, list(zeros)
    sums_s = [before[cell, block, 0] for block in range(BLOCKS)]
    return sums_s, [before[cell, block, 1] for block in range(BLOCKS)]


def lines_of(packed, columns, z):
    def line(column, half):
        return lambda k: spread(packed[column * CZ + z, half, k : k + 1, :])

    return [line(column, half) for column in columns for half in range(2)]


def rest_line(rest, cell):
    return lambda k: spread(rest[cell, k : k + 1, :])


def parts_of(value):
    high = value.astype(jnp.bfloat16).astype(jnp.float32)
    rest = value - high
    middle = rest.astype(jnp.bfloat16).astype(jnp.float32)
    return high, middle, rest - middle


def turn_cells(core, turned):
    chosen = row_index((24, 4 * LANES)) & 7
    ones = jnp.where(chosen == lane_index((24, 4 * LANES)) >> 7, 1.0, 0.0).astype(jnp.bfloat16)
    for cell in range(CELLS):
        here = core[(cell // CZ) * EZ + cell % CZ + 1]
        left = jnp.concatenate(parts_of(here), axis=0).T[: 8 * BLOCKS + 8].astype(jnp.bfloat16)
        wide = lax.dot_general(
            left, ones, (((1,), (0,)), ((), ())), preferred_element_type=jnp.float32
        )
        for block in range(BLOCKS):
            for k in range(4):
                turned[cell, block, k] = wide[8 * block : 8 * block + 8, k * LANES : (k + 1) * LANES]


def core_spills(spills, spill):
    for z in range(CZ):
        spill[z] = overflow_of(spills, range(QUADS), z)


def face_spills(spills, before, spill):
    for cell in range(CELLS):
        q, z = cell // CZ, cell % CZ
        spill[cell] = before[z] + overflow_of(spills, face_columns(q), z)


def corner_spills(spills, before, rest):
    for cell in range(CELLS):
        rest[cell] = before[cell] + spills[cell]


def core_kernel(core, kernels, sums, spill, turned, packed, spills):
    turn_cells(core, turned)
    pack_core(core, core, packed, spills, True)
    core_spills(spills, spill)

    def one_cell(cell, _):
        q, z = cell // CZ, cell % CZ
        below = spread(core[q * EZ + z, 7:8, :]).astype(jnp.int32)
        build_cell(cell, lines_of(packed, core_columns(q), z), turned, kernels, None, sums, below)
        return 0

    lax.fori_loop(0, CELLS, one_cell, 0)


def face_kernel(
    x_low, x_high, beyond, turned, before, spill_before, kernels, sums, spill, packed, spills
):
    pieces = [x_low, x_high, beyond]
    pack_faces(pieces, pieces, packed, spills, True)
    face_spills(spills, spill_before, spill)

    def one_cell(cell, _):
        lines = lines_of(packed, face_columns(cell // CZ), cell % CZ)
        build_cell(cell, lines, turned, kernels, before, sums, None)
        return 0

    lax.fori_loop(0, CELLS, one_cell, 0)


def corner_kernel(
    x_low, x_high, turned, before, spill_before, core, diagonal, kernels, out,
    packed, spills, rest, sums,
):
    corners = [x_low, x_high]
    pack_corners(corners, corners, packed, spills, True)
    corner_spills(spills, spill_before, rest)

    def one_cell(cell, _):
        finish_cell(jnp.maximum(cell - 1, 0), core, sums, diagonal, out)
        lines = lines_of(packed, [cell // CZ], cell % CZ) + [rest_line(rest, cell)]
        build_cell(cell, lines, turned, kernels, before, sums, None)
        return 0

    sums[0] = jnp.zeros(SUMS.shape[1:], jnp.float32)
    lax.fori_loop(0, CELLS, one_cell, 0)
    finish_cell(CELLS - 1, core, sums, diagonal, out)


IN_VMEM = pl.BlockSpec(memory_space=VMEM)
IN_SMEM = pl.BlockSpec(memory_space=SMEM)
PAIR = jax.ShapeDtypeStruct((CELLS, 2, LANES), jnp.float32)
SPILL = jax.ShapeDtypeStruct((CELLS, 8, LANES), jnp.float32)
SUMS = jax.ShapeDtypeStruct((CELLS, BLOCKS, 2, 8, LANES), jnp.float32)
TURNED = jax.ShapeDtypeStruct((CELLS, BLOCKS, 4, 8, LANES), jnp.float32)
CORE_SPILL = jax.ShapeDtypeStruct((CZ, 8, LANES), jnp.float32)
CORE_TILES, FACE_TILES, CORNER_TILES = 8, 8, 3


def held(tiles):
    return VMEM((CELLS, BLOCKS, tiles, 8, LANES), jnp.float32)


def call(kernel, outs, scratch, tiles, *arrays):
    work = CELLS * BLOCKS * tiles * 8 * LANES
    return pl.pallas_call(
        kernel,
        out_shape=outs,
        in_specs=[IN_SMEM if array.ndim == 1 else IN_VMEM for array in arrays],
        out_specs=jax.tree.map(lambda _: IN_VMEM, outs),
        scratch_shapes=scratch,
        compiler_params=params(8),
        cost_estimate=pl.CostEstimate(
            flops=30 * work, bytes_accessed=8 * work, transcendentals=4 * work
        ),
    )(*arrays)


def packs(columns):
    return [
        VMEM((columns * CZ, 2, 8, LANES), jnp.float32),
        VMEM((columns * CZ, 8, LANES), jnp.float32),
    ]


def build_core(core):
    outs = (held(CORE_TILES), SUMS, CORE_SPILL, TURNED)
    return call(core_kernel, outs, packs(4), CORE_TILES, core)


def build_faces(pieces, turned, before, spill):
    outs = (held(FACE_TILES), SUMS, SPILL)
    return call(face_kernel, outs, packs(8), FACE_TILES, *pieces, turned, before, spill)


def corner_scratch():
    return packs(4) + [VMEM(SPILL.shape, jnp.float32), VMEM(SUMS.shape, jnp.float32)]


def build_corners(corners, turned, before, spill, core, diagonal):
    arrays = [*corners, turned, before, spill, core, diagonal]
    return call(corner_kernel, (held(CORNER_TILES), PAIR), corner_scratch(), CORNER_TILES, *arrays)


def apply_cell(cell, lines, stored, before, sums):
    sums_s, sums_t = start_sums(cell, before)
    for index, line in enumerate(lines):
        line_s, line_t = line(0), line(1)
        for block in range(BLOCKS):
            value = stored[cell, block, index]
            sums_s[block] = sums_s[block] + value * line_s
            sums_t[block] = sums_t[block] + value * line_t
    for block in range(BLOCKS):
        sums[cell, block, 0] = sums_s[block]
        sums[cell, block, 1] = sums_t[block]


def widen(pieces, wides):
    for piece, wide in zip(pieces, wides):
        wide[:, 0:2, :] = piece[...]


def invert_core_kernel(counts, atoms, info, core, stored, sums, spill, places, wide, packed, spills):
    invert(counts, atoms, places)
    apply_core_kernel(info, core, stored, sums, spill, wide, packed, spills)


def apply_core_kernel(info, core, stored, sums, spill, wide, packed, spills):
    widen([core], [wide])
    pack_core(info, wide, packed, spills, False)
    core_spills(spills, spill)

    def one_cell(cell, _):
        lines = lines_of(packed, core_columns(cell // CZ), cell % CZ)
        apply_cell(cell, lines, stored, None, sums)
        return 0

    lax.fori_loop(0, CELLS, one_cell, 0, unroll=2)


def apply_face_kernel(*refs):
    infos, pieces, (stored, before, spill_before, sums, spill), wides, (packed, spills) = split(
        refs, 3, 3, 5, 3, 2
    )
    widen(pieces, wides)
    pack_faces(infos, wides, packed, spills, False)
    face_spills(spills, spill_before, spill)

    def one_cell(cell, _):
        lines = lines_of(packed, face_columns(cell // CZ), cell % CZ)
        apply_cell(cell, lines, stored, before, sums)
        return 0

    lax.fori_loop(0, CELLS, one_cell, 0, unroll=2)


def apply_corner_tiles(
    info_low, info_high, x_low, x_high, stored, before, spill_before, core, diagonal, out,
    wide_low, wide_high, packed, spills, rest, sums,
):
    wides = [wide_low, wide_high]
    widen([x_low, x_high], wides)
    pack_corners([info_low, info_high], wides, packed, spills, False)
    corner_spills(spills, spill_before, rest)

    def one_cell(cell, _):
        finish_cell(jnp.maximum(cell - 1, 0), core, sums, diagonal, out)
        lines = lines_of(packed, [cell // CZ], cell % CZ) + [rest_line(rest, cell)]
        apply_cell(cell, lines, stored, before, sums)
        return 0

    sums[0] = jnp.zeros(SUMS.shape[1:], jnp.float32)
    lax.fori_loop(0, CELLS, one_cell, 0, unroll=2)
    finish_cell(CELLS - 1, core, sums, diagonal, out)


def split(refs, *sizes):
    parts = []
    for size in sizes:
        parts.append(refs[:size])
        refs = refs[size:]
    return parts


def apply_last_kernel(*refs):
    ins, (slots, first, second, moments, third), work = split(refs, 9, 5, 6)
    diagonal = ins[8]
    apply_corner_tiles(*ins, third, *work)
    d = diagonal[...][:, None, :]
    v_0 = slots[:, 4:6, :]
    v_1 = first[...]
    v_2 = second[...]
    d_0 = d * v_0
    d_2 = d * v_2
    parts = [d_0 * v_0, d_0 * v_1, d * v_1 * v_1, d_2 * v_1, d_2 * v_2, d_2 * third[...]]
    row = row_index((2, LANES))
    line = jnp.zeros((2, LANES), jnp.float32)
    for index, part in enumerate(parts + [v_0, v_1, v_2]):
        total = jnp.sum(jnp.sum(part, axis=0), axis=1, keepdims=True)
        line = jnp.where(lane_index((2, LANES)) - row == 2 * index, total, line)
    moments[...] = jnp.sum(line, axis=0, keepdims=True)


def wide(piece):
    return VMEM((piece.shape[0], 8, LANES), jnp.float32)


def apply_core(info, core, stored, lists):
    stored = pltpu.with_memory_space_constraint(stored, VMEM)
    scratch = [wide(core)] + packs(4)
    outs = (SUMS, CORE_SPILL)
    if lists is None:
        return call(apply_core_kernel, outs, scratch, 2, info, core, stored)
    counts, atoms, atoms_local = lists
    rows = (atoms_local // LANES + 15) // 16 * 16
    places = jax.ShapeDtypeStruct((2, rows, LANES), jnp.int32)
    return call(
        invert_core_kernel, outs + (places,), scratch, 2, counts, atoms, info, core, stored
    )


def apply_faces(infos, pieces, stored, before, spill):
    stored = pltpu.with_memory_space_constraint(stored, VMEM)
    scratch = [wide(piece) for piece in pieces] + packs(8)
    return call(
        apply_face_kernel, (SUMS, SPILL), scratch, 2, *infos, *pieces, stored, before, spill
    )


def apply_corners(infos, corners, stored, before, spill, core, diagonal, last):
    stored = pltpu.with_memory_space_constraint(stored, VMEM)
    scratch = [wide(piece) for piece in corners] + corner_scratch()
    arrays = [*infos, *corners, stored, before, spill, core, diagonal]
    if last is None:
        return call(apply_corner_tiles, PAIR, scratch, 2, *arrays)
    third = VMEM((CELLS, 2, LANES), jnp.float32)
    out = jax.ShapeDtypeStruct((1, LANES), jnp.float32)
    return call(apply_last_kernel, out, [third] + scratch, 2, *arrays, *last)


def solve(g):
    tiny = 1e-6
    h = [g[k] + g[k + 1] for k in range(5)]
    ratio_1 = h[1] / h[0]
    ratio_2 = h[2] / h[0]
    pivot_1 = h[2] - ratio_1 * h[1]
    mixed = h[3] - ratio_1 * h[2]
    rest_1 = g[1] - ratio_1 * g[0]
    live_1 = pivot_1 > tiny * h[2]
    safe_1 = jnp.where(live_1, pivot_1, 1.0)
    ratio_3 = jnp.where(live_1, mixed / safe_1, 0.0)
    pivot_2 = h[4] - ratio_2 * h[2] - ratio_3 * mixed
    rest_2 = g[2] - ratio_2 * g[0] - ratio_3 * rest_1
    live_2 = live_1 & (pivot_2 > tiny * h[4])
    c_2 = jnp.where(live_2, rest_2 / jnp.where(live_2, pivot_2, 1.0), 0.0)
    c_1 = jnp.where(live_1, (rest_1 - mixed * c_2) / safe_1, 0.0)
    c_0 = (g[0] - h[1] * c_1 - h[2] * c_2) / h[0]
    return c_0, c_1, c_2


def invert(counts, atoms, places):
    rows = places.shape[1]
    row_low = row_index((LANES, LANES))
    row_high = row_index((rows, LANES))
    lane = lane_index((rows, LANES))

    def one_cell(cell, total):
        live = lane_index((1, LANES)) < counts[cell]
        pointer = jnp.where(live, atoms[pl.ds(cell, 1), :], -1)
        here = (pointer >> 7) == row_high
        cells = jnp.where(here, cell, 0).astype(jnp.float32)
        slots = jnp.where(here, lane, 0).astype(jnp.float32)
        parts = jnp.concatenate([cells, slots], axis=0).astype(jnp.bfloat16)
        lows = jnp.where((pointer & 127) == row_low, 1.0, 0.0).astype(jnp.bfloat16)
        return total + lax.dot_general(
            parts, lows, (((1,), (1,)), ((), ())), preferred_element_type=jnp.float32
        )

    total = jnp.zeros((2 * rows, LANES), jnp.float32)
    total = lax.fori_loop(0, CELLS, one_cell, total, unroll=8).astype(jnp.int32)
    places[0] = total[:rows]
    places[1] = total[rows:]


def finish_kernel(moments, slots, first, second, places, out, charges):
    summed = jnp.sum(moments[...], axis=0)
    lane = lane_index((2, LANES))
    row = row_index((2, LANES))

    def pair(index):
        picked = jnp.where(lane - row == 2 * index, summed, 0.0)
        return jnp.broadcast_to(jnp.sum(picked, axis=1, keepdims=True), (2, LANES))

    rows = [pair(index) for index in range(9)]
    c_0, c_1, c_2 = solve(rows[:6])
    totals = c_0 * rows[6] + c_1 * rows[7] + c_2 * rows[8]
    balance = totals[0:1] / totals[1:2]
    sign = jnp.concatenate([jnp.ones((1, LANES), jnp.float32), -balance], axis=0)
    c_0, c_1, c_2 = c_0 * sign, c_1 * sign, c_2 * sign
    for cell in range(CELLS):
        mixed = c_0 * slots[cell, 4:6, :] + c_1 * first[cell] + c_2 * second[cell]
        charges[cell : cell + 1, :] = jnp.sum(mixed, axis=0, keepdims=True)
    tiles = [jnp.zeros((8, LANES), jnp.float32) for _ in range(places.shape[1] // 8)]
    for cell in range(CELLS):
        line = spread(charges[cell : cell + 1, :])
        for at in range(len(tiles)):
            here = slice(8 * at, 8 * at + 8)
            moved = jnp.take_along_axis(line, places[1, here, :], axis=1)
            tiles[at] = jnp.where(places[0, here, :] == cell, moved, tiles[at])
    out[...] = jnp.concatenate(tiles, axis=0)[: out.shape[0]]


def finish(moments, slots, first, second, places, atoms_local):
    return pl.pallas_call(
        finish_kernel,
        out_shape=jax.ShapeDtypeStruct((atoms_local // LANES, LANES), jnp.float32),
        in_specs=[IN_VMEM] * 5,
        out_specs=IN_VMEM,
        scratch_shapes=[VMEM((CELLS, LANES), jnp.float32)],
        compiler_params=params(8),
    )(moments, slots, first, second, places)


def partner(block, axis, mask):
    count = lax.axis_size(axis)
    return lax.ppermute(block, axis, [(low, low ^ mask) for low in range(count)])


def shifted(block, along_x, across_y):
    count = lax.axis_size("gx")
    route = [(i, ((i + 4 * along_x) % count) ^ (2 * across_y)) for i in range(count)]
    return lax.ppermute(block, "gx", route)


def with_z_faces(cells):
    cells = cells.reshape((QUADS, CZ) + cells.shape[1:])
    faces = jnp.concatenate([cells[:, -1:], cells[:, :1]], axis=1)
    other = partner(faces, "gx", 1)
    return jnp.concatenate([other[:, 0:1], cells, other[:, 1:2]], axis=1)


def flat(columns):
    return columns.reshape((-1,) + columns.shape[-2:])


def exchange(cells, on_core, on_faces, on_corners):
    core = with_z_faces(cells)
    low = shifted(core[2:], 1, 0)
    high = shifted(core[:2], -1, 0)
    beyond = shifted(core, 0, 1)
    corner_low = shifted(core[2:], 1, 1)
    corner_high = shifted(core[:2], -1, 1)
    sums, spill, *more = on_core(flat(core))
    low, high, beyond, sums = lax.optimization_barrier((low, high, beyond, sums))
    pieces = [flat(part) for part in (low, high, beyond)]
    sums, spill, *more = on_faces(pieces, sums, spill, *more)
    corner_low, corner_high, sums = lax.optimization_barrier((corner_low, corner_high, sums))
    corners = [flat(corner_low), flat(corner_high)]
    return flat(core), pieces, corners, on_corners(corners, sums, spill, flat(core), *more)


def from_all(values):
    copies = jnp.broadcast_to(values[None], (lax.axis_size("gx"),) + values.shape)
    return lax.all_to_all(copies, "gx", 0, 0)


def local(cell_offsets, electronegativity, hardness, charge_widths, cell_counts, cell_atoms):
    slots, diagonal = prepare(
        cell_counts, cell_offsets, electronegativity, hardness, charge_widths, cell_atoms
    )
    stored = []

    def keep(tiles, *others):
        stored.append(tiles)
        return others

    core, pieces, corners, (first,) = exchange(
        slots,
        lambda core: keep(*build_core(core)),
        lambda faces, sums, spill, *own: keep(*build_faces(faces, *own, sums, spill)) + own,
        lambda corners, sums, spill, core, *own: keep(
            *build_corners(corners, *own, sums, spill, core, diagonal)
        ),
    )

    def apply(cells, lists, last):
        def on_faces(faces, sums, spill, *found):
            return (*apply_faces(pieces, faces, stored[1], sums, spill), *found)

        def on_corners(others, sums, spill, _, *found):
            result = apply_corners(
                corners, others, stored[2], sums, spill, core, diagonal, last
            )
            return result, found

        return exchange(
            cells, lambda own: apply_core(core, own, stored[0], lists), on_faces, on_corners
        )[3]

    atoms_local = cell_offsets.shape[1]
    second, (places,) = apply(first, (cell_counts, cell_atoms, atoms_local), None)
    moments, _ = apply(second, None, (slots, first, second))
    charges = finish(from_all(moments), slots, first, second, places, atoms_local)
    return charges.reshape(-1)


def solution(mesh):
    placed = (
        P(None, ("grp", "gx")),
        P(("grp", "gx")),
        P(("grp", "gx")),
        P(("grp", "gx")),
        P(("grp", "gx")),
        P(("grp", "gx"), None),
    )
    return jax.shard_map(
        local, mesh=mesh, in_specs=placed, out_specs=P(("grp", "gx")), check_vma=False
    )
```

```python
import functools
import math

import jax
import jax.numpy as jnp
from jax import lax
from jax.experimental import pallas as pl
from jax.experimental.pallas import tpu as pltpu
from jax.sharding import PartitionSpec as P

CX = 2
CY = 2
CZ = 8
EZ = CZ + 2
CELLS = CX * CY * CZ
QUADS = CX * CY
LANES = 128
BLOCKS = 11

COULOMB = 14.399645
ROOT_PI = math.sqrt(math.pi)
SCREEN = 1.0 / (math.sqrt(2.0) * 3.0)
EWALD_SELF = math.sqrt(2.0 / math.pi) / 3.0
SIDE = 12.0 * SCREEN
CUT_SQUARED = (12.0 * SCREEN) ** 2
CLOSEST_SQUARED = (0.5 * SCREEN) ** 2
PAIR_SCALE = COULOMB * SCREEN

VMEM = pltpu.VMEM
SMEM = pltpu.SMEM


def params(mib):
    return pltpu.CompilerParams(vmem_limit_bytes=mib * 2**20)


def lane_index(shape):
    return lax.broadcasted_iota(jnp.int32, shape, len(shape) - 1)


def row_index(shape):
    return lax.broadcasted_iota(jnp.int32, shape, len(shape) - 2)


def prepare_kernel(
    counts_hbm, offsets, negativity, hardness, widths, atoms, slots, diagonal,
    counts, raw_offsets, raw_negativity, raw_hardness, raw_widths, raw_atoms, table, sems,
):
    copies = [
        pltpu.make_async_copy(source, target, sems.at[index])
        for index, (source, target) in enumerate(
            [
                (counts_hbm, counts),
                (offsets, raw_offsets),
                (negativity, raw_negativity),
                (hardness, raw_hardness),
                (widths, raw_widths),
                (atoms, raw_atoms),
            ]
        )
    ]
    for copy in copies:
        copy.start()
    for copy in copies:
        copy.wait()
    chunks = table.shape[0]
    for chunk in range(chunks):
        here = slice(chunk * LANES, (chunk + 1) * LANES)
        table[chunk, 0:3, :] = raw_offsets[:, here]
        table[chunk, 3:4, :] = raw_widths[chunk : chunk + 1, :]
        table[chunk, 4:5, :] = raw_negativity[chunk : chunk + 1, :]
        table[chunk, 5:6, :] = raw_hardness[chunk : chunk + 1, :]
        table[chunk, 6:8, :] = jnp.zeros((2, LANES), jnp.float32)

    def one_cell(cell, _):
        count = counts[cell]
        occupied = lane_index((1, LANES)) < count
        pointer = jnp.where(occupied, raw_atoms[pl.ds(cell, 1), :], 0)
        high = jnp.broadcast_to(pointer >> 7, (8, LANES))
        low = jnp.broadcast_to(pointer & 127, (8, LANES))
        picked = jnp.zeros((8, LANES), jnp.float32)
        for chunk in range(chunks):
            part = jnp.take_along_axis(table[chunk], low, axis=1)
            picked = jnp.where(high == chunk, part, picked)
        width = jnp.where(occupied, picked[3:4], 1.0)
        diag = jnp.where(
            occupied, picked[5:6] + COULOMB * (1.0 / (width * ROOT_PI) - EWALD_SELF), 1.0
        )
        negative = jnp.where(occupied, picked[4:5], 0.0)
        place = jnp.where(
            row_index((8, LANES)) == 0, cell // (CY * CZ), (cell // CZ) % CY
        ).astype(jnp.float32)
        place = jnp.where(row_index((8, LANES)) < 2, place, 0.0)
        slots[cell, 0:3, :] = ((picked + place) * SIDE)[0:3]
        slots[cell, 3:4, :] = (2.0 * SCREEN * SCREEN) * width * width
        slots[cell, 4:5, :] = -negative / diag
        slots[cell, 5:6, :] = jnp.where(occupied, 1.0 / diag, 0.0)
        slots[cell, 6:7, :] = jnp.zeros((1, LANES), jnp.float32)
        slots[cell, 7:8, :] = jnp.full((1, LANES), count.astype(jnp.float32))
        diagonal[pl.ds(cell, 1), :] = diag
        return 0

    lax.fori_loop(0, CELLS, one_cell, 0, unroll=4)


def prepare(counts, offsets, negativity, hardness, widths, atoms):
    chunks = offsets.shape[1] // LANES
    plane = (chunks, LANES)
    return pl.pallas_call(
        prepare_kernel,
        out_shape=(
            jax.ShapeDtypeStruct((CELLS, 8, LANES), jnp.float32),
            jax.ShapeDtypeStruct((CELLS, LANES), jnp.float32),
        ),
        in_specs=[pl.BlockSpec(memory_space=pltpu.HBM)] * 6,
        out_specs=(pl.BlockSpec(memory_space=VMEM), pl.BlockSpec(memory_space=VMEM)),
        scratch_shapes=[
            SMEM(counts.shape, jnp.int32),
            VMEM(offsets.shape, jnp.float32),
            VMEM(plane, jnp.float32),
            VMEM(plane, jnp.float32),
            VMEM(plane, jnp.float32),
            VMEM(atoms.shape, jnp.int32),
            VMEM((chunks, 8, LANES), jnp.float32),
            pltpu.SemaphoreType.DMA((6,)),
        ],
        compiler_params=params(8),
    )(
        *[
            pltpu.with_memory_space_constraint(array, pltpu.HBM)
            for array in (
                counts,
                offsets,
                negativity.reshape(plane),
                hardness.reshape(plane),
                widths.reshape(plane),
                atoms,
            )
        ]
    )


def pack_column(info, cells, source, packed, spills, target, at, shift):
    lane = lane_index((8, LANES))
    row = row_index((8, LANES))
    for z in range(CZ):
        base = source * EZ + z
        low, mid, top = [spread(info[base + k, 7:8, :]).astype(jnp.int32) for k in range(3)]
        end = low + mid - LANES
        tiles = [cells[base + k] for k in range(3)]
        if shift is not None:
            for k in range(3):
                offset = jnp.where(row == 2, (k - 1) * SIDE, 0.0)
                for axis in range(2):
                    offset = jnp.where(row == axis, shift[axis] * SIDE, offset)
                tiles[k] = tiles[k] + offset
        second = jnp.take_along_axis(tiles[1], (lane - low) & 127, axis=1)
        third = jnp.take_along_axis(tiles[2], (lane - end) & 127, axis=1)
        packed[target * CZ + z, 0] = jnp.where(lane < low, tiles[0], second)
        packed[target * CZ + z, 1] = jnp.where(lane < end, second, third)
        spill = jnp.where(lane < end + top - LANES, third, 0.0)
        spills[target * CZ + z] = pltpu.roll(spill, at, 1) if at else spill


def pack_core(info, cells, packed, spills, build):
    for q in range(QUADS):
        pack_column(info, cells, q, packed, spills, q, 8 * q, (0, 0) if build else None)


def pack_faces(infos, pieces, packed, spills, build):
    for side in range(2):
        sign = 2 * side - 1
        for y in range(CY):
            shift = (sign * CX, 0) if build else None
            at = 32 + 8 * y
            pack_column(infos[side], pieces[side], y, packed, spills, 2 * side + y, at, shift)
        for x in range(CX):
            shift = (0, sign * CY) if build else None
            source = 2 * x + 1 - side
            target = 4 + 2 * x + side
            at = 48 + 8 * x
            pack_column(infos[2], pieces[2], source, packed, spills, target, at, shift)


def pack_corners(info, cells, packed, spills, build):
    for side_x in range(2):
        for side_y in range(2):
            shift = ((2 * side_x - 1) * CX, (2 * side_y - 1) * CY) if build else None
            source = 2 * side_x + 1 - side_y
            pack_column(info, cells, source, packed, spills, 2 * side_x + side_y, 64, shift)


def core_columns(q):
    return [q ^ k for k in range(4)]


def face_columns(q):
    x, y = q >> 1, q & 1
    return [2 * x, 2 * x + 1, 4 + y, 6 + y]


def overflow_of(spills, columns, z):
    return sum(spills[column * CZ + z] for column in columns)


def spread(row):
    return jnp.broadcast_to(row, (8, LANES))


def couple(x_i, y_i, z_i, w_i, x_j, y_j, z_j, w_j):
    delta_x = x_j - x_i
    delta_y = y_j - y_i
    delta_z = z_j - z_i
    squared = delta_x * delta_x + delta_y * delta_y + delta_z * delta_z
    held = jnp.maximum(squared, CLOSEST_SQUARED)
    inverse = lax.rsqrt(held)
    distance = held * inverse
    scaled = distance * lax.rsqrt(w_i + w_j)
    value = (lax.erf(scaled) - lax.erf(distance)) * inverse
    return jnp.where(squared < CUT_SQUARED, value, 0.0)


def to_rows(sums, block):
    here = lane_index((8, LANES)) - row_index((8, LANES)) == 8 * block
    return jnp.where(here, jnp.sum(sums, axis=1, keepdims=True), 0.0)


def add_rows(cell, sums, rows):
    for index in range(2):
        total = jnp.zeros((8, LANES), jnp.float32)
        for block in range(BLOCKS):
            total = total + to_rows(sums[cell, block, index], block)
        rows.append(jnp.sum(total, axis=0, keepdims=True))


def finish_cell(cell, info, sums, diagonal, out):
    rows = []
    add_rows(cell, sums, rows)
    here = (cell // CZ) * EZ + cell % CZ + 1
    scale = PAIR_SCALE / diagonal[pl.ds(cell, 1), :]
    live = lane_index((1, LANES)) < info[here, 7:8, :].astype(jnp.int32)
    out[cell, 0:1, :] = jnp.where(live, rows[0] * scale, 0.0)
    out[cell, 1:2, :] = jnp.where(live, rows[1] * scale, 0.0)


def build_cell(cell, lines, turned, kernels, before, sums, below):
    own = None
    if below is not None:
        own = lane_index((8, LANES)) - row_index((8, LANES)) - below
    sums_s, sums_t = start_sums(cell, before)
    for index, line in enumerate(lines):
        beside = [line(k) for k in range(6)]
        for block in range(BLOCKS):
            value = couple(*[turned[cell, block, k] for k in range(4)], *beside[:4])
            if own is not None and index < 2:
                value = jnp.where(own == 8 * block - LANES * index, 0.0, value)
            kernels[cell, block, index] = value
            sums_s[block] = sums_s[block] + value * beside[4]
            sums_t[block] = sums_t[block] + value * beside[5]
    for block in range(BLOCKS):
        sums[cell, block, 0] = sums_s[block]
        sums[cell, block, 1] = sums_t[block]


def start_sums(cell, before):
    if before is None:
        zeros = [jnp.zeros((8, LANES), jnp.float32) for _ in range(BLOCKS)]
        return zeros, list(zeros)
    sums_s = [before[cell, block, 0] for block in range(BLOCKS)]
    return sums_s, [before[cell, block, 1] for block in range(BLOCKS)]


def lines_of(packed, columns, z):
    def line(column, half):
        return lambda k: spread(packed[column * CZ + z, half, k : k + 1, :])

    return [line(column, half) for column in columns for half in range(2)]


def rest_line(rest, cell):
    return lambda k: spread(rest[cell, k : k + 1, :])


def parts_of(value):
    high = value.astype(jnp.bfloat16).astype(jnp.float32)
    rest = value - high
    middle = rest.astype(jnp.bfloat16).astype(jnp.float32)
    return high, middle, rest - middle


def turn_cells(core, turned):
    chosen = row_index((24, 4 * LANES)) & 7
    ones = jnp.where(chosen == lane_index((24, 4 * LANES)) >> 7, 1.0, 0.0).astype(jnp.bfloat16)
    for cell in range(CELLS):
        here = core[(cell // CZ) * EZ + cell % CZ + 1]
        left = jnp.concatenate(parts_of(here), axis=0).T[: 8 * BLOCKS + 8].astype(jnp.bfloat16)
        wide = lax.dot_general(
            left, ones, (((1,), (0,)), ((), ())), preferred_element_type=jnp.float32
        )
        for block in range(BLOCKS):
            for k in range(4):
                turned[cell, block, k] = wide[8 * block : 8 * block + 8, k * LANES : (k + 1) * LANES]


def core_spills(spills, spill):
    for z in range(CZ):
        spill[z] = overflow_of(spills, range(QUADS), z)


def face_spills(spills, before, spill):
    for cell in range(CELLS):
        q, z = cell // CZ, cell % CZ
        spill[cell] = before[z] + overflow_of(spills, face_columns(q), z)


def corner_spills(spills, before, rest):
    for cell in range(CELLS):
        rest[cell] = before[cell] + spills[cell]


def core_kernel(core, kernels, sums, spill, turned, packed, spills):
    turn_cells(core, turned)
    pack_core(core, core, packed, spills, True)
    core_spills(spills, spill)

    def one_cell(cell, _):
        q, z = cell // CZ, cell % CZ
        below = spread(core[q * EZ + z, 7:8, :]).astype(jnp.int32)
        build_cell(cell, lines_of(packed, core_columns(q), z), turned, kernels, None, sums, below)
        return 0

    lax.fori_loop(0, CELLS, one_cell, 0)


def face_kernel(
    x_low, x_high, beyond, turned, before, spill_before, kernels, sums, spill, packed, spills
):
    pieces = [x_low, x_high, beyond]
    pack_faces(pieces, pieces, packed, spills, True)
    face_spills(spills, spill_before, spill)

    def one_cell(cell, _):
        lines = lines_of(packed, face_columns(cell // CZ), cell % CZ)
        build_cell(cell, lines, turned, kernels, before, sums, None)
        return 0

    lax.fori_loop(0, CELLS, one_cell, 0)


def corner_kernel(
    corners, turned, before, spill_before, core, diagonal, kernels, out, packed, spills, rest, sums
):
    pack_corners(corners, corners, packed, spills, True)
    corner_spills(spills, spill_before, rest)

    def one_cell(cell, _):
        finish_cell(jnp.maximum(cell - 1, 0), core, sums, diagonal, out)
        lines = lines_of(packed, [cell // CZ], cell % CZ) + [rest_line(rest, cell)]
        build_cell(cell, lines, turned, kernels, before, sums, None)
        return 0

    sums[0] = jnp.zeros(SUMS.shape[1:], jnp.float32)
    lax.fori_loop(0, CELLS, one_cell, 0)
    finish_cell(CELLS - 1, core, sums, diagonal, out)


IN_VMEM = pl.BlockSpec(memory_space=VMEM)
IN_SMEM = pl.BlockSpec(memory_space=SMEM)
PAIR = jax.ShapeDtypeStruct((CELLS, 2, LANES), jnp.float32)
SPILL = jax.ShapeDtypeStruct((CELLS, 8, LANES), jnp.float32)
SUMS = jax.ShapeDtypeStruct((CELLS, BLOCKS, 2, 8, LANES), jnp.float32)
TURNED = jax.ShapeDtypeStruct((CELLS, BLOCKS, 4, 8, LANES), jnp.float32)
CORE_SPILL = jax.ShapeDtypeStruct((CZ, 8, LANES), jnp.float32)
CORE_TILES, FACE_TILES, CORNER_TILES = 8, 8, 3


def held(tiles):
    return VMEM((CELLS, BLOCKS, tiles, 8, LANES), jnp.float32)


def call(kernel, outs, scratch, tiles, *arrays):
    work = CELLS * BLOCKS * tiles * 8 * LANES
    return pl.pallas_call(
        kernel,
        out_shape=outs,
        in_specs=[IN_SMEM if array.ndim == 1 else IN_VMEM for array in arrays],
        out_specs=jax.tree.map(lambda _: IN_VMEM, outs),
        scratch_shapes=scratch,
        compiler_params=params(8),
        cost_estimate=pl.CostEstimate(
            flops=30 * work, bytes_accessed=8 * work, transcendentals=4 * work
        ),
    )(*arrays)


def packs(columns):
    return [
        VMEM((columns * CZ, 2, 8, LANES), jnp.float32),
        VMEM((columns * CZ, 8, LANES), jnp.float32),
    ]


def build_core(core):
    outs = (held(CORE_TILES), SUMS, CORE_SPILL, TURNED)
    return call(core_kernel, outs, packs(4), CORE_TILES, core)


def build_faces(pieces, turned, before, spill):
    outs = (held(FACE_TILES), SUMS, SPILL)
    return call(face_kernel, outs, packs(8), FACE_TILES, *pieces, turned, before, spill)


def corner_scratch():
    return packs(4) + [VMEM(SPILL.shape, jnp.float32), VMEM(SUMS.shape, jnp.float32)]


def build_corners(corners, turned, before, spill, core, diagonal):
    arrays = [corners, turned, before, spill, core, diagonal]
    return call(corner_kernel, (held(CORNER_TILES), PAIR), corner_scratch(), CORNER_TILES, *arrays)


def apply_cell(cell, lines, stored, before, sums):
    sums_s, sums_t = start_sums(cell, before)
    for index, line in enumerate(lines):
        line_s, line_t = line(0), line(1)
        for block in range(BLOCKS):
            value = stored[cell, block, index]
            sums_s[block] = sums_s[block] + value * line_s
            sums_t[block] = sums_t[block] + value * line_t
    for block in range(BLOCKS):
        sums[cell, block, 0] = sums_s[block]
        sums[cell, block, 1] = sums_t[block]


def widen(pieces, wides):
    for piece, wide in zip(pieces, wides):
        wide[:, 0:2, :] = piece[...]


def invert_core_kernel(counts, atoms, info, core, stored, sums, spill, places, wide, packed, spills):
    invert(counts, atoms, places)
    apply_core_kernel(info, core, stored, sums, spill, wide, packed, spills)


def apply_core_kernel(info, core, stored, sums, spill, wide, packed, spills):
    widen([core], [wide])
    pack_core(info, wide, packed, spills, False)
    core_spills(spills, spill)

    def one_cell(cell, _):
        lines = lines_of(packed, core_columns(cell // CZ), cell % CZ)
        apply_cell(cell, lines, stored, None, sums)
        return 0

    lax.fori_loop(0, CELLS, one_cell, 0, unroll=2)


def apply_face_kernel(*refs):
    infos, pieces, (stored, before, spill_before, sums, spill), wides, (packed, spills) = split(
        refs, 3, 3, 5, 3, 2
    )
    widen(pieces, wides)
    pack_faces(infos, wides, packed, spills, False)
    face_spills(spills, spill_before, spill)

    def one_cell(cell, _):
        lines = lines_of(packed, face_columns(cell // CZ), cell % CZ)
        apply_cell(cell, lines, stored, before, sums)
        return 0

    lax.fori_loop(0, CELLS, one_cell, 0, unroll=2)


def apply_corner_tiles(
    info, corners, stored, before, spill_before, core, diagonal, out, wide, packed, spills, rest, sums
):
    widen([corners], [wide])
    pack_corners(info, wide, packed, spills, False)
    corner_spills(spills, spill_before, rest)

    def one_cell(cell, _):
        finish_cell(jnp.maximum(cell - 1, 0), core, sums, diagonal, out)
        lines = lines_of(packed, [cell // CZ], cell % CZ) + [rest_line(rest, cell)]
        apply_cell(cell, lines, stored, before, sums)
        return 0

    sums[0] = jnp.zeros(SUMS.shape[1:], jnp.float32)
    lax.fori_loop(0, CELLS, one_cell, 0, unroll=2)
    finish_cell(CELLS - 1, core, sums, diagonal, out)


def split(refs, *sizes):
    parts = []
    for size in sizes:
        parts.append(refs[:size])
        refs = refs[size:]
    return parts


def apply_last_kernel(*refs):
    ins, (slots, first, second, moments, third), work = split(refs, 7, 5, 5)
    diagonal = ins[6]
    apply_corner_tiles(*ins, third, *work)
    d = diagonal[...][:, None, :]
    v_0 = slots[:, 4:6, :]
    v_1 = first[...]
    v_2 = second[...]
    d_0 = d * v_0
    d_2 = d * v_2
    parts = [d_0 * v_0, d_0 * v_1, d * v_1 * v_1, d_2 * v_1, d_2 * v_2, d_2 * third[...]]
    row = row_index((2, LANES))
    line = jnp.zeros((2, LANES), jnp.float32)
    for index, part in enumerate(parts + [v_0, v_1, v_2]):
        total = jnp.sum(jnp.sum(part, axis=0), axis=1, keepdims=True)
        line = jnp.where(lane_index((2, LANES)) - row == 2 * index, total, line)
    moments[...] = jnp.sum(line, axis=0, keepdims=True)


def wide(piece):
    return VMEM((piece.shape[0], 8, LANES), jnp.float32)


def apply_core(info, core, stored, lists):
    stored = pltpu.with_memory_space_constraint(stored, VMEM)
    scratch = [wide(core)] + packs(4)
    outs = (SUMS, CORE_SPILL)
    if lists is None:
        return call(apply_core_kernel, outs, scratch, 2, info, core, stored)
    counts, atoms, atoms_local = lists
    rows = (atoms_local // LANES + 15) // 16 * 16
    places = jax.ShapeDtypeStruct((2, rows, LANES), jnp.int32)
    return call(
        invert_core_kernel, outs + (places,), scratch, 2, counts, atoms, info, core, stored
    )


def apply_faces(infos, pieces, stored, before, spill):
    stored = pltpu.with_memory_space_constraint(stored, VMEM)
    scratch = [wide(piece) for piece in pieces] + packs(8)
    return call(
        apply_face_kernel, (SUMS, SPILL), scratch, 2, *infos, *pieces, stored, before, spill
    )


def apply_corners(info, corners, stored, before, spill, core, diagonal, last):
    stored = pltpu.with_memory_space_constraint(stored, VMEM)
    scratch = [wide(corners)] + corner_scratch()
    arrays = [info, corners, stored, before, spill, core, diagonal]
    if last is None:
        return call(apply_corner_tiles, PAIR, scratch, 2, *arrays)
    third = VMEM((CELLS, 2, LANES), jnp.float32)
    out = jax.ShapeDtypeStruct((1, LANES), jnp.float32)
    return call(apply_last_kernel, out, [third] + scratch, 2, *arrays, *last)


def solve(g):
    tiny = 1e-6
    h = [g[k] + g[k + 1] for k in range(5)]
    ratio_1 = h[1] / h[0]
    ratio_2 = h[2] / h[0]
    pivot_1 = h[2] - ratio_1 * h[1]
    mixed = h[3] - ratio_1 * h[2]
    rest_1 = g[1] - ratio_1 * g[0]
    live_1 = pivot_1 > tiny * h[2]
    safe_1 = jnp.where(live_1, pivot_1, 1.0)
    ratio_3 = jnp.where(live_1, mixed / safe_1, 0.0)
    pivot_2 = h[4] - ratio_2 * h[2] - ratio_3 * mixed
    rest_2 = g[2] - ratio_2 * g[0] - ratio_3 * rest_1
    live_2 = live_1 & (pivot_2 > tiny * h[4])
    c_2 = jnp.where(live_2, rest_2 / jnp.where(live_2, pivot_2, 1.0), 0.0)
    c_1 = jnp.where(live_1, (rest_1 - mixed * c_2) / safe_1, 0.0)
    c_0 = (g[0] - h[1] * c_1 - h[2] * c_2) / h[0]
    return c_0, c_1, c_2


def invert(counts, atoms, places):
    rows = places.shape[1]
    row_low = row_index((LANES, LANES))
    row_high = row_index((rows, LANES))
    lane = lane_index((rows, LANES))

    def one_cell(cell, total):
        live = lane_index((1, LANES)) < counts[cell]
        pointer = jnp.where(live, atoms[pl.ds(cell, 1), :], -1)
        here = (pointer >> 7) == row_high
        cells = jnp.where(here, cell, 0).astype(jnp.float32)
        slots = jnp.where(here, lane, 0).astype(jnp.float32)
        parts = jnp.concatenate([cells, slots], axis=0).astype(jnp.bfloat16)
        lows = jnp.where((pointer & 127) == row_low, 1.0, 0.0).astype(jnp.bfloat16)
        return total + lax.dot_general(
            parts, lows, (((1,), (1,)), ((), ())), preferred_element_type=jnp.float32
        )

    total = jnp.zeros((2 * rows, LANES), jnp.float32)
    total = lax.fori_loop(0, CELLS, one_cell, total, unroll=8).astype(jnp.int32)
    places[0] = total[:rows]
    places[1] = total[rows:]


def finish_kernel(moments, slots, first, second, places, out, charges):
    summed = moments[...]
    lane = lane_index((2, LANES))
    row = row_index((2, LANES))

    def pair(index):
        picked = jnp.where(lane - row == 2 * index, summed, 0.0)
        return jnp.broadcast_to(jnp.sum(picked, axis=1, keepdims=True), (2, LANES))

    rows = [pair(index) for index in range(9)]
    c_0, c_1, c_2 = solve(rows[:6])
    totals = c_0 * rows[6] + c_1 * rows[7] + c_2 * rows[8]
    balance = totals[0:1] / totals[1:2]
    sign = jnp.concatenate([jnp.ones((1, LANES), jnp.float32), -balance], axis=0)
    c_0, c_1, c_2 = c_0 * sign, c_1 * sign, c_2 * sign
    for cell in range(CELLS):
        mixed = c_0 * slots[cell, 4:6, :] + c_1 * first[cell] + c_2 * second[cell]
        charges[cell : cell + 1, :] = jnp.sum(mixed, axis=0, keepdims=True)
    tiles = [jnp.zeros((8, LANES), jnp.float32) for _ in range(places.shape[1] // 8)]
    for cell in range(CELLS):
        line = spread(charges[cell : cell + 1, :])
        for at in range(len(tiles)):
            here = slice(8 * at, 8 * at + 8)
            moved = jnp.take_along_axis(line, places[1, here, :], axis=1)
            tiles[at] = jnp.where(places[0, here, :] == cell, moved, tiles[at])
    out[...] = jnp.concatenate(tiles, axis=0)[: out.shape[0]]


def finish(moments, slots, first, second, places, atoms_local):
    return pl.pallas_call(
        finish_kernel,
        out_shape=jax.ShapeDtypeStruct((atoms_local // LANES, LANES), jnp.float32),
        in_specs=[IN_VMEM] * 5,
        out_specs=IN_VMEM,
        scratch_shapes=[VMEM((CELLS, LANES), jnp.float32)],
        compiler_params=params(8),
    )(moments, slots, first, second, places)


def partner(block, axis, mask):
    count = lax.axis_size(axis)
    return lax.ppermute(block, axis, [(low, low ^ mask) for low in range(count)])


def shifted(block, along_x):
    count = lax.axis_size("gx")
    return lax.ppermute(block, "gx", [(i, (i + 4 * along_x) % count) for i in range(count)])


def with_z_faces(cells):
    cells = cells.reshape((QUADS, CZ) + cells.shape[1:])
    faces = jnp.concatenate([cells[:, -1:], cells[:, :1]], axis=1)
    other = partner(faces, "gx", 1)
    return jnp.concatenate([other[:, 0:1], cells, other[:, 1:2]], axis=1)


def flat(columns):
    return columns.reshape((-1,) + columns.shape[-2:])


def x_faces(core):
    count = lax.axis_size("gx")
    rows = count // 4
    odd = (lax.axis_index("gx") // 4) % 2 == 1
    if rows % 2:
        return shifted(core[2:], 1), shifted(core[:2], -1)
    first = lax.ppermute(jnp.where(odd, core[:2], core[2:]), "gx", [(i, i ^ 4) for i in range(count)])
    route = [(i, (i + (4 if (i // 4) % 2 else -4)) % count) for i in range(count)]
    second = lax.ppermute(jnp.where(odd, core[2:], core[:2]), "gx", route)
    return first, second


def sorted_faces(first, second):
    odd = (lax.axis_index("gx") // 4) % 2 == 1
    if (lax.axis_size("gx") // 4) % 2:
        return first, second
    return jnp.where(odd, first, second), jnp.where(odd, second, first)


def exchange(cells, on_core, on_faces, on_corners):
    core = with_z_faces(cells)
    first, second = x_faces(core)
    beyond = partner(core, "gx", 2)
    sums, spill, *more = on_core(flat(core))
    first, second, sums = lax.optimization_barrier((first, second, sums))
    low, high = sorted_faces(first, second)
    corners = partner(jnp.concatenate([low, high], axis=0), "gx", 2)
    pieces = [flat(part) for part in (low, high, beyond)]
    sums, spill, *more = on_faces(pieces, sums, spill, *more)
    corners = flat(corners)
    return flat(core), pieces, corners, on_corners(corners, sums, spill, flat(core), *more)


def global_sum(values):
    count = lax.axis_size("gx")
    if count & (count - 1):
        return lax.psum(values, "gx")
    step = 1
    while step < count:
        if step >= 4 and 4 * step <= count:
            others = [partner(values, "gx", k * step) for k in (3, 2, 1)]
            values = (values + others[0]) + (others[1] + others[2])
            step *= 4
        else:
            values = values + partner(values, "gx", step)
            step *= 2
    return values


def local(cell_offsets, electronegativity, hardness, charge_widths, cell_counts, cell_atoms):
    slots, diagonal = prepare(
        cell_counts, cell_offsets, electronegativity, hardness, charge_widths, cell_atoms
    )
    stored = []

    def keep(tiles, *others):
        stored.append(tiles)
        return others

    core, pieces, corners, (first,) = exchange(
        slots,
        lambda core: keep(*build_core(core)),
        lambda faces, sums, spill, *own: keep(*build_faces(faces, *own, sums, spill)) + own,
        lambda corners, sums, spill, core, *own: keep(
            *build_corners(corners, *own, sums, spill, core, diagonal)
        ),
    )

    def apply(cells, lists, last):
        def on_faces(faces, sums, spill, *found):
            return (*apply_faces(pieces, faces, stored[1], sums, spill), *found)

        def on_corners(others, sums, spill, _, *found):
            result = apply_corners(
                corners, others, stored[2], sums, spill, core, diagonal, last
            )
            return result, found

        return exchange(
            cells, lambda own: apply_core(core, own, stored[0], lists), on_faces, on_corners
        )[3]

    atoms_local = cell_offsets.shape[1]
    second, (places,) = apply(first, (cell_counts, cell_atoms, atoms_local), None)
    moments, _ = apply(second, None, (slots, first, second))
    charges = finish(global_sum(moments), slots, first, second, places, atoms_local)
    return charges.reshape(-1)


def solution(mesh):
    placed = (
        P(None, ("grp", "gx")),
        P(("grp", "gx")),
        P(("grp", "gx")),
        P(("grp", "gx")),
        P(("grp", "gx")),
        P(("grp", "gx"), None),
    )
    return jax.shard_map(
        local, mesh=mesh, in_specs=placed, out_specs=P(("grp", "gx")), check_vma=False
    )
```

```python
import functools
import math

import jax
import jax.numpy as jnp
from jax import lax
from jax.experimental import pallas as pl
from jax.experimental.pallas import tpu as pltpu
from jax.sharding import PartitionSpec as P

CX = 2
CY = 2
CZ = 8
EZ = CZ + 2
CELLS = CX * CY * CZ
QUADS = CX * CY
LANES = 128
BLOCKS = 11
GROUPS = ((0, 1, 2, 3), (4, 5, 6, 7), (8, 9, 10))

COULOMB = 14.399645
ROOT_PI = math.sqrt(math.pi)
SCREEN = 1.0 / (math.sqrt(2.0) * 3.0)
EWALD_SELF = math.sqrt(2.0 / math.pi) / 3.0
SIDE = 12.0 * SCREEN
CUT_SQUARED = (12.0 * SCREEN) ** 2
CLOSEST_SQUARED = (0.5 * SCREEN) ** 2
PAIR_SCALE = COULOMB * SCREEN

VMEM = pltpu.VMEM
SMEM = pltpu.SMEM


def params(mib):
    return pltpu.CompilerParams(vmem_limit_bytes=mib * 2**20)


def lane_index(shape):
    return lax.broadcasted_iota(jnp.int32, shape, len(shape) - 1)


def row_index(shape):
    return lax.broadcasted_iota(jnp.int32, shape, len(shape) - 2)


def prepare_kernel(
    counts_hbm, offsets, negativity, hardness, widths, atoms, slots, diagonal,
    counts, raw_offsets, raw_negativity, raw_hardness, raw_widths, raw_atoms, table, sems,
):
    copies = [
        pltpu.make_async_copy(source, target, sems.at[index])
        for index, (source, target) in enumerate(
            [
                (counts_hbm, counts),
                (offsets, raw_offsets),
                (negativity, raw_negativity),
                (hardness, raw_hardness),
                (widths, raw_widths),
                (atoms, raw_atoms),
            ]
        )
    ]
    for copy in copies:
        copy.start()
    for copy in copies:
        copy.wait()
    chunks = table.shape[0]
    for chunk in range(chunks):
        here = slice(chunk * LANES, (chunk + 1) * LANES)
        table[chunk, 0:3, :] = raw_offsets[:, here]
        table[chunk, 3:4, :] = raw_widths[chunk : chunk + 1, :]
        table[chunk, 4:5, :] = raw_negativity[chunk : chunk + 1, :]
        table[chunk, 5:6, :] = raw_hardness[chunk : chunk + 1, :]
        table[chunk, 6:8, :] = jnp.zeros((2, LANES), jnp.float32)

    def one_cell(cell, _):
        count = counts[cell]
        occupied = lane_index((1, LANES)) < count
        pointer = jnp.where(occupied, raw_atoms[pl.ds(cell, 1), :], 0)
        high = jnp.broadcast_to(pointer >> 7, (8, LANES))
        low = jnp.broadcast_to(pointer & 127, (8, LANES))
        picked = jnp.zeros((8, LANES), jnp.float32)
        for chunk in range(chunks):
            part = jnp.take_along_axis(table[chunk], low, axis=1)
            picked = jnp.where(high == chunk, part, picked)
        width = jnp.where(occupied, picked[3:4], 1.0)
        diag = jnp.where(
            occupied, picked[5:6] + COULOMB * (1.0 / (width * ROOT_PI) - EWALD_SELF), 1.0
        )
        negative = jnp.where(occupied, picked[4:5], 0.0)
        place = jnp.where(
            row_index((8, LANES)) == 0, cell // (CY * CZ), (cell // CZ) % CY
        ).astype(jnp.float32)
        place = jnp.where(row_index((8, LANES)) < 2, place, 0.0)
        slots[cell, 0:3, :] = ((picked + place) * SIDE)[0:3]
        slots[cell, 3:4, :] = (2.0 * SCREEN * SCREEN) * width * width
        slots[cell, 4:5, :] = -negative / diag
        slots[cell, 5:6, :] = jnp.where(occupied, 1.0 / diag, 0.0)
        slots[cell, 6:7, :] = jnp.zeros((1, LANES), jnp.float32)
        slots[cell, 7:8, :] = jnp.full((1, LANES), count.astype(jnp.float32))
        diagonal[pl.ds(cell, 1), :] = diag
        return 0

    lax.fori_loop(0, CELLS, one_cell, 0, unroll=4)


def prepare(counts, offsets, negativity, hardness, widths, atoms):
    chunks = offsets.shape[1] // LANES
    plane = (chunks, LANES)
    return pl.pallas_call(
        prepare_kernel,
        out_shape=(
            jax.ShapeDtypeStruct((CELLS, 8, LANES), jnp.float32),
            jax.ShapeDtypeStruct((CELLS, LANES), jnp.float32),
        ),
        in_specs=[pl.BlockSpec(memory_space=pltpu.HBM)] * 6,
        out_specs=(pl.BlockSpec(memory_space=VMEM), pl.BlockSpec(memory_space=VMEM)),
        scratch_shapes=[
            SMEM(counts.shape, jnp.int32),
            VMEM(offsets.shape, jnp.float32),
            VMEM(plane, jnp.float32),
            VMEM(plane, jnp.float32),
            VMEM(plane, jnp.float32),
            VMEM(atoms.shape, jnp.int32),
            VMEM((chunks, 8, LANES), jnp.float32),
            pltpu.SemaphoreType.DMA((6,)),
        ],
        compiler_params=params(8),
    )(
        *[
            pltpu.with_memory_space_constraint(array, pltpu.HBM)
            for array in (
                counts,
                offsets,
                negativity.reshape(plane),
                hardness.reshape(plane),
                widths.reshape(plane),
                atoms,
            )
        ]
    )


def pack_column(info, cells, source, packed, spills, target, at, shift):
    lane = lane_index((8, LANES))
    row = row_index((8, LANES))
    for z in range(CZ):
        base = source * EZ + z
        low, mid, top = [spread(info[base + k, 7:8, :]).astype(jnp.int32) for k in range(3)]
        end = low + mid - LANES
        tiles = [cells[base + k] for k in range(3)]
        if shift is not None:
            for k in range(3):
                offset = jnp.where(row == 2, (k - 1) * SIDE, 0.0)
                for axis in range(2):
                    offset = jnp.where(row == axis, shift[axis] * SIDE, offset)
                tiles[k] = tiles[k] + offset
        second = jnp.take_along_axis(tiles[1], (lane - low) & 127, axis=1)
        third = jnp.take_along_axis(tiles[2], (lane - end) & 127, axis=1)
        packed[target * CZ + z, 0] = jnp.where(lane < low, tiles[0], second)
        packed[target * CZ + z, 1] = jnp.where(lane < end, second, third)
        spill = jnp.where(lane < end + top - LANES, third, 0.0)
        spills[target * CZ + z] = pltpu.roll(spill, at, 1) if at else spill


def pack_core(info, cells, packed, spills, build):
    for q in range(QUADS):
        pack_column(info, cells, q, packed, spills, q, 8 * q, (0, 0) if build else None)


def pack_faces(infos, pieces, packed, spills, build):
    for side in range(2):
        sign = 2 * side - 1
        for y in range(CY):
            shift = (sign * CX, 0) if build else None
            at = 32 + 8 * y
            pack_column(infos[side], pieces[side], y, packed, spills, 2 * side + y, at, shift)
        for x in range(CX):
            shift = (0, sign * CY) if build else None
            source = 2 * x + 1 - side
            target = 4 + 2 * x + side
            at = 48 + 8 * x
            pack_column(infos[2], pieces[2], source, packed, spills, target, at, shift)


def pack_corners(info, cells, packed, spills, build):
    for side_x in range(2):
        for side_y in range(2):
            shift = ((2 * side_x - 1) * CX, (2 * side_y - 1) * CY) if build else None
            source = 2 * side_x + 1 - side_y
            pack_column(info, cells, source, packed, spills, 2 * side_x + side_y, 64, shift)


def core_columns(q):
    return [q ^ k for k in range(4)]


def face_columns(q):
    x, y = q >> 1, q & 1
    return [2 * x, 2 * x + 1, 4 + y, 6 + y]


def overflow_of(spills, columns, z):
    return sum(spills[column * CZ + z] for column in columns)


def spread(row):
    return jnp.broadcast_to(row, (8, LANES))


def couple(x_i, y_i, z_i, w_i, x_j, y_j, z_j, w_j):
    delta_x = x_j - x_i
    delta_y = y_j - y_i
    delta_z = z_j - z_i
    squared = delta_x * delta_x + delta_y * delta_y + delta_z * delta_z
    held = jnp.maximum(squared, CLOSEST_SQUARED)
    inverse = lax.rsqrt(held)
    distance = held * inverse
    scaled = distance * lax.rsqrt(w_i + w_j)
    value = (lax.erf(scaled) - lax.erf(distance)) * inverse
    return jnp.where(squared < CUT_SQUARED, value, 0.0)


def to_rows(sums, block):
    here = lane_index((8, LANES)) - row_index((8, LANES)) == 8 * block
    return jnp.where(here, jnp.sum(sums, axis=1, keepdims=True), 0.0)


def add_rows(cell, sums, rows):
    for index in range(2):
        total = jnp.zeros((8, LANES), jnp.float32)
        for block in range(BLOCKS):
            total = total + to_rows(sums[cell, block, index], block)
        rows.append(jnp.sum(total, axis=0, keepdims=True))


def finish_cell(cell, info, sums, diagonal, out):
    rows = []
    add_rows(cell, sums, rows)
    here = (cell // CZ) * EZ + cell % CZ + 1
    scale = PAIR_SCALE / diagonal[pl.ds(cell, 1), :]
    live = lane_index((1, LANES)) < info[here, 7:8, :].astype(jnp.int32)
    out[cell, 0:1, :] = jnp.where(live, rows[0] * scale, 0.0)
    out[cell, 1:2, :] = jnp.where(live, rows[1] * scale, 0.0)


def build_cell(cell, lines, turned, kernels, before, sums, below):
    own = None
    if below is not None:
        own = lane_index((8, LANES)) - row_index((8, LANES)) - below
    for group in GROUPS:
        sums_s, sums_t = start_sums(cell, before, group)
        for index, line in enumerate(lines):
            beside = [line(k) for k in range(6)]
            for at, block in enumerate(group):
                value = couple(*[turned[cell, block, k] for k in range(4)], *beside[:4])
                if own is not None and index < 2:
                    value = jnp.where(own == 8 * block - LANES * index, 0.0, value)
                kernels[cell, block, index] = value
                sums_s[at] = sums_s[at] + value * beside[4]
                sums_t[at] = sums_t[at] + value * beside[5]
        for at, block in enumerate(group):
            sums[cell, block, 0] = sums_s[at]
            sums[cell, block, 1] = sums_t[at]


def start_sums(cell, before, blocks):
    if before is None:
        zeros = [jnp.zeros((8, LANES), jnp.float32) for _ in blocks]
        return zeros, list(zeros)
    sums_s = [before[cell, block, 0] for block in blocks]
    return sums_s, [before[cell, block, 1] for block in blocks]


def lines_of(packed, columns, z):
    def line(column, half):
        return lambda k: spread(packed[column * CZ + z, half, k : k + 1, :])

    return [line(column, half) for column in columns for half in range(2)]


def rest_line(rest, cell):
    return lambda k: spread(rest[cell, k : k + 1, :])


def parts_of(value):
    high = value.astype(jnp.bfloat16).astype(jnp.float32)
    rest = value - high
    middle = rest.astype(jnp.bfloat16).astype(jnp.float32)
    return high, middle, rest - middle


def turn_cells(core, turned):
    chosen = row_index((24, 4 * LANES)) & 7
    ones = jnp.where(chosen == lane_index((24, 4 * LANES)) >> 7, 1.0, 0.0).astype(jnp.bfloat16)
    for cell in range(CELLS):
        here = core[(cell // CZ) * EZ + cell % CZ + 1]
        left = jnp.concatenate(parts_of(here), axis=0).T[: 8 * BLOCKS + 8].astype(jnp.bfloat16)
        wide = lax.dot_general(
            left, ones, (((1,), (0,)), ((), ())), preferred_element_type=jnp.float32
        )
        for block in range(BLOCKS):
            for k in range(4):
                turned[cell, block, k] = wide[8 * block : 8 * block + 8, k * LANES : (k + 1) * LANES]


def core_spills(spills, spill):
    for z in range(CZ):
        spill[z] = overflow_of(spills, range(QUADS), z)


def face_spills(spills, before, spill):
    for cell in range(CELLS):
        q, z = cell // CZ, cell % CZ
        spill[cell] = before[z] + overflow_of(spills, face_columns(q), z)


def corner_spills(spills, before, rest):
    for cell in range(CELLS):
        rest[cell] = before[cell] + spills[cell]


def core_kernel(core, kernels, sums, spill, turned, packed, spills):
    turn_cells(core, turned)
    pack_core(core, core, packed, spills, True)
    core_spills(spills, spill)

    def one_cell(cell, _):
        q, z = cell // CZ, cell % CZ
        below = spread(core[q * EZ + z, 7:8, :]).astype(jnp.int32)
        build_cell(cell, lines_of(packed, core_columns(q), z), turned, kernels, None, sums, below)
        return 0

    lax.fori_loop(0, CELLS, one_cell, 0, unroll=2)


def face_kernel(
    x_low, x_high, beyond, turned, before, spill_before, kernels, sums, spill, packed, spills
):
    pieces = [x_low, x_high, beyond]
    pack_faces(pieces, pieces, packed, spills, True)
    face_spills(spills, spill_before, spill)

    def one_cell(cell, _):
        lines = lines_of(packed, face_columns(cell // CZ), cell % CZ)
        build_cell(cell, lines, turned, kernels, before, sums, None)
        return 0

    lax.fori_loop(0, CELLS, one_cell, 0, unroll=2)


def corner_kernel(
    corners, turned, before, spill_before, core, diagonal, kernels, out, packed, spills, rest, sums
):
    pack_corners(corners, corners, packed, spills, True)
    corner_spills(spills, spill_before, rest)

    def one_cell(cell, _):
        finish_cell(jnp.maximum(cell - 1, 0), core, sums, diagonal, out)
        lines = lines_of(packed, [cell // CZ], cell % CZ) + [rest_line(rest, cell)]
        build_cell(cell, lines, turned, kernels, before, sums, None)
        return 0

    sums[0] = jnp.zeros(SUMS.shape[1:], jnp.float32)
    lax.fori_loop(0, CELLS, one_cell, 0, unroll=2)
    finish_cell(CELLS - 1, core, sums, diagonal, out)


IN_VMEM = pl.BlockSpec(memory_space=VMEM)
IN_SMEM = pl.BlockSpec(memory_space=SMEM)
PAIR = jax.ShapeDtypeStruct((CELLS, 2, LANES), jnp.float32)
SPILL = jax.ShapeDtypeStruct((CELLS, 8, LANES), jnp.float32)
SUMS = jax.ShapeDtypeStruct((CELLS, BLOCKS, 2, 8, LANES), jnp.float32)
TURNED = jax.ShapeDtypeStruct((CELLS, BLOCKS, 4, 8, LANES), jnp.float32)
CORE_SPILL = jax.ShapeDtypeStruct((CZ, 8, LANES), jnp.float32)
CORE_TILES, FACE_TILES, CORNER_TILES = 8, 8, 3


def held(tiles):
    return VMEM((CELLS, BLOCKS, tiles, 8, LANES), jnp.float32)


def call(kernel, outs, scratch, tiles, *arrays):
    work = CELLS * BLOCKS * tiles * 8 * LANES
    return pl.pallas_call(
        kernel,
        out_shape=outs,
        in_specs=[IN_SMEM if array.ndim == 1 else IN_VMEM for array in arrays],
        out_specs=jax.tree.map(lambda _: IN_VMEM, outs),
        scratch_shapes=scratch,
        compiler_params=params(8),
        cost_estimate=pl.CostEstimate(
            flops=30 * work, bytes_accessed=8 * work, transcendentals=4 * work
        ),
    )(*arrays)


def packs(columns):
    return [
        VMEM((columns * CZ, 2, 8, LANES), jnp.float32),
        VMEM((columns * CZ, 8, LANES), jnp.float32),
    ]


def build_core(core):
    outs = (held(CORE_TILES), SUMS, CORE_SPILL, TURNED)
    return call(core_kernel, outs, packs(4), CORE_TILES, core)


def build_faces(pieces, turned, before, spill):
    outs = (held(FACE_TILES), SUMS, SPILL)
    return call(face_kernel, outs, packs(8), FACE_TILES, *pieces, turned, before, spill)


def corner_scratch():
    return packs(4) + [VMEM(SPILL.shape, jnp.float32), VMEM(SUMS.shape, jnp.float32)]


def build_corners(corners, turned, before, spill, core, diagonal):
    arrays = [corners, turned, before, spill, core, diagonal]
    return call(corner_kernel, (held(CORNER_TILES), PAIR), corner_scratch(), CORNER_TILES, *arrays)


def apply_cell(cell, lines, stored, before, sums):
    sums_s, sums_t = start_sums(cell, before, range(BLOCKS))
    for index, line in enumerate(lines):
        line_s, line_t = line(0), line(1)
        for block in range(BLOCKS):
            value = stored[cell, block, index]
            sums_s[block] = sums_s[block] + value * line_s
            sums_t[block] = sums_t[block] + value * line_t
    for block in range(BLOCKS):
        sums[cell, block, 0] = sums_s[block]
        sums[cell, block, 1] = sums_t[block]


def widen(pieces, wides):
    for piece, wide in zip(pieces, wides):
        wide[:, 0:2, :] = piece[...]


def invert_core_kernel(counts, atoms, info, core, stored, sums, spill, places, wide, packed, spills):
    invert(counts, atoms, places)
    apply_core_kernel(info, core, stored, sums, spill, wide, packed, spills)


def apply_core_kernel(info, core, stored, sums, spill, wide, packed, spills):
    widen([core], [wide])
    pack_core(info, wide, packed, spills, False)
    core_spills(spills, spill)

    def one_cell(cell, _):
        lines = lines_of(packed, core_columns(cell // CZ), cell % CZ)
        apply_cell(cell, lines, stored, None, sums)
        return 0

    lax.fori_loop(0, CELLS, one_cell, 0, unroll=2)


def apply_face_kernel(*refs):
    infos, pieces, (stored, before, spill_before, sums, spill), wides, (packed, spills) = split(
        refs, 3, 3, 5, 3, 2
    )
    widen(pieces, wides)
    pack_faces(infos, wides, packed, spills, False)
    face_spills(spills, spill_before, spill)

    def one_cell(cell, _):
        lines = lines_of(packed, face_columns(cell // CZ), cell % CZ)
        apply_cell(cell, lines, stored, before, sums)
        return 0

    lax.fori_loop(0, CELLS, one_cell, 0, unroll=2)


def apply_corner_tiles(
    info, corners, stored, before, spill_before, core, diagonal, out, wide, packed, spills, rest, sums
):
    widen([corners], [wide])
    pack_corners(info, wide, packed, spills, False)
    corner_spills(spills, spill_before, rest)

    def one_cell(cell, _):
        finish_cell(jnp.maximum(cell - 1, 0), core, sums, diagonal, out)
        lines = lines_of(packed, [cell // CZ], cell % CZ) + [rest_line(rest, cell)]
        apply_cell(cell, lines, stored, before, sums)
        return 0

    sums[0] = jnp.zeros(SUMS.shape[1:], jnp.float32)
    lax.fori_loop(0, CELLS, one_cell, 0, unroll=2)
    finish_cell(CELLS - 1, core, sums, diagonal, out)


def split(refs, *sizes):
    parts = []
    for size in sizes:
        parts.append(refs[:size])
        refs = refs[size:]
    return parts


def apply_last_kernel(*refs):
    ins, (slots, first, second, moments, third), work = split(refs, 7, 5, 5)
    diagonal = ins[6]
    apply_corner_tiles(*ins, third, *work)
    d = diagonal[...][:, None, :]
    v_0 = slots[:, 4:6, :]
    v_1 = first[...]
    v_2 = second[...]
    d_0 = d * v_0
    d_2 = d * v_2
    parts = [d_0 * v_0, d_0 * v_1, d * v_1 * v_1, d_2 * v_1, d_2 * v_2, d_2 * third[...]]
    row = row_index((2, LANES))
    line = jnp.zeros((2, LANES), jnp.float32)
    for index, part in enumerate(parts + [v_0, v_1, v_2]):
        total = jnp.sum(jnp.sum(part, axis=0), axis=1, keepdims=True)
        line = jnp.where(lane_index((2, LANES)) - row == 2 * index, total, line)
    moments[...] = jnp.sum(line, axis=0, keepdims=True)


def wide(piece):
    return VMEM((piece.shape[0], 8, LANES), jnp.float32)


def apply_core(info, core, stored, lists):
    stored = pltpu.with_memory_space_constraint(stored, VMEM)
    scratch = [wide(core)] + packs(4)
    outs = (SUMS, CORE_SPILL)
    if lists is None:
        return call(apply_core_kernel, outs, scratch, 2, info, core, stored)
    counts, atoms, atoms_local = lists
    rows = (atoms_local // LANES + 15) // 16 * 16
    places = jax.ShapeDtypeStruct((2, rows, LANES), jnp.int32)
    return call(
        invert_core_kernel, outs + (places,), scratch, 2, counts, atoms, info, core, stored
    )


def apply_faces(infos, pieces, stored, before, spill):
    stored = pltpu.with_memory_space_constraint(stored, VMEM)
    scratch = [wide(piece) for piece in pieces] + packs(8)
    return call(
        apply_face_kernel, (SUMS, SPILL), scratch, 2, *infos, *pieces, stored, before, spill
    )


def apply_corners(info, corners, stored, before, spill, core, diagonal, last):
    stored = pltpu.with_memory_space_constraint(stored, VMEM)
    scratch = [wide(corners)] + corner_scratch()
    arrays = [info, corners, stored, before, spill, core, diagonal]
    if last is None:
        return call(apply_corner_tiles, PAIR, scratch, 2, *arrays)
    third = VMEM((CELLS, 2, LANES), jnp.float32)
    out = jax.ShapeDtypeStruct((1, LANES), jnp.float32)
    return call(apply_last_kernel, out, [third] + scratch, 2, *arrays, *last)


def solve(g):
    tiny = 1e-6
    h = [g[k] + g[k + 1] for k in range(5)]
    ratio_1 = h[1] / h[0]
    ratio_2 = h[2] / h[0]
    pivot_1 = h[2] - ratio_1 * h[1]
    mixed = h[3] - ratio_1 * h[2]
    rest_1 = g[1] - ratio_1 * g[0]
    live_1 = pivot_1 > tiny * h[2]
    safe_1 = jnp.where(live_1, pivot_1, 1.0)
    ratio_3 = jnp.where(live_1, mixed / safe_1, 0.0)
    pivot_2 = h[4] - ratio_2 * h[2] - ratio_3 * mixed
    rest_2 = g[2] - ratio_2 * g[0] - ratio_3 * rest_1
    live_2 = live_1 & (pivot_2 > tiny * h[4])
    c_2 = jnp.where(live_2, rest_2 / jnp.where(live_2, pivot_2, 1.0), 0.0)
    c_1 = jnp.where(live_1, (rest_1 - mixed * c_2) / safe_1, 0.0)
    c_0 = (g[0] - h[1] * c_1 - h[2] * c_2) / h[0]
    return c_0, c_1, c_2


def invert(counts, atoms, places):
    rows = places.shape[1]
    row_low = row_index((LANES, LANES))
    row_high = row_index((rows, LANES))
    lane = lane_index((rows, LANES))

    def one_cell(cell, total):
        live = lane_index((1, LANES)) < counts[cell]
        pointer = jnp.where(live, atoms[pl.ds(cell, 1), :], -1)
        here = (pointer >> 7) == row_high
        cells = jnp.where(here, cell, 0).astype(jnp.float32)
        slots = jnp.where(here, lane, 0).astype(jnp.float32)
        parts = jnp.concatenate([cells, slots], axis=0).astype(jnp.bfloat16)
        lows = jnp.where((pointer & 127) == row_low, 1.0, 0.0).astype(jnp.bfloat16)
        return total + lax.dot_general(
            parts, lows, (((1,), (1,)), ((), ())), preferred_element_type=jnp.float32
        )

    total = jnp.zeros((2 * rows, LANES), jnp.float32)
    total = lax.fori_loop(0, CELLS, one_cell, total, unroll=8).astype(jnp.int32)
    places[0] = total[:rows]
    places[1] = total[rows:]


def finish_kernel(moments, slots, first, second, places, out, charges):
    summed = moments[...]
    lane = lane_index((2, LANES))
    row = row_index((2, LANES))

    def pair(index):
        picked = jnp.where(lane - row == 2 * index, summed, 0.0)
        return jnp.broadcast_to(jnp.sum(picked, axis=1, keepdims=True), (2, LANES))

    rows = [pair(index) for index in range(9)]
    c_0, c_1, c_2 = solve(rows[:6])
    totals = c_0 * rows[6] + c_1 * rows[7] + c_2 * rows[8]
    balance = totals[0:1] / totals[1:2]
    sign = jnp.concatenate([jnp.ones((1, LANES), jnp.float32), -balance], axis=0)
    c_0, c_1, c_2 = c_0 * sign, c_1 * sign, c_2 * sign
    for cell in range(CELLS):
        mixed = c_0 * slots[cell, 4:6, :] + c_1 * first[cell] + c_2 * second[cell]
        charges[cell : cell + 1, :] = jnp.sum(mixed, axis=0, keepdims=True)
    tiles = [jnp.zeros((8, LANES), jnp.float32) for _ in range(places.shape[1] // 8)]
    for cell in range(CELLS):
        line = spread(charges[cell : cell + 1, :])
        for at in range(len(tiles)):
            here = slice(8 * at, 8 * at + 8)
            moved = jnp.take_along_axis(line, places[1, here, :], axis=1)
            tiles[at] = jnp.where(places[0, here, :] == cell, moved, tiles[at])
    out[...] = jnp.concatenate(tiles, axis=0)[: out.shape[0]]


def finish(moments, slots, first, second, places, atoms_local):
    return pl.pallas_call(
        finish_kernel,
        out_shape=jax.ShapeDtypeStruct((atoms_local // LANES, LANES), jnp.float32),
        in_specs=[IN_VMEM] * 5,
        out_specs=IN_VMEM,
        scratch_shapes=[VMEM((CELLS, LANES), jnp.float32)],
        compiler_params=params(8),
    )(moments, slots, first, second, places)


def partner(block, axis, mask):
    count = lax.axis_size(axis)
    return lax.ppermute(block, axis, [(low, low ^ mask) for low in range(count)])


def shifted(block, along_x):
    count = lax.axis_size("gx")
    return lax.ppermute(block, "gx", [(i, (i + 4 * along_x) % count) for i in range(count)])


def with_z_faces(cells):
    cells = cells.reshape((QUADS, CZ) + cells.shape[1:])
    faces = jnp.concatenate([cells[:, -1:], cells[:, :1]], axis=1)
    other = partner(faces, "gx", 1)
    return jnp.concatenate([other[:, 0:1], cells, other[:, 1:2]], axis=1)


def flat(columns):
    return columns.reshape((-1,) + columns.shape[-2:])


def x_faces(core):
    count = lax.axis_size("gx")
    rows = count // 4
    odd = (lax.axis_index("gx") // 4) % 2 == 1
    if rows % 2:
        return shifted(core[2:], 1), shifted(core[:2], -1)
    first = lax.ppermute(jnp.where(odd, core[:2], core[2:]), "gx", [(i, i ^ 4) for i in range(count)])
    route = [(i, (i + (4 if (i // 4) % 2 else -4)) % count) for i in range(count)]
    second = lax.ppermute(jnp.where(odd, core[2:], core[:2]), "gx", route)
    return first, second


def sorted_faces(first, second):
    odd = (lax.axis_index("gx") // 4) % 2 == 1
    if (lax.axis_size("gx") // 4) % 2:
        return first, second
    return jnp.where(odd, first, second), jnp.where(odd, second, first)


def exchange(cells, on_core, on_faces, on_corners):
    core = with_z_faces(cells)
    first, second = x_faces(core)
    beyond = partner(core, "gx", 2)
    sums, spill, *more = on_core(flat(core))
    first, second, sums = lax.optimization_barrier((first, second, sums))
    low, high = sorted_faces(first, second)
    corners = partner(jnp.concatenate([low, high], axis=0), "gx", 2)
    pieces = [flat(part) for part in (low, high, beyond)]
    sums, spill, *more = on_faces(pieces, sums, spill, *more)
    corners = flat(corners)
    return flat(core), pieces, corners, on_corners(corners, sums, spill, flat(core), *more)


def global_sum(values):
    count = lax.axis_size("gx")
    if count & (count - 1) or count < 4:
        return lax.psum(values, "gx")
    values = values + partner(values, "gx", 1)

    def over(mask):
        route = [(i, i ^ mask) for i in range(count) if i & 1]
        return lax.ppermute(values, "gx", route)

    step = 2
    while step < count:
        if step >= 4 and 4 * step <= count:
            others = [over(k * step) for k in (3, 2, 1)]
            values = (values + others[0]) + (others[1] + others[2])
            step *= 4
        else:
            values = values + over(step)
            step *= 2
    back = lax.ppermute(values, "gx", [(i, i ^ 1) for i in range(count) if i & 1])
    return jnp.where(lax.axis_index("gx") % 2 == 1, values, back)


def local(cell_offsets, electronegativity, hardness, charge_widths, cell_counts, cell_atoms):
    slots, diagonal = prepare(
        cell_counts, cell_offsets, electronegativity, hardness, charge_widths, cell_atoms
    )
    stored = []

    def keep(tiles, *others):
        stored.append(tiles)
        return others

    core, pieces, corners, (first,) = exchange(
        slots,
        lambda core: keep(*build_core(core)),
        lambda faces, sums, spill, *own: keep(*build_faces(faces, *own, sums, spill)) + own,
        lambda corners, sums, spill, core, *own: keep(
            *build_corners(corners, *own, sums, spill, core, diagonal)
        ),
    )

    def apply(cells, lists, last):
        def on_faces(faces, sums, spill, *found):
            return (*apply_faces(pieces, faces, stored[1], sums, spill), *found)

        def on_corners(others, sums, spill, _, *found):
            result = apply_corners(
                corners, others, stored[2], sums, spill, core, diagonal, last
            )
            return result, found

        return exchange(
            cells, lambda own: apply_core(core, own, stored[0], lists), on_faces, on_corners
        )[3]

    atoms_local = cell_offsets.shape[1]
    second, (places,) = apply(first, (cell_counts, cell_atoms, atoms_local), None)
    moments, _ = apply(second, None, (slots, first, second))
    charges = finish(global_sum(moments), slots, first, second, places, atoms_local)
    return charges.reshape(-1)


def solution(mesh):
    placed = (
        P(None, ("grp", "gx")),
        P(("grp", "gx")),
        P(("grp", "gx")),
        P(("grp", "gx")),
        P(("grp", "gx")),
        P(("grp", "gx"), None),
    )
    return jax.shard_map(
        local, mesh=mesh, in_specs=placed, out_specs=P(("grp", "gx")), check_vma=False
    )
```

```python
import functools
import math

import jax
import jax.numpy as jnp
from jax import lax
from jax.experimental import pallas as pl
from jax.experimental.pallas import tpu as pltpu
from jax.sharding import PartitionSpec as P

CX = 2
CY = 2
CZ = 8
EZ = CZ + 2
CELLS = CX * CY * CZ
QUADS = CX * CY
LANES = 128
BLOCKS = 11
GROUPS = ((0, 1, 2, 3), (4, 5, 6, 7), (8, 9, 10))

COULOMB = 14.399645
ROOT_PI = math.sqrt(math.pi)
SCREEN = 1.0 / (math.sqrt(2.0) * 3.0)
EWALD_SELF = math.sqrt(2.0 / math.pi) / 3.0
SIDE = 12.0 * SCREEN
CUT_SQUARED = (12.0 * SCREEN) ** 2
CLOSEST_SQUARED = (0.5 * SCREEN) ** 2
PAIR_SCALE = COULOMB * SCREEN

VMEM = pltpu.VMEM
SMEM = pltpu.SMEM


def params(mib):
    return pltpu.CompilerParams(vmem_limit_bytes=mib * 2**20)


def lane_index(shape):
    return lax.broadcasted_iota(jnp.int32, shape, len(shape) - 1)


def row_index(shape):
    return lax.broadcasted_iota(jnp.int32, shape, len(shape) - 2)


def prepare_kernel(
    counts_hbm, offsets, negativity, hardness, widths, atoms, slots, diagonal,
    counts, raw_offsets, raw_negativity, raw_hardness, raw_widths, raw_atoms, table, sems,
):
    copies = [
        pltpu.make_async_copy(source, target, sems.at[index])
        for index, (source, target) in enumerate(
            [
                (counts_hbm, counts),
                (offsets, raw_offsets),
                (negativity, raw_negativity),
                (hardness, raw_hardness),
                (widths, raw_widths),
                (atoms, raw_atoms),
            ]
        )
    ]
    for copy in copies:
        copy.start()
    for copy in copies:
        copy.wait()
    chunks = table.shape[0]
    for chunk in range(chunks):
        here = slice(chunk * LANES, (chunk + 1) * LANES)
        table[chunk, 0:3, :] = raw_offsets[:, here]
        table[chunk, 3:4, :] = raw_widths[chunk : chunk + 1, :]
        table[chunk, 4:5, :] = raw_negativity[chunk : chunk + 1, :]
        table[chunk, 5:6, :] = raw_hardness[chunk : chunk + 1, :]
        table[chunk, 6:8, :] = jnp.zeros((2, LANES), jnp.float32)

    def one_cell(cell, _):
        count = counts[cell]
        occupied = lane_index((1, LANES)) < count
        pointer = jnp.where(occupied, raw_atoms[pl.ds(cell, 1), :], 0)
        high = jnp.broadcast_to(pointer >> 7, (8, LANES))
        low = jnp.broadcast_to(pointer & 127, (8, LANES))
        picked = jnp.zeros((8, LANES), jnp.float32)
        for chunk in range(chunks):
            part = jnp.take_along_axis(table[chunk], low, axis=1)
            picked = jnp.where(high == chunk, part, picked)
        width = jnp.where(occupied, picked[3:4], 1.0)
        diag = jnp.where(
            occupied, picked[5:6] + COULOMB * (1.0 / (width * ROOT_PI) - EWALD_SELF), 1.0
        )
        negative = jnp.where(occupied, picked[4:5], 0.0)
        place = jnp.where(
            row_index((8, LANES)) == 0, cell // (CY * CZ), (cell // CZ) % CY
        ).astype(jnp.float32)
        place = jnp.where(row_index((8, LANES)) < 2, place, 0.0)
        slots[cell, 0:3, :] = ((picked + place) * SIDE)[0:3]
        slots[cell, 3:4, :] = (2.0 * SCREEN * SCREEN) * width * width
        slots[cell, 4:5, :] = -negative / diag
        slots[cell, 5:6, :] = jnp.where(occupied, 1.0 / diag, 0.0)
        slots[cell, 6:7, :] = jnp.zeros((1, LANES), jnp.float32)
        slots[cell, 7:8, :] = jnp.full((1, LANES), count.astype(jnp.float32))
        diagonal[pl.ds(cell, 1), :] = diag
        return 0

    lax.fori_loop(0, CELLS, one_cell, 0, unroll=4)


def prepare(counts, offsets, negativity, hardness, widths, atoms):
    chunks = offsets.shape[1] // LANES
    plane = (chunks, LANES)
    return pl.pallas_call(
        prepare_kernel,
        out_shape=(
            jax.ShapeDtypeStruct((CELLS, 8, LANES), jnp.float32),
            jax.ShapeDtypeStruct((CELLS, LANES), jnp.float32),
        ),
        in_specs=[pl.BlockSpec(memory_space=pltpu.HBM)] * 6,
        out_specs=(pl.BlockSpec(memory_space=VMEM), pl.BlockSpec(memory_space=VMEM)),
        scratch_shapes=[
            SMEM(counts.shape, jnp.int32),
            VMEM(offsets.shape, jnp.float32),
            VMEM(plane, jnp.float32),
            VMEM(plane, jnp.float32),
            VMEM(plane, jnp.float32),
            VMEM(atoms.shape, jnp.int32),
            VMEM((chunks, 8, LANES), jnp.float32),
            pltpu.SemaphoreType.DMA((6,)),
        ],
        compiler_params=params(8),
    )(
        *[
            pltpu.with_memory_space_constraint(array, pltpu.HBM)
            for array in (
                counts,
                offsets,
                negativity.reshape(plane),
                hardness.reshape(plane),
                widths.reshape(plane),
                atoms,
            )
        ]
    )


def pack_column(info, cells, source, packed, spills, target, at, shift):
    lane = lane_index((8, LANES))
    row = row_index((8, LANES))
    for z in range(CZ):
        base = source * EZ + z
        low, mid, top = [spread(info[base + k, 7:8, :]).astype(jnp.int32) for k in range(3)]
        end = low + mid - LANES
        tiles = [cells[base + k] for k in range(3)]
        if shift is not None:
            for k in range(3):
                offset = jnp.where(row == 2, (k - 1) * SIDE, 0.0)
                for axis in range(2):
                    offset = jnp.where(row == axis, shift[axis] * SIDE, offset)
                tiles[k] = tiles[k] + offset
        second = jnp.take_along_axis(tiles[1], (lane - low) & 127, axis=1)
        third = jnp.take_along_axis(tiles[2], (lane - end) & 127, axis=1)
        packed[target * CZ + z, 0] = jnp.where(lane < low, tiles[0], second)
        packed[target * CZ + z, 1] = jnp.where(lane < end, second, third)
        spill = jnp.where(lane < end + top - LANES, third, 0.0)
        spills[target * CZ + z] = pltpu.roll(spill, at, 1) if at else spill


def pack_core(info, cells, packed, spills, build):
    for q in range(QUADS):
        pack_column(info, cells, q, packed, spills, q, 8 * q, (0, 0) if build else None)


def pack_faces(infos, pieces, packed, spills, build):
    for side in range(2):
        sign = 2 * side - 1
        for y in range(CY):
            shift = (sign * CX, 0) if build else None
            at = 32 + 8 * y
            pack_column(infos[side], pieces[side], y, packed, spills, 2 * side + y, at, shift)
        for x in range(CX):
            shift = (0, sign * CY) if build else None
            source = 2 * x + 1 - side
            target = 4 + 2 * x + side
            at = 48 + 8 * x
            pack_column(infos[2], pieces[2], source, packed, spills, target, at, shift)


def pack_corners(info, cells, packed, spills, build):
    for side_x in range(2):
        for side_y in range(2):
            shift = ((2 * side_x - 1) * CX, (2 * side_y - 1) * CY) if build else None
            source = 2 * side_x + 1 - side_y
            pack_column(info, cells, source, packed, spills, 2 * side_x + side_y, 64, shift)


def core_columns(q):
    return [q ^ k for k in range(4)]


def face_columns(q):
    x, y = q >> 1, q & 1
    return [2 * x, 2 * x + 1, 4 + y, 6 + y]


def overflow_of(spills, columns, z):
    return sum(spills[column * CZ + z] for column in columns)


def spread(row):
    return jnp.broadcast_to(row, (8, LANES))


def couple(x_i, y_i, z_i, w_i, x_j, y_j, z_j, w_j):
    delta_x = x_j - x_i
    delta_y = y_j - y_i
    delta_z = z_j - z_i
    squared = delta_x * delta_x + delta_y * delta_y + delta_z * delta_z
    held = jnp.maximum(squared, CLOSEST_SQUARED)
    inverse = lax.rsqrt(held)
    distance = held * inverse
    scaled = distance * lax.rsqrt(w_i + w_j)
    value = (lax.erf(scaled) - lax.erf(distance)) * inverse
    return jnp.where(squared < CUT_SQUARED, value, 0.0)


def to_rows(sums, block):
    here = lane_index((8, LANES)) - row_index((8, LANES)) == 8 * block
    return jnp.where(here, jnp.sum(sums, axis=1, keepdims=True), 0.0)


def add_rows(cell, sums, rows):
    for index in range(2):
        total = jnp.zeros((8, LANES), jnp.float32)
        for block in range(BLOCKS):
            total = total + to_rows(sums[cell, block, index], block)
        rows.append(jnp.sum(total, axis=0, keepdims=True))


def finish_cell(cell, info, sums, diagonal, out):
    rows = []
    add_rows(cell, sums, rows)
    here = (cell // CZ) * EZ + cell % CZ + 1
    scale = PAIR_SCALE / diagonal[pl.ds(cell, 1), :]
    live = lane_index((1, LANES)) < info[here, 7:8, :].astype(jnp.int32)
    out[cell, 0:1, :] = jnp.where(live, rows[0] * scale, 0.0)
    out[cell, 1:2, :] = jnp.where(live, rows[1] * scale, 0.0)


def build_cell(cell, lines, turned, kernels, before, sums, below):
    own = None
    if below is not None:
        own = lane_index((8, LANES)) - row_index((8, LANES)) - below
    for group in GROUPS:
        sums_s, sums_t = start_sums(cell, before, group)
        for index, line in enumerate(lines):
            beside = [line(k) for k in range(6)]
            for at, block in enumerate(group):
                value = couple(*[turned[cell, block, k] for k in range(4)], *beside[:4])
                if own is not None and index < 2:
                    value = jnp.where(own == 8 * block - LANES * index, 0.0, value)
                kernels[cell, block, index] = value
                sums_s[at] = sums_s[at] + value * beside[4]
                sums_t[at] = sums_t[at] + value * beside[5]
        for at, block in enumerate(group):
            sums[cell, block, 0] = sums_s[at]
            sums[cell, block, 1] = sums_t[at]


def start_sums(cell, before, blocks):
    if before is None:
        zeros = [jnp.zeros((8, LANES), jnp.float32) for _ in blocks]
        return zeros, list(zeros)
    sums_s = [before[cell, block, 0] for block in blocks]
    return sums_s, [before[cell, block, 1] for block in blocks]


def lines_of(packed, columns, z):
    def line(column, half):
        return lambda k: spread(packed[column * CZ + z, half, k : k + 1, :])

    return [line(column, half) for column in columns for half in range(2)]


def rest_line(rest, cell):
    return lambda k: spread(rest[cell, k : k + 1, :])


def parts_of(value):
    high = value.astype(jnp.bfloat16).astype(jnp.float32)
    rest = value - high
    middle = rest.astype(jnp.bfloat16).astype(jnp.float32)
    return high, middle, rest - middle


def turn_cells(core, turned):
    chosen = row_index((24, 4 * LANES)) & 7
    ones = jnp.where(chosen == lane_index((24, 4 * LANES)) >> 7, 1.0, 0.0).astype(jnp.bfloat16)
    for cell in range(CELLS):
        here = core[(cell // CZ) * EZ + cell % CZ + 1]
        left = jnp.concatenate(parts_of(here), axis=0).T[: 8 * BLOCKS + 8].astype(jnp.bfloat16)
        wide = lax.dot_general(
            left, ones, (((1,), (0,)), ((), ())), preferred_element_type=jnp.float32
        )
        for block in range(BLOCKS):
            for k in range(4):
                turned[cell, block, k] = wide[8 * block : 8 * block + 8, k * LANES : (k + 1) * LANES]


def core_spills(spills, spill):
    for z in range(CZ):
        spill[z] = overflow_of(spills, range(QUADS), z)


def face_spills(spills, before, spill):
    for cell in range(CELLS):
        q, z = cell // CZ, cell % CZ
        spill[cell] = before[z] + overflow_of(spills, face_columns(q), z)


def corner_spills(spills, before, rest):
    for cell in range(CELLS):
        rest[cell] = before[cell] + spills[cell]


def core_kernel(core, kernels, sums, spill, turned, packed, spills):
    turn_cells(core, turned)
    pack_core(core, core, packed, spills, True)
    core_spills(spills, spill)

    def one_cell(cell, _):
        q, z = cell // CZ, cell % CZ
        below = spread(core[q * EZ + z, 7:8, :]).astype(jnp.int32)
        build_cell(cell, lines_of(packed, core_columns(q), z), turned, kernels, None, sums, below)
        return 0

    lax.fori_loop(0, CELLS, one_cell, 0, unroll=2)


def face_kernel(
    x_low, x_high, beyond, turned, before, spill_before, kernels, sums, spill, packed, spills
):
    pieces = [x_low, x_high, beyond]
    pack_faces(pieces, pieces, packed, spills, True)
    face_spills(spills, spill_before, spill)

    def one_cell(cell, _):
        lines = lines_of(packed, face_columns(cell // CZ), cell % CZ)
        build_cell(cell, lines, turned, kernels, before, sums, None)
        return 0

    lax.fori_loop(0, CELLS, one_cell, 0, unroll=2)


def corner_kernel(
    corners, turned, before, spill_before, core, diagonal, kernels, out, packed, spills, rest, sums
):
    pack_corners(corners, corners, packed, spills, True)
    corner_spills(spills, spill_before, rest)

    def one_cell(cell, _):
        finish_cell(jnp.maximum(cell - 1, 0), core, sums, diagonal, out)
        lines = lines_of(packed, [cell // CZ], cell % CZ) + [rest_line(rest, cell)]
        build_cell(cell, lines, turned, kernels, before, sums, None)
        return 0

    sums[0] = jnp.zeros(SUMS.shape[1:], jnp.float32)
    lax.fori_loop(0, CELLS, one_cell, 0, unroll=2)
    finish_cell(CELLS - 1, core, sums, diagonal, out)


IN_VMEM = pl.BlockSpec(memory_space=VMEM)
IN_SMEM = pl.BlockSpec(memory_space=SMEM)
PAIR = jax.ShapeDtypeStruct((CELLS, 2, LANES), jnp.float32)
SPILL = jax.ShapeDtypeStruct((CELLS, 8, LANES), jnp.float32)
SUMS = jax.ShapeDtypeStruct((CELLS, BLOCKS, 2, 8, LANES), jnp.float32)
TURNED = jax.ShapeDtypeStruct((CELLS, BLOCKS, 4, 8, LANES), jnp.float32)
CORE_SPILL = jax.ShapeDtypeStruct((CZ, 8, LANES), jnp.float32)
CORE_TILES, FACE_TILES, CORNER_TILES = 8, 8, 3


def held(tiles):
    return VMEM((CELLS, BLOCKS, tiles, 8, LANES), jnp.float32)


def call(kernel, outs, scratch, tiles, *arrays):
    work = CELLS * BLOCKS * tiles * 8 * LANES
    return pl.pallas_call(
        kernel,
        out_shape=outs,
        in_specs=[IN_SMEM if array.ndim == 1 else IN_VMEM for array in arrays],
        out_specs=jax.tree.map(lambda _: IN_VMEM, outs),
        scratch_shapes=scratch,
        compiler_params=params(8),
        cost_estimate=pl.CostEstimate(
            flops=30 * work, bytes_accessed=8 * work, transcendentals=4 * work
        ),
    )(*arrays)


def packs(columns):
    return [
        VMEM((columns * CZ, 2, 8, LANES), jnp.float32),
        VMEM((columns * CZ, 8, LANES), jnp.float32),
    ]


def build_core(core):
    outs = (held(CORE_TILES), SUMS, CORE_SPILL, TURNED)
    return call(core_kernel, outs, packs(4), CORE_TILES, core)


def build_faces(pieces, turned, before, spill):
    outs = (held(FACE_TILES), SUMS, SPILL)
    return call(face_kernel, outs, packs(8), FACE_TILES, *pieces, turned, before, spill)


def corner_scratch():
    return packs(4) + [VMEM(SPILL.shape, jnp.float32), VMEM(SUMS.shape, jnp.float32)]


def build_corners(corners, turned, before, spill, core, diagonal):
    arrays = [corners, turned, before, spill, core, diagonal]
    return call(corner_kernel, (held(CORNER_TILES), PAIR), corner_scratch(), CORNER_TILES, *arrays)


def apply_cell(cell, lines, stored, before, sums):
    sums_s, sums_t = start_sums(cell, before, range(BLOCKS))
    for index, line in enumerate(lines):
        line_s, line_t = line(0), line(1)
        for block in range(BLOCKS):
            value = stored[cell, block, index]
            sums_s[block] = sums_s[block] + value * line_s
            sums_t[block] = sums_t[block] + value * line_t
    for block in range(BLOCKS):
        sums[cell, block, 0] = sums_s[block]
        sums[cell, block, 1] = sums_t[block]


def widen(pieces, wides):
    for piece, wide in zip(pieces, wides):
        wide[:, 0:2, :] = piece[...]


def invert_core_kernel(counts, atoms, info, core, stored, sums, spill, places, wide, packed, spills):
    invert(counts, atoms, places)
    apply_core_kernel(info, core, stored, sums, spill, wide, packed, spills)


def apply_core_kernel(info, core, stored, sums, spill, wide, packed, spills):
    widen([core], [wide])
    pack_core(info, wide, packed, spills, False)
    core_spills(spills, spill)

    def one_cell(cell, _):
        lines = lines_of(packed, core_columns(cell // CZ), cell % CZ)
        apply_cell(cell, lines, stored, None, sums)
        return 0

    lax.fori_loop(0, CELLS, one_cell, 0, unroll=4)


def apply_face_kernel(*refs):
    infos, pieces, (stored, before, spill_before, sums, spill), wides, (packed, spills) = split(
        refs, 3, 3, 5, 3, 2
    )
    widen(pieces, wides)
    pack_faces(infos, wides, packed, spills, False)
    face_spills(spills, spill_before, spill)

    def one_cell(cell, _):
        lines = lines_of(packed, face_columns(cell // CZ), cell % CZ)
        apply_cell(cell, lines, stored, before, sums)
        return 0

    lax.fori_loop(0, CELLS, one_cell, 0, unroll=4)


def apply_corner_tiles(
    info, corners, stored, before, spill_before, core, diagonal, out, wide, packed, spills, rest, sums
):
    widen([corners], [wide])
    pack_corners(info, wide, packed, spills, False)
    corner_spills(spills, spill_before, rest)

    def one_cell(cell, _):
        finish_cell(jnp.maximum(cell - 1, 0), core, sums, diagonal, out)
        lines = lines_of(packed, [cell // CZ], cell % CZ) + [rest_line(rest, cell)]
        apply_cell(cell, lines, stored, before, sums)
        return 0

    sums[0] = jnp.zeros(SUMS.shape[1:], jnp.float32)
    lax.fori_loop(0, CELLS, one_cell, 0, unroll=4)
    finish_cell(CELLS - 1, core, sums, diagonal, out)


def split(refs, *sizes):
    parts = []
    for size in sizes:
        parts.append(refs[:size])
        refs = refs[size:]
    return parts


def apply_last_kernel(*refs):
    ins, (slots, first, second, moments, third), work = split(refs, 7, 5, 5)
    diagonal = ins[6]
    apply_corner_tiles(*ins, third, *work)
    d = diagonal[...][:, None, :]
    v_0 = slots[:, 4:6, :]
    v_1 = first[...]
    v_2 = second[...]
    d_0 = d * v_0
    d_2 = d * v_2
    parts = [d_0 * v_0, d_0 * v_1, d * v_1 * v_1, d_2 * v_1, d_2 * v_2, d_2 * third[...]]
    row = row_index((2, LANES))
    line = jnp.zeros((2, LANES), jnp.float32)
    for index, part in enumerate(parts + [v_0, v_1, v_2]):
        total = jnp.sum(jnp.sum(part, axis=0), axis=1, keepdims=True)
        line = jnp.where(lane_index((2, LANES)) - row == 2 * index, total, line)
    moments[...] = jnp.sum(line, axis=0, keepdims=True)


def wide(piece):
    return VMEM((piece.shape[0], 8, LANES), jnp.float32)


def apply_core(info, core, stored, lists):
    stored = pltpu.with_memory_space_constraint(stored, VMEM)
    scratch = [wide(core)] + packs(4)
    outs = (SUMS, CORE_SPILL)
    if lists is None:
        return call(apply_core_kernel, outs, scratch, 2, info, core, stored)
    counts, atoms, atoms_local = lists
    rows = (atoms_local // LANES + 15) // 16 * 16
    places = jax.ShapeDtypeStruct((2, rows, LANES), jnp.int32)
    return call(
        invert_core_kernel, outs + (places,), scratch, 2, counts, atoms, info, core, stored
    )


def apply_faces(infos, pieces, stored, before, spill):
    stored = pltpu.with_memory_space_constraint(stored, VMEM)
    scratch = [wide(piece) for piece in pieces] + packs(8)
    return call(
        apply_face_kernel, (SUMS, SPILL), scratch, 2, *infos, *pieces, stored, before, spill
    )


def apply_corners(info, corners, stored, before, spill, core, diagonal, last):
    stored = pltpu.with_memory_space_constraint(stored, VMEM)
    scratch = [wide(corners)] + corner_scratch()
    arrays = [info, corners, stored, before, spill, core, diagonal]
    if last is None:
        return call(apply_corner_tiles, PAIR, scratch, 2, *arrays)
    third = VMEM((CELLS, 2, LANES), jnp.float32)
    out = jax.ShapeDtypeStruct((1, LANES), jnp.float32)
    return call(apply_last_kernel, out, [third] + scratch, 2, *arrays, *last)


def solve(g):
    tiny = 1e-6
    h = [g[k] + g[k + 1] for k in range(5)]
    ratio_1 = h[1] / h[0]
    ratio_2 = h[2] / h[0]
    pivot_1 = h[2] - ratio_1 * h[1]
    mixed = h[3] - ratio_1 * h[2]
    rest_1 = g[1] - ratio_1 * g[0]
    live_1 = pivot_1 > tiny * h[2]
    safe_1 = jnp.where(live_1, pivot_1, 1.0)
    ratio_3 = jnp.where(live_1, mixed / safe_1, 0.0)
    pivot_2 = h[4] - ratio_2 * h[2] - ratio_3 * mixed
    rest_2 = g[2] - ratio_2 * g[0] - ratio_3 * rest_1
    live_2 = live_1 & (pivot_2 > tiny * h[4])
    c_2 = jnp.where(live_2, rest_2 / jnp.where(live_2, pivot_2, 1.0), 0.0)
    c_1 = jnp.where(live_1, (rest_1 - mixed * c_2) / safe_1, 0.0)
    c_0 = (g[0] - h[1] * c_1 - h[2] * c_2) / h[0]
    return c_0, c_1, c_2


def invert(counts, atoms, places):
    rows = places.shape[1]
    row_low = row_index((LANES, LANES))
    row_high = row_index((rows, LANES))
    lane = lane_index((rows, LANES))

    def one_cell(cell, total):
        live = lane_index((1, LANES)) < counts[cell]
        pointer = jnp.where(live, atoms[pl.ds(cell, 1), :], -1)
        here = (pointer >> 7) == row_high
        cells = jnp.where(here, cell, 0).astype(jnp.float32)
        slots = jnp.where(here, lane, 0).astype(jnp.float32)
        parts = jnp.concatenate([cells, slots], axis=0).astype(jnp.bfloat16)
        lows = jnp.where((pointer & 127) == row_low, 1.0, 0.0).astype(jnp.bfloat16)
        return total + lax.dot_general(
            parts, lows, (((1,), (1,)), ((), ())), preferred_element_type=jnp.float32
        )

    total = jnp.zeros((2 * rows, LANES), jnp.float32)
    total = lax.fori_loop(0, CELLS, one_cell, total, unroll=8).astype(jnp.int32)
    places[0] = total[:rows]
    places[1] = total[rows:]


def finish_kernel(moments, slots, first, second, places, out, charges):
    summed = moments[...]
    lane = lane_index((2, LANES))
    row = row_index((2, LANES))

    def pair(index):
        picked = jnp.where(lane - row == 2 * index, summed, 0.0)
        return jnp.broadcast_to(jnp.sum(picked, axis=1, keepdims=True), (2, LANES))

    rows = [pair(index) for index in range(9)]
    c_0, c_1, c_2 = solve(rows[:6])
    totals = c_0 * rows[6] + c_1 * rows[7] + c_2 * rows[8]
    balance = totals[0:1] / totals[1:2]
    sign = jnp.concatenate([jnp.ones((1, LANES), jnp.float32), -balance], axis=0)
    c_0, c_1, c_2 = c_0 * sign, c_1 * sign, c_2 * sign
    for cell in range(CELLS):
        mixed = c_0 * slots[cell, 4:6, :] + c_1 * first[cell] + c_2 * second[cell]
        charges[cell : cell + 1, :] = jnp.sum(mixed, axis=0, keepdims=True)
    tiles = [jnp.zeros((8, LANES), jnp.float32) for _ in range(places.shape[1] // 8)]
    for cell in range(CELLS):
        line = spread(charges[cell : cell + 1, :])
        for at in range(len(tiles)):
            here = slice(8 * at, 8 * at + 8)
            moved = jnp.take_along_axis(line, places[1, here, :], axis=1)
            tiles[at] = jnp.where(places[0, here, :] == cell, moved, tiles[at])
    out[...] = jnp.concatenate(tiles, axis=0)[: out.shape[0]]


def finish(moments, slots, first, second, places, atoms_local):
    return pl.pallas_call(
        finish_kernel,
        out_shape=jax.ShapeDtypeStruct((atoms_local // LANES, LANES), jnp.float32),
        in_specs=[IN_VMEM] * 5,
        out_specs=IN_VMEM,
        scratch_shapes=[VMEM((CELLS, LANES), jnp.float32)],
        compiler_params=params(8),
    )(moments, slots, first, second, places)


def partner(block, axis, mask):
    count = lax.axis_size(axis)
    return lax.ppermute(block, axis, [(low, low ^ mask) for low in range(count)])


def shifted(block, along_x):
    count = lax.axis_size("gx")
    return lax.ppermute(block, "gx", [(i, (i + 4 * along_x) % count) for i in range(count)])


def with_z_faces(cells):
    cells = cells.reshape((QUADS, CZ) + cells.shape[1:])
    faces = jnp.concatenate([cells[:, -1:], cells[:, :1]], axis=1)
    other = partner(faces, "gx", 1)
    return jnp.concatenate([other[:, 0:1], cells, other[:, 1:2]], axis=1)


def flat(columns):
    return columns.reshape((-1,) + columns.shape[-2:])


def x_faces(core):
    count = lax.axis_size("gx")
    rows = count // 4
    odd = (lax.axis_index("gx") // 4) % 2 == 1
    if rows % 2:
        return shifted(core[2:], 1), shifted(core[:2], -1)
    first = lax.ppermute(jnp.where(odd, core[:2], core[2:]), "gx", [(i, i ^ 4) for i in range(count)])
    route = [(i, (i + (4 if (i // 4) % 2 else -4)) % count) for i in range(count)]
    second = lax.ppermute(jnp.where(odd, core[2:], core[:2]), "gx", route)
    return first, second


def sorted_faces(first, second):
    odd = (lax.axis_index("gx") // 4) % 2 == 1
    if (lax.axis_size("gx") // 4) % 2:
        return first, second
    return jnp.where(odd, first, second), jnp.where(odd, second, first)


def exchange(cells, on_core, on_faces, on_corners):
    core = with_z_faces(cells)
    first, second = x_faces(core)
    beyond = partner(core, "gx", 2)
    sums, spill, *more = on_core(flat(core))
    first, second, sums = lax.optimization_barrier((first, second, sums))
    low, high = sorted_faces(first, second)
    corners = partner(jnp.concatenate([low, high], axis=0), "gx", 2)
    pieces = [flat(part) for part in (low, high, beyond)]
    sums, spill, *more = on_faces(pieces, sums, spill, *more)
    corners = flat(corners)
    return flat(core), pieces, corners, on_corners(corners, sums, spill, flat(core), *more)


def global_sum(values):
    count = lax.axis_size("gx")
    if count & (count - 1):
        return lax.psum(values, "gx")
    step = 1
    while step < count:
        if step >= 2 and 4 * step <= count:
            others = [partner(values, "gx", k * step) for k in (3, 2, 1)]
            values = (values + others[0]) + (others[1] + others[2])
            step *= 4
        else:
            values = values + partner(values, "gx", step)
            step *= 2
    return values


def local(cell_offsets, electronegativity, hardness, charge_widths, cell_counts, cell_atoms):
    slots, diagonal = prepare(
        cell_counts, cell_offsets, electronegativity, hardness, charge_widths, cell_atoms
    )
    stored = []

    def keep(tiles, *others):
        stored.append(tiles)
        return others

    core, pieces, corners, (first,) = exchange(
        slots,
        lambda core: keep(*build_core(core)),
        lambda faces, sums, spill, *own: keep(*build_faces(faces, *own, sums, spill)) + own,
        lambda corners, sums, spill, core, *own: keep(
            *build_corners(corners, *own, sums, spill, core, diagonal)
        ),
    )

    def apply(cells, lists, last):
        def on_faces(faces, sums, spill, *found):
            return (*apply_faces(pieces, faces, stored[1], sums, spill), *found)

        def on_corners(others, sums, spill, _, *found):
            result = apply_corners(
                corners, others, stored[2], sums, spill, core, diagonal, last
            )
            return result, found

        return exchange(
            cells, lambda own: apply_core(core, own, stored[0], lists), on_faces, on_corners
        )[3]

    atoms_local = cell_offsets.shape[1]
    second, (places,) = apply(first, (cell_counts, cell_atoms, atoms_local), None)
    moments, _ = apply(second, None, (slots, first, second))
    charges = finish(global_sum(moments), slots, first, second, places, atoms_local)
    return charges.reshape(-1)


def solution(mesh):
    placed = (
        P(None, ("grp", "gx")),
        P(("grp", "gx")),
        P(("grp", "gx")),
        P(("grp", "gx")),
        P(("grp", "gx")),
        P(("grp", "gx"), None),
    )
    return jax.shard_map(
        local, mesh=mesh, in_specs=placed, out_specs=P(("grp", "gx")), check_vma=False
    )
```

```python
import functools
import math

import jax
import jax.numpy as jnp
from jax import lax
from jax.experimental import pallas as pl
from jax.experimental.pallas import tpu as pltpu
from jax.sharding import PartitionSpec as P

CX = 2
CY = 2
CZ = 8
EZ = CZ + 2
CELLS = CX * CY * CZ
QUADS = CX * CY
LANES = 128
BLOCKS = 11
GROUPS = ((0, 1, 2, 3), (4, 5, 6, 7), (8, 9, 10))

COULOMB = 14.399645
ROOT_PI = math.sqrt(math.pi)
SCREEN = 1.0 / (math.sqrt(2.0) * 3.0)
EWALD_SELF = math.sqrt(2.0 / math.pi) / 3.0
SIDE = 12.0 * SCREEN
CUT_SQUARED = (12.0 * SCREEN) ** 2
CLOSEST_SQUARED = (0.5 * SCREEN) ** 2
PAIR_SCALE = COULOMB * SCREEN

VMEM = pltpu.VMEM
SMEM = pltpu.SMEM


def params(mib):
    return pltpu.CompilerParams(vmem_limit_bytes=mib * 2**20)


def lane_index(shape):
    return lax.broadcasted_iota(jnp.int32, shape, len(shape) - 1)


def row_index(shape):
    return lax.broadcasted_iota(jnp.int32, shape, len(shape) - 2)


def prepare_kernel(
    counts_hbm, offsets, negativity, hardness, widths, atoms, slots, diagonal,
    counts, raw_offsets, raw_negativity, raw_hardness, raw_widths, raw_atoms, table, others, sems,
):
    copies = [
        pltpu.make_async_copy(source, target, sems.at[index])
        for index, (source, target) in enumerate(
            [
                (counts_hbm, counts),
                (offsets, raw_offsets),
                (negativity, raw_negativity),
                (hardness, raw_hardness),
                (widths, raw_widths),
                (atoms, raw_atoms),
            ]
        )
    ]
    for copy in copies:
        copy.start()
    for copy in copies:
        copy.wait()
    chunks = table.shape[0]
    for chunk in range(chunks):
        here = slice(chunk * LANES, (chunk + 1) * LANES)
        for first in (0, 4):
            table[chunk, first : first + 3, :] = raw_offsets[:, here]
            table[chunk, first + 3 : first + 4, :] = raw_widths[chunk : chunk + 1, :]
        for first in (0, 2, 4, 6):
            others[chunk, first : first + 1, :] = raw_negativity[chunk : chunk + 1, :]
            others[chunk, first + 1 : first + 2, :] = raw_hardness[chunk : chunk + 1, :]
    row = row_index((8, LANES))

    def pick(source, pointers):
        share = 8 // len(pointers)
        pointer = spread(pointers[-1])
        for k in range(len(pointers) - 2, -1, -1):
            pointer = jnp.where(row < share * (k + 1), pointers[k], pointer)
        high = pointer >> 7
        low = pointer & 127
        picked = jnp.zeros((8, LANES), jnp.float32)
        for chunk in range(chunks):
            part = jnp.take_along_axis(source[chunk], low, axis=1)
            picked = jnp.where(high == chunk, part, picked)
        return picked

    def four_cells(step, _):
        cells = [4 * step + k for k in range(4)]
        occupied = [lane_index((1, LANES)) < counts[cell] for cell in cells]
        pointers = [
            jnp.where(live, raw_atoms[pl.ds(cell, 1), :], 0) for cell, live in zip(cells, occupied)
        ]
        pairs = [pick(table, pointers[:2]), pick(table, pointers[2:])]
        both = pick(others, pointers)
        for k, (cell, live) in enumerate(zip(cells, occupied)):
            at = 4 * (k % 2)
            picked = pairs[k // 2][at : at + 4]
            width = jnp.where(live, picked[3:4], 1.0)
            hard = both[2 * k + 1 : 2 * k + 2]
            diag = jnp.where(live, hard + COULOMB * (1.0 / (width * ROOT_PI) - EWALD_SELF), 1.0)
            negative = jnp.where(live, both[2 * k : 2 * k + 1], 0.0)
            place_x = (cell // (CY * CZ)).astype(jnp.float32)
            place_y = ((cell // CZ) % CY).astype(jnp.float32)
            slots[cell, 0:1, :] = (picked[0:1] + place_x) * SIDE
            slots[cell, 1:2, :] = (picked[1:2] + place_y) * SIDE
            slots[cell, 2:3, :] = picked[2:3] * SIDE
            slots[cell, 3:4, :] = (2.0 * SCREEN * SCREEN) * width * width
            slots[cell, 4:5, :] = -negative / diag
            slots[cell, 5:6, :] = jnp.where(live, 1.0 / diag, 0.0)
            slots[cell, 6:7, :] = jnp.zeros((1, LANES), jnp.float32)
            slots[cell, 7:8, :] = jnp.full((1, LANES), counts[cell].astype(jnp.float32))
            diagonal[pl.ds(cell, 1), :] = diag
        return 0

    lax.fori_loop(0, CELLS // 4, four_cells, 0, unroll=2)


def prepare(counts, offsets, negativity, hardness, widths, atoms):
    chunks = offsets.shape[1] // LANES
    plane = (chunks, LANES)
    return pl.pallas_call(
        prepare_kernel,
        out_shape=(
            jax.ShapeDtypeStruct((CELLS, 8, LANES), jnp.float32),
            jax.ShapeDtypeStruct((CELLS, LANES), jnp.float32),
        ),
        in_specs=[pl.BlockSpec(memory_space=pltpu.HBM)] * 6,
        out_specs=(pl.BlockSpec(memory_space=VMEM), pl.BlockSpec(memory_space=VMEM)),
        scratch_shapes=[
            SMEM(counts.shape, jnp.int32),
            VMEM(offsets.shape, jnp.float32),
            VMEM(plane, jnp.float32),
            VMEM(plane, jnp.float32),
            VMEM(plane, jnp.float32),
            VMEM(atoms.shape, jnp.int32),
            VMEM((chunks, 8, LANES), jnp.float32),
            VMEM((chunks, 8, LANES), jnp.float32),
            pltpu.SemaphoreType.DMA((6,)),
        ],
        compiler_params=params(8),
    )(
        *[
            pltpu.with_memory_space_constraint(array, pltpu.HBM)
            for array in (
                counts,
                offsets,
                negativity.reshape(plane),
                hardness.reshape(plane),
                widths.reshape(plane),
                atoms,
            )
        ]
    )


def pack_column(info, cells, source, packed, spills, target, at, shift):
    lane = lane_index((8, LANES))
    row = row_index((8, LANES))
    for z in range(CZ):
        base = source * EZ + z
        low, mid, top = [spread(info[base + k, 7:8, :]).astype(jnp.int32) for k in range(3)]
        end = low + mid - LANES
        tiles = [cells[base + k] for k in range(3)]
        if shift is not None:
            for k in range(3):
                offset = jnp.where(row == 2, (k - 1) * SIDE, 0.0)
                for axis in range(2):
                    offset = jnp.where(row == axis, shift[axis] * SIDE, offset)
                tiles[k] = tiles[k] + offset
        second = jnp.take_along_axis(tiles[1], (lane - low) & 127, axis=1)
        third = jnp.take_along_axis(tiles[2], (lane - end) & 127, axis=1)
        packed[target * CZ + z, 0] = jnp.where(lane < low, tiles[0], second)
        packed[target * CZ + z, 1] = jnp.where(lane < end, second, third)
        spill = jnp.where(lane < end + top - LANES, third, 0.0)
        spills[target * CZ + z] = pltpu.roll(spill, at, 1) if at else spill


def pack_core(info, cells, packed, spills, build):
    for q in range(QUADS):
        pack_column(info, cells, q, packed, spills, q, 8 * q, (0, 0) if build else None)


def pack_faces(infos, pieces, packed, spills, build):
    for side in range(2):
        sign = 2 * side - 1
        for y in range(CY):
            shift = (sign * CX, 0) if build else None
            at = 32 + 8 * y
            pack_column(infos[side], pieces[side], y, packed, spills, 2 * side + y, at, shift)
        for x in range(CX):
            shift = (0, sign * CY) if build else None
            source = 2 * x + 1 - side
            target = 4 + 2 * x + side
            at = 48 + 8 * x
            pack_column(infos[2], pieces[2], source, packed, spills, target, at, shift)


def pack_corners(info, cells, packed, spills, build):
    for side_x in range(2):
        for side_y in range(2):
            shift = ((2 * side_x - 1) * CX, (2 * side_y - 1) * CY) if build else None
            source = 2 * side_x + 1 - side_y
            pack_column(info, cells, source, packed, spills, 2 * side_x + side_y, 64, shift)


def core_columns(q):
    return [q ^ k for k in range(4)]


def face_columns(q):
    x, y = q >> 1, q & 1
    return [2 * x, 2 * x + 1, 4 + y, 6 + y]


def overflow_of(spills, columns, z):
    return sum(spills[column * CZ + z] for column in columns)


def spread(row):
    return jnp.broadcast_to(row, (8, LANES))


def couple(x_i, y_i, z_i, w_i, x_j, y_j, z_j, w_j):
    delta_x = x_j - x_i
    delta_y = y_j - y_i
    delta_z = z_j - z_i
    squared = delta_x * delta_x + delta_y * delta_y + delta_z * delta_z
    held = jnp.maximum(squared, CLOSEST_SQUARED)
    inverse = lax.rsqrt(held)
    distance = held * inverse
    scaled = distance * lax.rsqrt(w_i + w_j)
    value = (lax.erf(scaled) - lax.erf(distance)) * inverse
    return jnp.where(squared < CUT_SQUARED, value, 0.0)


def to_rows(sums, block):
    here = lane_index((8, LANES)) - row_index((8, LANES)) == 8 * block
    return jnp.where(here, jnp.sum(sums, axis=1, keepdims=True), 0.0)


def add_rows(cell, sums, rows):
    for index in range(2):
        total = jnp.zeros((8, LANES), jnp.float32)
        for block in range(BLOCKS):
            total = total + to_rows(sums[cell, block, index], block)
        rows.append(jnp.sum(total, axis=0, keepdims=True))


def finish_cell(cell, info, sums, diagonal, out):
    rows = []
    add_rows(cell, sums, rows)
    here = (cell // CZ) * EZ + cell % CZ + 1
    scale = PAIR_SCALE / diagonal[pl.ds(cell, 1), :]
    live = lane_index((1, LANES)) < info[here, 7:8, :].astype(jnp.int32)
    out[cell, 0:1, :] = jnp.where(live, rows[0] * scale, 0.0)
    out[cell, 1:2, :] = jnp.where(live, rows[1] * scale, 0.0)


def build_cell(cell, lines, turned, kernels, before, sums, below):
    own = None
    if below is not None:
        own = lane_index((8, LANES)) - row_index((8, LANES)) - below
    for group in GROUPS:
        sums_s, sums_t = start_sums(cell, before, group)
        for index, line in enumerate(lines):
            beside = [line(k) for k in range(6)]
            for at, block in enumerate(group):
                value = couple(*[turned[cell, block, k] for k in range(4)], *beside[:4])
                if own is not None and index < 2:
                    value = jnp.where(own == 8 * block - LANES * index, 0.0, value)
                kernels[cell, block, index] = value
                sums_s[at] = sums_s[at] + value * beside[4]
                sums_t[at] = sums_t[at] + value * beside[5]
        for at, block in enumerate(group):
            sums[cell, block, 0] = sums_s[at]
            sums[cell, block, 1] = sums_t[at]


def start_sums(cell, before, blocks):
    if before is None:
        zeros = [jnp.zeros((8, LANES), jnp.float32) for _ in blocks]
        return zeros, list(zeros)
    sums_s = [before[cell, block, 0] for block in blocks]
    return sums_s, [before[cell, block, 1] for block in blocks]


def lines_of(packed, columns, z):
    def line(column, half):
        return lambda k: spread(packed[column * CZ + z, half, k : k + 1, :])

    return [line(column, half) for column in columns for half in range(2)]


def rest_line(rest, cell):
    return lambda k: spread(rest[cell, k : k + 1, :])


def parts_of(value):
    high = value.astype(jnp.bfloat16).astype(jnp.float32)
    rest = value - high
    middle = rest.astype(jnp.bfloat16).astype(jnp.float32)
    return high, middle, rest - middle


def turn_cells(core, turned):
    chosen = row_index((24, 4 * LANES)) & 7
    ones = jnp.where(chosen == lane_index((24, 4 * LANES)) >> 7, 1.0, 0.0).astype(jnp.bfloat16)
    for cell in range(CELLS):
        here = core[(cell // CZ) * EZ + cell % CZ + 1]
        left = jnp.concatenate(parts_of(here), axis=0).T[: 8 * BLOCKS + 8].astype(jnp.bfloat16)
        wide = lax.dot_general(
            left, ones, (((1,), (0,)), ((), ())), preferred_element_type=jnp.float32
        )
        for block in range(BLOCKS):
            for k in range(4):
                turned[cell, block, k] = wide[8 * block : 8 * block + 8, k * LANES : (k + 1) * LANES]


def core_spills(spills, spill):
    for z in range(CZ):
        spill[z] = overflow_of(spills, range(QUADS), z)


def face_spills(spills, before, spill):
    for cell in range(CELLS):
        q, z = cell // CZ, cell % CZ
        spill[cell] = before[z] + overflow_of(spills, face_columns(q), z)


def corner_spills(spills, before, rest):
    for cell in range(CELLS):
        rest[cell] = before[cell] + spills[cell]


def core_kernel(core, kernels, sums, spill, turned, packed, spills):
    turn_cells(core, turned)
    pack_core(core, core, packed, spills, True)
    core_spills(spills, spill)

    def one_cell(cell, _):
        q, z = cell // CZ, cell % CZ
        below = spread(core[q * EZ + z, 7:8, :]).astype(jnp.int32)
        build_cell(cell, lines_of(packed, core_columns(q), z), turned, kernels, None, sums, below)
        return 0

    lax.fori_loop(0, CELLS, one_cell, 0, unroll=2)


def face_kernel(
    x_low, x_high, beyond, turned, before, spill_before, kernels, sums, spill, packed, spills
):
    pieces = [x_low, x_high, beyond]
    pack_faces(pieces, pieces, packed, spills, True)
    face_spills(spills, spill_before, spill)

    def one_cell(cell, _):
        lines = lines_of(packed, face_columns(cell // CZ), cell % CZ)
        build_cell(cell, lines, turned, kernels, before, sums, None)
        return 0

    lax.fori_loop(0, CELLS, one_cell, 0, unroll=2)


def corner_kernel(
    corners, turned, before, spill_before, core, diagonal, kernels, out, packed, spills, rest, sums
):
    pack_corners(corners, corners, packed, spills, True)
    corner_spills(spills, spill_before, rest)

    def one_cell(cell, _):
        finish_cell(jnp.maximum(cell - 1, 0), core, sums, diagonal, out)
        lines = lines_of(packed, [cell // CZ], cell % CZ) + [rest_line(rest, cell)]
        build_cell(cell, lines, turned, kernels, before, sums, None)
        return 0

    sums[0] = jnp.zeros(SUMS.shape[1:], jnp.float32)
    lax.fori_loop(0, CELLS, one_cell, 0, unroll=4)
    finish_cell(CELLS - 1, core, sums, diagonal, out)


IN_VMEM = pl.BlockSpec(memory_space=VMEM)
IN_SMEM = pl.BlockSpec(memory_space=SMEM)
PAIR = jax.ShapeDtypeStruct((CELLS, 2, LANES), jnp.float32)
SPILL = jax.ShapeDtypeStruct((CELLS, 8, LANES), jnp.float32)
SUMS = jax.ShapeDtypeStruct((CELLS, BLOCKS, 2, 8, LANES), jnp.float32)
TURNED = jax.ShapeDtypeStruct((CELLS, BLOCKS, 4, 8, LANES), jnp.float32)
CORE_SPILL = jax.ShapeDtypeStruct((CZ, 8, LANES), jnp.float32)
CORE_TILES, FACE_TILES, CORNER_TILES = 8, 8, 3


def held(tiles):
    return VMEM((CELLS, BLOCKS, tiles, 8, LANES), jnp.float32)


def call(kernel, outs, scratch, tiles, *arrays):
    work = CELLS * BLOCKS * tiles * 8 * LANES
    return pl.pallas_call(
        kernel,
        out_shape=outs,
        in_specs=[IN_SMEM if array.ndim == 1 else IN_VMEM for array in arrays],
        out_specs=jax.tree.map(lambda _: IN_VMEM, outs),
        scratch_shapes=scratch,
        compiler_params=params(8),
        cost_estimate=pl.CostEstimate(
            flops=30 * work, bytes_accessed=8 * work, transcendentals=4 * work
        ),
    )(*arrays)


def packs(columns):
    return [
        VMEM((columns * CZ, 2, 8, LANES), jnp.float32),
        VMEM((columns * CZ, 8, LANES), jnp.float32),
    ]


def build_core(core):
    outs = (held(CORE_TILES), SUMS, CORE_SPILL, TURNED)
    return call(core_kernel, outs, packs(4), CORE_TILES, core)


def build_faces(pieces, turned, before, spill):
    outs = (held(FACE_TILES), SUMS, SPILL)
    return call(face_kernel, outs, packs(8), FACE_TILES, *pieces, turned, before, spill)


def corner_scratch():
    return packs(4) + [VMEM(SPILL.shape, jnp.float32), VMEM(SUMS.shape, jnp.float32)]


def build_corners(corners, turned, before, spill, core, diagonal):
    arrays = [corners, turned, before, spill, core, diagonal]
    return call(corner_kernel, (held(CORNER_TILES), PAIR), corner_scratch(), CORNER_TILES, *arrays)


def apply_cell(cell, lines, stored, before, sums):
    sums_s, sums_t = start_sums(cell, before, range(BLOCKS))
    for index, line in enumerate(lines):
        line_s, line_t = line(0), line(1)
        for block in range(BLOCKS):
            value = stored[cell, block, index]
            sums_s[block] = sums_s[block] + value * line_s
            sums_t[block] = sums_t[block] + value * line_t
    for block in range(BLOCKS):
        sums[cell, block, 0] = sums_s[block]
        sums[cell, block, 1] = sums_t[block]


def widen(pieces, wides):
    for piece, wide in zip(pieces, wides):
        wide[:, 0:2, :] = piece[...]


def invert_core_kernel(counts, atoms, info, core, stored, sums, spill, places, wide, packed, spills):
    invert(counts, atoms, places)
    apply_core_kernel(info, core, stored, sums, spill, wide, packed, spills)


def apply_core_kernel(info, core, stored, sums, spill, wide, packed, spills):
    widen([core], [wide])
    pack_core(info, wide, packed, spills, False)
    core_spills(spills, spill)

    def one_cell(cell, _):
        lines = lines_of(packed, core_columns(cell // CZ), cell % CZ)
        apply_cell(cell, lines, stored, None, sums)
        return 0

    lax.fori_loop(0, CELLS, one_cell, 0, unroll=4)


def apply_face_kernel(*refs):
    infos, pieces, (stored, before, spill_before, sums, spill), wides, (packed, spills) = split(
        refs, 3, 3, 5, 3, 2
    )
    widen(pieces, wides)
    pack_faces(infos, wides, packed, spills, False)
    face_spills(spills, spill_before, spill)

    def one_cell(cell, _):
        lines = lines_of(packed, face_columns(cell // CZ), cell % CZ)
        apply_cell(cell, lines, stored, before, sums)
        return 0

    lax.fori_loop(0, CELLS, one_cell, 0, unroll=4)


def apply_corner_tiles(
    info, corners, stored, before, spill_before, core, diagonal, out, wide, packed, spills, rest, sums
):
    widen([corners], [wide])
    pack_corners(info, wide, packed, spills, False)
    corner_spills(spills, spill_before, rest)

    def one_cell(cell, _):
        finish_cell(jnp.maximum(cell - 1, 0), core, sums, diagonal, out)
        lines = lines_of(packed, [cell // CZ], cell % CZ) + [rest_line(rest, cell)]
        apply_cell(cell, lines, stored, before, sums)
        return 0

    sums[0] = jnp.zeros(SUMS.shape[1:], jnp.float32)
    lax.fori_loop(0, CELLS, one_cell, 0, unroll=4)
    finish_cell(CELLS - 1, core, sums, diagonal, out)


def split(refs, *sizes):
    parts = []
    for size in sizes:
        parts.append(refs[:size])
        refs = refs[size:]
    return parts


def apply_last_kernel(*refs):
    ins, (slots, first, second, moments, third), work = split(refs, 7, 5, 5)
    diagonal = ins[6]
    apply_corner_tiles(*ins, third, *work)
    d = diagonal[...][:, None, :]
    v_0 = slots[:, 4:6, :]
    v_1 = first[...]
    v_2 = second[...]
    d_0 = d * v_0
    d_2 = d * v_2
    parts = [d_0 * v_0, d_0 * v_1, d * v_1 * v_1, d_2 * v_1, d_2 * v_2, d_2 * third[...]]
    row = row_index((2, LANES))
    line = jnp.zeros((2, LANES), jnp.float32)
    for index, part in enumerate(parts + [v_0, v_1, v_2]):
        total = jnp.sum(jnp.sum(part, axis=0), axis=1, keepdims=True)
        line = jnp.where(lane_index((2, LANES)) - row == 2 * index, total, line)
    moments[...] = jnp.sum(line, axis=0, keepdims=True)


def wide(piece):
    return VMEM((piece.shape[0], 8, LANES), jnp.float32)


def apply_core(info, core, stored, lists):
    stored = pltpu.with_memory_space_constraint(stored, VMEM)
    scratch = [wide(core)] + packs(4)
    outs = (SUMS, CORE_SPILL)
    if lists is None:
        return call(apply_core_kernel, outs, scratch, 2, info, core, stored)
    counts, atoms, atoms_local = lists
    rows = (atoms_local // LANES + 15) // 16 * 16
    places = jax.ShapeDtypeStruct((2, rows, LANES), jnp.int32)
    return call(
        invert_core_kernel, outs + (places,), scratch, 2, counts, atoms, info, core, stored
    )


def apply_faces(infos, pieces, stored, before, spill):
    stored = pltpu.with_memory_space_constraint(stored, VMEM)
    scratch = [wide(piece) for piece in pieces] + packs(8)
    return call(
        apply_face_kernel, (SUMS, SPILL), scratch, 2, *infos, *pieces, stored, before, spill
    )


def apply_corners(info, corners, stored, before, spill, core, diagonal, last):
    stored = pltpu.with_memory_space_constraint(stored, VMEM)
    scratch = [wide(corners)] + corner_scratch()
    arrays = [info, corners, stored, before, spill, core, diagonal]
    if last is None:
        return call(apply_corner_tiles, PAIR, scratch, 2, *arrays)
    third = VMEM((CELLS, 2, LANES), jnp.float32)
    out = jax.ShapeDtypeStruct((1, LANES), jnp.float32)
    return call(apply_last_kernel, out, [third] + scratch, 2, *arrays, *last)


def solve(g):
    tiny = 1e-6
    h = [g[k] + g[k + 1] for k in range(5)]
    ratio_1 = h[1] / h[0]
    ratio_2 = h[2] / h[0]
    pivot_1 = h[2] - ratio_1 * h[1]
    mixed = h[3] - ratio_1 * h[2]
    rest_1 = g[1] - ratio_1 * g[0]
    live_1 = pivot_1 > tiny * h[2]
    safe_1 = jnp.where(live_1, pivot_1, 1.0)
    ratio_3 = jnp.where(live_1, mixed / safe_1, 0.0)
    pivot_2 = h[4] - ratio_2 * h[2] - ratio_3 * mixed
    rest_2 = g[2] - ratio_2 * g[0] - ratio_3 * rest_1
    live_2 = live_1 & (pivot_2 > tiny * h[4])
    c_2 = jnp.where(live_2, rest_2 / jnp.where(live_2, pivot_2, 1.0), 0.0)
    c_1 = jnp.where(live_1, (rest_1 - mixed * c_2) / safe_1, 0.0)
    c_0 = (g[0] - h[1] * c_1 - h[2] * c_2) / h[0]
    return c_0, c_1, c_2


def invert(counts, atoms, places):
    rows = places.shape[1]
    row_low = row_index((LANES, LANES))
    row_high = row_index((rows, LANES))
    lane = lane_index((rows, LANES))

    def one_cell(cell, total):
        live = lane_index((1, LANES)) < counts[cell]
        pointer = jnp.where(live, atoms[pl.ds(cell, 1), :], -1)
        here = (pointer >> 7) == row_high
        cells = jnp.where(here, cell, 0).astype(jnp.float32)
        slots = jnp.where(here, lane, 0).astype(jnp.float32)
        parts = jnp.concatenate([cells, slots], axis=0).astype(jnp.bfloat16)
        lows = jnp.where((pointer & 127) == row_low, 1.0, 0.0).astype(jnp.bfloat16)
        return total + lax.dot_general(
            parts, lows, (((1,), (1,)), ((), ())), preferred_element_type=jnp.float32
        )

    total = jnp.zeros((2 * rows, LANES), jnp.float32)
    total = lax.fori_loop(0, CELLS, one_cell, total, unroll=8).astype(jnp.int32)
    places[0] = total[:rows]
    places[1] = total[rows:]


def finish_kernel(moments, slots, first, second, places, out, charges):
    summed = moments[...]
    lane = lane_index((2, LANES))
    row = row_index((2, LANES))

    def pair(index):
        picked = jnp.where(lane - row == 2 * index, summed, 0.0)
        return jnp.broadcast_to(jnp.sum(picked, axis=1, keepdims=True), (2, LANES))

    rows = [pair(index) for index in range(9)]
    c_0, c_1, c_2 = solve(rows[:6])
    totals = c_0 * rows[6] + c_1 * rows[7] + c_2 * rows[8]
    balance = totals[0:1] / totals[1:2]
    sign = jnp.concatenate([jnp.ones((1, LANES), jnp.float32), -balance], axis=0)
    c_0, c_1, c_2 = c_0 * sign, c_1 * sign, c_2 * sign
    for cell in range(CELLS):
        mixed = c_0 * slots[cell, 4:6, :] + c_1 * first[cell] + c_2 * second[cell]
        charges[cell : cell + 1, :] = jnp.sum(mixed, axis=0, keepdims=True)
    tiles = [jnp.zeros((8, LANES), jnp.float32) for _ in range(places.shape[1] // 8)]
    for cell in range(CELLS):
        line = spread(charges[cell : cell + 1, :])
        for at in range(len(tiles)):
            here = slice(8 * at, 8 * at + 8)
            moved = jnp.take_along_axis(line, places[1, here, :], axis=1)
            tiles[at] = jnp.where(places[0, here, :] == cell, moved, tiles[at])
    out[...] = jnp.concatenate(tiles, axis=0)[: out.shape[0]]


def finish(moments, slots, first, second, places, atoms_local):
    return pl.pallas_call(
        finish_kernel,
        out_shape=jax.ShapeDtypeStruct((atoms_local // LANES, LANES), jnp.float32),
        in_specs=[IN_VMEM] * 5,
        out_specs=IN_VMEM,
        scratch_shapes=[VMEM((CELLS, LANES), jnp.float32)],
        compiler_params=params(8),
    )(moments, slots, first, second, places)


def partner(block, axis, mask):
    count = lax.axis_size(axis)
    return lax.ppermute(block, axis, [(low, low ^ mask) for low in range(count)])


def shifted(block, along_x):
    count = lax.axis_size("gx")
    return lax.ppermute(block, "gx", [(i, (i + 4 * along_x) % count) for i in range(count)])


def with_z_faces(cells):
    cells = cells.reshape((QUADS, CZ) + cells.shape[1:])
    faces = jnp.concatenate([cells[:, -1:], cells[:, :1]], axis=1)
    other = partner(faces, "gx", 1)
    return jnp.concatenate([other[:, 0:1], cells, other[:, 1:2]], axis=1)


def flat(columns):
    return columns.reshape((-1,) + columns.shape[-2:])


def x_faces(core):
    count = lax.axis_size("gx")
    rows = count // 4
    odd = (lax.axis_index("gx") // 4) % 2 == 1
    if rows % 2:
        return shifted(core[2:], 1), shifted(core[:2], -1)
    route = [(i, (i + (4 if (i // 4) % 2 else -4)) % count) for i in range(count)]
    second = lax.ppermute(jnp.where(odd, core[2:], core[:2]), "gx", route)
    first = lax.ppermute(jnp.where(odd, core[:2], core[2:]), "gx", [(i, i ^ 4) for i in range(count)])
    return first, second


def sorted_faces(first, second):
    odd = (lax.axis_index("gx") // 4) % 2 == 1
    if (lax.axis_size("gx") // 4) % 2:
        return first, second
    return jnp.where(odd, first, second), jnp.where(odd, second, first)


def exchange(cells, on_core, on_faces, on_corners):
    core = with_z_faces(cells)
    first, second = x_faces(core)
    beyond = partner(core, "gx", 2)
    sums, spill, *more = on_core(flat(core))
    first, second, sums = lax.optimization_barrier((first, second, sums))
    low, high = sorted_faces(first, second)
    corners = partner(jnp.concatenate([low, high], axis=0), "gx", 2)
    pieces = [flat(part) for part in (low, high, beyond)]
    sums, spill, *more = on_faces(pieces, sums, spill, *more)
    corners = flat(corners)
    return flat(core), pieces, corners, on_corners(corners, sums, spill, flat(core), *more)


def global_sum(values):
    count = lax.axis_size("gx")
    if count & (count - 1):
        return lax.psum(values, "gx")
    step = 1
    while step < count:
        if step >= 2 and 4 * step <= count:
            others = [partner(values, "gx", k * step) for k in (3, 2, 1)]
            values = (values + others[0]) + (others[1] + others[2])
            step *= 4
        else:
            values = values + partner(values, "gx", step)
            step *= 2
    return values


def local(cell_offsets, electronegativity, hardness, charge_widths, cell_counts, cell_atoms):
    slots, diagonal = prepare(
        cell_counts, cell_offsets, electronegativity, hardness, charge_widths, cell_atoms
    )
    stored = []

    def keep(tiles, *others):
        stored.append(tiles)
        return others

    core, pieces, corners, (first,) = exchange(
        slots,
        lambda core: keep(*build_core(core)),
        lambda faces, sums, spill, *own: keep(*build_faces(faces, *own, sums, spill)) + own,
        lambda corners, sums, spill, core, *own: keep(
            *build_corners(corners, *own, sums, spill, core, diagonal)
        ),
    )

    def apply(cells, lists, last):
        def on_faces(faces, sums, spill, *found):
            return (*apply_faces(pieces, faces, stored[1], sums, spill), *found)

        def on_corners(others, sums, spill, _, *found):
            result = apply_corners(
                corners, others, stored[2], sums, spill, core, diagonal, last
            )
            return result, found

        return exchange(
            cells, lambda own: apply_core(core, own, stored[0], lists), on_faces, on_corners
        )[3]

    atoms_local = cell_offsets.shape[1]
    second, (places,) = apply(first, (cell_counts, cell_atoms, atoms_local), None)
    moments, _ = apply(second, None, (slots, first, second))
    charges = finish(global_sum(moments), slots, first, second, places, atoms_local)
    return charges.reshape(-1)


def solution(mesh):
    placed = (
        P(None, ("grp", "gx")),
        P(("grp", "gx")),
        P(("grp", "gx")),
        P(("grp", "gx")),
        P(("grp", "gx")),
        P(("grp", "gx"), None),
    )
    return jax.shard_map(
        local, mesh=mesh, in_specs=placed, out_specs=P(("grp", "gx")), check_vma=False
    )
```

```python
import functools
import math

import jax
import jax.numpy as jnp
from jax import lax
from jax.experimental import pallas as pl
from jax.experimental.pallas import tpu as pltpu
from jax.sharding import PartitionSpec as P

CX = 2
CY = 2
CZ = 8
EZ = CZ + 2
CELLS = CX * CY * CZ
QUADS = CX * CY
LANES = 128
BLOCKS = 11
GROUPS = ((0, 1, 2, 3), (4, 5, 6, 7), (8, 9, 10))

COULOMB = 14.399645
ROOT_PI = math.sqrt(math.pi)
SCREEN = 1.0 / (math.sqrt(2.0) * 3.0)
EWALD_SELF = math.sqrt(2.0 / math.pi) / 3.0
SIDE = 12.0 * SCREEN
CUT_SQUARED = (12.0 * SCREEN) ** 2
CLOSEST_SQUARED = (0.5 * SCREEN) ** 2
PAIR_SCALE = COULOMB * SCREEN

VMEM = pltpu.VMEM
SMEM = pltpu.SMEM


def params(mib):
    return pltpu.CompilerParams(vmem_limit_bytes=mib * 2**20)


def lane_index(shape):
    return lax.broadcasted_iota(jnp.int32, shape, len(shape) - 1)


def row_index(shape):
    return lax.broadcasted_iota(jnp.int32, shape, len(shape) - 2)


def prepare_kernel(
    counts_hbm, offsets, negativity, hardness, widths, atoms, slots, diagonal,
    counts, raw_offsets, raw_negativity, raw_hardness, raw_widths, raw_atoms, table, others, sems,
):
    copies = [
        pltpu.make_async_copy(source, target, sems.at[index])
        for index, (source, target) in enumerate(
            [
                (counts_hbm, counts),
                (offsets, raw_offsets),
                (negativity, raw_negativity),
                (hardness, raw_hardness),
                (widths, raw_widths),
                (atoms, raw_atoms),
            ]
        )
    ]
    for copy in copies:
        copy.start()
    for copy in copies:
        copy.wait()
    chunks = table.shape[0]
    for chunk in range(chunks):
        here = slice(chunk * LANES, (chunk + 1) * LANES)
        for first in (0, 4):
            table[chunk, first : first + 3, :] = raw_offsets[:, here]
            table[chunk, first + 3 : first + 4, :] = raw_widths[chunk : chunk + 1, :]
        for first in (0, 2, 4, 6):
            others[chunk, first : first + 1, :] = raw_negativity[chunk : chunk + 1, :]
            others[chunk, first + 1 : first + 2, :] = raw_hardness[chunk : chunk + 1, :]
    row = row_index((8, LANES))

    def pick(source, pointers):
        share = 8 // len(pointers)
        pointer = spread(pointers[-1])
        for k in range(len(pointers) - 2, -1, -1):
            pointer = jnp.where(row < share * (k + 1), pointers[k], pointer)
        high = pointer >> 7
        low = pointer & 127
        picked = jnp.zeros((8, LANES), jnp.float32)
        for chunk in range(chunks):
            part = jnp.take_along_axis(source[chunk], low, axis=1)
            picked = jnp.where(high == chunk, part, picked)
        return picked

    def four_cells(step, _):
        cells = [4 * step + k for k in range(4)]
        occupied = [lane_index((1, LANES)) < counts[cell] for cell in cells]
        pointers = [
            jnp.where(live, raw_atoms[pl.ds(cell, 1), :], 0) for cell, live in zip(cells, occupied)
        ]
        pairs = [pick(table, pointers[:2]), pick(table, pointers[2:])]
        both = pick(others, pointers)
        for k, (cell, live) in enumerate(zip(cells, occupied)):
            at = 4 * (k % 2)
            picked = pairs[k // 2][at : at + 4]
            width = jnp.where(live, picked[3:4], 1.0)
            hard = both[2 * k + 1 : 2 * k + 2]
            diag = jnp.where(live, hard + COULOMB * (1.0 / (width * ROOT_PI) - EWALD_SELF), 1.0)
            negative = jnp.where(live, both[2 * k : 2 * k + 1], 0.0)
            place_x = (cell // (CY * CZ)).astype(jnp.float32)
            place_y = ((cell // CZ) % CY).astype(jnp.float32)
            slots[cell, 0:1, :] = (picked[0:1] + place_x) * SIDE
            slots[cell, 1:2, :] = (picked[1:2] + place_y) * SIDE
            slots[cell, 2:3, :] = picked[2:3] * SIDE
            slots[cell, 3:4, :] = (2.0 * SCREEN * SCREEN) * width * width
            slots[cell, 4:5, :] = -negative / diag
            slots[cell, 5:6, :] = jnp.where(live, 1.0 / diag, 0.0)
            slots[cell, 6:7, :] = jnp.zeros((1, LANES), jnp.float32)
            slots[cell, 7:8, :] = jnp.full((1, LANES), counts[cell].astype(jnp.float32))
            diagonal[pl.ds(cell, 1), :] = diag
        return 0

    lax.fori_loop(0, CELLS // 4, four_cells, 0, unroll=2)


def prepare(counts, offsets, negativity, hardness, widths, atoms):
    chunks = offsets.shape[1] // LANES
    plane = (chunks, LANES)
    return pl.pallas_call(
        prepare_kernel,
        out_shape=(
            jax.ShapeDtypeStruct((CELLS, 8, LANES), jnp.float32),
            jax.ShapeDtypeStruct((CELLS, LANES), jnp.float32),
        ),
        in_specs=[pl.BlockSpec(memory_space=pltpu.HBM)] * 6,
        out_specs=(pl.BlockSpec(memory_space=VMEM), pl.BlockSpec(memory_space=VMEM)),
        scratch_shapes=[
            SMEM(counts.shape, jnp.int32),
            VMEM(offsets.shape, jnp.float32),
            VMEM(plane, jnp.float32),
            VMEM(plane, jnp.float32),
            VMEM(plane, jnp.float32),
            VMEM(atoms.shape, jnp.int32),
            VMEM((chunks, 8, LANES), jnp.float32),
            VMEM((chunks, 8, LANES), jnp.float32),
            pltpu.SemaphoreType.DMA((6,)),
        ],
        compiler_params=params(8),
    )(
        *[
            pltpu.with_memory_space_constraint(array, pltpu.HBM)
            for array in (
                counts,
                offsets,
                negativity.reshape(plane),
                hardness.reshape(plane),
                widths.reshape(plane),
                atoms,
            )
        ]
    )


def pack_column(info, cells, source, packed, spills, target, at, shift, layers=range(CZ)):
    lane = lane_index((8, LANES))
    row = row_index((8, LANES))
    for z in layers:
        base = source * EZ + z
        low, mid, top = [spread(info[base + k, 7:8, :]).astype(jnp.int32) for k in range(3)]
        end = low + mid - LANES
        tiles = [cells[base + k] for k in range(3)]
        if shift is not None:
            for k in range(3):
                offset = jnp.where(row == 2, (k - 1) * SIDE, 0.0)
                for axis in range(2):
                    offset = jnp.where(row == axis, shift[axis] * SIDE, offset)
                tiles[k] = tiles[k] + offset
        second = jnp.take_along_axis(tiles[1], (lane - low) & 127, axis=1)
        third = jnp.take_along_axis(tiles[2], (lane - end) & 127, axis=1)
        packed[target * CZ + z, 0] = jnp.where(lane < low, tiles[0], second)
        packed[target * CZ + z, 1] = jnp.where(lane < end, second, third)
        spill = jnp.where(lane < end + top - LANES, third, 0.0)
        spills[target * CZ + z] = pltpu.roll(spill, at, 1) if at else spill


def pack_core(info, cells, packed, spills, build):
    for q in range(QUADS):
        pack_column(info, cells, q, packed, spills, q, 8 * q, (0, 0) if build else None)


def pack_faces(infos, pieces, packed, spills, build):
    for side in range(2):
        sign = 2 * side - 1
        for y in range(CY):
            shift = (sign * CX, 0) if build else None
            at = 32 + 8 * y
            pack_column(infos[side], pieces[side], y, packed, spills, 2 * side + y, at, shift)
        for x in range(CX):
            shift = (0, sign * CY) if build else None
            source = 2 * x + 1 - side
            target = 4 + 2 * x + side
            at = 48 + 8 * x
            pack_column(infos[2], pieces[2], source, packed, spills, target, at, shift)


def pack_corners(info, cells, packed, spills, build, layers):
    for side_x in range(2):
        for side_y in range(2):
            shift = ((2 * side_x - 1) * CX, (2 * side_y - 1) * CY) if build else None
            source = 2 * side_x + 1 - side_y
            target = 2 * side_x + side_y
            pack_column(info, cells, source, packed, spills, target, 64, shift, layers)


def core_columns(q):
    return [q ^ k for k in range(4)]


def face_columns(q):
    x, y = q >> 1, q & 1
    return [2 * x, 2 * x + 1, 4 + y, 6 + y]


def overflow_of(spills, columns, z):
    return sum(spills[column * CZ + z] for column in columns)


def spread(row):
    return jnp.broadcast_to(row, (8, LANES))


def couple(x_i, y_i, z_i, w_i, x_j, y_j, z_j, w_j):
    delta_x = x_j - x_i
    delta_y = y_j - y_i
    delta_z = z_j - z_i
    squared = delta_x * delta_x + delta_y * delta_y + delta_z * delta_z
    held = jnp.maximum(squared, CLOSEST_SQUARED)
    inverse = lax.rsqrt(held)
    distance = held * inverse
    scaled = distance * lax.rsqrt(w_i + w_j)
    value = (lax.erf(scaled) - lax.erf(distance)) * inverse
    return jnp.where(squared < CUT_SQUARED, value, 0.0)


def to_rows(sums, block):
    here = lane_index((8, LANES)) - row_index((8, LANES)) == 8 * block
    return jnp.where(here, jnp.sum(sums, axis=1, keepdims=True), 0.0)


def add_rows(cell, sums, rows):
    for index in range(2):
        total = jnp.zeros((8, LANES), jnp.float32)
        for block in range(BLOCKS):
            total = total + to_rows(sums[cell, block, index], block)
        rows.append(jnp.sum(total, axis=0, keepdims=True))


def finish_cell(slot, place, target, info, sums, diagonal, out):
    q, z = place(slot)
    rows = []
    add_rows(slot, sums, rows)
    scale = PAIR_SCALE / diagonal[pl.ds(q * CZ + z, 1), :]
    live = lane_index((1, LANES)) < info[q * EZ + z + 1, 7:8, :].astype(jnp.int32)
    out[target, 0:1, :] = jnp.where(live, rows[0] * scale, 0.0)
    out[target, 1:2, :] = jnp.where(live, rows[1] * scale, 0.0)


def build_cell(cell, slot, lines, turned, kernels, before, sums, below):
    own = None
    if below is not None:
        own = lane_index((8, LANES)) - row_index((8, LANES)) - below
    for group in GROUPS:
        sums_s, sums_t = start_sums(cell, before, group)
        for index, line in enumerate(lines):
            beside = [line(k) for k in range(6)]
            for at, block in enumerate(group):
                value = couple(*[turned[cell, block, k] for k in range(4)], *beside[:4])
                if own is not None and index < 2:
                    value = jnp.where(own == 8 * block - LANES * index, 0.0, value)
                kernels[slot, block, index] = value
                sums_s[at] = sums_s[at] + value * beside[4]
                sums_t[at] = sums_t[at] + value * beside[5]
        for at, block in enumerate(group):
            sums[slot, block, 0] = sums_s[at]
            sums[slot, block, 1] = sums_t[at]


def start_sums(cell, before, blocks):
    if before is None:
        zeros = [jnp.zeros((8, LANES), jnp.float32) for _ in blocks]
        return zeros, list(zeros)
    sums_s = [before[cell, block, 0] for block in blocks]
    return sums_s, [before[cell, block, 1] for block in blocks]


def lines_of(packed, columns, z):
    def line(column, half):
        return lambda k: spread(packed[column * CZ + z, half, k : k + 1, :])

    return [line(column, half) for column in columns for half in range(2)]


def rest_line(rest, cell):
    return lambda k: spread(rest[cell, k : k + 1, :])


def parts_of(value):
    high = value.astype(jnp.bfloat16).astype(jnp.float32)
    rest = value - high
    middle = rest.astype(jnp.bfloat16).astype(jnp.float32)
    return high, middle, rest - middle


def turn_cells(core, turned):
    chosen = row_index((24, 4 * LANES)) & 7
    ones = jnp.where(chosen == lane_index((24, 4 * LANES)) >> 7, 1.0, 0.0).astype(jnp.bfloat16)
    for cell in range(CELLS):
        here = core[(cell // CZ) * EZ + cell % CZ + 1]
        left = jnp.concatenate(parts_of(here), axis=0).T[: 8 * BLOCKS + 8].astype(jnp.bfloat16)
        wide = lax.dot_general(
            left, ones, (((1,), (0,)), ((), ())), preferred_element_type=jnp.float32
        )
        for block in range(BLOCKS):
            for k in range(4):
                turned[cell, block, k] = wide[8 * block : 8 * block + 8, k * LANES : (k + 1) * LANES]


def core_spills(spills, spill):
    for z in range(CZ):
        spill[z] = overflow_of(spills, range(QUADS), z)


def face_spills(spills, before, spill):
    for cell in range(CELLS):
        q, z = cell // CZ, cell % CZ
        spill[cell] = before[z] + overflow_of(spills, face_columns(q), z)


def edge_place(slot):
    return slot // 2, (CZ - 1) * (1 - slot % 2)


def inner_place(slot):
    return slot // (CZ - 2), 1 + slot % (CZ - 2)


EDGES = 2 * QUADS
INNER = CELLS - EDGES
PLACES = {EDGES: edge_place, INNER: inner_place}
LAYERS = {EDGES: (0, CZ - 1), INNER: range(1, CZ - 1)}


def corner_loop(slots, work, finish, sums):
    def one_cell(slot, _):
        finish(jnp.maximum(slot - 1, 0))
        work(slot)
        return 0

    sums[0] = jnp.zeros(sums.shape[1:], jnp.float32)
    lax.fori_loop(0, slots, one_cell, 0, unroll=4)
    finish(slots - 1)


def corner_spills(spills, before, rest, place):
    for slot in range(rest.shape[0]):
        q, z = place(slot)
        rest[slot] = before[q * CZ + z] + spills[q * CZ + z]


def core_kernel(core, kernels, sums, spill, turned, packed, spills):
    turn_cells(core, turned)
    pack_core(core, core, packed, spills, True)
    core_spills(spills, spill)

    def one_cell(cell, _):
        q, z = cell // CZ, cell % CZ
        below = spread(core[q * EZ + z, 7:8, :]).astype(jnp.int32)
        lines = lines_of(packed, core_columns(q), z)
        build_cell(cell, cell, lines, turned, kernels, None, sums, below)
        return 0

    lax.fori_loop(0, CELLS, one_cell, 0, unroll=2)


def face_kernel(
    x_low, x_high, beyond, turned, before, spill_before, kernels, sums, spill, packed, spills
):
    pieces = [x_low, x_high, beyond]
    pack_faces(pieces, pieces, packed, spills, True)
    face_spills(spills, spill_before, spill)

    def one_cell(cell, _):
        lines = lines_of(packed, face_columns(cell // CZ), cell % CZ)
        build_cell(cell, cell, lines, turned, kernels, before, sums, None)
        return 0

    lax.fori_loop(0, CELLS, one_cell, 0, unroll=2)


def corner_kernel(
    corners, turned, before, spill_before, core, diagonal, kernels, out, packed, spills, rest, sums
):
    slots = kernels.shape[0]
    place = PLACES[slots]
    pack_corners(corners, corners, packed, spills, True, LAYERS[slots])
    corner_spills(spills, spill_before, rest, place)

    def work(slot):
        q, z = place(slot)
        lines = lines_of(packed, [q], z) + [rest_line(rest, slot)]
        build_cell(q * CZ + z, slot, lines, turned, kernels, before, sums, None)

    def finish(slot):
        finish_cell(slot, place, slot, core, sums, diagonal, out)

    corner_loop(slots, work, finish, sums)


IN_VMEM = pl.BlockSpec(memory_space=VMEM)
IN_SMEM = pl.BlockSpec(memory_space=SMEM)
PAIR = jax.ShapeDtypeStruct((CELLS, 2, LANES), jnp.float32)
SPILL = jax.ShapeDtypeStruct((CELLS, 8, LANES), jnp.float32)
SUMS = jax.ShapeDtypeStruct((CELLS, BLOCKS, 2, 8, LANES), jnp.float32)
TURNED = jax.ShapeDtypeStruct((CELLS, BLOCKS, 4, 8, LANES), jnp.float32)
CORE_SPILL = jax.ShapeDtypeStruct((CZ, 8, LANES), jnp.float32)
CORE_TILES, FACE_TILES, CORNER_TILES = 8, 8, 3


def held(tiles, cells=CELLS):
    return VMEM((cells, BLOCKS, tiles, 8, LANES), jnp.float32)


def pairs(cells):
    return jax.ShapeDtypeStruct((cells, 2, LANES), jnp.float32)


def call(kernel, outs, scratch, tiles, *arrays):
    work = CELLS * BLOCKS * tiles * 8 * LANES
    return pl.pallas_call(
        kernel,
        out_shape=outs,
        in_specs=[IN_SMEM if array.ndim == 1 else IN_VMEM for array in arrays],
        out_specs=jax.tree.map(lambda _: IN_VMEM, outs),
        scratch_shapes=scratch,
        compiler_params=params(8),
        cost_estimate=pl.CostEstimate(
            flops=30 * work, bytes_accessed=8 * work, transcendentals=4 * work
        ),
    )(*arrays)


def packs(columns):
    return [
        VMEM((columns * CZ, 2, 8, LANES), jnp.float32),
        VMEM((columns * CZ, 8, LANES), jnp.float32),
    ]


def build_core(core):
    outs = (held(CORE_TILES), SUMS, CORE_SPILL, TURNED)
    return call(core_kernel, outs, packs(4), CORE_TILES, core)


def build_faces(pieces, turned, before, spill):
    outs = (held(FACE_TILES), SUMS, SPILL)
    return call(face_kernel, outs, packs(8), FACE_TILES, *pieces, turned, before, spill)


def corner_scratch(cells):
    rest = VMEM((cells, 8, LANES), jnp.float32)
    return packs(4) + [rest, VMEM((cells, BLOCKS, 2, 8, LANES), jnp.float32)]


def build_corners(cells, corners, turned, before, spill, core, diagonal):
    outs = (held(CORNER_TILES, cells), pairs(cells))
    arrays = [corners, turned, before, spill, core, diagonal]
    return call(corner_kernel, outs, corner_scratch(cells), CORNER_TILES, *arrays)


def apply_cell(cell, slot, lines, stored, before, sums):
    sums_s, sums_t = start_sums(cell, before, range(BLOCKS))
    for index, line in enumerate(lines):
        line_s, line_t = line(0), line(1)
        for block in range(BLOCKS):
            value = stored[slot, block, index]
            sums_s[block] = sums_s[block] + value * line_s
            sums_t[block] = sums_t[block] + value * line_t
    for block in range(BLOCKS):
        sums[slot, block, 0] = sums_s[block]
        sums[slot, block, 1] = sums_t[block]


def widen(pieces, wides):
    for piece, wide in zip(pieces, wides):
        wide[:, 0:2, :] = piece[...]


def invert_core_kernel(counts, atoms, info, core, stored, sums, spill, places, wide, packed, spills):
    invert(counts, atoms, places)
    apply_core_kernel(info, core, stored, sums, spill, wide, packed, spills)


def apply_core_kernel(info, core, stored, sums, spill, wide, packed, spills):
    widen([core], [wide])
    pack_core(info, wide, packed, spills, False)
    core_spills(spills, spill)

    def one_cell(cell, _):
        lines = lines_of(packed, core_columns(cell // CZ), cell % CZ)
        apply_cell(cell, cell, lines, stored, None, sums)
        return 0

    lax.fori_loop(0, CELLS, one_cell, 0, unroll=4)


def apply_face_kernel(*refs):
    infos, pieces, (stored, before, spill_before, sums, spill), wides, (packed, spills) = split(
        refs, 3, 3, 5, 3, 2
    )
    widen(pieces, wides)
    pack_faces(infos, wides, packed, spills, False)
    face_spills(spills, spill_before, spill)

    def one_cell(cell, _):
        lines = lines_of(packed, face_columns(cell // CZ), cell % CZ)
        apply_cell(cell, cell, lines, stored, before, sums)
        return 0

    lax.fori_loop(0, CELLS, one_cell, 0, unroll=4)


def apply_corner_cells(stored, before, spill_before, core, diagonal, out, target, packed, spills, rest, sums):
    slots = stored.shape[0]
    place = PLACES[slots]
    corner_spills(spills, spill_before, rest, place)

    def work(slot):
        q, z = place(slot)
        lines = lines_of(packed, [q], z) + [rest_line(rest, slot)]
        apply_cell(q * CZ + z, slot, lines, stored, before, sums)

    def finish(slot):
        finish_cell(slot, place, target(slot), core, sums, diagonal, out)

    corner_loop(slots, work, finish, sums)


def apply_corner_kernel(
    info, corners, stored, before, spill_before, core, diagonal, out, wide, packed, spills, rest, sums
):
    widen([corners], [wide])
    pack_corners(info, wide, packed, spills, False, LAYERS[stored.shape[0]])
    apply_corner_cells(
        stored, before, spill_before, core, diagonal, out, lambda slot: slot,
        packed, spills, rest, sums,
    )


def split(refs, *sizes):
    parts = []
    for size in sizes:
        parts.append(refs[:size])
        refs = refs[size:]
    return parts


def apply_last_kernel(
    info, corners, edge, inner, before, spill_before, core, diagonal, slots, first, second,
    moments, third, wide, packed, spills, edge_rest, edge_sums, inner_rest, inner_sums,
):
    widen([corners], [wide])
    pack_corners(info, wide, packed, spills, False, range(CZ))
    for stored, rest, sums in ((edge, edge_rest, edge_sums), (inner, inner_rest, inner_sums)):
        place = PLACES[stored.shape[0]]

        def target(slot, place=place):
            q, z = place(slot)
            return q * CZ + z

        apply_corner_cells(
            stored, before, spill_before, core, diagonal, third, target, packed, spills, rest, sums
        )
    d = diagonal[...][:, None, :]
    v_0 = slots[:, 4:6, :]
    v_1 = first[:, 1 : 1 + CZ].reshape(v_0.shape)
    v_2 = second[:, 1 : 1 + CZ].reshape(v_0.shape)
    d_0 = d * v_0
    d_2 = d * v_2
    parts = [d_0 * v_0, d_0 * v_1, d * v_1 * v_1, d_2 * v_1, d_2 * v_2, d_2 * third[...]]
    row = row_index((2, LANES))
    line = jnp.zeros((2, LANES), jnp.float32)
    for index, part in enumerate(parts + [v_0, v_1, v_2]):
        total = jnp.sum(jnp.sum(part, axis=0), axis=1, keepdims=True)
        line = jnp.where(lane_index((2, LANES)) - row == 2 * index, total, line)
    moments[...] = jnp.sum(line, axis=0, keepdims=True)


def wide(piece):
    return VMEM((piece.shape[0], 8, LANES), jnp.float32)


def apply_core(info, core, stored, lists):
    stored = pltpu.with_memory_space_constraint(stored, VMEM)
    scratch = [wide(core)] + packs(4)
    outs = (SUMS, CORE_SPILL)
    if lists is None:
        return call(apply_core_kernel, outs, scratch, 2, info, core, stored)
    counts, atoms, atoms_local = lists
    rows = (atoms_local // LANES + 15) // 16 * 16
    places = jax.ShapeDtypeStruct((2, rows, LANES), jnp.int32)
    return call(
        invert_core_kernel, outs + (places,), scratch, 2, counts, atoms, info, core, stored
    )


def apply_faces(infos, pieces, stored, before, spill):
    stored = pltpu.with_memory_space_constraint(stored, VMEM)
    scratch = [wide(piece) for piece in pieces] + packs(8)
    return call(
        apply_face_kernel, (SUMS, SPILL), scratch, 2, *infos, *pieces, stored, before, spill
    )


def apply_corners(info, corners, stored, before, spill, core, diagonal):
    stored = pltpu.with_memory_space_constraint(stored, VMEM)
    cells = stored.shape[0]
    arrays = [info, corners, stored, before, spill, core, diagonal]
    scratch = [wide(corners)] + corner_scratch(cells)
    return call(apply_corner_kernel, pairs(cells), scratch, 2, *arrays)


def apply_last(info, corners, edge, inner, before, spill, core, diagonal, slots, first, second):
    edge = pltpu.with_memory_space_constraint(edge, VMEM)
    inner = pltpu.with_memory_space_constraint(inner, VMEM)
    arrays = [info, corners, edge, inner, before, spill, core, diagonal, slots, first, second]
    scratch = [VMEM((CELLS, 2, LANES), jnp.float32), wide(corners)] + corner_scratch(EDGES)
    scratch += corner_scratch(INNER)[2:]
    out = jax.ShapeDtypeStruct((1, LANES), jnp.float32)
    return call(apply_last_kernel, out, scratch, 2, *arrays)


def solve(g):
    tiny = 1e-6
    h = [g[k] + g[k + 1] for k in range(5)]
    ratio_1 = h[1] / h[0]
    ratio_2 = h[2] / h[0]
    pivot_1 = h[2] - ratio_1 * h[1]
    mixed = h[3] - ratio_1 * h[2]
    rest_1 = g[1] - ratio_1 * g[0]
    live_1 = pivot_1 > tiny * h[2]
    safe_1 = jnp.where(live_1, pivot_1, 1.0)
    ratio_3 = jnp.where(live_1, mixed / safe_1, 0.0)
    pivot_2 = h[4] - ratio_2 * h[2] - ratio_3 * mixed
    rest_2 = g[2] - ratio_2 * g[0] - ratio_3 * rest_1
    live_2 = live_1 & (pivot_2 > tiny * h[4])
    c_2 = jnp.where(live_2, rest_2 / jnp.where(live_2, pivot_2, 1.0), 0.0)
    c_1 = jnp.where(live_1, (rest_1 - mixed * c_2) / safe_1, 0.0)
    c_0 = (g[0] - h[1] * c_1 - h[2] * c_2) / h[0]
    return c_0, c_1, c_2


def invert(counts, atoms, places):
    rows = places.shape[1]
    row_low = row_index((LANES, LANES))
    row_high = row_index((rows, LANES))
    lane = lane_index((rows, LANES))

    def one_cell(cell, total):
        live = lane_index((1, LANES)) < counts[cell]
        pointer = jnp.where(live, atoms[pl.ds(cell, 1), :], -1)
        here = (pointer >> 7) == row_high
        cells = jnp.where(here, cell, 0).astype(jnp.float32)
        slots = jnp.where(here, lane, 0).astype(jnp.float32)
        parts = jnp.concatenate([cells, slots], axis=0).astype(jnp.bfloat16)
        lows = jnp.where((pointer & 127) == row_low, 1.0, 0.0).astype(jnp.bfloat16)
        return total + lax.dot_general(
            parts, lows, (((1,), (1,)), ((), ())), preferred_element_type=jnp.float32
        )

    total = jnp.zeros((2 * rows, LANES), jnp.float32)
    total = lax.fori_loop(0, CELLS, one_cell, total, unroll=8).astype(jnp.int32)
    places[0] = total[:rows]
    places[1] = total[rows:]


def finish_kernel(moments, slots, first, second, places, out, charges):
    summed = moments[...]
    lane = lane_index((2, LANES))
    row = row_index((2, LANES))

    def pair(index):
        picked = jnp.where(lane - row == 2 * index, summed, 0.0)
        return jnp.broadcast_to(jnp.sum(picked, axis=1, keepdims=True), (2, LANES))

    rows = [pair(index) for index in range(9)]
    c_0, c_1, c_2 = solve(rows[:6])
    totals = c_0 * rows[6] + c_1 * rows[7] + c_2 * rows[8]
    balance = totals[0:1] / totals[1:2]
    sign = jnp.concatenate([jnp.ones((1, LANES), jnp.float32), -balance], axis=0)
    c_0, c_1, c_2 = c_0 * sign, c_1 * sign, c_2 * sign
    for cell in range(CELLS):
        q, z = cell // CZ, cell % CZ + 1
        mixed = c_0 * slots[cell, 4:6, :] + c_1 * first[q, z] + c_2 * second[q, z]
        charges[cell : cell + 1, :] = jnp.sum(mixed, axis=0, keepdims=True)
    tiles = [jnp.zeros((8, LANES), jnp.float32) for _ in range(places.shape[1] // 8)]
    for cell in range(CELLS):
        line = spread(charges[cell : cell + 1, :])
        for at in range(len(tiles)):
            here = slice(8 * at, 8 * at + 8)
            moved = jnp.take_along_axis(line, places[1, here, :], axis=1)
            tiles[at] = jnp.where(places[0, here, :] == cell, moved, tiles[at])
    out[...] = jnp.concatenate(tiles, axis=0)[: out.shape[0]]


def finish(moments, slots, first, second, places, atoms_local):
    return pl.pallas_call(
        finish_kernel,
        out_shape=jax.ShapeDtypeStruct((atoms_local // LANES, LANES), jnp.float32),
        in_specs=[IN_VMEM] * 5,
        out_specs=IN_VMEM,
        scratch_shapes=[VMEM((CELLS, LANES), jnp.float32)],
        compiler_params=params(8),
    )(moments, slots, first, second, places)


def partner(block, axis, mask):
    count = lax.axis_size(axis)
    return lax.ppermute(block, axis, [(low, low ^ mask) for low in range(count)])


def shifted(block, along_x):
    count = lax.axis_size("gx")
    return lax.ppermute(block, "gx", [(i, (i + 4 * along_x) % count) for i in range(count)])


def with_z_faces(edge, inner):
    other = partner(edge, "gx", 1)
    parts = [other[:, 0:1], edge[:, 1:2], inner, edge[:, 0:1], other[:, 1:2]]
    return jnp.concatenate(parts, axis=1)


def flat(columns):
    return columns.reshape((-1,) + columns.shape[-2:])


def x_faces(core):
    count = lax.axis_size("gx")
    rows = count // 4
    odd = (lax.axis_index("gx") // 4) % 2 == 1
    if rows % 2:
        return shifted(core[2:], 1), shifted(core[:2], -1)
    route = [(i, (i + (4 if (i // 4) % 2 else -4)) % count) for i in range(count)]
    second = lax.ppermute(jnp.where(odd, core[2:], core[:2]), "gx", route)
    first = lax.ppermute(jnp.where(odd, core[:2], core[2:]), "gx", [(i, i ^ 4) for i in range(count)])
    return first, second


def sorted_faces(first, second):
    odd = (lax.axis_index("gx") // 4) % 2 == 1
    if (lax.axis_size("gx") // 4) % 2:
        return first, second
    return jnp.where(odd, first, second), jnp.where(odd, second, first)


def exchange(edge, inner, on_core, on_faces, on_corners):
    core = with_z_faces(edge, inner)
    first, second = x_faces(core)
    beyond = partner(core, "gx", 2)
    sums, spill, *more = on_core(flat(core))
    second, first, sums = lax.optimization_barrier((second, first, sums))
    low, high = sorted_faces(first, second)
    corners = partner(jnp.concatenate([low, high], axis=0), "gx", 2)
    pieces = [flat(part) for part in (low, high, beyond)]
    sums, spill, *more = on_faces(pieces, sums, spill, *more)
    corners = flat(corners)
    return core, pieces, corners, on_corners(corners, sums, spill, core, *more)


def global_sum(values):
    count = lax.axis_size("gx")
    if count & (count - 1):
        return lax.psum(values, "gx")
    step = 1
    while step < count:
        if step >= 2 and 4 * step <= count:
            others = [partner(values, "gx", k * step) for k in (3, 2, 1)]
            values = (values + others[0]) + (others[1] + others[2])
            step *= 4
        else:
            values = values + partner(values, "gx", step)
            step *= 2
    return values


def local(cell_offsets, electronegativity, hardness, charge_widths, cell_counts, cell_atoms):
    slots, diagonal = prepare(
        cell_counts, cell_offsets, electronegativity, hardness, charge_widths, cell_atoms
    )
    stored = []

    def keep(tiles, *others):
        stored.append(tiles)
        return others

    def build_ends(corners, sums, spill, core, *own):
        (edge,) = keep(*build_corners(EDGES, corners, *own, sums, spill, flat(core), diagonal))
        (inner,) = keep(*build_corners(INNER, corners, *own, sums, spill, flat(core), diagonal))
        return by_column(edge), by_column(inner)

    def by_column(cells):
        return cells.reshape((QUADS, -1) + cells.shape[1:])

    grid = by_column(slots)
    core, pieces, corners, ends = exchange(
        jnp.concatenate([grid[:, -1:], grid[:, :1]], axis=1),
        grid[:, 1:-1],
        lambda core: keep(*build_core(core)),
        lambda faces, sums, spill, *own: keep(*build_faces(faces, *own, sums, spill)) + own,
        build_ends,
    )
    info = flat(core)

    def apply(edge, inner, lists, on_corners):
        def on_faces(faces, sums, spill, *found):
            return (*apply_faces(pieces, faces, stored[1], sums, spill), *found)

        def on_core(own):
            return apply_core(info, own, stored[0], lists)

        return exchange(edge, inner, on_core, on_faces, on_corners)

    def apply_ends(others, sums, spill, _, *found):
        edge = apply_corners(corners, others, stored[2], sums, spill, info, diagonal)
        inner = apply_corners(corners, others, stored[3], sums, spill, info, diagonal)
        return by_column(edge), by_column(inner), found

    atoms_local = cell_offsets.shape[1]
    lists = (cell_counts, cell_atoms, atoms_local)
    first, _, _, (edge, inner, (places,)) = apply(*ends, lists, apply_ends)

    def sum_up(others, sums, spill, second):
        return apply_last(
            corners, others, stored[2], stored[3], sums, spill, info, diagonal, slots, first, second
        )

    second, _, _, moments = apply(edge, inner, None, sum_up)
    charges = finish(global_sum(moments), slots, first, second, places, atoms_local)
    return charges.reshape(-1)


def solution(mesh):
    placed = (
        P(None, ("grp", "gx")),
        P(("grp", "gx")),
        P(("grp", "gx")),
        P(("grp", "gx")),
        P(("grp", "gx")),
        P(("grp", "gx"), None),
    )
    return jax.shard_map(
        local, mesh=mesh, in_specs=placed, out_specs=P(("grp", "gx")), check_vma=False
    )
```

```python
import functools
import math

import jax
import jax.numpy as jnp
from jax import lax
from jax.experimental import pallas as pl
from jax.experimental.pallas import tpu as pltpu
from jax.sharding import PartitionSpec as P

CX = 2
CY = 2
CZ = 8
EZ = CZ + 2
CELLS = CX * CY * CZ
QUADS = CX * CY
LANES = 128
BLOCKS = 11
GROUPS = ((0, 1, 2, 3), (4, 5, 6, 7), (8, 9, 10))

COULOMB = 14.399645
ROOT_PI = math.sqrt(math.pi)
SCREEN = 1.0 / (math.sqrt(2.0) * 3.0)
EWALD_SELF = math.sqrt(2.0 / math.pi) / 3.0
SIDE = 12.0 * SCREEN
CUT_SQUARED = (12.0 * SCREEN) ** 2
CLOSEST_SQUARED = (0.5 * SCREEN) ** 2
PAIR_SCALE = COULOMB * SCREEN

VMEM = pltpu.VMEM
SMEM = pltpu.SMEM


def params(mib):
    return pltpu.CompilerParams(vmem_limit_bytes=mib * 2**20)


def lane_index(shape):
    return lax.broadcasted_iota(jnp.int32, shape, len(shape) - 1)


def row_index(shape):
    return lax.broadcasted_iota(jnp.int32, shape, len(shape) - 2)


def edge_place(slot):
    return slot // 2, (CZ - 1) * (1 - slot % 2)


def inner_place(slot):
    return slot // (CZ - 2), 1 + slot % (CZ - 2)


EDGES = 2 * QUADS
INNER = CELLS - EDGES
PLACES = {EDGES: edge_place, INNER: inner_place}
LAYERS = {EDGES: (0, CZ - 1), INNER: range(1, CZ - 1)}


def gather_cells(counted, atoms, table, others, out):
    place = PLACES[out.shape[0]]
    row = row_index((8, LANES))
    lane = lane_index((1, LANES))

    def pick(source, pointers):
        share = 8 // len(pointers)
        pointer = spread(pointers[-1])
        for k in range(len(pointers) - 2, -1, -1):
            pointer = jnp.where(row < share * (k + 1), pointers[k], pointer)
        high = pointer >> 7
        low = pointer & 127
        picked = jnp.zeros((8, LANES), jnp.float32)
        for chunk in range(source.shape[0]):
            part = jnp.take_along_axis(source[chunk], low, axis=1)
            picked = jnp.where(high == chunk, part, picked)
        return picked

    def four_cells(step, _):
        slots = [4 * step + k for k in range(4)]
        places = [place(slot) for slot in slots]
        counts = [counted[pl.ds(q * CZ + z, 1), :] for q, z in places]
        occupied = [lane < count for count in counts]
        pointers = [
            jnp.where(live, atoms[pl.ds(q * CZ + z, 1), :], 0)
            for (q, z), live in zip(places, occupied)
        ]
        pairs = [pick(table, pointers[:2]), pick(table, pointers[2:])]
        both = pick(others, pointers)
        for k, (slot, live) in enumerate(zip(slots, occupied)):
            q = places[k][0]
            at = 4 * (k % 2)
            picked = pairs[k // 2][at : at + 4]
            width = jnp.where(live, picked[3:4], 1.0)
            hard = both[2 * k + 1 : 2 * k + 2]
            diag = jnp.where(live, hard + COULOMB * (1.0 / (width * ROOT_PI) - EWALD_SELF), 1.0)
            negative = jnp.where(live, both[2 * k : 2 * k + 1], 0.0)
            out[slot, 0:1, :] = (picked[0:1] + (q // CY).astype(jnp.float32)) * SIDE
            out[slot, 1:2, :] = (picked[1:2] + (q % CY).astype(jnp.float32)) * SIDE
            out[slot, 2:3, :] = picked[2:3] * SIDE
            out[slot, 3:4, :] = (2.0 * SCREEN * SCREEN) * width * width
            out[slot, 4:5, :] = -negative / diag
            out[slot, 5:6, :] = jnp.where(live, 1.0 / diag, 0.0)
            out[slot, 6:7, :] = diag
            out[slot, 7:8, :] = counts[k].astype(jnp.float32)
        return 0

    lax.fori_loop(0, out.shape[0] // 4, four_cells, 0, unroll=2)


def prepare_kernel(
    counts_hbm, offsets, negativity, hardness, widths, atoms_hbm, edge, counted, atoms, table, others,
    counts, raw_offsets, raw_negativity, raw_hardness, raw_widths, sems,
):
    copies = [
        pltpu.make_async_copy(source, target, sems.at[index])
        for index, (source, target) in enumerate(
            [
                (counts_hbm, counts),
                (offsets, raw_offsets),
                (negativity, raw_negativity),
                (hardness, raw_hardness),
                (widths, raw_widths),
                (atoms_hbm, atoms),
            ]
        )
    ]
    for copy in copies:
        copy.start()
    for copy in copies:
        copy.wait()
    for chunk in range(table.shape[0]):
        here = slice(chunk * LANES, (chunk + 1) * LANES)
        for first in (0, 4):
            table[chunk, first : first + 3, :] = raw_offsets[:, here]
            table[chunk, first + 3 : first + 4, :] = raw_widths[chunk : chunk + 1, :]
        for first in (0, 2, 4, 6):
            others[chunk, first : first + 1, :] = raw_negativity[chunk : chunk + 1, :]
            others[chunk, first + 1 : first + 2, :] = raw_hardness[chunk : chunk + 1, :]
    for cell in range(CELLS):
        counted[cell : cell + 1, :] = jnp.full((1, LANES), counts[cell])
    gather_cells(counted, atoms, table, others, edge)


def prepare_rest_kernel(counted, atoms, table, others, inner):
    gather_cells(counted, atoms, table, others, inner)


def prepare(counts, offsets, negativity, hardness, widths, atoms):
    chunks = offsets.shape[1] // LANES
    plane = (chunks, LANES)
    tables = jax.ShapeDtypeStruct((chunks, 8, LANES), jnp.float32)
    lists = jax.ShapeDtypeStruct(atoms.shape, jnp.int32)
    edge, *rest = pl.pallas_call(
        prepare_kernel,
        out_shape=(
            jax.ShapeDtypeStruct((EDGES, 8, LANES), jnp.float32),
            lists,
            lists,
            tables,
            tables,
        ),
        in_specs=[pl.BlockSpec(memory_space=pltpu.HBM)] * 6,
        out_specs=(pl.BlockSpec(memory_space=VMEM),) * 5,
        scratch_shapes=[
            SMEM(counts.shape, jnp.int32),
            VMEM(offsets.shape, jnp.float32),
            VMEM(plane, jnp.float32),
            VMEM(plane, jnp.float32),
            VMEM(plane, jnp.float32),
            pltpu.SemaphoreType.DMA((6,)),
        ],
        compiler_params=params(8),
    )(
        *[
            pltpu.with_memory_space_constraint(array, pltpu.HBM)
            for array in (
                counts,
                offsets,
                negativity.reshape(plane),
                hardness.reshape(plane),
                widths.reshape(plane),
                atoms,
            )
        ]
    )
    inner = pl.pallas_call(
        prepare_rest_kernel,
        out_shape=jax.ShapeDtypeStruct((INNER, 8, LANES), jnp.float32),
        in_specs=[pl.BlockSpec(memory_space=VMEM)] * 4,
        out_specs=pl.BlockSpec(memory_space=VMEM),
        compiler_params=params(8),
        cost_estimate=pl.CostEstimate(flops=2**20, bytes_accessed=2**22, transcendentals=0),
    )(*rest)
    return edge, inner


def pack_column(info, cells, source, packed, spills, target, at, shift, layers=range(CZ)):
    lane = lane_index((8, LANES))
    row = row_index((8, LANES))
    for z in layers:
        base = source * EZ + z
        low, mid, top = [spread(info[base + k, 7:8, :]).astype(jnp.int32) for k in range(3)]
        end = low + mid - LANES
        tiles = [cells[base + k] for k in range(3)]
        if shift is not None:
            for k in range(3):
                offset = jnp.where(row == 2, (k - 1) * SIDE, 0.0)
                for axis in range(2):
                    offset = jnp.where(row == axis, shift[axis] * SIDE, offset)
                tiles[k] = tiles[k] + offset
        second = jnp.take_along_axis(tiles[1], (lane - low) & 127, axis=1)
        third = jnp.take_along_axis(tiles[2], (lane - end) & 127, axis=1)
        packed[target * CZ + z, 0] = jnp.where(lane < low, tiles[0], second)
        packed[target * CZ + z, 1] = jnp.where(lane < end, second, third)
        spill = jnp.where(lane < end + top - LANES, third, 0.0)
        spills[target * CZ + z] = pltpu.roll(spill, at, 1) if at else spill


def pack_core(info, cells, packed, spills, build):
    for q in range(QUADS):
        pack_column(info, cells, q, packed, spills, q, 8 * q, (0, 0) if build else None)


def pack_faces(infos, pieces, packed, spills, build):
    for side in range(2):
        sign = 2 * side - 1
        for y in range(CY):
            shift = (sign * CX, 0) if build else None
            at = 32 + 8 * y
            pack_column(infos[side], pieces[side], y, packed, spills, 2 * side + y, at, shift)
        for x in range(CX):
            shift = (0, sign * CY) if build else None
            source = 2 * x + 1 - side
            target = 4 + 2 * x + side
            at = 48 + 8 * x
            pack_column(infos[2], pieces[2], source, packed, spills, target, at, shift)


def pack_corners(info, cells, packed, spills, build, layers):
    for side_x in range(2):
        for side_y in range(2):
            shift = ((2 * side_x - 1) * CX, (2 * side_y - 1) * CY) if build else None
            source = 2 * side_x + 1 - side_y
            target = 2 * side_x + side_y
            pack_column(info, cells, source, packed, spills, target, 64, shift, layers)


def core_columns(q):
    return [q ^ k for k in range(4)]


def face_columns(q):
    x, y = q >> 1, q & 1
    return [2 * x, 2 * x + 1, 4 + y, 6 + y]


def overflow_of(spills, columns, z):
    return sum(spills[column * CZ + z] for column in columns)


def spread(row):
    return jnp.broadcast_to(row, (8, LANES))


def couple(x_i, y_i, z_i, w_i, x_j, y_j, z_j, w_j):
    delta_x = x_j - x_i
    delta_y = y_j - y_i
    delta_z = z_j - z_i
    squared = delta_x * delta_x + delta_y * delta_y + delta_z * delta_z
    held = jnp.maximum(squared, CLOSEST_SQUARED)
    inverse = lax.rsqrt(held)
    distance = held * inverse
    scaled = distance * lax.rsqrt(w_i + w_j)
    value = (lax.erf(scaled) - lax.erf(distance)) * inverse
    return jnp.where(squared < CUT_SQUARED, value, 0.0)


def to_rows(sums, block):
    here = lane_index((8, LANES)) - row_index((8, LANES)) == 8 * block
    return jnp.where(here, jnp.sum(sums, axis=1, keepdims=True), 0.0)


def add_rows(cell, sums, rows):
    for index in range(2):
        total = jnp.zeros((8, LANES), jnp.float32)
        for block in range(BLOCKS):
            total = total + to_rows(sums[cell, block, index], block)
        rows.append(jnp.sum(total, axis=0, keepdims=True))


def finish_cell(slot, place, target, info, sums, out):
    q, z = place(slot)
    rows = []
    add_rows(slot, sums, rows)
    own = info.at[q * EZ + z + 1]
    scale = PAIR_SCALE / own[6:7, :]
    live = lane_index((1, LANES)) < own[7:8, :].astype(jnp.int32)
    out[target, 0:1, :] = jnp.where(live, rows[0] * scale, 0.0)
    out[target, 1:2, :] = jnp.where(live, rows[1] * scale, 0.0)


def build_cell(cell, slot, lines, turned, kernels, before, sums, below):
    own = None
    if below is not None:
        own = lane_index((8, LANES)) - row_index((8, LANES)) - below
    for group in GROUPS:
        sums_s, sums_t = start_sums(cell, before, group)
        for index, line in enumerate(lines):
            beside = [line(k) for k in range(6)]
            for at, block in enumerate(group):
                value = couple(*[turned[cell, block, k] for k in range(4)], *beside[:4])
                if own is not None and index < 2:
                    value = jnp.where(own == 8 * block - LANES * index, 0.0, value)
                kernels[slot, block, index] = value
                sums_s[at] = sums_s[at] + value * beside[4]
                sums_t[at] = sums_t[at] + value * beside[5]
        for at, block in enumerate(group):
            sums[slot, block, 0] = sums_s[at]
            sums[slot, block, 1] = sums_t[at]


def start_sums(cell, before, blocks):
    if before is None:
        zeros = [jnp.zeros((8, LANES), jnp.float32) for _ in blocks]
        return zeros, list(zeros)
    sums_s = [before[cell, block, 0] for block in blocks]
    return sums_s, [before[cell, block, 1] for block in blocks]


def lines_of(packed, columns, z):
    def line(column, half):
        return lambda k: spread(packed[column * CZ + z, half, k : k + 1, :])

    return [line(column, half) for column in columns for half in range(2)]


def rest_line(rest, cell):
    return lambda k: spread(rest[cell, k : k + 1, :])


def parts_of(value):
    high = value.astype(jnp.bfloat16).astype(jnp.float32)
    rest = value - high
    middle = rest.astype(jnp.bfloat16).astype(jnp.float32)
    return high, middle, rest - middle


def turn_cells(core, turned):
    chosen = row_index((24, 4 * LANES)) & 7
    ones = jnp.where(chosen == lane_index((24, 4 * LANES)) >> 7, 1.0, 0.0).astype(jnp.bfloat16)
    for cell in range(CELLS):
        here = core[(cell // CZ) * EZ + cell % CZ + 1]
        left = jnp.concatenate(parts_of(here), axis=0).T[: 8 * BLOCKS + 8].astype(jnp.bfloat16)
        wide = lax.dot_general(
            left, ones, (((1,), (0,)), ((), ())), preferred_element_type=jnp.float32
        )
        for block in range(BLOCKS):
            for k in range(4):
                turned[cell, block, k] = wide[8 * block : 8 * block + 8, k * LANES : (k + 1) * LANES]


def core_spills(spills, spill):
    for z in range(CZ):
        spill[z] = overflow_of(spills, range(QUADS), z)


def face_spills(spills, before, spill):
    for cell in range(CELLS):
        q, z = cell // CZ, cell % CZ
        spill[cell] = before[z] + overflow_of(spills, face_columns(q), z)


def corner_loop(slots, work, finish, sums):
    def one_cell(slot, _):
        finish(jnp.maximum(slot - 1, 0))
        work(slot)
        return 0

    sums[0] = jnp.zeros(sums.shape[1:], jnp.float32)
    lax.fori_loop(0, slots, one_cell, 0, unroll=4)
    finish(slots - 1)


def corner_spills(spills, before, rest, place):
    for slot in range(rest.shape[0]):
        q, z = place(slot)
        rest[slot] = before[q * CZ + z] + spills[q * CZ + z]


def core_kernel(core, kernels, sums, spill, turned, packed, spills):
    turn_cells(core, turned)
    pack_core(core, core, packed, spills, True)
    core_spills(spills, spill)

    def one_cell(cell, _):
        q, z = cell // CZ, cell % CZ
        below = spread(core[q * EZ + z, 7:8, :]).astype(jnp.int32)
        lines = lines_of(packed, core_columns(q), z)
        build_cell(cell, cell, lines, turned, kernels, None, sums, below)
        return 0

    lax.fori_loop(0, CELLS, one_cell, 0, unroll=2)


def face_kernel(
    x_low, x_high, beyond, turned, before, spill_before, kernels, sums, spill, packed, spills
):
    pieces = [x_low, x_high, beyond]
    pack_faces(pieces, pieces, packed, spills, True)
    face_spills(spills, spill_before, spill)

    def one_cell(cell, _):
        lines = lines_of(packed, face_columns(cell // CZ), cell % CZ)
        build_cell(cell, cell, lines, turned, kernels, before, sums, None)
        return 0

    lax.fori_loop(0, CELLS, one_cell, 0, unroll=2)


def corner_kernel(
    corners, turned, before, spill_before, core, kernels, out, packed, spills, rest, sums
):
    slots = kernels.shape[0]
    place = PLACES[slots]
    pack_corners(corners, corners, packed, spills, True, LAYERS[slots])
    corner_spills(spills, spill_before, rest, place)

    def work(slot):
        q, z = place(slot)
        lines = lines_of(packed, [q], z) + [rest_line(rest, slot)]
        build_cell(q * CZ + z, slot, lines, turned, kernels, before, sums, None)

    def finish(slot):
        finish_cell(slot, place, slot, core, sums, out)

    corner_loop(slots, work, finish, sums)


IN_VMEM = pl.BlockSpec(memory_space=VMEM)
IN_SMEM = pl.BlockSpec(memory_space=SMEM)
PAIR = jax.ShapeDtypeStruct((CELLS, 2, LANES), jnp.float32)
SPILL = jax.ShapeDtypeStruct((CELLS, 8, LANES), jnp.float32)
SUMS = jax.ShapeDtypeStruct((CELLS, BLOCKS, 2, 8, LANES), jnp.float32)
TURNED = jax.ShapeDtypeStruct((CELLS, BLOCKS, 4, 8, LANES), jnp.float32)
CORE_SPILL = jax.ShapeDtypeStruct((CZ, 8, LANES), jnp.float32)
CORE_TILES, FACE_TILES, CORNER_TILES = 8, 8, 3


def held(tiles, cells=CELLS):
    return VMEM((cells, BLOCKS, tiles, 8, LANES), jnp.float32)


def pairs(cells):
    return jax.ShapeDtypeStruct((cells, 2, LANES), jnp.float32)


def call(kernel, outs, scratch, tiles, *arrays):
    work = CELLS * BLOCKS * tiles * 8 * LANES
    return pl.pallas_call(
        kernel,
        out_shape=outs,
        in_specs=[IN_SMEM if array.ndim == 1 else IN_VMEM for array in arrays],
        out_specs=jax.tree.map(lambda _: IN_VMEM, outs),
        scratch_shapes=scratch,
        compiler_params=params(8),
        cost_estimate=pl.CostEstimate(
            flops=30 * work, bytes_accessed=8 * work, transcendentals=4 * work
        ),
    )(*arrays)


def packs(columns):
    return [
        VMEM((columns * CZ, 2, 8, LANES), jnp.float32),
        VMEM((columns * CZ, 8, LANES), jnp.float32),
    ]


def build_core(core):
    outs = (held(CORE_TILES), SUMS, CORE_SPILL, TURNED)
    return call(core_kernel, outs, packs(4), CORE_TILES, core)


def build_faces(pieces, turned, before, spill):
    outs = (held(FACE_TILES), SUMS, SPILL)
    return call(face_kernel, outs, packs(8), FACE_TILES, *pieces, turned, before, spill)


def corner_scratch(cells):
    rest = VMEM((cells, 8, LANES), jnp.float32)
    return packs(4) + [rest, VMEM((cells, BLOCKS, 2, 8, LANES), jnp.float32)]


def build_corners(cells, corners, turned, before, spill, core):
    outs = (held(CORNER_TILES, cells), pairs(cells))
    arrays = [corners, turned, before, spill, core]
    return call(corner_kernel, outs, corner_scratch(cells), CORNER_TILES, *arrays)


def apply_cell(cell, slot, lines, stored, before, sums):
    sums_s, sums_t = start_sums(cell, before, range(BLOCKS))
    for index, line in enumerate(lines):
        line_s, line_t = line(0), line(1)
        for block in range(BLOCKS):
            value = stored[slot, block, index]
            sums_s[block] = sums_s[block] + value * line_s
            sums_t[block] = sums_t[block] + value * line_t
    for block in range(BLOCKS):
        sums[slot, block, 0] = sums_s[block]
        sums[slot, block, 1] = sums_t[block]


def widen(pieces, wides):
    for piece, wide in zip(pieces, wides):
        wide[:, 0:2, :] = piece[...]


def apply_core_kernel(info, core, stored, sums, spill, wide, packed, spills):
    widen([core], [wide])
    pack_core(info, wide, packed, spills, False)
    core_spills(spills, spill)

    def one_cell(cell, _):
        lines = lines_of(packed, core_columns(cell // CZ), cell % CZ)
        apply_cell(cell, cell, lines, stored, None, sums)
        return 0

    lax.fori_loop(0, CELLS, one_cell, 0, unroll=4)


def apply_face_kernel(*refs):
    infos, pieces, (stored, before, spill_before, sums, spill), wides, (packed, spills) = split(
        refs, 3, 3, 5, 3, 2
    )
    widen(pieces, wides)
    pack_faces(infos, wides, packed, spills, False)
    face_spills(spills, spill_before, spill)

    def one_cell(cell, _):
        lines = lines_of(packed, face_columns(cell // CZ), cell % CZ)
        apply_cell(cell, cell, lines, stored, before, sums)
        return 0

    lax.fori_loop(0, CELLS, one_cell, 0, unroll=4)


def apply_corner_cells(stored, before, spill_before, core, out, target, packed, spills, rest, sums):
    slots = stored.shape[0]
    place = PLACES[slots]
    corner_spills(spills, spill_before, rest, place)

    def work(slot):
        q, z = place(slot)
        lines = lines_of(packed, [q], z) + [rest_line(rest, slot)]
        apply_cell(q * CZ + z, slot, lines, stored, before, sums)

    def finish(slot):
        finish_cell(slot, place, target(slot), core, sums, out)

    corner_loop(slots, work, finish, sums)


def apply_corner_kernel(
    info, corners, stored, before, spill_before, core, out, wide, packed, spills, rest, sums
):
    widen([corners], [wide])
    pack_corners(info, wide, packed, spills, False, LAYERS[stored.shape[0]])
    apply_corner_cells(
        stored, before, spill_before, core, out, lambda slot: slot,
        packed, spills, rest, sums,
    )


def split(refs, *sizes):
    parts = []
    for size in sizes:
        parts.append(refs[:size])
        refs = refs[size:]
    return parts


def apply_last_kernel(
    info, corners, edge, inner, before, spill_before, core, slots, first, second,
    moments, third, wide, packed, spills, edge_rest, edge_sums, inner_rest, inner_sums,
):
    widen([corners], [wide])
    pack_corners(info, wide, packed, spills, False, range(CZ))
    for stored, rest, sums in ((edge, edge_rest, edge_sums), (inner, inner_rest, inner_sums)):
        place = PLACES[stored.shape[0]]

        def target(slot, place=place):
            q, z = place(slot)
            return q * CZ + z

        apply_corner_cells(
            stored, before, spill_before, core, third, target, packed, spills, rest, sums
        )
    d = slots[:, 1 : 1 + CZ, 6:7, :].reshape(CELLS, 1, LANES)
    v_0 = slots[:, 1 : 1 + CZ, 4:6, :].reshape(CELLS, 2, LANES)
    v_1 = first[:, 1 : 1 + CZ].reshape(v_0.shape)
    v_2 = second[:, 1 : 1 + CZ].reshape(v_0.shape)
    d_0 = d * v_0
    d_2 = d * v_2
    parts = [d_0 * v_0, d_0 * v_1, d * v_1 * v_1, d_2 * v_1, d_2 * v_2, d_2 * third[...]]
    row = row_index((2, LANES))
    line = jnp.zeros((2, LANES), jnp.float32)
    for index, part in enumerate(parts + [v_0, v_1, v_2]):
        total = jnp.sum(jnp.sum(part, axis=0), axis=1, keepdims=True)
        line = jnp.where(lane_index((2, LANES)) - row == 2 * index, total, line)
    moments[...] = jnp.sum(line, axis=0, keepdims=True)


def wide(piece):
    return VMEM((piece.shape[0], 8, LANES), jnp.float32)


def apply_core(info, core, stored):
    stored = pltpu.with_memory_space_constraint(stored, VMEM)
    scratch = [wide(core)] + packs(4)
    return call(apply_core_kernel, (SUMS, CORE_SPILL), scratch, 2, info, core, stored)


def apply_faces(infos, pieces, stored, before, spill):
    stored = pltpu.with_memory_space_constraint(stored, VMEM)
    scratch = [wide(piece) for piece in pieces] + packs(8)
    return call(
        apply_face_kernel, (SUMS, SPILL), scratch, 2, *infos, *pieces, stored, before, spill
    )


def apply_corners(info, corners, stored, before, spill, core):
    stored = pltpu.with_memory_space_constraint(stored, VMEM)
    cells = stored.shape[0]
    arrays = [info, corners, stored, before, spill, core]
    scratch = [wide(corners)] + corner_scratch(cells)
    return call(apply_corner_kernel, pairs(cells), scratch, 2, *arrays)


def apply_last(info, corners, edge, inner, before, spill, core, slots, first, second):
    edge = pltpu.with_memory_space_constraint(edge, VMEM)
    inner = pltpu.with_memory_space_constraint(inner, VMEM)
    arrays = [info, corners, edge, inner, before, spill, core, slots, first, second]
    scratch = [VMEM((CELLS, 2, LANES), jnp.float32), wide(corners)] + corner_scratch(EDGES)
    scratch += corner_scratch(INNER)[2:]
    out = jax.ShapeDtypeStruct((1, LANES), jnp.float32)
    return call(apply_last_kernel, out, scratch, 2, *arrays)


def solve(g):
    tiny = 1e-6
    h = [g[k] + g[k + 1] for k in range(5)]
    ratio_1 = h[1] / h[0]
    ratio_2 = h[2] / h[0]
    pivot_1 = h[2] - ratio_1 * h[1]
    mixed = h[3] - ratio_1 * h[2]
    rest_1 = g[1] - ratio_1 * g[0]
    live_1 = pivot_1 > tiny * h[2]
    safe_1 = jnp.where(live_1, pivot_1, 1.0)
    ratio_3 = jnp.where(live_1, mixed / safe_1, 0.0)
    pivot_2 = h[4] - ratio_2 * h[2] - ratio_3 * mixed
    rest_2 = g[2] - ratio_2 * g[0] - ratio_3 * rest_1
    live_2 = live_1 & (pivot_2 > tiny * h[4])
    c_2 = jnp.where(live_2, rest_2 / jnp.where(live_2, pivot_2, 1.0), 0.0)
    c_1 = jnp.where(live_1, (rest_1 - mixed * c_2) / safe_1, 0.0)
    c_0 = (g[0] - h[1] * c_1 - h[2] * c_2) / h[0]
    return c_0, c_1, c_2


def invert(counts, atoms, places):
    rows = places.shape[1]
    row_low = row_index((LANES, LANES))
    row_high = row_index((rows, LANES))
    lane = lane_index((rows, LANES))

    def one_cell(cell, total):
        live = lane_index((1, LANES)) < counts[cell]
        pointer = jnp.where(live, atoms[pl.ds(cell, 1), :], -1)
        here = (pointer >> 7) == row_high
        cells = jnp.where(here, cell, 0).astype(jnp.float32)
        slots = jnp.where(here, lane, 0).astype(jnp.float32)
        parts = jnp.concatenate([cells, slots], axis=0).astype(jnp.bfloat16)
        lows = jnp.where((pointer & 127) == row_low, 1.0, 0.0).astype(jnp.bfloat16)
        return total + lax.dot_general(
            parts, lows, (((1,), (1,)), ((), ())), preferred_element_type=jnp.float32
        )

    total = jnp.zeros((2 * rows, LANES), jnp.float32)
    total = lax.fori_loop(0, CELLS, one_cell, total, unroll=8).astype(jnp.int32)
    places[0] = total[:rows]
    places[1] = total[rows:]


def inverted(counts, atoms, atoms_local):
    rows = (atoms_local // LANES + 15) // 16 * 16
    return call(invert, jax.ShapeDtypeStruct((2, rows, LANES), jnp.int32), [], 2, counts, atoms)


def finish_kernel(moments, slots, first, second, places, out, charges):
    summed = moments[...]
    lane = lane_index((2, LANES))
    row = row_index((2, LANES))

    def pair(index):
        picked = jnp.where(lane - row == 2 * index, summed, 0.0)
        return jnp.broadcast_to(jnp.sum(picked, axis=1, keepdims=True), (2, LANES))

    rows = [pair(index) for index in range(9)]
    c_0, c_1, c_2 = solve(rows[:6])
    totals = c_0 * rows[6] + c_1 * rows[7] + c_2 * rows[8]
    balance = totals[0:1] / totals[1:2]
    sign = jnp.concatenate([jnp.ones((1, LANES), jnp.float32), -balance], axis=0)
    c_0, c_1, c_2 = c_0 * sign, c_1 * sign, c_2 * sign
    for cell in range(CELLS):
        q, z = cell // CZ, cell % CZ + 1
        mixed = c_0 * slots[q, z, 4:6, :] + c_1 * first[q, z] + c_2 * second[q, z]
        charges[cell : cell + 1, :] = jnp.sum(mixed, axis=0, keepdims=True)
    tiles = [jnp.zeros((8, LANES), jnp.float32) for _ in range(places.shape[1] // 8)]
    for cell in range(CELLS):
        line = spread(charges[cell : cell + 1, :])
        for at in range(len(tiles)):
            here = slice(8 * at, 8 * at + 8)
            moved = jnp.take_along_axis(line, places[1, here, :], axis=1)
            tiles[at] = jnp.where(places[0, here, :] == cell, moved, tiles[at])
    out[...] = jnp.concatenate(tiles, axis=0)[: out.shape[0]]


def finish(moments, slots, first, second, places, atoms_local):
    return pl.pallas_call(
        finish_kernel,
        out_shape=jax.ShapeDtypeStruct((atoms_local // LANES, LANES), jnp.float32),
        in_specs=[IN_VMEM] * 5,
        out_specs=IN_VMEM,
        scratch_shapes=[VMEM((CELLS, LANES), jnp.float32)],
        compiler_params=params(8),
    )(moments, slots, first, second, places)


def partner(block, axis, mask):
    count = lax.axis_size(axis)
    return lax.ppermute(block, axis, [(low, low ^ mask) for low in range(count)])


def shifted(block, along_x):
    count = lax.axis_size("gx")
    return lax.ppermute(block, "gx", [(i, (i + 4 * along_x) % count) for i in range(count)])


def with_z_faces(edge, inner):
    other = partner(edge, "gx", 1)
    parts = [other[:, 0:1], edge[:, 1:2], inner, edge[:, 0:1], other[:, 1:2]]
    return jnp.concatenate(parts, axis=1)


def flat(columns):
    return columns.reshape((-1,) + columns.shape[-2:])


def x_faces(core):
    count = lax.axis_size("gx")
    rows = count // 4
    odd = (lax.axis_index("gx") // 4) % 2 == 1
    if rows % 2:
        return shifted(core[2:], 1), shifted(core[:2], -1)
    route = [(i, (i + (4 if (i // 4) % 2 else -4)) % count) for i in range(count)]
    second = lax.ppermute(jnp.where(odd, core[2:], core[:2]), "gx", route)
    first = lax.ppermute(jnp.where(odd, core[:2], core[2:]), "gx", [(i, i ^ 4) for i in range(count)])
    return first, second


def sorted_faces(first, second):
    odd = (lax.axis_index("gx") // 4) % 2 == 1
    if (lax.axis_size("gx") // 4) % 2:
        return first, second
    return jnp.where(odd, first, second), jnp.where(odd, second, first)


def exchange(edge, inner, on_core, on_faces, on_corners):
    core = with_z_faces(edge, inner)
    first, second = x_faces(core)
    beyond = partner(core, "gx", 2)
    sums, spill, *more = on_core(flat(core))
    second, first, sums = lax.optimization_barrier((second, first, sums))
    low, high = sorted_faces(first, second)
    corners = partner(jnp.concatenate([low, high], axis=0), "gx", 2)
    pieces = [flat(part) for part in (low, high, beyond)]
    sums, spill, *more = on_faces(pieces, sums, spill, *more)
    corners = flat(corners)
    return core, pieces, corners, on_corners(corners, sums, spill, core, *more)


def global_sum(values):
    count = lax.axis_size("gx")
    if count & (count - 1):
        return lax.psum(values, "gx")
    step = 1
    while step < count:
        if step >= 2 and 4 * step <= count:
            others = [partner(values, "gx", k * step) for k in (3, 2, 1)]
            values = (values + others[0]) + (others[1] + others[2])
            step *= 4
        else:
            values = values + partner(values, "gx", step)
            step *= 2
    return values


def local(cell_offsets, electronegativity, hardness, charge_widths, cell_counts, cell_atoms):
    edge, inner = prepare(
        cell_counts, cell_offsets, electronegativity, hardness, charge_widths, cell_atoms
    )
    stored = []

    def keep(tiles, *others):
        stored.append(tiles)
        return others

    def build_ends(corners, sums, spill, core, *own):
        (edge,) = keep(*build_corners(EDGES, corners, *own, sums, spill, flat(core)))
        (inner,) = keep(*build_corners(INNER, corners, *own, sums, spill, flat(core)))
        return by_column(edge), by_column(inner)

    def by_column(cells):
        return cells.reshape((QUADS, -1) + cells.shape[1:])

    slots, pieces, corners, ends = exchange(
        by_column(edge),
        by_column(inner),
        lambda core: keep(*build_core(core)),
        lambda faces, sums, spill, *own: keep(*build_faces(faces, *own, sums, spill)) + own,
        build_ends,
    )
    info = flat(slots)

    def apply(edge, inner, on_corners):
        return exchange(
            edge,
            inner,
            lambda own: apply_core(info, own, stored[0]),
            lambda faces, sums, spill: apply_faces(pieces, faces, stored[1], sums, spill),
            on_corners,
        )

    def apply_ends(others, sums, spill, _):
        edge = apply_corners(corners, others, stored[2], sums, spill, info)
        inner = apply_corners(corners, others, stored[3], sums, spill, info)
        return by_column(edge), by_column(inner)

    def sum_up(others, sums, spill, second):
        return apply_last(
            corners, others, stored[2], stored[3], sums, spill, info, slots, first, second
        )

    first, _, _, ends = apply(*ends, apply_ends)
    second, _, _, moments = apply(*ends, sum_up)
    moments, cell_counts, cell_atoms = lax.optimization_barrier((moments, cell_counts, cell_atoms))
    atoms_local = cell_offsets.shape[1]
    places = inverted(cell_counts, cell_atoms, atoms_local)
    charges = finish(global_sum(moments), slots, first, second, places, atoms_local)
    return charges.reshape(-1)


def solution(mesh):
    placed = (
        P(None, ("grp", "gx")),
        P(("grp", "gx")),
        P(("grp", "gx")),
        P(("grp", "gx")),
        P(("grp", "gx")),
        P(("grp", "gx"), None),
    )
    return jax.shard_map(
        local, mesh=mesh, in_specs=placed, out_specs=P(("grp", "gx")), check_vma=False
    )
```

```python
import functools
import math

import jax
import jax.numpy as jnp
from jax import lax
from jax.experimental import pallas as pl
from jax.experimental.pallas import tpu as pltpu
from jax.sharding import PartitionSpec as P

CX = 2
CY = 2
CZ = 8
EZ = CZ + 2
CELLS = CX * CY * CZ
QUADS = CX * CY
LANES = 128
BLOCKS = 11
GROUPS = ((0, 1, 2, 3), (4, 5, 6, 7), (8, 9, 10))

COULOMB = 14.399645
ROOT_PI = math.sqrt(math.pi)
SCREEN = 1.0 / (math.sqrt(2.0) * 3.0)
EWALD_SELF = math.sqrt(2.0 / math.pi) / 3.0
SIDE = 12.0 * SCREEN
CUT_SQUARED = (12.0 * SCREEN) ** 2
CLOSEST_SQUARED = (0.5 * SCREEN) ** 2
PAIR_SCALE = COULOMB * SCREEN

VMEM = pltpu.VMEM
SMEM = pltpu.SMEM


def params(mib):
    return pltpu.CompilerParams(vmem_limit_bytes=mib * 2**20)


def lane_index(shape):
    return lax.broadcasted_iota(jnp.int32, shape, len(shape) - 1)


def row_index(shape):
    return lax.broadcasted_iota(jnp.int32, shape, len(shape) - 2)


def edge_place(slot):
    return slot // 2, (CZ - 1) * (1 - slot % 2)


def inner_place(slot):
    return slot // (CZ - 2), 1 + slot % (CZ - 2)


EDGES = 2 * QUADS
INNER = CELLS - EDGES
PLACES = {EDGES: edge_place, INNER: inner_place}
LAYERS = {EDGES: (0, CZ - 1), INNER: range(1, CZ - 1)}


def gather_cells(counted, atoms, table, others, out):
    place = PLACES[out.shape[0]]
    row = row_index((8, LANES))
    lane = lane_index((1, LANES))

    def pick(source, pointers):
        share = 8 // len(pointers)
        pointer = spread(pointers[-1])
        for k in range(len(pointers) - 2, -1, -1):
            pointer = jnp.where(row < share * (k + 1), pointers[k], pointer)
        high = pointer >> 7
        low = pointer & 127
        picked = jnp.zeros((8, LANES), jnp.float32)
        for chunk in range(source.shape[0]):
            part = jnp.take_along_axis(source[chunk], low, axis=1)
            picked = jnp.where(high == chunk, part, picked)
        return picked

    def four_cells(step, _):
        slots = [4 * step + k for k in range(4)]
        places = [place(slot) for slot in slots]
        counts = [counted[pl.ds(q * CZ + z, 1), :] for q, z in places]
        occupied = [lane < count for count in counts]
        pointers = [
            jnp.where(live, atoms[pl.ds(q * CZ + z, 1), :], 0)
            for (q, z), live in zip(places, occupied)
        ]
        pairs = [pick(table, pointers[:2]), pick(table, pointers[2:])]
        both = pick(others, pointers)
        for k, (slot, live) in enumerate(zip(slots, occupied)):
            q = places[k][0]
            at = 4 * (k % 2)
            picked = pairs[k // 2][at : at + 4]
            width = jnp.where(live, picked[3:4], 1.0)
            hard = both[2 * k + 1 : 2 * k + 2]
            diag = jnp.where(live, hard + COULOMB * (1.0 / (width * ROOT_PI) - EWALD_SELF), 1.0)
            negative = jnp.where(live, both[2 * k : 2 * k + 1], 0.0)
            out[slot, 0:1, :] = (picked[0:1] + (q // CY).astype(jnp.float32)) * SIDE
            out[slot, 1:2, :] = (picked[1:2] + (q % CY).astype(jnp.float32)) * SIDE
            out[slot, 2:3, :] = picked[2:3] * SIDE
            out[slot, 3:4, :] = (2.0 * SCREEN * SCREEN) * width * width
            out[slot, 4:5, :] = -negative / diag
            out[slot, 5:6, :] = jnp.where(live, 1.0 / diag, 0.0)
            out[slot, 6:7, :] = diag
            out[slot, 7:8, :] = counts[k].astype(jnp.float32)
        return 0

    lax.fori_loop(0, out.shape[0] // 4, four_cells, 0, unroll=2)


def prepare_kernel(
    counts_hbm, offsets, negativity, hardness, widths, atoms_hbm, edge, counted, atoms, table, others,
    counts, raw_offsets, raw_negativity, raw_hardness, raw_widths, sems,
):
    copies = [
        pltpu.make_async_copy(source, target, sems.at[index])
        for index, (source, target) in enumerate(
            [
                (counts_hbm, counts),
                (offsets, raw_offsets),
                (negativity, raw_negativity),
                (hardness, raw_hardness),
                (widths, raw_widths),
                (atoms_hbm, atoms),
            ]
        )
    ]
    for copy in copies:
        copy.start()
    for copy in copies:
        copy.wait()
    for chunk in range(table.shape[0]):
        here = slice(chunk * LANES, (chunk + 1) * LANES)
        for first in (0, 4):
            table[chunk, first : first + 3, :] = raw_offsets[:, here]
            table[chunk, first + 3 : first + 4, :] = raw_widths[chunk : chunk + 1, :]
        for first in (0, 2, 4, 6):
            others[chunk, first : first + 1, :] = raw_negativity[chunk : chunk + 1, :]
            others[chunk, first + 1 : first + 2, :] = raw_hardness[chunk : chunk + 1, :]
    for cell in range(CELLS):
        counted[cell : cell + 1, :] = jnp.full((1, LANES), counts[cell])
    gather_cells(counted, atoms, table, others, edge)


def prepare_rest_kernel(counted, atoms, table, others, inner):
    gather_cells(counted, atoms, table, others, inner)


def prepare(counts, offsets, negativity, hardness, widths, atoms):
    chunks = offsets.shape[1] // LANES
    plane = (chunks, LANES)
    tables = jax.ShapeDtypeStruct((chunks, 8, LANES), jnp.float32)
    lists = jax.ShapeDtypeStruct(atoms.shape, jnp.int32)
    edge, *rest = pl.pallas_call(
        prepare_kernel,
        out_shape=(
            jax.ShapeDtypeStruct((EDGES, 8, LANES), jnp.float32),
            lists,
            lists,
            tables,
            tables,
        ),
        in_specs=[pl.BlockSpec(memory_space=pltpu.HBM)] * 6,
        out_specs=(pl.BlockSpec(memory_space=VMEM),) * 5,
        scratch_shapes=[
            SMEM(counts.shape, jnp.int32),
            VMEM(offsets.shape, jnp.float32),
            VMEM(plane, jnp.float32),
            VMEM(plane, jnp.float32),
            VMEM(plane, jnp.float32),
            pltpu.SemaphoreType.DMA((6,)),
        ],
        compiler_params=params(8),
    )(
        *[
            pltpu.with_memory_space_constraint(array, pltpu.HBM)
            for array in (
                counts,
                offsets,
                negativity.reshape(plane),
                hardness.reshape(plane),
                widths.reshape(plane),
                atoms,
            )
        ]
    )
    inner = pl.pallas_call(
        prepare_rest_kernel,
        out_shape=jax.ShapeDtypeStruct((INNER, 8, LANES), jnp.float32),
        in_specs=[pl.BlockSpec(memory_space=VMEM)] * 4,
        out_specs=pl.BlockSpec(memory_space=VMEM),
        compiler_params=params(8),
        cost_estimate=pl.CostEstimate(flops=2**20, bytes_accessed=2**22, transcendentals=0),
    )(*rest)
    return edge, inner


def pack_column(
    info, cells, source, packed, spills, target, at, shift, layers=range(CZ), info_source=None
):
    lane = lane_index((8, LANES))
    row = row_index((8, LANES))
    for z in layers:
        base = source * EZ + z
        known = base if info_source is None else info_source * EZ + z
        low, mid, top = [spread(info[known + k, 7:8, :]).astype(jnp.int32) for k in range(3)]
        end = low + mid - LANES
        tiles = [cells[base + k] for k in range(3)]
        if shift is not None:
            for k in range(3):
                offset = jnp.where(row == 2, (k - 1) * SIDE, 0.0)
                for axis in range(2):
                    offset = jnp.where(row == axis, shift[axis] * SIDE, offset)
                tiles[k] = tiles[k] + offset
        second = jnp.take_along_axis(tiles[1], (lane - low) & 127, axis=1)
        third = jnp.take_along_axis(tiles[2], (lane - end) & 127, axis=1)
        packed[target * CZ + z, 0] = jnp.where(lane < low, tiles[0], second)
        packed[target * CZ + z, 1] = jnp.where(lane < end, second, third)
        spill = jnp.where(lane < end + top - LANES, third, 0.0)
        spills[target * CZ + z] = pltpu.roll(spill, at, 1) if at else spill


def pack_core(info, cells, packed, spills, build):
    for q in range(QUADS):
        pack_column(info, cells, q, packed, spills, q, 8 * q, (0, 0) if build else None)


def pack_faces(infos, pieces, packed, spills, build):
    for side in range(2):
        sign = 2 * side - 1
        for y in range(CY):
            shift = (sign * CX, 0) if build else None
            at = 32 + 8 * y
            pack_column(infos[side], pieces[side], y, packed, spills, 2 * side + y, at, shift)
        for x in range(CX):
            shift = (0, sign * CY) if build else None
            source = 2 * x + 1 - side
            target = 4 + 2 * x + side
            at = 48 + 8 * x
            pack_column(infos[2], pieces[2], source, packed, spills, target, at, shift)


def pack_corners(info, cells, packed, spills, build, layers):
    for side_x in range(2):
        for side_y in range(2):
            shift = ((2 * side_x - 1) * CX, (2 * side_y - 1) * CY) if build else None
            source = 2 * side_x + 1 - side_y
            target = 2 * side_x + side_y
            pack_column(info, cells, source, packed, spills, target, 64, shift, layers)


def pack_upper_faces(infos, pieces, packed, spills):
    for y in range(CY):
        pack_column(infos[0], pieces[0], y, packed, spills, 2 + y, 32 + 8 * y, None)
    for x in range(CX):
        pack_column(infos[1], pieces[1], 2 * x, packed, spills, 5 + 2 * x, 48 + 8 * x, None)


def pack_upper_corners(info, cells, packed, spills):
    for side_y in range(2):
        source = 1 - side_y
        pack_column(info, cells, source, packed, spills, 2 + side_y, 64, None, info_source=2 + source)


def upper_columns(q):
    columns = face_columns(q)
    return [columns[2 * k : 2 * k + 2] for k in range(2) if (q >> (1 - k)) & 1], 4 * (q == 1)


def core_columns(q):
    return [q ^ k for k in range(4)]


def face_columns(q):
    x, y = q >> 1, q & 1
    return [2 * x, 2 * x + 1, 4 + y, 6 + y]


def overflow_of(spills, columns, z):
    return sum(spills[column * CZ + z] for column in columns)


def spread(row):
    return jnp.broadcast_to(row, (8, LANES))


def couple(x_i, y_i, z_i, w_i, x_j, y_j, z_j, w_j):
    delta_x = x_j - x_i
    delta_y = y_j - y_i
    delta_z = z_j - z_i
    squared = delta_x * delta_x + delta_y * delta_y + delta_z * delta_z
    held = jnp.maximum(squared, CLOSEST_SQUARED)
    inverse = lax.rsqrt(held)
    distance = held * inverse
    scaled = distance * lax.rsqrt(w_i + w_j)
    value = (lax.erf(scaled) - lax.erf(distance)) * inverse
    return jnp.where(squared < CUT_SQUARED, value, 0.0)


def to_rows(sums, block):
    here = lane_index((8, LANES)) - row_index((8, LANES)) == 8 * block
    return jnp.where(here, jnp.sum(sums, axis=1, keepdims=True), 0.0)


def add_rows(cell, sums, rows):
    for index in range(2):
        total = jnp.zeros((8, LANES), jnp.float32)
        for block in range(BLOCKS):
            total = total + to_rows(sums[cell, block, index], block)
        rows.append(jnp.sum(total, axis=0, keepdims=True))


def finish_cell(slot, place, target, info, sums, out):
    q, z = place(slot)
    rows = []
    add_rows(slot, sums, rows)
    own = info.at[q * EZ + z + 1]
    scale = PAIR_SCALE / own[6:7, :]
    live = lane_index((1, LANES)) < own[7:8, :].astype(jnp.int32)
    out[target, 0:1, :] = jnp.where(live, rows[0] * scale, 0.0)
    out[target, 1:2, :] = jnp.where(live, rows[1] * scale, 0.0)


def build_cell(cell, slot, lines, turned, kernels, before, sums, below):
    own = None
    if below is not None:
        own = lane_index((8, LANES)) - row_index((8, LANES)) - below
    for group in GROUPS:
        sums_s, sums_t = start_sums(cell, before, group)
        for index, line in enumerate(lines):
            beside = [line(k) for k in range(6)]
            for at, block in enumerate(group):
                value = couple(*[turned[cell, block, k] for k in range(4)], *beside[:4])
                if own is not None and index < 2:
                    value = jnp.where(own == 8 * block - LANES * index, 0.0, value)
                kernels[slot, block, index] = value
                sums_s[at] = sums_s[at] + value * beside[4]
                sums_t[at] = sums_t[at] + value * beside[5]
        for at, block in enumerate(group):
            sums[slot, block, 0] = sums_s[at]
            sums[slot, block, 1] = sums_t[at]


def start_sums(cell, before, blocks):
    if before is None:
        zeros = [jnp.zeros((8, LANES), jnp.float32) for _ in blocks]
        return zeros, list(zeros)
    sums_s = [before[cell, block, 0] for block in blocks]
    return sums_s, [before[cell, block, 1] for block in blocks]


def lines_of(packed, columns, z):
    def line(column, half):
        return lambda k: spread(packed[column * CZ + z, half, k : k + 1, :])

    return [line(column, half) for column in columns for half in range(2)]


def rest_line(rest, cell):
    return lambda k: spread(rest[cell, k : k + 1, :])


def parts_of(value):
    high = value.astype(jnp.bfloat16).astype(jnp.float32)
    rest = value - high
    middle = rest.astype(jnp.bfloat16).astype(jnp.float32)
    return high, middle, rest - middle


def turn_cells(core, turned):
    chosen = row_index((24, 4 * LANES)) & 7
    ones = jnp.where(chosen == lane_index((24, 4 * LANES)) >> 7, 1.0, 0.0).astype(jnp.bfloat16)
    for cell in range(CELLS):
        here = core[(cell // CZ) * EZ + cell % CZ + 1]
        left = jnp.concatenate(parts_of(here), axis=0).T[: 8 * BLOCKS + 8].astype(jnp.bfloat16)
        wide = lax.dot_general(
            left, ones, (((1,), (0,)), ((), ())), preferred_element_type=jnp.float32
        )
        for block in range(BLOCKS):
            for k in range(4):
                turned[cell, block, k] = wide[8 * block : 8 * block + 8, k * LANES : (k + 1) * LANES]


def core_spills(spills, spill):
    for z in range(CZ):
        spill[z] = overflow_of(spills, range(QUADS), z)


def face_spills(spills, before, spill):
    for cell in range(CELLS):
        q, z = cell // CZ, cell % CZ
        spill[cell] = before[z] + overflow_of(spills, face_columns(q), z)


def corner_loop(start, stop, work, finish, sums):
    def one_cell(slot, _):
        finish(jnp.maximum(slot - 1, start))
        work(slot)
        return 0

    sums[start] = jnp.zeros(sums.shape[1:], jnp.float32)
    lax.fori_loop(start, stop, one_cell, 0, unroll=4)
    finish(stop - 1)


def corner_spills(spills, before, rest, place):
    for slot in range(rest.shape[0]):
        q, z = place(slot)
        rest[slot] = before[q * CZ + z] + spills[q * CZ + z]


def core_kernel(core, kernels, sums, spill, turned, packed, spills):
    turn_cells(core, turned)
    pack_core(core, core, packed, spills, True)
    core_spills(spills, spill)

    def one_cell(cell, _):
        q, z = cell // CZ, cell % CZ
        below = spread(core[q * EZ + z, 7:8, :]).astype(jnp.int32)
        lines = lines_of(packed, core_columns(q), z)
        build_cell(cell, cell, lines, turned, kernels, None, sums, below)
        return 0

    lax.fori_loop(0, CELLS, one_cell, 0, unroll=2)


def face_kernel(
    x_low, x_high, beyond, turned, before, spill_before, kernels, sums, spill, packed, spills
):
    pieces = [x_low, x_high, beyond]
    pack_faces(pieces, pieces, packed, spills, True)
    face_spills(spills, spill_before, spill)

    def one_cell(cell, _):
        lines = lines_of(packed, face_columns(cell // CZ), cell % CZ)
        build_cell(cell, cell, lines, turned, kernels, before, sums, None)
        return 0

    lax.fori_loop(0, CELLS, one_cell, 0, unroll=2)


def corner_kernel(
    corners, turned, before, spill_before, core, kernels, out, packed, spills, rest, sums
):
    slots = kernels.shape[0]
    place = PLACES[slots]
    pack_corners(corners, corners, packed, spills, True, LAYERS[slots])
    corner_spills(spills, spill_before, rest, place)

    def work(slot):
        q, z = place(slot)
        lines = lines_of(packed, [q], z) + [rest_line(rest, slot)]
        build_cell(q * CZ + z, slot, lines, turned, kernels, before, sums, None)

    def finish(slot):
        finish_cell(slot, place, slot, core, sums, out)

    corner_loop(0, slots, work, finish, sums)


IN_VMEM = pl.BlockSpec(memory_space=VMEM)
IN_SMEM = pl.BlockSpec(memory_space=SMEM)
PAIR = jax.ShapeDtypeStruct((CELLS, 2, LANES), jnp.float32)
SPILL = jax.ShapeDtypeStruct((CELLS, 8, LANES), jnp.float32)
SUMS = jax.ShapeDtypeStruct((CELLS, BLOCKS, 2, 8, LANES), jnp.float32)
TURNED = jax.ShapeDtypeStruct((CELLS, BLOCKS, 4, 8, LANES), jnp.float32)
CORE_SPILL = jax.ShapeDtypeStruct((CZ, 8, LANES), jnp.float32)
CORE_TILES, FACE_TILES, CORNER_TILES = 8, 8, 3


def held(tiles, cells=CELLS):
    return VMEM((cells, BLOCKS, tiles, 8, LANES), jnp.float32)


def pairs(cells):
    return jax.ShapeDtypeStruct((cells, 2, LANES), jnp.float32)


def call(kernel, outs, scratch, tiles, *arrays):
    work = CELLS * BLOCKS * tiles * 8 * LANES
    return pl.pallas_call(
        kernel,
        out_shape=outs,
        in_specs=[IN_SMEM if array.ndim == 1 else IN_VMEM for array in arrays],
        out_specs=jax.tree.map(lambda _: IN_VMEM, outs),
        scratch_shapes=scratch,
        compiler_params=params(8),
        cost_estimate=pl.CostEstimate(
            flops=30 * work, bytes_accessed=8 * work, transcendentals=4 * work
        ),
    )(*arrays)


def packs(columns):
    return [
        VMEM((columns * CZ, 2, 8, LANES), jnp.float32),
        VMEM((columns * CZ, 8, LANES), jnp.float32),
    ]


def build_core(core):
    outs = (held(CORE_TILES), SUMS, CORE_SPILL, TURNED)
    return call(core_kernel, outs, packs(4), CORE_TILES, core)


def build_faces(pieces, turned, before, spill):
    outs = (held(FACE_TILES), SUMS, SPILL)
    return call(face_kernel, outs, packs(8), FACE_TILES, *pieces, turned, before, spill)


def corner_scratch(cells):
    rest = VMEM((cells, 8, LANES), jnp.float32)
    return packs(4) + [rest, VMEM((cells, BLOCKS, 2, 8, LANES), jnp.float32)]


def build_corners(cells, corners, turned, before, spill, core):
    outs = (held(CORNER_TILES, cells), pairs(cells))
    arrays = [corners, turned, before, spill, core]
    return call(corner_kernel, outs, corner_scratch(cells), CORNER_TILES, *arrays)


def apply_cell(cell, slot, lines, stored, before, sums, first=0):
    sums_s, sums_t = start_sums(cell, before, range(BLOCKS))
    for index, line in enumerate(lines):
        line_s, line_t = line(0), line(1)
        for block in range(BLOCKS):
            value = stored[slot, block, first + index]
            sums_s[block] = sums_s[block] + value * line_s
            sums_t[block] = sums_t[block] + value * line_t
    for block in range(BLOCKS):
        sums[slot, block, 0] = sums_s[block]
        sums[slot, block, 1] = sums_t[block]


def widen(pieces, wides, scale=None):
    for piece, wide in zip(pieces, wides):
        wide[:, 0:2, :] = piece[...] if scale is None else scale * piece[...]


def apply_core_kernel(info, core, stored, sums, spill, wide, packed, spills):
    widen([core], [wide])
    pack_core(info, wide, packed, spills, False)
    core_spills(spills, spill)

    def one_cell(cell, _):
        lines = lines_of(packed, core_columns(cell // CZ), cell % CZ)
        apply_cell(cell, cell, lines, stored, None, sums)
        return 0

    lax.fori_loop(0, CELLS, one_cell, 0, unroll=4)


def apply_face_kernel(*refs):
    infos, pieces, (stored, before, spill_before, sums, spill), wides, (packed, spills) = split(
        refs, 3, 3, 5, 3, 2
    )
    widen(pieces, wides)
    pack_faces(infos, wides, packed, spills, False)
    face_spills(spills, spill_before, spill)

    def one_cell(cell, _):
        lines = lines_of(packed, face_columns(cell // CZ), cell % CZ)
        apply_cell(cell, cell, lines, stored, before, sums)
        return 0

    lax.fori_loop(0, CELLS, one_cell, 0, unroll=4)


def apply_corner_cells(stored, before, spill_before, core, out, packed, spills, rest, sums):
    slots = stored.shape[0]
    place = PLACES[slots]
    corner_spills(spills, spill_before, rest, place)

    def work(slot):
        q, z = place(slot)
        lines = lines_of(packed, [q], z) + [rest_line(rest, slot)]
        apply_cell(q * CZ + z, slot, lines, stored, before, sums)

    def finish(slot):
        finish_cell(slot, place, slot, core, sums, out)

    corner_loop(0, slots, work, finish, sums)


def upper_corner_cells(stored, before, spill_before, core, out, packed, spills, rest, sums):
    slots = stored.shape[0]
    place = PLACES[slots]
    for slot in range(slots):
        q, z = place(slot)
        tile = spill_before[q * CZ + z]
        rest[slot] = tile + spills[q * CZ + z] if q >= CY else tile

    def low(slot):
        q, z = place(slot)
        apply_cell(q * CZ + z, slot, [rest_line(rest, slot)], stored, before, sums, first=2)

    def high(slot):
        q, z = place(slot)
        lines = lines_of(packed, [q], z) + [rest_line(rest, slot)]
        apply_cell(q * CZ + z, slot, lines, stored, before, sums)

    def finish(slot):
        q, z = place(slot)
        finish_cell(slot, place, q * CZ + z, core, sums, out)

    corner_loop(0, slots // 2, low, finish, sums)
    corner_loop(slots // 2, slots, high, finish, sums)


def upper_face_kernel(
    info_high, info_beyond, high, beyond, stored, before, spill_before, sums, spill,
    wide_high, wide_beyond, packed, spills,
):
    wides = [wide_high, wide_beyond]
    widen([high, beyond], wides, 2.0)
    pack_upper_faces([info_high, info_beyond], wides, packed, spills)
    for cell in range(CELLS):
        q, z = cell // CZ, cell % CZ
        groups, _ = upper_columns(q)
        spill[cell] = sum([spills[c * CZ + z] for group in groups for c in group], spill_before[z])
    sums[0:CZ] = before[0:CZ]
    for q in range(1, QUADS):
        groups, first = upper_columns(q)
        columns = [column for group in groups for column in group]

        def one_cell(z, _, q=q, columns=columns, first=first):
            cell = q * CZ + z
            apply_cell(cell, cell, lines_of(packed, columns, z), stored, before, sums, first)
            return 0

        lax.fori_loop(0, CZ, one_cell, 0, unroll=4)


def apply_corner_kernel(
    info, corners, stored, before, spill_before, core, out, wide, packed, spills, rest, sums
):
    widen([corners], [wide])
    pack_corners(info, wide, packed, spills, False, LAYERS[stored.shape[0]])
    apply_corner_cells(
        stored, before, spill_before, core, out, packed, spills, rest, sums
    )


def split(refs, *sizes):
    parts = []
    for size in sizes:
        parts.append(refs[:size])
        refs = refs[size:]
    return parts


def apply_last_kernel(
    info, corners, edge, inner, before, spill_before, core, slots, first, second,
    moments, third, wide, packed, spills, edge_rest, edge_sums, inner_rest, inner_sums,
):
    widen([corners], [wide], 2.0)
    pack_upper_corners(info, wide, packed, spills)
    for stored, rest, sums in ((edge, edge_rest, edge_sums), (inner, inner_rest, inner_sums)):
        upper_corner_cells(stored, before, spill_before, core, third, packed, spills, rest, sums)
    d = slots[:, 1 : 1 + CZ, 6:7, :].reshape(CELLS, 1, LANES)
    v_0 = slots[:, 1 : 1 + CZ, 4:6, :].reshape(CELLS, 2, LANES)
    v_1 = first[:, 1 : 1 + CZ].reshape(v_0.shape)
    v_2 = second[:, 1 : 1 + CZ].reshape(v_0.shape)
    d_0 = d * v_0
    d_2 = d * v_2
    parts = [d_0 * v_0, d_0 * v_1, d * v_1 * v_1, d_2 * v_1, d_2 * v_2, d_2 * third[...]]
    row = row_index((2, LANES))
    line = jnp.zeros((2, LANES), jnp.float32)
    for index, part in enumerate(parts + [v_0, v_1, v_2]):
        total = jnp.sum(jnp.sum(part, axis=0), axis=1, keepdims=True)
        line = jnp.where(lane_index((2, LANES)) - row == 2 * index, total, line)
    moments[...] = jnp.sum(line, axis=0, keepdims=True)


def wide(piece):
    return VMEM((piece.shape[0], 8, LANES), jnp.float32)


def apply_core(info, core, stored):
    stored = pltpu.with_memory_space_constraint(stored, VMEM)
    scratch = [wide(core)] + packs(4)
    return call(apply_core_kernel, (SUMS, CORE_SPILL), scratch, 2, info, core, stored)


def apply_faces(infos, pieces, stored, before, spill):
    stored = pltpu.with_memory_space_constraint(stored, VMEM)
    scratch = [wide(piece) for piece in pieces] + packs(8)
    return call(
        apply_face_kernel, (SUMS, SPILL), scratch, 2, *infos, *pieces, stored, before, spill
    )


def apply_upper_faces(infos, pieces, stored, before, spill):
    stored = pltpu.with_memory_space_constraint(stored, VMEM)
    scratch = [wide(piece) for piece in pieces] + packs(8)
    return call(
        upper_face_kernel, (SUMS, SPILL), scratch, 2, *infos, *pieces, stored, before, spill
    )


def apply_corners(info, corners, stored, before, spill, core):
    stored = pltpu.with_memory_space_constraint(stored, VMEM)
    cells = stored.shape[0]
    arrays = [info, corners, stored, before, spill, core]
    scratch = [wide(corners)] + corner_scratch(cells)
    return call(apply_corner_kernel, pairs(cells), scratch, 2, *arrays)


def apply_last(info, corners, edge, inner, before, spill, core, slots, first, second):
    edge = pltpu.with_memory_space_constraint(edge, VMEM)
    inner = pltpu.with_memory_space_constraint(inner, VMEM)
    arrays = [info, corners, edge, inner, before, spill, core, slots, first, second]
    scratch = [VMEM((CELLS, 2, LANES), jnp.float32), wide(corners)] + corner_scratch(EDGES)
    scratch += corner_scratch(INNER)[2:]
    out = jax.ShapeDtypeStruct((1, LANES), jnp.float32)
    return call(apply_last_kernel, out, scratch, 2, *arrays)


def solve(g):
    tiny = 1e-6
    h = [g[k] + g[k + 1] for k in range(5)]
    ratio_1 = h[1] / h[0]
    ratio_2 = h[2] / h[0]
    pivot_1 = h[2] - ratio_1 * h[1]
    mixed = h[3] - ratio_1 * h[2]
    rest_1 = g[1] - ratio_1 * g[0]
    live_1 = pivot_1 > tiny * h[2]
    safe_1 = jnp.where(live_1, pivot_1, 1.0)
    ratio_3 = jnp.where(live_1, mixed / safe_1, 0.0)
    pivot_2 = h[4] - ratio_2 * h[2] - ratio_3 * mixed
    rest_2 = g[2] - ratio_2 * g[0] - ratio_3 * rest_1
    live_2 = live_1 & (pivot_2 > tiny * h[4])
    c_2 = jnp.where(live_2, rest_2 / jnp.where(live_2, pivot_2, 1.0), 0.0)
    c_1 = jnp.where(live_1, (rest_1 - mixed * c_2) / safe_1, 0.0)
    c_0 = (g[0] - h[1] * c_1 - h[2] * c_2) / h[0]
    return c_0, c_1, c_2


def invert(counts, atoms, places):
    rows = places.shape[1]
    row_low = row_index((LANES, LANES))
    row_high = row_index((rows, LANES))
    lane = lane_index((rows, LANES))

    def one_cell(cell, total):
        live = lane_index((1, LANES)) < counts[cell]
        pointer = jnp.where(live, atoms[pl.ds(cell, 1), :], -1)
        here = (pointer >> 7) == row_high
        cells = jnp.where(here, cell, 0).astype(jnp.float32)
        slots = jnp.where(here, lane, 0).astype(jnp.float32)
        parts = jnp.concatenate([cells, slots], axis=0).astype(jnp.bfloat16)
        lows = jnp.where((pointer & 127) == row_low, 1.0, 0.0).astype(jnp.bfloat16)
        return total + lax.dot_general(
            parts, lows, (((1,), (1,)), ((), ())), preferred_element_type=jnp.float32
        )

    total = jnp.zeros((2 * rows, LANES), jnp.float32)
    total = lax.fori_loop(0, CELLS, one_cell, total, unroll=8).astype(jnp.int32)
    places[0] = total[:rows]
    places[1] = total[rows:]


def inverted(counts, atoms, atoms_local):
    rows = (atoms_local // LANES + 15) // 16 * 16
    return call(invert, jax.ShapeDtypeStruct((2, rows, LANES), jnp.int32), [], 2, counts, atoms)


def finish_kernel(moments, slots, first, second, places, out, charges):
    summed = moments[...]
    lane = lane_index((2, LANES))
    row = row_index((2, LANES))

    def pair(index):
        picked = jnp.where(lane - row == 2 * index, summed, 0.0)
        return jnp.broadcast_to(jnp.sum(picked, axis=1, keepdims=True), (2, LANES))

    rows = [pair(index) for index in range(9)]
    c_0, c_1, c_2 = solve(rows[:6])
    totals = c_0 * rows[6] + c_1 * rows[7] + c_2 * rows[8]
    balance = totals[0:1] / totals[1:2]
    sign = jnp.concatenate([jnp.ones((1, LANES), jnp.float32), -balance], axis=0)
    c_0, c_1, c_2 = c_0 * sign, c_1 * sign, c_2 * sign
    for cell in range(CELLS):
        q, z = cell // CZ, cell % CZ + 1
        mixed = c_0 * slots[q, z, 4:6, :] + c_1 * first[q, z] + c_2 * second[q, z]
        charges[cell : cell + 1, :] = jnp.sum(mixed, axis=0, keepdims=True)
    tiles = [jnp.zeros((8, LANES), jnp.float32) for _ in range(places.shape[1] // 8)]
    for cell in range(CELLS):
        line = spread(charges[cell : cell + 1, :])
        for at in range(len(tiles)):
            here = slice(8 * at, 8 * at + 8)
            moved = jnp.take_along_axis(line, places[1, here, :], axis=1)
            tiles[at] = jnp.where(places[0, here, :] == cell, moved, tiles[at])
    out[...] = jnp.concatenate(tiles, axis=0)[: out.shape[0]]


def finish(moments, slots, first, second, places, atoms_local):
    return pl.pallas_call(
        finish_kernel,
        out_shape=jax.ShapeDtypeStruct((atoms_local // LANES, LANES), jnp.float32),
        in_specs=[IN_VMEM] * 5,
        out_specs=IN_VMEM,
        scratch_shapes=[VMEM((CELLS, LANES), jnp.float32)],
        compiler_params=params(8),
    )(moments, slots, first, second, places)


def partner(block, axis, mask):
    count = lax.axis_size(axis)
    return lax.ppermute(block, axis, [(low, low ^ mask) for low in range(count)])


def shifted(block, along_x, across_y=0):
    count = lax.axis_size("gx")
    route = [(i, ((i + 4 * along_x) % count) ^ (2 * across_y)) for i in range(count)]
    return lax.ppermute(block, "gx", route)


def with_z_faces(edge, inner):
    other = partner(edge, "gx", 1)
    parts = [other[:, 0:1], edge[:, 1:2], inner, edge[:, 0:1], other[:, 1:2]]
    return jnp.concatenate(parts, axis=1)


def flat(columns):
    return columns.reshape((-1,) + columns.shape[-2:])


def x_faces(core):
    count = lax.axis_size("gx")
    rows = count // 4
    odd = (lax.axis_index("gx") // 4) % 2 == 1
    if rows % 2:
        return shifted(core[2:], 1), shifted(core[:2], -1)
    route = [(i, (i + (4 if (i // 4) % 2 else -4)) % count) for i in range(count)]
    second = lax.ppermute(jnp.where(odd, core[2:], core[:2]), "gx", route)
    first = lax.ppermute(jnp.where(odd, core[:2], core[2:]), "gx", [(i, i ^ 4) for i in range(count)])
    return first, second


def sorted_faces(first, second):
    odd = (lax.axis_index("gx") // 4) % 2 == 1
    if (lax.axis_size("gx") // 4) % 2:
        return first, second
    return jnp.where(odd, first, second), jnp.where(odd, second, first)


def exchange(edge, inner, on_core, on_faces, on_corners):
    core = with_z_faces(edge, inner)
    first, second = x_faces(core)
    beyond = partner(core, "gx", 2)
    sums, spill, *more = on_core(flat(core))
    second, first, sums = lax.optimization_barrier((second, first, sums))
    low, high = sorted_faces(first, second)
    corners = partner(jnp.concatenate([low, high], axis=0), "gx", 2)
    pieces = [flat(part) for part in (low, high, beyond)]
    sums, spill, *more = on_faces(pieces, sums, spill, *more)
    corners = flat(corners)
    return core, pieces, corners, on_corners(corners, sums, spill, core, *more)


def global_sum(values):
    count = lax.axis_size("gx")
    if count & (count - 1):
        return lax.psum(values, "gx")
    step = 1
    while step < count:
        if step >= 2 and 4 * step <= count:
            others = [partner(values, "gx", k * step) for k in (3, 2, 1)]
            values = (values + others[0]) + (others[1] + others[2])
            step *= 4
        else:
            values = values + partner(values, "gx", step)
            step *= 2
    return values


def local(cell_offsets, electronegativity, hardness, charge_widths, cell_counts, cell_atoms):
    edge, inner = prepare(
        cell_counts, cell_offsets, electronegativity, hardness, charge_widths, cell_atoms
    )
    stored = []

    def keep(tiles, *others):
        stored.append(tiles)
        return others

    def build_ends(corners, sums, spill, core, *own):
        (edge,) = keep(*build_corners(EDGES, corners, *own, sums, spill, flat(core)))
        (inner,) = keep(*build_corners(INNER, corners, *own, sums, spill, flat(core)))
        return by_column(edge), by_column(inner)

    def by_column(cells):
        return cells.reshape((QUADS, -1) + cells.shape[1:])

    slots, pieces, corners, ends = exchange(
        by_column(edge),
        by_column(inner),
        lambda core: keep(*build_core(core)),
        lambda faces, sums, spill, *own: keep(*build_faces(faces, *own, sums, spill)) + own,
        build_ends,
    )
    info = flat(slots)

    def apply(edge, inner, on_corners):
        return exchange(
            edge,
            inner,
            lambda own: apply_core(info, own, stored[0]),
            lambda faces, sums, spill: apply_faces(pieces, faces, stored[1], sums, spill),
            on_corners,
        )

    def apply_ends(others, sums, spill, _):
        edge = apply_corners(corners, others, stored[2], sums, spill, info)
        inner = apply_corners(corners, others, stored[3], sums, spill, info)
        return by_column(edge), by_column(inner)

    first, _, _, ends = apply(*ends, apply_ends)
    second = with_z_faces(*ends)
    high = shifted(second[:2], -1)
    beyond = partner(second, "gx", 2)
    corner = shifted(second[:2], -1, 1)
    sums, spill = apply_core(info, flat(second), stored[0])
    high, beyond, sums = lax.optimization_barrier((high, beyond, sums))
    upper = [flat(high), flat(beyond)]
    sums, spill = apply_upper_faces(pieces[1:], upper, stored[1], sums, spill)
    corner, sums = lax.optimization_barrier((corner, sums))
    moments = apply_last(
        corners, flat(corner), stored[2], stored[3], sums, spill, info, slots, first, second
    )
    moments, cell_counts, cell_atoms = lax.optimization_barrier((moments, cell_counts, cell_atoms))
    atoms_local = cell_offsets.shape[1]
    places = inverted(cell_counts, cell_atoms, atoms_local)
    charges = finish(global_sum(moments), slots, first, second, places, atoms_local)
    return charges.reshape(-1)


def solution(mesh):
    placed = (
        P(None, ("grp", "gx")),
        P(("grp", "gx")),
        P(("grp", "gx")),
        P(("grp", "gx")),
        P(("grp", "gx")),
        P(("grp", "gx"), None),
    )
    return jax.shard_map(
        local, mesh=mesh, in_specs=placed, out_specs=P(("grp", "gx")), check_vma=False
    )
```

```python
import functools
import math

import jax
import jax.numpy as jnp
from jax import lax
from jax.experimental import pallas as pl
from jax.experimental.pallas import tpu as pltpu
from jax.sharding import PartitionSpec as P

CX = 2
CY = 2
CZ = 8
EZ = CZ + 2
CELLS = CX * CY * CZ
QUADS = CX * CY
LANES = 128
BLOCKS = 11
GROUPS = ((0, 1, 2, 3), (4, 5, 6, 7), (8, 9, 10))

COULOMB = 14.399645
ROOT_PI = math.sqrt(math.pi)
SCREEN = 1.0 / (math.sqrt(2.0) * 3.0)
EWALD_SELF = math.sqrt(2.0 / math.pi) / 3.0
SIDE = 12.0 * SCREEN
CUT_SQUARED = (12.0 * SCREEN) ** 2
CLOSEST_SQUARED = (0.5 * SCREEN) ** 2
PAIR_SCALE = COULOMB * SCREEN

VMEM = pltpu.VMEM
SMEM = pltpu.SMEM


def params(mib):
    return pltpu.CompilerParams(vmem_limit_bytes=mib * 2**20)


def lane_index(shape):
    return lax.broadcasted_iota(jnp.int32, shape, len(shape) - 1)


def row_index(shape):
    return lax.broadcasted_iota(jnp.int32, shape, len(shape) - 2)


def edge_place(slot):
    return slot // 2, (CZ - 1) * (1 - slot % 2)


def inner_place(slot):
    return slot // (CZ - 2), 1 + slot % (CZ - 2)


EDGES = 2 * QUADS
INNER = CELLS - EDGES
PLACES = {EDGES: edge_place, INNER: inner_place}
LAYERS = {EDGES: (0, CZ - 1), INNER: range(1, CZ - 1)}


def gather_cells(counted, atoms, table, others, out):
    place = PLACES[out.shape[0]]
    row = row_index((8, LANES))
    lane = lane_index((1, LANES))

    def pick(source, pointers):
        share = 8 // len(pointers)
        pointer = spread(pointers[-1])
        for k in range(len(pointers) - 2, -1, -1):
            pointer = jnp.where(row < share * (k + 1), pointers[k], pointer)
        high = pointer >> 7
        low = pointer & 127
        picked = jnp.zeros((8, LANES), jnp.float32)
        for chunk in range(source.shape[0]):
            part = jnp.take_along_axis(source[chunk], low, axis=1)
            picked = jnp.where(high == chunk, part, picked)
        return picked

    def four_cells(step, _):
        slots = [4 * step + k for k in range(4)]
        places = [place(slot) for slot in slots]
        counts = [counted[pl.ds(q * CZ + z, 1), :] for q, z in places]
        occupied = [lane < count for count in counts]
        pointers = [
            jnp.where(live, atoms[pl.ds(q * CZ + z, 1), :], 0)
            for (q, z), live in zip(places, occupied)
        ]
        pairs = [pick(table, pointers[:2]), pick(table, pointers[2:])]
        both = pick(others, pointers)
        for k, (slot, live) in enumerate(zip(slots, occupied)):
            q = places[k][0]
            at = 4 * (k % 2)
            picked = pairs[k // 2][at : at + 4]
            width = jnp.where(live, picked[3:4], 1.0)
            hard = both[2 * k + 1 : 2 * k + 2]
            diag = jnp.where(live, hard + COULOMB * (1.0 / (width * ROOT_PI) - EWALD_SELF), 1.0)
            negative = jnp.where(live, both[2 * k : 2 * k + 1], 0.0)
            out[slot, 0:1, :] = (picked[0:1] + (q // CY).astype(jnp.float32)) * SIDE
            out[slot, 1:2, :] = (picked[1:2] + (q % CY).astype(jnp.float32)) * SIDE
            out[slot, 2:3, :] = picked[2:3] * SIDE
            out[slot, 3:4, :] = (2.0 * SCREEN * SCREEN) * width * width
            out[slot, 4:5, :] = -negative / diag
            out[slot, 5:6, :] = jnp.where(live, 1.0 / diag, 0.0)
            out[slot, 6:7, :] = diag
            out[slot, 7:8, :] = counts[k].astype(jnp.float32)
        return 0

    lax.fori_loop(0, out.shape[0] // 4, four_cells, 0, unroll=2)


def prepare_kernel(
    counts_hbm, offsets, negativity, hardness, widths, atoms_hbm, edge, counted, atoms, table, others,
    counts, raw_offsets, raw_negativity, raw_hardness, raw_widths, sems,
):
    copies = [
        pltpu.make_async_copy(source, target, sems.at[index])
        for index, (source, target) in enumerate(
            [
                (counts_hbm, counts),
                (offsets, raw_offsets),
                (negativity, raw_negativity),
                (hardness, raw_hardness),
                (widths, raw_widths),
                (atoms_hbm, atoms),
            ]
        )
    ]
    for copy in copies:
        copy.start()
    for copy in copies:
        copy.wait()
    for chunk in range(table.shape[0]):
        here = slice(chunk * LANES, (chunk + 1) * LANES)
        for first in (0, 4):
            table[chunk, first : first + 3, :] = raw_offsets[:, here]
            table[chunk, first + 3 : first + 4, :] = raw_widths[chunk : chunk + 1, :]
        for first in (0, 2, 4, 6):
            others[chunk, first : first + 1, :] = raw_negativity[chunk : chunk + 1, :]
            others[chunk, first + 1 : first + 2, :] = raw_hardness[chunk : chunk + 1, :]
    for cell in range(CELLS):
        counted[cell : cell + 1, :] = jnp.full((1, LANES), counts[cell])
    gather_cells(counted, atoms, table, others, edge)


def prepare_rest_kernel(counted, atoms, table, others, inner):
    gather_cells(counted, atoms, table, others, inner)


def prepare(counts, offsets, negativity, hardness, widths, atoms):
    chunks = offsets.shape[1] // LANES
    plane = (chunks, LANES)
    tables = jax.ShapeDtypeStruct((chunks, 8, LANES), jnp.float32)
    lists = jax.ShapeDtypeStruct(atoms.shape, jnp.int32)
    edge, *rest = pl.pallas_call(
        prepare_kernel,
        out_shape=(
            jax.ShapeDtypeStruct((EDGES, 8, LANES), jnp.float32),
            lists,
            lists,
            tables,
            tables,
        ),
        in_specs=[pl.BlockSpec(memory_space=pltpu.HBM)] * 6,
        out_specs=(pl.BlockSpec(memory_space=VMEM),) * 5,
        scratch_shapes=[
            SMEM(counts.shape, jnp.int32),
            VMEM(offsets.shape, jnp.float32),
            VMEM(plane, jnp.float32),
            VMEM(plane, jnp.float32),
            VMEM(plane, jnp.float32),
            pltpu.SemaphoreType.DMA((6,)),
        ],
        compiler_params=params(8),
    )(
        *[
            pltpu.with_memory_space_constraint(array, pltpu.HBM)
            for array in (
                counts,
                offsets,
                negativity.reshape(plane),
                hardness.reshape(plane),
                widths.reshape(plane),
                atoms,
            )
        ]
    )
    inner = pl.pallas_call(
        prepare_rest_kernel,
        out_shape=jax.ShapeDtypeStruct((INNER, 8, LANES), jnp.float32),
        in_specs=[pl.BlockSpec(memory_space=VMEM)] * 4,
        out_specs=pl.BlockSpec(memory_space=VMEM),
        compiler_params=params(8),
        cost_estimate=pl.CostEstimate(flops=2**20, bytes_accessed=2**22, transcendentals=0),
    )(*rest)
    return edge, inner


def pack_column(
    info, cells, source, packed, spills, target, at, shift, layers=range(CZ), info_source=None
):
    lane = lane_index((8, LANES))
    row = row_index((8, LANES))
    for z in layers:
        base = source * EZ + z
        known = base if info_source is None else info_source * EZ + z
        low, mid, top = [spread(info[known + k, 7:8, :]).astype(jnp.int32) for k in range(3)]
        end = low + mid - LANES
        tiles = [cells[base + k] for k in range(3)]
        if shift is not None:
            for k in range(3):
                offset = jnp.where(row == 2, (k - 1) * SIDE, 0.0)
                for axis in range(2):
                    offset = jnp.where(row == axis, shift[axis] * SIDE, offset)
                tiles[k] = tiles[k] + offset
        second = jnp.take_along_axis(tiles[1], (lane - low) & 127, axis=1)
        third = jnp.take_along_axis(tiles[2], (lane - end) & 127, axis=1)
        packed[target * CZ + z, 0] = jnp.where(lane < low, tiles[0], second)
        packed[target * CZ + z, 1] = jnp.where(lane < end, second, third)
        spill = jnp.where(lane < end + top - LANES, third, 0.0)
        spills[target * CZ + z] = pltpu.roll(spill, at, 1) if at else spill


def pack_core(info, cells, packed, spills, build):
    for q in range(QUADS):
        pack_column(info, cells, q, packed, spills, q, 8 * q, (0, 0) if build else None)


def pack_faces(infos, pieces, packed, spills, build):
    for side in range(2):
        sign = 2 * side - 1
        for y in range(CY):
            shift = (sign * CX, 0) if build else None
            at = 32 + 8 * y
            pack_column(infos[side], pieces[side], y, packed, spills, 2 * side + y, at, shift)
        for x in range(CX):
            shift = (0, sign * CY) if build else None
            source = 2 * x + 1 - side
            target = 4 + 2 * x + side
            at = 48 + 8 * x
            pack_column(infos[2], pieces[2], source, packed, spills, target, at, shift)


def pack_corners(info, cells, packed, spills, build, layers):
    for side_x in range(2):
        for side_y in range(2):
            shift = ((2 * side_x - 1) * CX, (2 * side_y - 1) * CY) if build else None
            source = 2 * side_x + 1 - side_y
            target = 2 * side_x + side_y
            pack_column(info, cells, source, packed, spills, target, 64, shift, layers)


def pack_upper_faces(infos, pieces, packed, spills):
    for y in range(CY):
        pack_column(infos[0], pieces[0], y, packed, spills, 2 + y, 32 + 8 * y, None)
    for x in range(CX):
        pack_column(infos[1], pieces[1], 2 * x, packed, spills, 5 + 2 * x, 48 + 8 * x, None)


def pack_upper_corners(info, cells, packed, spills):
    for side_y in range(2):
        source = 1 - side_y
        pack_column(info, cells, source, packed, spills, 2 + side_y, 64, None, info_source=2 + source)


def upper_columns(q):
    columns = face_columns(q)
    return [columns[2 * k : 2 * k + 2] for k in range(2) if (q >> (1 - k)) & 1], 4 * (q == 1)


def core_columns(q):
    return [q ^ k for k in range(4)]


def face_columns(q):
    x, y = q >> 1, q & 1
    return [2 * x, 2 * x + 1, 4 + y, 6 + y]


def overflow_of(spills, columns, z):
    return sum(spills[column * CZ + z] for column in columns)


def spread(row):
    return jnp.broadcast_to(row, (8, LANES))


def couple(x_i, y_i, z_i, w_i, x_j, y_j, z_j, w_j):
    delta_x = x_j - x_i
    delta_y = y_j - y_i
    delta_z = z_j - z_i
    squared = delta_x * delta_x + delta_y * delta_y + delta_z * delta_z
    held = jnp.maximum(squared, CLOSEST_SQUARED)
    inverse = lax.rsqrt(held)
    distance = held * inverse
    scaled = distance * lax.rsqrt(w_i + w_j)
    value = (lax.erf(scaled) - lax.erf(distance)) * inverse
    return jnp.where(squared < CUT_SQUARED, value, 0.0)


def to_rows(sums, block):
    here = lane_index((8, LANES)) - row_index((8, LANES)) == 8 * block
    return jnp.where(here, jnp.sum(sums, axis=1, keepdims=True), 0.0)


def add_rows(cell, sums, rows):
    for index in range(2):
        total = jnp.zeros((8, LANES), jnp.float32)
        for block in range(BLOCKS):
            total = total + to_rows(sums[cell, block, index], block)
        rows.append(jnp.sum(total, axis=0, keepdims=True))


def finish_cell(slot, place, target, info, sums, out):
    q, z = place(slot)
    rows = []
    add_rows(slot, sums, rows)
    own = info.at[q * EZ + z + 1]
    scale = PAIR_SCALE / own[6:7, :]
    live = lane_index((1, LANES)) < own[7:8, :].astype(jnp.int32)
    out[target, 0:1, :] = jnp.where(live, rows[0] * scale, 0.0)
    out[target, 1:2, :] = jnp.where(live, rows[1] * scale, 0.0)


def build_cell(cell, slot, lines, turned, kernels, before, sums, below):
    own = None
    if below is not None:
        own = lane_index((8, LANES)) - row_index((8, LANES)) - below
    for group in GROUPS:
        sums_s, sums_t = start_sums(cell, before, group)
        for index, line in enumerate(lines):
            beside = [line(k) for k in range(6)]
            for at, block in enumerate(group):
                value = couple(*[turned[cell, block, k] for k in range(4)], *beside[:4])
                if own is not None and index < 2:
                    value = jnp.where(own == 8 * block - LANES * index, 0.0, value)
                kernels[slot, block, index] = value
                sums_s[at] = sums_s[at] + value * beside[4]
                sums_t[at] = sums_t[at] + value * beside[5]
        for at, block in enumerate(group):
            sums[slot, block, 0] = sums_s[at]
            sums[slot, block, 1] = sums_t[at]


def start_sums(cell, before, blocks):
    if before is None:
        zeros = [jnp.zeros((8, LANES), jnp.float32) for _ in blocks]
        return zeros, list(zeros)
    sums_s = [before[cell, block, 0] for block in blocks]
    return sums_s, [before[cell, block, 1] for block in blocks]


def lines_of(packed, columns, z):
    def line(column, half):
        return lambda k: spread(packed[column * CZ + z, half, k : k + 1, :])

    return [line(column, half) for column in columns for half in range(2)]


def rest_line(rest, cell):
    return lambda k: spread(rest[cell, k : k + 1, :])


def parts_of(value):
    high = value.astype(jnp.bfloat16).astype(jnp.float32)
    rest = value - high
    middle = rest.astype(jnp.bfloat16).astype(jnp.float32)
    return high, middle, rest - middle


def turn_cells(core, turned):
    chosen = row_index((24, 4 * LANES)) & 7
    ones = jnp.where(chosen == lane_index((24, 4 * LANES)) >> 7, 1.0, 0.0).astype(jnp.bfloat16)
    for cell in range(CELLS):
        here = core[(cell // CZ) * EZ + cell % CZ + 1]
        left = jnp.concatenate(parts_of(here), axis=0).T[: 8 * BLOCKS + 8].astype(jnp.bfloat16)
        wide = lax.dot_general(
            left, ones, (((1,), (0,)), ((), ())), preferred_element_type=jnp.float32
        )
        for block in range(BLOCKS):
            for k in range(4):
                turned[cell, block, k] = wide[8 * block : 8 * block + 8, k * LANES : (k + 1) * LANES]


def core_spills(spills, spill):
    for z in range(CZ):
        spill[z] = overflow_of(spills, range(QUADS), z)


def face_spills(spills, before, spill):
    for cell in range(CELLS):
        q, z = cell // CZ, cell % CZ
        spill[cell] = before[z] + overflow_of(spills, face_columns(q), z)


def corner_loop(start, stop, work, finish, sums):
    def one_cell(slot, _):
        finish(jnp.maximum(slot - 1, start))
        work(slot)
        return 0

    sums[start] = jnp.zeros(sums.shape[1:], jnp.float32)
    lax.fori_loop(start, stop, one_cell, 0, unroll=4)
    finish(stop - 1)


def corner_spills(spills, before, rest, place):
    for slot in range(rest.shape[0]):
        q, z = place(slot)
        rest[slot] = before[q * CZ + z] + spills[q * CZ + z]


def core_kernel(core, kernels, sums, spill, turned, packed, spills):
    turn_cells(core, turned)
    pack_core(core, core, packed, spills, True)
    core_spills(spills, spill)

    def one_cell(cell, _):
        q, z = cell // CZ, cell % CZ
        below = spread(core[q * EZ + z, 7:8, :]).astype(jnp.int32)
        lines = lines_of(packed, core_columns(q), z)
        build_cell(cell, cell, lines, turned, kernels, None, sums, below)
        return 0

    lax.fori_loop(0, CELLS, one_cell, 0, unroll=2)


def face_kernel(
    x_low, x_high, beyond, turned, before, spill_before, kernels, sums, spill, packed, spills
):
    pieces = [x_low, x_high, beyond]
    pack_faces(pieces, pieces, packed, spills, True)
    face_spills(spills, spill_before, spill)

    def one_cell(cell, _):
        lines = lines_of(packed, face_columns(cell // CZ), cell % CZ)
        build_cell(cell, cell, lines, turned, kernels, before, sums, None)
        return 0

    lax.fori_loop(0, CELLS, one_cell, 0, unroll=2)


def corner_kernel(
    corners, turned, before, spill_before, core, kernels, out, packed, spills, rest, sums
):
    slots = kernels.shape[0]
    place = PLACES[slots]
    pack_corners(corners, corners, packed, spills, True, LAYERS[slots])
    corner_spills(spills, spill_before, rest, place)

    def work(slot):
        q, z = place(slot)
        lines = lines_of(packed, [q], z) + [rest_line(rest, slot)]
        build_cell(q * CZ + z, slot, lines, turned, kernels, before, sums, None)

    def finish(slot):
        finish_cell(slot, place, slot, core, sums, out)

    corner_loop(0, slots, work, finish, sums)


IN_VMEM = pl.BlockSpec(memory_space=VMEM)
IN_SMEM = pl.BlockSpec(memory_space=SMEM)
PAIR = jax.ShapeDtypeStruct((CELLS, 2, LANES), jnp.float32)
SPILL = jax.ShapeDtypeStruct((CELLS, 8, LANES), jnp.float32)
SUMS = jax.ShapeDtypeStruct((CELLS, BLOCKS, 2, 8, LANES), jnp.float32)
TURNED = jax.ShapeDtypeStruct((CELLS, BLOCKS, 4, 8, LANES), jnp.float32)
CORE_SPILL = jax.ShapeDtypeStruct((CZ, 8, LANES), jnp.float32)
CORE_TILES, FACE_TILES, CORNER_TILES = 8, 8, 3


def held(tiles, cells=CELLS):
    return VMEM((cells, BLOCKS, tiles, 8, LANES), jnp.float32)


def pairs(cells):
    return jax.ShapeDtypeStruct((cells, 2, LANES), jnp.float32)


def call(kernel, outs, scratch, tiles, *arrays):
    work = CELLS * BLOCKS * tiles * 8 * LANES
    return pl.pallas_call(
        kernel,
        out_shape=outs,
        in_specs=[IN_SMEM if array.ndim == 1 else IN_VMEM for array in arrays],
        out_specs=jax.tree.map(lambda _: IN_VMEM, outs),
        scratch_shapes=scratch,
        compiler_params=params(8),
        cost_estimate=pl.CostEstimate(
            flops=30 * work, bytes_accessed=8 * work, transcendentals=4 * work
        ),
    )(*arrays)


def packs(columns):
    return [
        VMEM((columns * CZ, 2, 8, LANES), jnp.float32),
        VMEM((columns * CZ, 8, LANES), jnp.float32),
    ]


def build_core(core):
    outs = (held(CORE_TILES), SUMS, CORE_SPILL, TURNED)
    return call(core_kernel, outs, packs(4), CORE_TILES, core)


def build_faces(pieces, turned, before, spill):
    outs = (held(FACE_TILES), SUMS, SPILL)
    return call(face_kernel, outs, packs(8), FACE_TILES, *pieces, turned, before, spill)


def corner_scratch(cells):
    rest = VMEM((cells, 8, LANES), jnp.float32)
    return packs(4) + [rest, VMEM((cells, BLOCKS, 2, 8, LANES), jnp.float32)]


def build_corners(cells, corners, turned, before, spill, core):
    outs = (held(CORNER_TILES, cells), pairs(cells))
    arrays = [corners, turned, before, spill, core]
    return call(corner_kernel, outs, corner_scratch(cells), CORNER_TILES, *arrays)


def cell_sums(cell, slot, lines, stored, before, first=0):
    sums_s, sums_t = start_sums(cell, before, range(BLOCKS))
    for index, line in enumerate(lines):
        line_s, line_t = line(0), line(1)
        for block in range(BLOCKS):
            value = stored[slot, block, first + index]
            sums_s[block] = sums_s[block] + value * line_s
            sums_t[block] = sums_t[block] + value * line_t
    return sums_s, sums_t


def apply_cell(cell, slot, lines, stored, before, sums, first=0):
    sums_s, sums_t = cell_sums(cell, slot, lines, stored, before, first)
    for block in range(BLOCKS):
        sums[slot, block, 0] = sums_s[block]
        sums[slot, block, 1] = sums_t[block]


def widen(pieces, wides, scale=None):
    for piece, wide in zip(pieces, wides):
        wide[:, 0:2, :] = piece[...] if scale is None else scale * piece[...]


def apply_core_kernel(info, core, stored, sums, spill, wide, packed, spills):
    widen([core], [wide])
    pack_core(info, wide, packed, spills, False)
    core_spills(spills, spill)

    def one_cell(cell, _):
        lines = lines_of(packed, core_columns(cell // CZ), cell % CZ)
        apply_cell(cell, cell, lines, stored, None, sums)
        return 0

    lax.fori_loop(0, CELLS, one_cell, 0, unroll=4)


def apply_face_kernel(*refs):
    infos, pieces, (stored, before, spill_before, sums, spill), wides, (packed, spills) = split(
        refs, 3, 3, 5, 3, 2
    )
    widen(pieces, wides)
    pack_faces(infos, wides, packed, spills, False)
    face_spills(spills, spill_before, spill)

    def one_cell(cell, _):
        lines = lines_of(packed, face_columns(cell // CZ), cell % CZ)
        apply_cell(cell, cell, lines, stored, before, sums)
        return 0

    lax.fori_loop(0, CELLS, one_cell, 0, unroll=4)


def apply_corner_cells(stored, before, spill_before, core, out, packed, spills, rest, sums):
    slots = stored.shape[0]
    place = PLACES[slots]
    corner_spills(spills, spill_before, rest, place)

    def work(slot):
        q, z = place(slot)
        lines = lines_of(packed, [q], z) + [rest_line(rest, slot)]
        apply_cell(q * CZ + z, slot, lines, stored, before, sums)

    def finish(slot):
        finish_cell(slot, place, slot, core, sums, out)

    corner_loop(0, slots, work, finish, sums)


def upper_corner_cells(stored, before, spill_before, turned, packed, spills, rest, total):
    slots = stored.shape[0]
    place = PLACES[slots]
    for slot in range(slots):
        q, z = place(slot)
        tile = spill_before[q * CZ + z]
        rest[slot] = tile + spills[q * CZ + z] if q >= CY else tile

    def weigh(cell, sums, total):
        total_s, total_t = total
        for block in range(BLOCKS):
            total_s = total_s + sums[0][block] * turned[cell, block, 0]
            total_t = total_t + sums[1][block] * turned[cell, block, 1]
        return total_s, total_t

    def low(slot, total):
        q, z = place(slot)
        cell = q * CZ + z
        return weigh(cell, cell_sums(cell, slot, [rest_line(rest, slot)], stored, before, 2), total)

    def high(slot, total):
        q, z = place(slot)
        cell = q * CZ + z
        lines = lines_of(packed, [q], z) + [rest_line(rest, slot)]
        return weigh(cell, cell_sums(cell, slot, lines, stored, before), total)

    total = lax.fori_loop(0, slots // 2, low, total, unroll=4)
    return lax.fori_loop(slots // 2, slots, high, total, unroll=4)


def upper_face_kernel(
    info_high, info_beyond, high, beyond, stored, before, spill_before, sums, spill,
    wide_high, wide_beyond, packed, spills,
):
    wides = [wide_high, wide_beyond]
    widen([high, beyond], wides, 2.0)
    pack_upper_faces([info_high, info_beyond], wides, packed, spills)
    for cell in range(CELLS):
        q, z = cell // CZ, cell % CZ
        groups, _ = upper_columns(q)
        spill[cell] = sum([spills[c * CZ + z] for group in groups for c in group], spill_before[z])
    sums[0:CZ] = before[0:CZ]
    for q in range(1, QUADS):
        groups, first = upper_columns(q)
        columns = [column for group in groups for column in group]

        def one_cell(z, _, q=q, columns=columns, first=first):
            cell = q * CZ + z
            apply_cell(cell, cell, lines_of(packed, columns, z), stored, before, sums, first)
            return 0

        lax.fori_loop(0, CZ, one_cell, 0, unroll=4)


def apply_corner_kernel(
    info, corners, stored, before, spill_before, core, out, wide, packed, spills, rest, sums
):
    widen([corners], [wide])
    pack_corners(info, wide, packed, spills, False, LAYERS[stored.shape[0]])
    apply_corner_cells(
        stored, before, spill_before, core, out, packed, spills, rest, sums
    )


def split(refs, *sizes):
    parts = []
    for size in sizes:
        parts.append(refs[:size])
        refs = refs[size:]
    return parts


def turn_pairs(core, turned):
    row = row_index((8, 2 * LANES))
    chosen = ((row & 1) == lane_index((8, 2 * LANES)) >> 7) & (row < 6)
    ones = jnp.where(chosen, 1.0, 0.0).astype(jnp.bfloat16)
    for cell in range(CELLS):
        pair = core[(cell // CZ) * EZ + cell % CZ + 1]
        parts = jnp.concatenate(parts_of(pair) + (jnp.zeros_like(pair),), axis=0)
        left = parts.T[: 8 * BLOCKS + 8].astype(jnp.bfloat16)
        wide = lax.dot_general(
            left, ones, (((1,), (0,)), ((), ())), preferred_element_type=jnp.float32
        )
        for block in range(BLOCKS):
            for k in range(2):
                turned[cell, block, k] = wide[8 * block : 8 * block + 8, k * LANES : (k + 1) * LANES]


def pair_place(index):
    return lane_index((2, LANES)) - row_index((2, LANES)) == 2 * index


def last_core_kernel(
    info, core, stored, slots, first, second, sums, spill, turned, line, wide, packed, spills
):
    turn_pairs(core, turned)
    apply_core_kernel(info, core, stored, sums, spill, wide, packed, spills)
    d = slots[:, 1 : 1 + CZ, 6:7, :].reshape(CELLS, 1, LANES)
    v_0 = slots[:, 1 : 1 + CZ, 4:6, :].reshape(CELLS, 2, LANES)
    v_1 = first[:, 1 : 1 + CZ].reshape(v_0.shape)
    v_2 = second[:, 1 : 1 + CZ].reshape(v_0.shape)
    d_0 = d * v_0
    d_2 = d * v_2
    parts = [d_0 * v_0, d_0 * v_1, d * v_1 * v_1, d_2 * v_1, d_2 * v_2, None, v_0, v_1, v_2]
    found = jnp.zeros((2, LANES), jnp.float32)
    for index, part in enumerate(parts):
        if part is not None:
            total = jnp.sum(jnp.sum(part, axis=0), axis=1, keepdims=True)
            found = jnp.where(pair_place(index), total, found)
    line[...] = found


def apply_last_kernel(
    info, corners, edge, inner, before, spill_before, turned, line, moments,
    wide, packed, spills, edge_rest, inner_rest,
):
    widen([corners], [wide], 2.0)
    pack_upper_corners(info, wide, packed, spills)
    total = (jnp.zeros((8, LANES), jnp.float32), jnp.zeros((8, LANES), jnp.float32))
    for stored, rest in ((edge, edge_rest), (inner, inner_rest)):
        total = upper_corner_cells(
            stored, before, spill_before, turned, packed, spills, rest, total
        )
    last = [jnp.sum(part, axis=0, keepdims=True) for part in total]
    last = PAIR_SCALE * jnp.sum(jnp.concatenate(last, axis=0), axis=1, keepdims=True)
    found = jnp.where(pair_place(5), last, line[...])
    moments[...] = jnp.sum(found, axis=0, keepdims=True)


def wide(piece):
    return VMEM((piece.shape[0], 8, LANES), jnp.float32)


def apply_core(info, core, stored):
    stored = pltpu.with_memory_space_constraint(stored, VMEM)
    scratch = [wide(core)] + packs(4)
    return call(apply_core_kernel, (SUMS, CORE_SPILL), scratch, 2, info, core, stored)


def apply_faces(infos, pieces, stored, before, spill):
    stored = pltpu.with_memory_space_constraint(stored, VMEM)
    scratch = [wide(piece) for piece in pieces] + packs(8)
    return call(
        apply_face_kernel, (SUMS, SPILL), scratch, 2, *infos, *pieces, stored, before, spill
    )


def apply_upper_faces(infos, pieces, stored, before, spill):
    stored = pltpu.with_memory_space_constraint(stored, VMEM)
    scratch = [wide(piece) for piece in pieces] + packs(8)
    return call(
        upper_face_kernel, (SUMS, SPILL), scratch, 2, *infos, *pieces, stored, before, spill
    )


def apply_corners(info, corners, stored, before, spill, core):
    stored = pltpu.with_memory_space_constraint(stored, VMEM)
    cells = stored.shape[0]
    arrays = [info, corners, stored, before, spill, core]
    scratch = [wide(corners)] + corner_scratch(cells)
    return call(apply_corner_kernel, pairs(cells), scratch, 2, *arrays)


def apply_last_core(info, core, stored, slots, first, second):
    stored = pltpu.with_memory_space_constraint(stored, VMEM)
    outs = (SUMS, CORE_SPILL, SUMS, jax.ShapeDtypeStruct((2, LANES), jnp.float32))
    scratch = [wide(core)] + packs(4)
    return call(last_core_kernel, outs, scratch, 2, info, core, stored, slots, first, second)


def apply_last(info, corners, edge, inner, before, spill, turned, line):
    edge = pltpu.with_memory_space_constraint(edge, VMEM)
    inner = pltpu.with_memory_space_constraint(inner, VMEM)
    arrays = [info, corners, edge, inner, before, spill, turned, line]
    scratch = [wide(corners)] + packs(4)
    scratch += [VMEM((cells, 8, LANES), jnp.float32) for cells in (EDGES, INNER)]
    out = jax.ShapeDtypeStruct((1, LANES), jnp.float32)
    return call(apply_last_kernel, out, scratch, 2, *arrays)


def solve(g):
    tiny = 1e-6
    h = [g[k] + g[k + 1] for k in range(5)]
    ratio_1 = h[1] / h[0]
    ratio_2 = h[2] / h[0]
    pivot_1 = h[2] - ratio_1 * h[1]
    mixed = h[3] - ratio_1 * h[2]
    rest_1 = g[1] - ratio_1 * g[0]
    live_1 = pivot_1 > tiny * h[2]
    safe_1 = jnp.where(live_1, pivot_1, 1.0)
    ratio_3 = jnp.where(live_1, mixed / safe_1, 0.0)
    pivot_2 = h[4] - ratio_2 * h[2] - ratio_3 * mixed
    rest_2 = g[2] - ratio_2 * g[0] - ratio_3 * rest_1
    live_2 = live_1 & (pivot_2 > tiny * h[4])
    c_2 = jnp.where(live_2, rest_2 / jnp.where(live_2, pivot_2, 1.0), 0.0)
    c_1 = jnp.where(live_1, (rest_1 - mixed * c_2) / safe_1, 0.0)
    c_0 = (g[0] - h[1] * c_1 - h[2] * c_2) / h[0]
    return c_0, c_1, c_2


def invert(counts, atoms, places):
    rows = places.shape[1]
    row_low = row_index((LANES, LANES))
    row_high = row_index((rows, LANES))
    lane = lane_index((rows, LANES))

    def one_cell(cell, total):
        live = lane_index((1, LANES)) < counts[cell]
        pointer = jnp.where(live, atoms[pl.ds(cell, 1), :], -1)
        here = (pointer >> 7) == row_high
        cells = jnp.where(here, cell, 0).astype(jnp.float32)
        slots = jnp.where(here, lane, 0).astype(jnp.float32)
        parts = jnp.concatenate([cells, slots], axis=0).astype(jnp.bfloat16)
        lows = jnp.where((pointer & 127) == row_low, 1.0, 0.0).astype(jnp.bfloat16)
        return total + lax.dot_general(
            parts, lows, (((1,), (1,)), ((), ())), preferred_element_type=jnp.float32
        )

    total = jnp.zeros((2 * rows, LANES), jnp.float32)
    total = lax.fori_loop(0, CELLS, one_cell, total, unroll=8).astype(jnp.int32)
    places[0] = total[:rows]
    places[1] = total[rows:]


def inverted(counts, atoms, atoms_local):
    rows = (atoms_local // LANES + 15) // 16 * 16
    return call(invert, jax.ShapeDtypeStruct((2, rows, LANES), jnp.int32), [], 2, counts, atoms)


def finish_kernel(moments, slots, first, second, places, out, charges):
    summed = moments[...]
    lane = lane_index((2, LANES))
    row = row_index((2, LANES))

    def pair(index):
        picked = jnp.where(lane - row == 2 * index, summed, 0.0)
        return jnp.broadcast_to(jnp.sum(picked, axis=1, keepdims=True), (2, LANES))

    rows = [pair(index) for index in range(9)]
    c_0, c_1, c_2 = solve(rows[:6])
    totals = c_0 * rows[6] + c_1 * rows[7] + c_2 * rows[8]
    balance = totals[0:1] / totals[1:2]
    sign = jnp.concatenate([jnp.ones((1, LANES), jnp.float32), -balance], axis=0)
    c_0, c_1, c_2 = c_0 * sign, c_1 * sign, c_2 * sign
    for cell in range(CELLS):
        q, z = cell // CZ, cell % CZ + 1
        mixed = c_0 * slots[q, z, 4:6, :] + c_1 * first[q, z] + c_2 * second[q, z]
        charges[cell : cell + 1, :] = jnp.sum(mixed, axis=0, keepdims=True)
    tiles = [jnp.zeros((8, LANES), jnp.float32) for _ in range(places.shape[1] // 8)]
    for cell in range(CELLS):
        line = spread(charges[cell : cell + 1, :])
        for at in range(len(tiles)):
            here = slice(8 * at, 8 * at + 8)
            moved = jnp.take_along_axis(line, places[1, here, :], axis=1)
            tiles[at] = jnp.where(places[0, here, :] == cell, moved, tiles[at])
    out[...] = jnp.concatenate(tiles, axis=0)[: out.shape[0]]


def finish(moments, slots, first, second, places, atoms_local):
    return pl.pallas_call(
        finish_kernel,
        out_shape=jax.ShapeDtypeStruct((atoms_local // LANES, LANES), jnp.float32),
        in_specs=[IN_VMEM] * 5,
        out_specs=IN_VMEM,
        scratch_shapes=[VMEM((CELLS, LANES), jnp.float32)],
        compiler_params=params(8),
    )(moments, slots, first, second, places)


def partner(block, axis, mask):
    count = lax.axis_size(axis)
    return lax.ppermute(block, axis, [(low, low ^ mask) for low in range(count)])


def shifted(block, along_x, across_y=0):
    count = lax.axis_size("gx")
    route = [(i, ((i + 4 * along_x) % count) ^ (2 * across_y)) for i in range(count)]
    return lax.ppermute(block, "gx", route)


def with_z_faces(edge, inner):
    other = partner(edge, "gx", 1)
    parts = [other[:, 0:1], edge[:, 1:2], inner, edge[:, 0:1], other[:, 1:2]]
    return jnp.concatenate(parts, axis=1)


def flat(columns):
    return columns.reshape((-1,) + columns.shape[-2:])


def x_faces(core):
    count = lax.axis_size("gx")
    rows = count // 4
    odd = (lax.axis_index("gx") // 4) % 2 == 1
    if rows % 2:
        return shifted(core[2:], 1), shifted(core[:2], -1)
    route = [(i, (i + (4 if (i // 4) % 2 else -4)) % count) for i in range(count)]
    second = lax.ppermute(jnp.where(odd, core[2:], core[:2]), "gx", route)
    first = lax.ppermute(jnp.where(odd, core[:2], core[2:]), "gx", [(i, i ^ 4) for i in range(count)])
    return first, second


def sorted_faces(first, second):
    odd = (lax.axis_index("gx") // 4) % 2 == 1
    if (lax.axis_size("gx") // 4) % 2:
        return first, second
    return jnp.where(odd, first, second), jnp.where(odd, second, first)


def exchange(edge, inner, on_core, on_faces, on_corners, faces_last=False):
    core = with_z_faces(edge, inner)
    first, second = x_faces(core)
    beyond = partner(core, "gx", 2)
    sums, spill, *more = on_core(flat(core))
    if faces_last:
        second, first, beyond, sums = lax.optimization_barrier((second, first, beyond, sums))
    else:
        second, first, sums = lax.optimization_barrier((second, first, sums))
    low, high = sorted_faces(first, second)
    corners = partner(jnp.concatenate([low, high], axis=0), "gx", 2)
    pieces = [flat(part) for part in (low, high, beyond)]
    sums, spill, *more = on_faces(pieces, sums, spill, *more)
    corners = flat(corners)
    return core, pieces, corners, on_corners(corners, sums, spill, core, *more)


def global_sum(values):
    count = lax.axis_size("gx")
    if count & (count - 1):
        return lax.psum(values, "gx")
    step = 1
    while step < count:
        if step >= 2 and 4 * step <= count:
            others = [partner(values, "gx", k * step) for k in (3, 2, 1)]
            values = (values + others[0]) + (others[1] + others[2])
            step *= 4
        else:
            values = values + partner(values, "gx", step)
            step *= 2
    return values


def local(cell_offsets, electronegativity, hardness, charge_widths, cell_counts, cell_atoms):
    edge, inner = prepare(
        cell_counts, cell_offsets, electronegativity, hardness, charge_widths, cell_atoms
    )
    stored = []

    def keep(tiles, *others):
        stored.append(tiles)
        return others

    def build_ends(corners, sums, spill, core, *own):
        (edge,) = keep(*build_corners(EDGES, corners, *own, sums, spill, flat(core)))
        (inner,) = keep(*build_corners(INNER, corners, *own, sums, spill, flat(core)))
        return by_column(edge), by_column(inner)

    def by_column(cells):
        return cells.reshape((QUADS, -1) + cells.shape[1:])

    slots, pieces, corners, ends = exchange(
        by_column(edge),
        by_column(inner),
        lambda core: keep(*build_core(core)),
        lambda faces, sums, spill, *own: keep(*build_faces(faces, *own, sums, spill)) + own,
        build_ends,
        faces_last=True,
    )
    info = flat(slots)

    def apply(edge, inner, on_corners):
        return exchange(
            edge,
            inner,
            lambda own: apply_core(info, own, stored[0]),
            lambda faces, sums, spill: apply_faces(pieces, faces, stored[1], sums, spill),
            on_corners,
        )

    def apply_ends(others, sums, spill, _):
        edge = apply_corners(corners, others, stored[2], sums, spill, info)
        inner = apply_corners(corners, others, stored[3], sums, spill, info)
        return by_column(edge), by_column(inner)

    first, _, _, ends = apply(*ends, apply_ends)
    second = with_z_faces(*ends)
    high = shifted(second[:2], -1)
    beyond = partner(second, "gx", 2)
    corner = shifted(second[:2], -1, 1)
    sums, spill, turned, line = apply_last_core(
        info, flat(second), stored[0], slots, first, second
    )
    high, beyond, sums = lax.optimization_barrier((high, beyond, sums))
    upper = [flat(high), flat(beyond)]
    sums, spill = apply_upper_faces(pieces[1:], upper, stored[1], sums, spill)
    corner, sums = lax.optimization_barrier((corner, sums))
    moments = apply_last(
        corners, flat(corner), stored[2], stored[3], sums, spill, turned, line
    )
    moments, cell_counts, cell_atoms = lax.optimization_barrier((moments, cell_counts, cell_atoms))
    atoms_local = cell_offsets.shape[1]
    places = inverted(cell_counts, cell_atoms, atoms_local)
    charges = finish(global_sum(moments), slots, first, second, places, atoms_local)
    return charges.reshape(-1)


def solution(mesh):
    placed = (
        P(None, ("grp", "gx")),
        P(("grp", "gx")),
        P(("grp", "gx")),
        P(("grp", "gx")),
        P(("grp", "gx")),
        P(("grp", "gx"), None),
    )
    return jax.shard_map(
        local, mesh=mesh, in_specs=placed, out_specs=P(("grp", "gx")), check_vma=False
    )
```

```python
import functools
import math

import jax
import jax.numpy as jnp
from jax import lax
from jax.experimental import pallas as pl
from jax.experimental.pallas import tpu as pltpu
from jax.sharding import PartitionSpec as P

CX = 2
CY = 2
CZ = 8
EZ = CZ + 2
CELLS = CX * CY * CZ
QUADS = CX * CY
LANES = 128
BLOCKS = 11
GROUPS = ((0, 1, 2, 3), (4, 5, 6, 7), (8, 9, 10))

COULOMB = 14.399645
ROOT_PI = math.sqrt(math.pi)
SCREEN = 1.0 / (math.sqrt(2.0) * 3.0)
EWALD_SELF = math.sqrt(2.0 / math.pi) / 3.0
SIDE = 12.0 * SCREEN
CUT_SQUARED = (12.0 * SCREEN) ** 2
CLOSEST_SQUARED = (0.5 * SCREEN) ** 2
PAIR_SCALE = COULOMB * SCREEN

VMEM = pltpu.VMEM
SMEM = pltpu.SMEM


def params(mib):
    return pltpu.CompilerParams(vmem_limit_bytes=mib * 2**20)


def lane_index(shape):
    return lax.broadcasted_iota(jnp.int32, shape, len(shape) - 1)


def row_index(shape):
    return lax.broadcasted_iota(jnp.int32, shape, len(shape) - 2)


def edge_place(slot):
    return slot // 2, (CZ - 1) * (1 - slot % 2)


def inner_place(slot):
    return slot // (CZ - 2), 1 + slot % (CZ - 2)


EDGES = 2 * QUADS
INNER = CELLS - EDGES
PLACES = {EDGES: edge_place, INNER: inner_place}
LAYERS = {EDGES: (0, CZ - 1), INNER: range(1, CZ - 1)}


def gather_cells(counted, atoms, table, others, out):
    place = PLACES[out.shape[0]]
    row = row_index((8, LANES))
    lane = lane_index((1, LANES))

    def pick(source, pointers):
        share = 8 // len(pointers)
        pointer = spread(pointers[-1])
        for k in range(len(pointers) - 2, -1, -1):
            pointer = jnp.where(row < share * (k + 1), pointers[k], pointer)
        high = pointer >> 7
        low = pointer & 127
        picked = jnp.zeros((8, LANES), jnp.float32)
        for chunk in range(source.shape[0]):
            part = jnp.take_along_axis(source[chunk], low, axis=1)
            picked = jnp.where(high == chunk, part, picked)
        return picked

    def four_cells(step, _):
        slots = [4 * step + k for k in range(4)]
        places = [place(slot) for slot in slots]
        counts = [counted[pl.ds(q * CZ + z, 1), :] for q, z in places]
        occupied = [lane < count for count in counts]
        pointers = [
            jnp.where(live, atoms[pl.ds(q * CZ + z, 1), :], 0)
            for (q, z), live in zip(places, occupied)
        ]
        pairs = [pick(table, pointers[:2]), pick(table, pointers[2:])]
        both = pick(others, pointers)
        for k, (slot, live) in enumerate(zip(slots, occupied)):
            q = places[k][0]
            at = 4 * (k % 2)
            picked = pairs[k // 2][at : at + 4]
            width = jnp.where(live, picked[3:4], 1.0)
            hard = both[2 * k + 1 : 2 * k + 2]
            diag = jnp.where(live, hard + COULOMB * (1.0 / (width * ROOT_PI) - EWALD_SELF), 1.0)
            negative = jnp.where(live, both[2 * k : 2 * k + 1], 0.0)
            out[slot, 0:1, :] = (picked[0:1] + (q // CY).astype(jnp.float32)) * SIDE
            out[slot, 1:2, :] = (picked[1:2] + (q % CY).astype(jnp.float32)) * SIDE
            out[slot, 2:3, :] = picked[2:3] * SIDE
            out[slot, 3:4, :] = (2.0 * SCREEN * SCREEN) * width * width
            out[slot, 4:5, :] = -negative / diag
            out[slot, 5:6, :] = jnp.where(live, 1.0 / diag, 0.0)
            out[slot, 6:7, :] = diag
            out[slot, 7:8, :] = counts[k].astype(jnp.float32)
        return 0

    lax.fori_loop(0, out.shape[0] // 4, four_cells, 0, unroll=2)


def prepare_kernel(
    counts_hbm, offsets, negativity, hardness, widths, atoms_hbm, edge, counted, atoms, table, others,
    counts, raw_offsets, raw_negativity, raw_hardness, raw_widths, sems,
):
    copies = [
        pltpu.make_async_copy(source, target, sems.at[index])
        for index, (source, target) in enumerate(
            [
                (counts_hbm, counts),
                (offsets, raw_offsets),
                (negativity, raw_negativity),
                (hardness, raw_hardness),
                (widths, raw_widths),
                (atoms_hbm, atoms),
            ]
        )
    ]
    for copy in copies:
        copy.start()
    for copy in copies:
        copy.wait()
    for chunk in range(table.shape[0]):
        here = slice(chunk * LANES, (chunk + 1) * LANES)
        for first in (0, 4):
            table[chunk, first : first + 3, :] = raw_offsets[:, here]
            table[chunk, first + 3 : first + 4, :] = raw_widths[chunk : chunk + 1, :]
        for first in (0, 2, 4, 6):
            others[chunk, first : first + 1, :] = raw_negativity[chunk : chunk + 1, :]
            others[chunk, first + 1 : first + 2, :] = raw_hardness[chunk : chunk + 1, :]
    for cell in range(CELLS):
        counted[cell : cell + 1, :] = jnp.full((1, LANES), counts[cell])
    gather_cells(counted, atoms, table, others, edge)


def prepare_rest_kernel(counted, atoms, table, others, inner):
    gather_cells(counted, atoms, table, others, inner)


def prepare(counts, offsets, negativity, hardness, widths, atoms):
    chunks = offsets.shape[1] // LANES
    plane = (chunks, LANES)
    tables = jax.ShapeDtypeStruct((chunks, 8, LANES), jnp.float32)
    lists = jax.ShapeDtypeStruct(atoms.shape, jnp.int32)
    edge, *rest = pl.pallas_call(
        prepare_kernel,
        out_shape=(
            jax.ShapeDtypeStruct((EDGES, 8, LANES), jnp.float32),
            lists,
            lists,
            tables,
            tables,
        ),
        in_specs=[pl.BlockSpec(memory_space=pltpu.HBM)] * 6,
        out_specs=(pl.BlockSpec(memory_space=VMEM),) * 5,
        scratch_shapes=[
            SMEM(counts.shape, jnp.int32),
            VMEM(offsets.shape, jnp.float32),
            VMEM(plane, jnp.float32),
            VMEM(plane, jnp.float32),
            VMEM(plane, jnp.float32),
            pltpu.SemaphoreType.DMA((6,)),
        ],
        compiler_params=params(8),
    )(
        *[
            pltpu.with_memory_space_constraint(array, pltpu.HBM)
            for array in (
                counts,
                offsets,
                negativity.reshape(plane),
                hardness.reshape(plane),
                widths.reshape(plane),
                atoms,
            )
        ]
    )
    inner = pl.pallas_call(
        prepare_rest_kernel,
        out_shape=jax.ShapeDtypeStruct((INNER, 8, LANES), jnp.float32),
        in_specs=[pl.BlockSpec(memory_space=VMEM)] * 4,
        out_specs=pl.BlockSpec(memory_space=VMEM),
        compiler_params=params(8),
        cost_estimate=pl.CostEstimate(flops=2**20, bytes_accessed=2**22, transcendentals=0),
    )(*rest)
    return edge, inner


def pack_column(
    info, cells, source, packed, spills, target, at, shift, layers=range(CZ), info_source=None
):
    lane = lane_index((8, LANES))
    row = row_index((8, LANES))
    for z in layers:
        base = source * EZ + z
        known = base if info_source is None else info_source * EZ + z
        low, mid, top = [spread(info[known + k, 7:8, :]).astype(jnp.int32) for k in range(3)]
        end = low + mid - LANES
        tiles = [cells[base + k] for k in range(3)]
        if shift is not None:
            for k in range(3):
                offset = jnp.where(row == 2, (k - 1) * SIDE, 0.0)
                for axis in range(2):
                    offset = jnp.where(row == axis, shift[axis] * SIDE, offset)
                tiles[k] = tiles[k] + offset
        second = jnp.take_along_axis(tiles[1], (lane - low) & 127, axis=1)
        third = jnp.take_along_axis(tiles[2], (lane - end) & 127, axis=1)
        packed[target * CZ + z, 0] = jnp.where(lane < low, tiles[0], second)
        packed[target * CZ + z, 1] = jnp.where(lane < end, second, third)
        spill = jnp.where(lane < end + top - LANES, third, 0.0)
        spills[target * CZ + z] = pltpu.roll(spill, at, 1) if at else spill


def pack_core(info, cells, packed, spills, build):
    for q in range(QUADS):
        pack_column(info, cells, q, packed, spills, q, 8 * q, (0, 0) if build else None)


def pack_faces(infos, pieces, packed, spills, build):
    for side in range(2):
        sign = 2 * side - 1
        for y in range(CY):
            shift = (sign * CX, 0) if build else None
            at = 32 + 8 * y
            pack_column(infos[side], pieces[side], y, packed, spills, 2 * side + y, at, shift)
        for x in range(CX):
            shift = (0, sign * CY) if build else None
            source = 2 * x + 1 - side
            target = 4 + 2 * x + side
            at = 48 + 8 * x
            pack_column(infos[2], pieces[2], source, packed, spills, target, at, shift)


def pack_corners(info, cells, packed, spills, build, layers):
    for side_x in range(2):
        for side_y in range(2):
            shift = ((2 * side_x - 1) * CX, (2 * side_y - 1) * CY) if build else None
            source = 2 * side_x + 1 - side_y
            target = 2 * side_x + side_y
            pack_column(info, cells, source, packed, spills, target, 64, shift, layers)


def pack_upper_faces(infos, pieces, packed, spills):
    for y in range(CY):
        pack_column(infos[0], pieces[0], y, packed, spills, 2 + y, 32 + 8 * y, None)
    for x in range(CX):
        pack_column(infos[1], pieces[1], 2 * x, packed, spills, 5 + 2 * x, 48 + 8 * x, None)


def pack_upper_corners(info, cells, packed, spills):
    for side_y in range(2):
        source = 1 - side_y
        pack_column(info, cells, source, packed, spills, 2 + side_y, 64, None, info_source=2 + source)


def upper_columns(q):
    columns = face_columns(q)
    return [columns[2 * k : 2 * k + 2] for k in range(2) if (q >> (1 - k)) & 1], 4 * (q == 1)


def core_columns(q):
    return [q ^ k for k in range(4)]


def face_columns(q):
    x, y = q >> 1, q & 1
    return [2 * x, 2 * x + 1, 4 + y, 6 + y]


def overflow_of(spills, columns, z):
    return sum(spills[column * CZ + z] for column in columns)


def spread(row):
    return jnp.broadcast_to(row, (8, LANES))


def couple(x_i, y_i, z_i, w_i, x_j, y_j, z_j, w_j):
    delta_x = x_j - x_i
    delta_y = y_j - y_i
    delta_z = z_j - z_i
    squared = delta_x * delta_x + delta_y * delta_y + delta_z * delta_z
    held = jnp.maximum(squared, CLOSEST_SQUARED)
    inverse = lax.rsqrt(held)
    distance = held * inverse
    scaled = distance * lax.rsqrt(w_i + w_j)
    value = (lax.erf(scaled) - lax.erf(distance)) * inverse
    return jnp.where(squared < CUT_SQUARED, value, 0.0)


def to_rows(sums, block):
    here = lane_index((8, LANES)) - row_index((8, LANES)) == 8 * block
    return jnp.where(here, jnp.sum(sums, axis=1, keepdims=True), 0.0)


def add_rows(cell, sums, rows):
    for index in range(2):
        total = jnp.zeros((8, LANES), jnp.float32)
        for block in range(BLOCKS):
            total = total + to_rows(sums[cell, block, index], block)
        rows.append(jnp.sum(total, axis=0, keepdims=True))


def finish_cell(slot, place, target, info, sums, out):
    q, z = place(slot)
    rows = []
    add_rows(slot, sums, rows)
    own = info.at[q * EZ + z + 1]
    scale = PAIR_SCALE / own[6:7, :]
    live = lane_index((1, LANES)) < own[7:8, :].astype(jnp.int32)
    out[target, 0:1, :] = jnp.where(live, rows[0] * scale, 0.0)
    out[target, 1:2, :] = jnp.where(live, rows[1] * scale, 0.0)


def build_cell(cell, slot, lines, turned, kernels, before, sums, below):
    own = None
    if below is not None:
        own = lane_index((8, LANES)) - row_index((8, LANES)) - below
    for group in GROUPS:
        sums_s, sums_t = start_sums(cell, before, group)
        mine = [[turned[cell, block, k] for k in range(4)] for block in group]
        for index, line in enumerate(lines):
            beside = [line(k) for k in range(6)]
            for at, block in enumerate(group):
                value = couple(*mine[at], *beside[:4])
                if own is not None and index < 2:
                    value = jnp.where(own == 8 * block - LANES * index, 0.0, value)
                kernels[slot, block, index] = value
                sums_s[at] = sums_s[at] + value * beside[4]
                sums_t[at] = sums_t[at] + value * beside[5]
        for at, block in enumerate(group):
            sums[slot, block, 0] = sums_s[at]
            sums[slot, block, 1] = sums_t[at]


def start_sums(cell, before, blocks):
    if before is None:
        zeros = [jnp.zeros((8, LANES), jnp.float32) for _ in blocks]
        return zeros, list(zeros)
    sums_s = [before[cell, block, 0] for block in blocks]
    return sums_s, [before[cell, block, 1] for block in blocks]


def lines_of(packed, columns, z):
    def line(column, half):
        return lambda k: spread(packed[column * CZ + z, half, k : k + 1, :])

    return [line(column, half) for column in columns for half in range(2)]


def rest_line(rest, cell):
    return lambda k: spread(rest[cell, k : k + 1, :])


def parts_of(value):
    high = value.astype(jnp.bfloat16).astype(jnp.float32)
    rest = value - high
    middle = rest.astype(jnp.bfloat16).astype(jnp.float32)
    return high, middle, rest - middle


def turn_cells(core, turned):
    chosen = row_index((24, 4 * LANES)) & 7
    ones = jnp.where(chosen == lane_index((24, 4 * LANES)) >> 7, 1.0, 0.0).astype(jnp.bfloat16)
    for cell in range(CELLS):
        here = core[(cell // CZ) * EZ + cell % CZ + 1]
        left = jnp.concatenate(parts_of(here), axis=0).T[: 8 * BLOCKS + 8].astype(jnp.bfloat16)
        wide = lax.dot_general(
            left, ones, (((1,), (0,)), ((), ())), preferred_element_type=jnp.float32
        )
        for block in range(BLOCKS):
            for k in range(4):
                turned[cell, block, k] = wide[8 * block : 8 * block + 8, k * LANES : (k + 1) * LANES]


def core_spills(spills, spill):
    for z in range(CZ):
        spill[z] = overflow_of(spills, range(QUADS), z)


def face_spills(spills, before, spill):
    for cell in range(CELLS):
        q, z = cell // CZ, cell % CZ
        spill[cell] = before[z] + overflow_of(spills, face_columns(q), z)


def corner_loop(start, stop, work, finish, sums):
    def one_cell(slot, _):
        finish(jnp.maximum(slot - 1, start))
        work(slot)
        return 0

    sums[start] = jnp.zeros(sums.shape[1:], jnp.float32)
    lax.fori_loop(start, stop, one_cell, 0, unroll=4)
    finish(stop - 1)


def corner_spills(spills, before, rest, place):
    for slot in range(rest.shape[0]):
        q, z = place(slot)
        rest[slot] = before[q * CZ + z] + spills[q * CZ + z]


def core_kernel(core, kernels, sums, spill, turned, packed, spills):
    turn_cells(core, turned)
    pack_core(core, core, packed, spills, True)
    core_spills(spills, spill)

    def one_cell(cell, _):
        q, z = cell // CZ, cell % CZ
        below = spread(core[q * EZ + z, 7:8, :]).astype(jnp.int32)
        lines = lines_of(packed, core_columns(q), z)
        build_cell(cell, cell, lines, turned, kernels, None, sums, below)
        return 0

    lax.fori_loop(0, CELLS, one_cell, 0, unroll=2)


def face_kernel(
    x_low, x_high, beyond, turned, before, spill_before, kernels, sums, spill, packed, spills
):
    pieces = [x_low, x_high, beyond]
    pack_faces(pieces, pieces, packed, spills, True)
    face_spills(spills, spill_before, spill)

    def one_cell(cell, _):
        lines = lines_of(packed, face_columns(cell // CZ), cell % CZ)
        build_cell(cell, cell, lines, turned, kernels, before, sums, None)
        return 0

    lax.fori_loop(0, CELLS, one_cell, 0, unroll=2)


def corner_kernel(
    corners, turned, before, spill_before, core, kernels, out, packed, spills, rest, sums
):
    slots = kernels.shape[0]
    place = PLACES[slots]
    pack_corners(corners, corners, packed, spills, True, LAYERS[slots])
    corner_spills(spills, spill_before, rest, place)

    def work(slot):
        q, z = place(slot)
        lines = lines_of(packed, [q], z) + [rest_line(rest, slot)]
        build_cell(q * CZ + z, slot, lines, turned, kernels, before, sums, None)

    def finish(slot):
        finish_cell(slot, place, slot, core, sums, out)

    corner_loop(0, slots, work, finish, sums)


IN_VMEM = pl.BlockSpec(memory_space=VMEM)
IN_SMEM = pl.BlockSpec(memory_space=SMEM)
PAIR = jax.ShapeDtypeStruct((CELLS, 2, LANES), jnp.float32)
SPILL = jax.ShapeDtypeStruct((CELLS, 8, LANES), jnp.float32)
SUMS = jax.ShapeDtypeStruct((CELLS, BLOCKS, 2, 8, LANES), jnp.float32)
TURNED = jax.ShapeDtypeStruct((CELLS, BLOCKS, 4, 8, LANES), jnp.float32)
CORE_SPILL = jax.ShapeDtypeStruct((CZ, 8, LANES), jnp.float32)
CORE_TILES, FACE_TILES, CORNER_TILES = 8, 8, 3


def held(tiles, cells=CELLS):
    return VMEM((cells, BLOCKS, tiles, 8, LANES), jnp.float32)


def pairs(cells):
    return jax.ShapeDtypeStruct((cells, 2, LANES), jnp.float32)


def call(kernel, outs, scratch, tiles, *arrays):
    work = CELLS * BLOCKS * tiles * 8 * LANES
    return pl.pallas_call(
        kernel,
        out_shape=outs,
        in_specs=[IN_SMEM if array.ndim == 1 else IN_VMEM for array in arrays],
        out_specs=jax.tree.map(lambda _: IN_VMEM, outs),
        scratch_shapes=scratch,
        compiler_params=params(8),
        cost_estimate=pl.CostEstimate(
            flops=30 * work, bytes_accessed=8 * work, transcendentals=4 * work
        ),
    )(*arrays)


def packs(columns):
    return [
        VMEM((columns * CZ, 2, 8, LANES), jnp.float32),
        VMEM((columns * CZ, 8, LANES), jnp.float32),
    ]


def build_core(core):
    outs = (held(CORE_TILES), SUMS, CORE_SPILL, TURNED)
    return call(core_kernel, outs, packs(4), CORE_TILES, core)


def build_faces(pieces, turned, before, spill):
    outs = (held(FACE_TILES), SUMS, SPILL)
    return call(face_kernel, outs, packs(8), FACE_TILES, *pieces, turned, before, spill)


def corner_scratch(cells):
    rest = VMEM((cells, 8, LANES), jnp.float32)
    return packs(4) + [rest, VMEM((cells, BLOCKS, 2, 8, LANES), jnp.float32)]


def build_corners(cells, corners, turned, before, spill, core):
    outs = (held(CORNER_TILES, cells), pairs(cells))
    arrays = [corners, turned, before, spill, core]
    return call(corner_kernel, outs, corner_scratch(cells), CORNER_TILES, *arrays)


def cell_sums(cell, slot, lines, stored, before, first=0):
    sums_s, sums_t = start_sums(cell, before, range(BLOCKS))
    for index, line in enumerate(lines):
        line_s, line_t = line(0), line(1)
        for block in range(BLOCKS):
            value = stored[slot, block, first + index]
            sums_s[block] = sums_s[block] + value * line_s
            sums_t[block] = sums_t[block] + value * line_t
    return sums_s, sums_t


def apply_cell(cell, slot, lines, stored, before, sums, first=0):
    sums_s, sums_t = cell_sums(cell, slot, lines, stored, before, first)
    for block in range(BLOCKS):
        sums[slot, block, 0] = sums_s[block]
        sums[slot, block, 1] = sums_t[block]


def widen(pieces, wides, scale=None):
    for piece, wide in zip(pieces, wides):
        wide[:, 0:2, :] = piece[...] if scale is None else scale * piece[...]


def apply_core_kernel(info, core, stored, sums, spill, wide, packed, spills):
    widen([core], [wide])
    pack_core(info, wide, packed, spills, False)
    core_spills(spills, spill)

    def one_cell(cell, _):
        lines = lines_of(packed, core_columns(cell // CZ), cell % CZ)
        apply_cell(cell, cell, lines, stored, None, sums)
        return 0

    lax.fori_loop(0, CELLS, one_cell, 0, unroll=4)


def apply_face_kernel(*refs):
    infos, pieces, (stored, before, spill_before, sums, spill), wides, (packed, spills) = split(
        refs, 3, 3, 5, 3, 2
    )
    widen(pieces, wides)
    pack_faces(infos, wides, packed, spills, False)
    face_spills(spills, spill_before, spill)

    def one_cell(cell, _):
        lines = lines_of(packed, face_columns(cell // CZ), cell % CZ)
        apply_cell(cell, cell, lines, stored, before, sums)
        return 0

    lax.fori_loop(0, CELLS, one_cell, 0, unroll=4)


def apply_corner_cells(stored, before, spill_before, core, out, packed, spills, rest, sums):
    slots = stored.shape[0]
    place = PLACES[slots]
    corner_spills(spills, spill_before, rest, place)

    def work(slot):
        q, z = place(slot)
        lines = lines_of(packed, [q], z) + [rest_line(rest, slot)]
        apply_cell(q * CZ + z, slot, lines, stored, before, sums)

    def finish(slot):
        finish_cell(slot, place, slot, core, sums, out)

    corner_loop(0, slots, work, finish, sums)


def upper_corner_cells(stored, before, spill_before, turned, packed, spills, rest, total):
    slots = stored.shape[0]
    place = PLACES[slots]
    for slot in range(slots):
        q, z = place(slot)
        tile = spill_before[q * CZ + z]
        rest[slot] = tile + spills[q * CZ + z] if q >= CY else tile

    def weigh(cell, sums, total):
        total_s, total_t = total
        for block in range(BLOCKS):
            total_s = total_s + sums[0][block] * turned[cell, block, 0]
            total_t = total_t + sums[1][block] * turned[cell, block, 1]
        return total_s, total_t

    def low(slot, total):
        q, z = place(slot)
        cell = q * CZ + z
        return weigh(cell, cell_sums(cell, slot, [rest_line(rest, slot)], stored, before, 2), total)

    def high(slot, total):
        q, z = place(slot)
        cell = q * CZ + z
        lines = lines_of(packed, [q], z) + [rest_line(rest, slot)]
        return weigh(cell, cell_sums(cell, slot, lines, stored, before), total)

    total = lax.fori_loop(0, slots // 2, low, total, unroll=4)
    return lax.fori_loop(slots // 2, slots, high, total, unroll=4)


def upper_face_kernel(
    info_high, info_beyond, high, beyond, stored, before, spill_before, sums, spill,
    wide_high, wide_beyond, packed, spills,
):
    wides = [wide_high, wide_beyond]
    widen([high, beyond], wides, 2.0)
    pack_upper_faces([info_high, info_beyond], wides, packed, spills)
    for cell in range(CELLS):
        q, z = cell // CZ, cell % CZ
        groups, _ = upper_columns(q)
        spill[cell] = sum([spills[c * CZ + z] for group in groups for c in group], spill_before[z])
    sums[0:CZ] = before[0:CZ]
    for q in range(1, QUADS):
        groups, first = upper_columns(q)
        columns = [column for group in groups for column in group]

        def one_cell(z, _, q=q, columns=columns, first=first):
            cell = q * CZ + z
            apply_cell(cell, cell, lines_of(packed, columns, z), stored, before, sums, first)
            return 0

        lax.fori_loop(0, CZ, one_cell, 0, unroll=4)


def apply_corner_kernel(
    info, corners, stored, before, spill_before, core, out, wide, packed, spills, rest, sums
):
    widen([corners], [wide])
    pack_corners(info, wide, packed, spills, False, LAYERS[stored.shape[0]])
    apply_corner_cells(
        stored, before, spill_before, core, out, packed, spills, rest, sums
    )


def split(refs, *sizes):
    parts = []
    for size in sizes:
        parts.append(refs[:size])
        refs = refs[size:]
    return parts


def turn_pairs(core, turned):
    row = row_index((8, 2 * LANES))
    chosen = ((row & 1) == lane_index((8, 2 * LANES)) >> 7) & (row < 6)
    ones = jnp.where(chosen, 1.0, 0.0).astype(jnp.bfloat16)
    for cell in range(CELLS):
        pair = core[(cell // CZ) * EZ + cell % CZ + 1]
        parts = jnp.concatenate(parts_of(pair) + (jnp.zeros_like(pair),), axis=0)
        left = parts.T[: 8 * BLOCKS + 8].astype(jnp.bfloat16)
        wide = lax.dot_general(
            left, ones, (((1,), (0,)), ((), ())), preferred_element_type=jnp.float32
        )
        for block in range(BLOCKS):
            for k in range(2):
                turned[cell, block, k] = wide[8 * block : 8 * block + 8, k * LANES : (k + 1) * LANES]


def pair_place(index):
    return lane_index((2, LANES)) - row_index((2, LANES)) == 2 * index


def last_core_kernel(
    info, core, stored, slots, first, second, sums, spill, turned, line, wide, packed, spills
):
    turn_pairs(core, turned)
    apply_core_kernel(info, core, stored, sums, spill, wide, packed, spills)
    d = slots[:, 1 : 1 + CZ, 6:7, :].reshape(CELLS, 1, LANES)
    v_0 = slots[:, 1 : 1 + CZ, 4:6, :].reshape(CELLS, 2, LANES)
    v_1 = first[:, 1 : 1 + CZ].reshape(v_0.shape)
    v_2 = second[:, 1 : 1 + CZ].reshape(v_0.shape)
    d_0 = d * v_0
    d_2 = d * v_2
    parts = [d_0 * v_0, d_0 * v_1, d * v_1 * v_1, d_2 * v_1, d_2 * v_2, None, v_0, v_1, v_2]
    found = jnp.zeros((2, LANES), jnp.float32)
    for index, part in enumerate(parts):
        if part is not None:
            total = jnp.sum(jnp.sum(part, axis=0), axis=1, keepdims=True)
            found = jnp.where(pair_place(index), total, found)
    line[...] = found


def apply_last_kernel(
    info, corners, edge, inner, before, spill_before, turned, line, moments,
    wide, packed, spills, edge_rest, inner_rest,
):
    widen([corners], [wide], 2.0)
    pack_upper_corners(info, wide, packed, spills)
    total = (jnp.zeros((8, LANES), jnp.float32), jnp.zeros((8, LANES), jnp.float32))
    for stored, rest in ((edge, edge_rest), (inner, inner_rest)):
        total = upper_corner_cells(
            stored, before, spill_before, turned, packed, spills, rest, total
        )
    last = [jnp.sum(part, axis=0, keepdims=True) for part in total]
    last = PAIR_SCALE * jnp.sum(jnp.concatenate(last, axis=0), axis=1, keepdims=True)
    found = jnp.where(pair_place(5), last, line[...])
    moments[...] = jnp.sum(found, axis=0, keepdims=True)


def wide(piece):
    return VMEM((piece.shape[0], 8, LANES), jnp.float32)


def apply_core(info, core, stored):
    stored = pltpu.with_memory_space_constraint(stored, VMEM)
    scratch = [wide(core)] + packs(4)
    return call(apply_core_kernel, (SUMS, CORE_SPILL), scratch, 2, info, core, stored)


def apply_faces(infos, pieces, stored, before, spill):
    stored = pltpu.with_memory_space_constraint(stored, VMEM)
    scratch = [wide(piece) for piece in pieces] + packs(8)
    return call(
        apply_face_kernel, (SUMS, SPILL), scratch, 2, *infos, *pieces, stored, before, spill
    )


def apply_upper_faces(infos, pieces, stored, before, spill):
    stored = pltpu.with_memory_space_constraint(stored, VMEM)
    scratch = [wide(piece) for piece in pieces] + packs(8)
    return call(
        upper_face_kernel, (SUMS, SPILL), scratch, 2, *infos, *pieces, stored, before, spill
    )


def apply_corners(info, corners, stored, before, spill, core):
    stored = pltpu.with_memory_space_constraint(stored, VMEM)
    cells = stored.shape[0]
    arrays = [info, corners, stored, before, spill, core]
    scratch = [wide(corners)] + corner_scratch(cells)
    return call(apply_corner_kernel, pairs(cells), scratch, 2, *arrays)


def apply_last_core(info, core, stored, slots, first, second):
    stored = pltpu.with_memory_space_constraint(stored, VMEM)
    outs = (SUMS, CORE_SPILL, SUMS, jax.ShapeDtypeStruct((2, LANES), jnp.float32))
    scratch = [wide(core)] + packs(4)
    return call(last_core_kernel, outs, scratch, 2, info, core, stored, slots, first, second)


def apply_last(info, corners, edge, inner, before, spill, turned, line):
    edge = pltpu.with_memory_space_constraint(edge, VMEM)
    inner = pltpu.with_memory_space_constraint(inner, VMEM)
    arrays = [info, corners, edge, inner, before, spill, turned, line]
    scratch = [wide(corners)] + packs(4)
    scratch += [VMEM((cells, 8, LANES), jnp.float32) for cells in (EDGES, INNER)]
    out = jax.ShapeDtypeStruct((1, LANES), jnp.float32)
    return call(apply_last_kernel, out, scratch, 2, *arrays)


def solve(g):
    tiny = 1e-6
    h = [g[k] + g[k + 1] for k in range(5)]
    ratio_1 = h[1] / h[0]
    ratio_2 = h[2] / h[0]
    pivot_1 = h[2] - ratio_1 * h[1]
    mixed = h[3] - ratio_1 * h[2]
    rest_1 = g[1] - ratio_1 * g[0]
    live_1 = pivot_1 > tiny * h[2]
    safe_1 = jnp.where(live_1, pivot_1, 1.0)
    ratio_3 = jnp.where(live_1, mixed / safe_1, 0.0)
    pivot_2 = h[4] - ratio_2 * h[2] - ratio_3 * mixed
    rest_2 = g[2] - ratio_2 * g[0] - ratio_3 * rest_1
    live_2 = live_1 & (pivot_2 > tiny * h[4])
    c_2 = jnp.where(live_2, rest_2 / jnp.where(live_2, pivot_2, 1.0), 0.0)
    c_1 = jnp.where(live_1, (rest_1 - mixed * c_2) / safe_1, 0.0)
    c_0 = (g[0] - h[1] * c_1 - h[2] * c_2) / h[0]
    return c_0, c_1, c_2


def invert(counts, atoms, places):
    rows = places.shape[1]
    row_low = row_index((LANES, LANES))
    row_high = row_index((rows, LANES))
    lane = lane_index((rows, LANES))

    def one_cell(cell, total):
        live = lane_index((1, LANES)) < counts[cell]
        pointer = jnp.where(live, atoms[pl.ds(cell, 1), :], -1)
        here = (pointer >> 7) == row_high
        cells = jnp.where(here, cell, 0).astype(jnp.float32)
        slots = jnp.where(here, lane, 0).astype(jnp.float32)
        parts = jnp.concatenate([cells, slots], axis=0).astype(jnp.bfloat16)
        lows = jnp.where((pointer & 127) == row_low, 1.0, 0.0).astype(jnp.bfloat16)
        return total + lax.dot_general(
            parts, lows, (((1,), (1,)), ((), ())), preferred_element_type=jnp.float32
        )

    total = jnp.zeros((2 * rows, LANES), jnp.float32)
    total = lax.fori_loop(0, CELLS, one_cell, total, unroll=8).astype(jnp.int32)
    places[0] = total[:rows]
    places[1] = total[rows:]


def inverted(counts, atoms, atoms_local):
    rows = (atoms_local // LANES + 15) // 16 * 16
    return call(invert, jax.ShapeDtypeStruct((2, rows, LANES), jnp.int32), [], 2, counts, atoms)


def finish_kernel(moments, slots, first, second, places, out, charges):
    summed = moments[...]
    lane = lane_index((2, LANES))
    row = row_index((2, LANES))

    def pair(index):
        picked = jnp.where(lane - row == 2 * index, summed, 0.0)
        return jnp.broadcast_to(jnp.sum(picked, axis=1, keepdims=True), (2, LANES))

    rows = [pair(index) for index in range(9)]
    c_0, c_1, c_2 = solve(rows[:6])
    totals = c_0 * rows[6] + c_1 * rows[7] + c_2 * rows[8]
    balance = totals[0:1] / totals[1:2]
    sign = jnp.concatenate([jnp.ones((1, LANES), jnp.float32), -balance], axis=0)
    c_0, c_1, c_2 = c_0 * sign, c_1 * sign, c_2 * sign
    for cell in range(CELLS):
        q, z = cell // CZ, cell % CZ + 1
        mixed = c_0 * slots[q, z, 4:6, :] + c_1 * first[q, z] + c_2 * second[q, z]
        charges[cell : cell + 1, :] = jnp.sum(mixed, axis=0, keepdims=True)
    tiles = [jnp.zeros((8, LANES), jnp.float32) for _ in range(places.shape[1] // 8)]
    for cell in range(CELLS):
        line = spread(charges[cell : cell + 1, :])
        for at in range(len(tiles)):
            here = slice(8 * at, 8 * at + 8)
            moved = jnp.take_along_axis(line, places[1, here, :], axis=1)
            tiles[at] = jnp.where(places[0, here, :] == cell, moved, tiles[at])
    out[...] = jnp.concatenate(tiles, axis=0)[: out.shape[0]]


def finish(moments, slots, first, second, places, atoms_local):
    return pl.pallas_call(
        finish_kernel,
        out_shape=jax.ShapeDtypeStruct((atoms_local // LANES, LANES), jnp.float32),
        in_specs=[IN_VMEM] * 5,
        out_specs=IN_VMEM,
        scratch_shapes=[VMEM((CELLS, LANES), jnp.float32)],
        compiler_params=params(8),
    )(moments, slots, first, second, places)


def partner(block, axis, mask):
    count = lax.axis_size(axis)
    return lax.ppermute(block, axis, [(low, low ^ mask) for low in range(count)])


def shifted(block, along_x, across_y=0):
    count = lax.axis_size("gx")
    route = [(i, ((i + 4 * along_x) % count) ^ (2 * across_y)) for i in range(count)]
    return lax.ppermute(block, "gx", route)


def with_z_faces(edge, inner):
    other = partner(edge, "gx", 1)
    parts = [other[:, 0:1], edge[:, 1:2], inner, edge[:, 0:1], other[:, 1:2]]
    return jnp.concatenate(parts, axis=1)


def flat(columns):
    return columns.reshape((-1,) + columns.shape[-2:])


def x_faces(core):
    count = lax.axis_size("gx")
    rows = count // 4
    odd = (lax.axis_index("gx") // 4) % 2 == 1
    if rows % 2:
        return shifted(core[2:], 1), shifted(core[:2], -1)
    route = [(i, (i + (4 if (i // 4) % 2 else -4)) % count) for i in range(count)]
    second = lax.ppermute(jnp.where(odd, core[2:], core[:2]), "gx", route)
    first = lax.ppermute(jnp.where(odd, core[:2], core[2:]), "gx", [(i, i ^ 4) for i in range(count)])
    return first, second


def sorted_faces(first, second):
    odd = (lax.axis_index("gx") // 4) % 2 == 1
    if (lax.axis_size("gx") // 4) % 2:
        return first, second
    return jnp.where(odd, first, second), jnp.where(odd, second, first)


def exchange(edge, inner, on_core, on_faces, on_corners, faces_last=False):
    core = with_z_faces(edge, inner)
    first, second = x_faces(core)
    beyond = partner(core, "gx", 2)
    sums, spill, *more = on_core(flat(core))
    if faces_last:
        second, first, beyond, sums = lax.optimization_barrier((second, first, beyond, sums))
    else:
        second, first, sums = lax.optimization_barrier((second, first, sums))
    low, high = sorted_faces(first, second)
    corners = partner(jnp.concatenate([low, high], axis=0), "gx", 2)
    pieces = [flat(part) for part in (low, high, beyond)]
    sums, spill, *more = on_faces(pieces, sums, spill, *more)
    corners = flat(corners)
    return core, pieces, corners, on_corners(corners, sums, spill, core, *more)


def global_sum(values):
    count = lax.axis_size("gx")
    if count & (count - 1):
        return lax.psum(values, "gx")
    step = 1
    while step < count:
        if step >= 2 and 4 * step <= count:
            others = [partner(values, "gx", k * step) for k in (3, 2, 1)]
            values = (values + others[0]) + (others[1] + others[2])
            step *= 4
        else:
            values = values + partner(values, "gx", step)
            step *= 2
    return values


def local(cell_offsets, electronegativity, hardness, charge_widths, cell_counts, cell_atoms):
    edge, inner = prepare(
        cell_counts, cell_offsets, electronegativity, hardness, charge_widths, cell_atoms
    )
    stored = []

    def keep(tiles, *others):
        stored.append(tiles)
        return others

    def build_ends(corners, sums, spill, core, *own):
        (edge,) = keep(*build_corners(EDGES, corners, *own, sums, spill, flat(core)))
        (inner,) = keep(*build_corners(INNER, corners, *own, sums, spill, flat(core)))
        return by_column(edge), by_column(inner)

    def by_column(cells):
        return cells.reshape((QUADS, -1) + cells.shape[1:])

    slots, pieces, corners, ends = exchange(
        by_column(edge),
        by_column(inner),
        lambda core: keep(*build_core(core)),
        lambda faces, sums, spill, *own: keep(*build_faces(faces, *own, sums, spill)) + own,
        build_ends,
        faces_last=True,
    )
    info = flat(slots)

    def apply(edge, inner, on_corners):
        return exchange(
            edge,
            inner,
            lambda own: apply_core(info, own, stored[0]),
            lambda faces, sums, spill: apply_faces(pieces, faces, stored[1], sums, spill),
            on_corners,
        )

    def apply_ends(others, sums, spill, _):
        edge = apply_corners(corners, others, stored[2], sums, spill, info)
        inner = apply_corners(corners, others, stored[3], sums, spill, info)
        return by_column(edge), by_column(inner)

    first, _, _, ends = apply(*ends, apply_ends)
    second = with_z_faces(*ends)
    high = shifted(second[:2], -1)
    beyond = partner(second, "gx", 2)
    corner = shifted(second[:2], -1, 1)
    sums, spill, turned, line = apply_last_core(
        info, flat(second), stored[0], slots, first, second
    )
    high, beyond, sums = lax.optimization_barrier((high, beyond, sums))
    upper = [flat(high), flat(beyond)]
    sums, spill = apply_upper_faces(pieces[1:], upper, stored[1], sums, spill)
    corner, sums = lax.optimization_barrier((corner, sums))
    moments = apply_last(
        corners, flat(corner), stored[2], stored[3], sums, spill, turned, line
    )
    moments, cell_counts, cell_atoms = lax.optimization_barrier((moments, cell_counts, cell_atoms))
    atoms_local = cell_offsets.shape[1]
    places = inverted(cell_counts, cell_atoms, atoms_local)
    charges = finish(global_sum(moments), slots, first, second, places, atoms_local)
    return charges.reshape(-1)


def solution(mesh):
    placed = (
        P(None, ("grp", "gx")),
        P(("grp", "gx")),
        P(("grp", "gx")),
        P(("grp", "gx")),
        P(("grp", "gx")),
        P(("grp", "gx"), None),
    )
    return jax.shard_map(
        local, mesh=mesh, in_specs=placed, out_specs=P(("grp", "gx")), check_vma=False
    )
```

```python
import functools
import math

import jax
import jax.numpy as jnp
from jax import lax
from jax.experimental import pallas as pl
from jax.experimental.pallas import tpu as pltpu
from jax.sharding import PartitionSpec as P

CX = 2
CY = 2
CZ = 8
EZ = CZ + 2
CELLS = CX * CY * CZ
QUADS = CX * CY
LANES = 128
BLOCKS = 11
GROUPS = ((0, 1, 2, 3), (4, 5, 6, 7), (8, 9, 10))

COULOMB = 14.399645
ROOT_PI = math.sqrt(math.pi)
SCREEN = 1.0 / (math.sqrt(2.0) * 3.0)
EWALD_SELF = math.sqrt(2.0 / math.pi) / 3.0
SIDE = 12.0 * SCREEN
CUT_SQUARED = (12.0 * SCREEN) ** 2
CLOSEST_SQUARED = (0.5 * SCREEN) ** 2
PAIR_SCALE = COULOMB * SCREEN

VMEM = pltpu.VMEM
SMEM = pltpu.SMEM


def params(mib):
    return pltpu.CompilerParams(vmem_limit_bytes=mib * 2**20)


def lane_index(shape):
    return lax.broadcasted_iota(jnp.int32, shape, len(shape) - 1)


def row_index(shape):
    return lax.broadcasted_iota(jnp.int32, shape, len(shape) - 2)


def edge_place(slot):
    return slot // 2, (CZ - 1) * (1 - slot % 2)


def inner_place(slot):
    return slot // (CZ - 2), 1 + slot % (CZ - 2)


EDGES = 2 * QUADS
INNER = CELLS - EDGES
PLACES = {EDGES: edge_place, INNER: inner_place}
LAYERS = {EDGES: (0, CZ - 1), INNER: range(1, CZ - 1)}


def gather_cells(counted, atoms, table, others, out):
    place = PLACES[out.shape[0]]
    row = row_index((8, LANES))
    lane = lane_index((1, LANES))

    def pick(source, pointers):
        share = 8 // len(pointers)
        pointer = spread(pointers[-1])
        for k in range(len(pointers) - 2, -1, -1):
            pointer = jnp.where(row < share * (k + 1), pointers[k], pointer)
        high = pointer >> 7
        low = pointer & 127
        picked = jnp.zeros((8, LANES), jnp.float32)
        for chunk in range(source.shape[0]):
            part = jnp.take_along_axis(source[chunk], low, axis=1)
            picked = jnp.where(high == chunk, part, picked)
        return picked

    def four_cells(step, _):
        slots = [4 * step + k for k in range(4)]
        places = [place(slot) for slot in slots]
        counts = [counted[pl.ds(q * CZ + z, 1), :] for q, z in places]
        occupied = [lane < count for count in counts]
        pointers = [
            jnp.where(live, atoms[pl.ds(q * CZ + z, 1), :], 0)
            for (q, z), live in zip(places, occupied)
        ]
        pairs = [pick(table, pointers[:2]), pick(table, pointers[2:])]
        both = pick(others, pointers)
        for k, (slot, live) in enumerate(zip(slots, occupied)):
            q = places[k][0]
            at = 4 * (k % 2)
            picked = pairs[k // 2][at : at + 4]
            width = jnp.where(live, picked[3:4], 1.0)
            hard = both[2 * k + 1 : 2 * k + 2]
            diag = jnp.where(live, hard + COULOMB * (1.0 / (width * ROOT_PI) - EWALD_SELF), 1.0)
            negative = jnp.where(live, both[2 * k : 2 * k + 1], 0.0)
            out[slot, 0:1, :] = (picked[0:1] + (q // CY).astype(jnp.float32)) * SIDE
            out[slot, 1:2, :] = (picked[1:2] + (q % CY).astype(jnp.float32)) * SIDE
            out[slot, 2:3, :] = picked[2:3] * SIDE
            out[slot, 3:4, :] = (2.0 * SCREEN * SCREEN) * width * width
            out[slot, 4:5, :] = -negative / diag
            out[slot, 5:6, :] = jnp.where(live, 1.0 / diag, 0.0)
            out[slot, 6:7, :] = diag
            out[slot, 7:8, :] = counts[k].astype(jnp.float32)
        return 0

    lax.fori_loop(0, out.shape[0] // 4, four_cells, 0, unroll=2)


def prepare_kernel(
    counts_hbm, offsets, negativity, hardness, widths, atoms_hbm, edge, counted, atoms, table, others,
    counts, raw_offsets, raw_negativity, raw_hardness, raw_widths, sems,
):
    copies = [
        pltpu.make_async_copy(source, target, sems.at[index])
        for index, (source, target) in enumerate(
            [
                (counts_hbm, counts),
                (offsets, raw_offsets),
                (negativity, raw_negativity),
                (hardness, raw_hardness),
                (widths, raw_widths),
                (atoms_hbm, atoms),
            ]
        )
    ]
    for copy in copies:
        copy.start()
    for copy in copies:
        copy.wait()
    for chunk in range(table.shape[0]):
        here = slice(chunk * LANES, (chunk + 1) * LANES)
        for first in (0, 4):
            table[chunk, first : first + 3, :] = raw_offsets[:, here]
            table[chunk, first + 3 : first + 4, :] = raw_widths[chunk : chunk + 1, :]
        for first in (0, 2, 4, 6):
            others[chunk, first : first + 1, :] = raw_negativity[chunk : chunk + 1, :]
            others[chunk, first + 1 : first + 2, :] = raw_hardness[chunk : chunk + 1, :]
    for cell in range(CELLS):
        counted[cell : cell + 1, :] = jnp.full((1, LANES), counts[cell])
    gather_cells(counted, atoms, table, others, edge)


def prepare_rest_kernel(counted, atoms, table, others, inner):
    gather_cells(counted, atoms, table, others, inner)


def prepare(counts, offsets, negativity, hardness, widths, atoms):
    chunks = offsets.shape[1] // LANES
    plane = (chunks, LANES)
    tables = jax.ShapeDtypeStruct((chunks, 8, LANES), jnp.float32)
    lists = jax.ShapeDtypeStruct(atoms.shape, jnp.int32)
    edge, *rest = pl.pallas_call(
        prepare_kernel,
        out_shape=(
            jax.ShapeDtypeStruct((EDGES, 8, LANES), jnp.float32),
            lists,
            lists,
            tables,
            tables,
        ),
        in_specs=[pl.BlockSpec(memory_space=pltpu.HBM)] * 6,
        out_specs=(pl.BlockSpec(memory_space=VMEM),) * 5,
        scratch_shapes=[
            SMEM(counts.shape, jnp.int32),
            VMEM(offsets.shape, jnp.float32),
            VMEM(plane, jnp.float32),
            VMEM(plane, jnp.float32),
            VMEM(plane, jnp.float32),
            pltpu.SemaphoreType.DMA((6,)),
        ],
        compiler_params=params(8),
    )(
        *[
            pltpu.with_memory_space_constraint(array, pltpu.HBM)
            for array in (
                counts,
                offsets,
                negativity.reshape(plane),
                hardness.reshape(plane),
                widths.reshape(plane),
                atoms,
            )
        ]
    )
    inner = pl.pallas_call(
        prepare_rest_kernel,
        out_shape=jax.ShapeDtypeStruct((INNER, 8, LANES), jnp.float32),
        in_specs=[pl.BlockSpec(memory_space=VMEM)] * 4,
        out_specs=pl.BlockSpec(memory_space=VMEM),
        compiler_params=params(8),
        cost_estimate=pl.CostEstimate(flops=2**20, bytes_accessed=2**22, transcendentals=0),
    )(*rest)
    return edge, inner


def pack_column(
    info, cells, source, packed, spills, target, at, shift, layers=range(CZ), info_source=None
):
    lane = lane_index((8, LANES))
    row = row_index((8, LANES))
    for z in layers:
        base = source * EZ + z
        known = base if info_source is None else info_source * EZ + z
        low, mid, top = [spread(info[known + k, 7:8, :]).astype(jnp.int32) for k in range(3)]
        end = low + mid - LANES
        tiles = [cells[base + k] for k in range(3)]
        if shift is not None:
            for k in range(3):
                offset = jnp.where(row == 2, (k - 1) * SIDE, 0.0)
                for axis in range(2):
                    offset = jnp.where(row == axis, shift[axis] * SIDE, offset)
                tiles[k] = tiles[k] + offset
        second = jnp.take_along_axis(tiles[1], (lane - low) & 127, axis=1)
        third = jnp.take_along_axis(tiles[2], (lane - end) & 127, axis=1)
        packed[target * CZ + z, 0] = jnp.where(lane < low, tiles[0], second)
        packed[target * CZ + z, 1] = jnp.where(lane < end, second, third)
        spill = jnp.where(lane < end + top - LANES, third, 0.0)
        spills[target * CZ + z] = pltpu.roll(spill, at, 1) if at else spill


def pack_core(info, cells, packed, spills, build):
    for q in range(QUADS):
        pack_column(info, cells, q, packed, spills, q, 8 * q, (0, 0) if build else None)


def pack_faces(infos, pieces, packed, spills, build):
    for side in range(2):
        sign = 2 * side - 1
        for y in range(CY):
            shift = (sign * CX, 0) if build else None
            at = 32 + 8 * y
            pack_column(infos[side], pieces[side], y, packed, spills, 2 * side + y, at, shift)
        for x in range(CX):
            shift = (0, sign * CY) if build else None
            source = 2 * x + 1 - side
            target = 4 + 2 * x + side
            at = 48 + 8 * x
            pack_column(infos[2], pieces[2], source, packed, spills, target, at, shift)


def pack_corners(info, cells, packed, spills, build, layers):
    for side_x in range(2):
        for side_y in range(2):
            shift = ((2 * side_x - 1) * CX, (2 * side_y - 1) * CY) if build else None
            source = 2 * side_x + 1 - side_y
            target = 2 * side_x + side_y
            pack_column(info, cells, source, packed, spills, target, 64, shift, layers)


def pack_upper_faces(infos, pieces, packed, spills):
    for y in range(CY):
        pack_column(infos[0], pieces[0], y, packed, spills, 2 + y, 32 + 8 * y, None)
    for x in range(CX):
        pack_column(infos[1], pieces[1], 2 * x, packed, spills, 5 + 2 * x, 48 + 8 * x, None)


def pack_upper_corners(info, cells, packed, spills):
    for side_y in range(2):
        source = 1 - side_y
        pack_column(info, cells, source, packed, spills, 2 + side_y, 64, None, info_source=2 + source)


def upper_columns(q):
    columns = face_columns(q)
    return [columns[2 * k : 2 * k + 2] for k in range(2) if (q >> (1 - k)) & 1], 4 * (q == 1)


def core_columns(q):
    return [q ^ k for k in range(4)]


def face_columns(q):
    x, y = q >> 1, q & 1
    return [2 * x, 2 * x + 1, 4 + y, 6 + y]


def overflow_of(spills, columns, z):
    return sum(spills[column * CZ + z] for column in columns)


def spread(row):
    return jnp.broadcast_to(row, (8, LANES))


def couple(x_i, y_i, z_i, w_i, x_j, y_j, z_j, w_j):
    delta_x = x_j - x_i
    delta_y = y_j - y_i
    delta_z = z_j - z_i
    squared = delta_x * delta_x + delta_y * delta_y + delta_z * delta_z
    held = jnp.maximum(squared, CLOSEST_SQUARED)
    inverse = lax.rsqrt(held)
    distance = held * inverse
    scaled = distance * lax.rsqrt(w_i + w_j)
    value = (lax.erf(scaled) - lax.erf(distance)) * inverse
    return jnp.where(squared < CUT_SQUARED, value, 0.0)


def to_rows(sums, block):
    here = lane_index((8, LANES)) - row_index((8, LANES)) == 8 * block
    return jnp.where(here, jnp.sum(sums, axis=1, keepdims=True), 0.0)


def add_rows(cell, sums, rows):
    for index in range(2):
        total = jnp.zeros((8, LANES), jnp.float32)
        for block in range(BLOCKS):
            total = total + to_rows(sums[cell, block, index], block)
        rows.append(jnp.sum(total, axis=0, keepdims=True))


def finish_cell(slot, place, target, info, sums, out):
    q, z = place(slot)
    rows = []
    add_rows(slot, sums, rows)
    own = info.at[q * EZ + z + 1]
    scale = PAIR_SCALE / own[6:7, :]
    live = lane_index((1, LANES)) < own[7:8, :].astype(jnp.int32)
    out[target, 0:1, :] = jnp.where(live, rows[0] * scale, 0.0)
    out[target, 1:2, :] = jnp.where(live, rows[1] * scale, 0.0)


def build_cell(cell, slot, lines, turned, kernels, before, sums, below):
    own = None
    if below is not None:
        own = lane_index((8, LANES)) - row_index((8, LANES)) - below
    for group in GROUPS:
        sums_s, sums_t = start_sums(cell, before, group)
        mine = [[turned[cell, block, k] for k in range(4)] for block in group]
        for index, line in enumerate(lines):
            beside = [line(k) for k in range(6)]
            for at, block in enumerate(group):
                value = couple(*mine[at], *beside[:4])
                if own is not None and index < 2:
                    value = jnp.where(own == 8 * block - LANES * index, 0.0, value)
                kernels[slot, block, index] = value
                sums_s[at] = sums_s[at] + value * beside[4]
                sums_t[at] = sums_t[at] + value * beside[5]
        for at, block in enumerate(group):
            sums[slot, block, 0] = sums_s[at]
            sums[slot, block, 1] = sums_t[at]


def start_sums(cell, before, blocks):
    if before is None:
        zeros = [jnp.zeros((8, LANES), jnp.float32) for _ in blocks]
        return zeros, list(zeros)
    sums_s = [before[cell, block, 0] for block in blocks]
    return sums_s, [before[cell, block, 1] for block in blocks]


def lines_of(packed, columns, z):
    def line(column, half):
        return lambda k: spread(packed[column * CZ + z, half, k : k + 1, :])

    return [line(column, half) for column in columns for half in range(2)]


def rest_line(rest, cell):
    return lambda k: spread(rest[cell, k : k + 1, :])


def parts_of(value):
    high = value.astype(jnp.bfloat16).astype(jnp.float32)
    rest = value - high
    middle = rest.astype(jnp.bfloat16).astype(jnp.float32)
    return high, middle, rest - middle


def turn_cells(core, turned):
    chosen = row_index((24, 4 * LANES)) & 7
    ones = jnp.where(chosen == lane_index((24, 4 * LANES)) >> 7, 1.0, 0.0).astype(jnp.bfloat16)
    for cell in range(CELLS):
        here = core[(cell // CZ) * EZ + cell % CZ + 1]
        left = jnp.concatenate(parts_of(here), axis=0).T[: 8 * BLOCKS + 8].astype(jnp.bfloat16)
        wide = lax.dot_general(
            left, ones, (((1,), (0,)), ((), ())), preferred_element_type=jnp.float32
        )
        for block in range(BLOCKS):
            for k in range(4):
                turned[cell, block, k] = wide[8 * block : 8 * block + 8, k * LANES : (k + 1) * LANES]


def core_spills(spills, spill):
    for z in range(CZ):
        spill[z] = overflow_of(spills, range(QUADS), z)


def face_spills(spills, before, spill):
    for cell in range(CELLS):
        q, z = cell // CZ, cell % CZ
        spill[cell] = before[z] + overflow_of(spills, face_columns(q), z)


def corner_loop(start, stop, work, finish, sums):
    def one_cell(slot, _):
        finish(jnp.maximum(slot - 1, start))
        work(slot)
        return 0

    sums[start] = jnp.zeros(sums.shape[1:], jnp.float32)
    lax.fori_loop(start, stop, one_cell, 0, unroll=4)
    finish(stop - 1)


def corner_spills(spills, before, rest, place):
    for slot in range(rest.shape[0]):
        q, z = place(slot)
        rest[slot] = before[q * CZ + z] + spills[q * CZ + z]


def core_kernel(core, kernels, sums, spill, turned, packed, spills):
    turn_cells(core, turned)
    pack_core(core, core, packed, spills, True)
    core_spills(spills, spill)

    def one_cell(cell, _):
        q, z = cell // CZ, cell % CZ
        below = spread(core[q * EZ + z, 7:8, :]).astype(jnp.int32)
        lines = lines_of(packed, core_columns(q), z)
        build_cell(cell, cell, lines, turned, kernels, None, sums, below)
        return 0

    lax.fori_loop(0, CELLS, one_cell, 0, unroll=2)


def face_kernel(
    x_low, x_high, beyond, turned, before, spill_before, kernels, sums, spill, packed, spills
):
    pieces = [x_low, x_high, beyond]
    pack_faces(pieces, pieces, packed, spills, True)
    face_spills(spills, spill_before, spill)

    def one_cell(cell, _):
        lines = lines_of(packed, face_columns(cell // CZ), cell % CZ)
        build_cell(cell, cell, lines, turned, kernels, before, sums, None)
        return 0

    lax.fori_loop(0, CELLS, one_cell, 0, unroll=2)


def corner_kernel(
    corners, turned, before, spill_before, core, kernels, out, packed, spills, rest, sums
):
    slots = kernels.shape[0]
    place = PLACES[slots]
    pack_corners(corners, corners, packed, spills, True, LAYERS[slots])
    corner_spills(spills, spill_before, rest, place)

    def work(slot):
        q, z = place(slot)
        lines = lines_of(packed, [q], z) + [rest_line(rest, slot)]
        build_cell(q * CZ + z, slot, lines, turned, kernels, before, sums, None)

    def finish(slot):
        finish_cell(slot, place, slot, core, sums, out)

    corner_loop(0, slots, work, finish, sums)


IN_VMEM = pl.BlockSpec(memory_space=VMEM)
IN_SMEM = pl.BlockSpec(memory_space=SMEM)
PAIR = jax.ShapeDtypeStruct((CELLS, 2, LANES), jnp.float32)
SPILL = jax.ShapeDtypeStruct((CELLS, 8, LANES), jnp.float32)
SUMS = jax.ShapeDtypeStruct((CELLS, BLOCKS, 2, 8, LANES), jnp.float32)
TURNED = jax.ShapeDtypeStruct((CELLS, BLOCKS, 4, 8, LANES), jnp.float32)
CORE_SPILL = jax.ShapeDtypeStruct((CZ, 8, LANES), jnp.float32)
CORE_TILES, FACE_TILES, CORNER_TILES = 8, 8, 3


def held(tiles, cells=CELLS):
    return VMEM((cells, BLOCKS, tiles, 8, LANES), jnp.float32)


def pairs(cells):
    return jax.ShapeDtypeStruct((cells, 2, LANES), jnp.float32)


def call(kernel, outs, scratch, tiles, *arrays):
    work = CELLS * BLOCKS * tiles * 8 * LANES
    return pl.pallas_call(
        kernel,
        out_shape=outs,
        in_specs=[IN_SMEM if array.ndim == 1 else IN_VMEM for array in arrays],
        out_specs=jax.tree.map(lambda _: IN_VMEM, outs),
        scratch_shapes=scratch,
        compiler_params=params(8),
        cost_estimate=pl.CostEstimate(
            flops=30 * work, bytes_accessed=8 * work, transcendentals=4 * work
        ),
    )(*arrays)


def packs(columns):
    return [
        VMEM((columns * CZ, 2, 8, LANES), jnp.float32),
        VMEM((columns * CZ, 8, LANES), jnp.float32),
    ]


def build_core(core):
    outs = (held(CORE_TILES), SUMS, CORE_SPILL, TURNED)
    return call(core_kernel, outs, packs(4), CORE_TILES, core)


def build_faces(pieces, turned, before, spill):
    outs = (held(FACE_TILES), SUMS, SPILL)
    return call(face_kernel, outs, packs(8), FACE_TILES, *pieces, turned, before, spill)


def corner_scratch(cells):
    rest = VMEM((cells, 8, LANES), jnp.float32)
    return packs(4) + [rest, VMEM((cells, BLOCKS, 2, 8, LANES), jnp.float32)]


def build_corners(cells, corners, turned, before, spill, core):
    outs = (held(CORNER_TILES, cells), pairs(cells))
    arrays = [corners, turned, before, spill, core]
    return call(corner_kernel, outs, corner_scratch(cells), CORNER_TILES, *arrays)


def cell_sums(cell, slot, lines, stored, before, first=0):
    sums_s, sums_t = start_sums(cell, before, range(BLOCKS))
    for index, line in enumerate(lines):
        line_s, line_t = line(0), line(1)
        for block in range(BLOCKS):
            value = stored[slot, block, first + index]
            sums_s[block] = sums_s[block] + value * line_s
            sums_t[block] = sums_t[block] + value * line_t
    return sums_s, sums_t


def apply_cell(cell, slot, lines, stored, before, sums, first=0):
    sums_s, sums_t = cell_sums(cell, slot, lines, stored, before, first)
    for block in range(BLOCKS):
        sums[slot, block, 0] = sums_s[block]
        sums[slot, block, 1] = sums_t[block]


def widen(pieces, wides, scale=None):
    for piece, wide in zip(pieces, wides):
        wide[:, 0:2, :] = piece[...] if scale is None else scale * piece[...]


def apply_core_kernel(info, core, stored, sums, spill, wide, packed, spills):
    widen([core], [wide])
    pack_core(info, wide, packed, spills, False)
    core_spills(spills, spill)

    def one_cell(cell, _):
        lines = lines_of(packed, core_columns(cell // CZ), cell % CZ)
        apply_cell(cell, cell, lines, stored, None, sums)
        return 0

    lax.fori_loop(0, CELLS, one_cell, 0, unroll=4)


def apply_face_kernel(*refs):
    infos, pieces, (stored, before, spill_before, sums, spill), wides, (packed, spills) = split(
        refs, 3, 3, 5, 3, 2
    )
    widen(pieces, wides)
    pack_faces(infos, wides, packed, spills, False)
    face_spills(spills, spill_before, spill)

    def one_cell(cell, _):
        lines = lines_of(packed, face_columns(cell // CZ), cell % CZ)
        apply_cell(cell, cell, lines, stored, before, sums)
        return 0

    lax.fori_loop(0, CELLS, one_cell, 0, unroll=4)


def apply_corner_cells(stored, before, spill_before, core, out, packed, spills, rest, sums):
    slots = stored.shape[0]
    place = PLACES[slots]
    corner_spills(spills, spill_before, rest, place)

    def work(slot):
        q, z = place(slot)
        lines = lines_of(packed, [q], z) + [rest_line(rest, slot)]
        apply_cell(q * CZ + z, slot, lines, stored, before, sums)

    def finish(slot):
        finish_cell(slot, place, slot, core, sums, out)

    corner_loop(0, slots, work, finish, sums)


def upper_corner_cells(stored, before, spill_before, turned, packed, spills, rest, total):
    slots = stored.shape[0]
    place = PLACES[slots]
    for slot in range(slots):
        q, z = place(slot)
        tile = spill_before[q * CZ + z]
        rest[slot] = tile + spills[q * CZ + z] if q >= CY else tile

    def weigh(cell, sums, total):
        total_s, total_t = total
        for block in range(BLOCKS):
            total_s = total_s + sums[0][block] * turned[cell, block, 0]
            total_t = total_t + sums[1][block] * turned[cell, block, 1]
        return total_s, total_t

    def low(slot, total):
        q, z = place(slot)
        cell = q * CZ + z
        return weigh(cell, cell_sums(cell, slot, [rest_line(rest, slot)], stored, before, 2), total)

    def high(slot, total):
        q, z = place(slot)
        cell = q * CZ + z
        lines = lines_of(packed, [q], z) + [rest_line(rest, slot)]
        return weigh(cell, cell_sums(cell, slot, lines, stored, before), total)

    total = lax.fori_loop(0, slots // 2, low, total, unroll=4)
    return lax.fori_loop(slots // 2, slots, high, total, unroll=4)


def upper_face_kernel(
    info_high, info_beyond, high, beyond, stored, before, spill_before, sums, spill,
    wide_high, wide_beyond, packed, spills,
):
    wides = [wide_high, wide_beyond]
    widen([high, beyond], wides, 2.0)
    pack_upper_faces([info_high, info_beyond], wides, packed, spills)
    for cell in range(CELLS):
        q, z = cell // CZ, cell % CZ
        groups, _ = upper_columns(q)
        spill[cell] = sum([spills[c * CZ + z] for group in groups for c in group], spill_before[z])
    sums[0:CZ] = before[0:CZ]
    for q in range(1, QUADS):
        groups, first = upper_columns(q)
        columns = [column for group in groups for column in group]

        def one_cell(z, _, q=q, columns=columns, first=first):
            cell = q * CZ + z
            apply_cell(cell, cell, lines_of(packed, columns, z), stored, before, sums, first)
            return 0

        lax.fori_loop(0, CZ, one_cell, 0, unroll=4)


def apply_corner_kernel(
    info, corners, stored, before, spill_before, core, out, wide, packed, spills, rest, sums
):
    widen([corners], [wide])
    pack_corners(info, wide, packed, spills, False, LAYERS[stored.shape[0]])
    apply_corner_cells(
        stored, before, spill_before, core, out, packed, spills, rest, sums
    )


def split(refs, *sizes):
    parts = []
    for size in sizes:
        parts.append(refs[:size])
        refs = refs[size:]
    return parts


def turn_pairs(core, turned):
    row = row_index((8, 2 * LANES))
    chosen = ((row & 1) == lane_index((8, 2 * LANES)) >> 7) & (row < 6)
    ones = jnp.where(chosen, 1.0, 0.0).astype(jnp.bfloat16)
    for cell in range(CELLS):
        pair = core[(cell // CZ) * EZ + cell % CZ + 1]
        parts = jnp.concatenate(parts_of(pair) + (jnp.zeros_like(pair),), axis=0)
        left = parts.T[: 8 * BLOCKS + 8].astype(jnp.bfloat16)
        wide = lax.dot_general(
            left, ones, (((1,), (0,)), ((), ())), preferred_element_type=jnp.float32
        )
        for block in range(BLOCKS):
            for k in range(2):
                turned[cell, block, k] = wide[8 * block : 8 * block + 8, k * LANES : (k + 1) * LANES]


def pair_place(index):
    return lane_index((2, LANES)) - row_index((2, LANES)) == 2 * index


def last_core_kernel(
    info, core, stored, slots, first, second, sums, spill, turned, line, wide, packed, spills
):
    turn_pairs(core, turned)
    apply_core_kernel(info, core, stored, sums, spill, wide, packed, spills)
    d = slots[:, 1 : 1 + CZ, 6:7, :].reshape(CELLS, 1, LANES)
    v_0 = slots[:, 1 : 1 + CZ, 4:6, :].reshape(CELLS, 2, LANES)
    v_1 = first[:, 1 : 1 + CZ].reshape(v_0.shape)
    v_2 = second[:, 1 : 1 + CZ].reshape(v_0.shape)
    d_0 = d * v_0
    d_2 = d * v_2
    parts = [d_0 * v_0, d_0 * v_1, d * v_1 * v_1, d_2 * v_1, d_2 * v_2, None, v_0, v_1, v_2]
    found = jnp.zeros((2, LANES), jnp.float32)
    for index, part in enumerate(parts):
        if part is not None:
            total = jnp.sum(jnp.sum(part, axis=0), axis=1, keepdims=True)
            found = jnp.where(pair_place(index), total, found)
    line[...] = found


def apply_last_kernel(
    info, corners, edge, inner, before, spill_before, turned, line, moments,
    wide, packed, spills, edge_rest, inner_rest,
):
    widen([corners], [wide], 2.0)
    pack_upper_corners(info, wide, packed, spills)
    total = (jnp.zeros((8, LANES), jnp.float32), jnp.zeros((8, LANES), jnp.float32))
    for stored, rest in ((edge, edge_rest), (inner, inner_rest)):
        total = upper_corner_cells(
            stored, before, spill_before, turned, packed, spills, rest, total
        )
    last = [jnp.sum(part, axis=0, keepdims=True) for part in total]
    last = PAIR_SCALE * jnp.sum(jnp.concatenate(last, axis=0), axis=1, keepdims=True)
    found = jnp.where(pair_place(5), last, line[...])
    moments[...] = jnp.sum(found, axis=0, keepdims=True)


def wide(piece):
    return VMEM((piece.shape[0], 8, LANES), jnp.float32)


def apply_core(info, core, stored):
    stored = pltpu.with_memory_space_constraint(stored, VMEM)
    scratch = [wide(core)] + packs(4)
    return call(apply_core_kernel, (SUMS, CORE_SPILL), scratch, 2, info, core, stored)


def apply_faces(infos, pieces, stored, before, spill):
    stored = pltpu.with_memory_space_constraint(stored, VMEM)
    scratch = [wide(piece) for piece in pieces] + packs(8)
    return call(
        apply_face_kernel, (SUMS, SPILL), scratch, 2, *infos, *pieces, stored, before, spill
    )


def apply_upper_faces(infos, pieces, stored, before, spill):
    stored = pltpu.with_memory_space_constraint(stored, VMEM)
    scratch = [wide(piece) for piece in pieces] + packs(8)
    return call(
        upper_face_kernel, (SUMS, SPILL), scratch, 2, *infos, *pieces, stored, before, spill
    )


def apply_corners(info, corners, stored, before, spill, core):
    stored = pltpu.with_memory_space_constraint(stored, VMEM)
    cells = stored.shape[0]
    arrays = [info, corners, stored, before, spill, core]
    scratch = [wide(corners)] + corner_scratch(cells)
    return call(apply_corner_kernel, pairs(cells), scratch, 2, *arrays)


def apply_last_core(info, core, stored, slots, first, second):
    stored = pltpu.with_memory_space_constraint(stored, VMEM)
    outs = (SUMS, CORE_SPILL, SUMS, jax.ShapeDtypeStruct((2, LANES), jnp.float32))
    scratch = [wide(core)] + packs(4)
    return call(last_core_kernel, outs, scratch, 2, info, core, stored, slots, first, second)


def apply_last(info, corners, edge, inner, before, spill, turned, line):
    edge = pltpu.with_memory_space_constraint(edge, VMEM)
    inner = pltpu.with_memory_space_constraint(inner, VMEM)
    arrays = [info, corners, edge, inner, before, spill, turned, line]
    scratch = [wide(corners)] + packs(4)
    scratch += [VMEM((cells, 8, LANES), jnp.float32) for cells in (EDGES, INNER)]
    out = jax.ShapeDtypeStruct((1, LANES), jnp.float32)
    return call(apply_last_kernel, out, scratch, 2, *arrays)


def solve(g):
    tiny = 1e-6
    h = [g[k] + g[k + 1] for k in range(5)]
    ratio_1 = h[1] / h[0]
    ratio_2 = h[2] / h[0]
    pivot_1 = h[2] - ratio_1 * h[1]
    mixed = h[3] - ratio_1 * h[2]
    rest_1 = g[1] - ratio_1 * g[0]
    live_1 = pivot_1 > tiny * h[2]
    safe_1 = jnp.where(live_1, pivot_1, 1.0)
    ratio_3 = jnp.where(live_1, mixed / safe_1, 0.0)
    pivot_2 = h[4] - ratio_2 * h[2] - ratio_3 * mixed
    rest_2 = g[2] - ratio_2 * g[0] - ratio_3 * rest_1
    live_2 = live_1 & (pivot_2 > tiny * h[4])
    c_2 = jnp.where(live_2, rest_2 / jnp.where(live_2, pivot_2, 1.0), 0.0)
    c_1 = jnp.where(live_1, (rest_1 - mixed * c_2) / safe_1, 0.0)
    c_0 = (g[0] - h[1] * c_1 - h[2] * c_2) / h[0]
    return c_0, c_1, c_2


def invert(counts, atoms, places):
    rows = places.shape[1]
    row_low = row_index((LANES, LANES))
    row_high = row_index((rows, LANES))
    lane = lane_index((rows, LANES))

    def one_cell(cell, total):
        live = lane_index((1, LANES)) < counts[cell]
        pointer = jnp.where(live, atoms[pl.ds(cell, 1), :], -1)
        here = (pointer >> 7) == row_high
        cells = jnp.where(here, cell, 0).astype(jnp.float32)
        slots = jnp.where(here, lane, 0).astype(jnp.float32)
        parts = jnp.concatenate([cells, slots], axis=0).astype(jnp.bfloat16)
        lows = jnp.where((pointer & 127) == row_low, 1.0, 0.0).astype(jnp.bfloat16)
        return total + lax.dot_general(
            parts, lows, (((1,), (1,)), ((), ())), preferred_element_type=jnp.float32
        )

    total = jnp.zeros((2 * rows, LANES), jnp.float32)
    total = lax.fori_loop(0, CELLS, one_cell, total, unroll=8).astype(jnp.int32)
    places[0] = total[:rows]
    places[1] = total[rows:]


def inverted(counts, atoms, atoms_local):
    rows = (atoms_local // LANES + 15) // 16 * 16
    return call(invert, jax.ShapeDtypeStruct((2, rows, LANES), jnp.int32), [], 2, counts, atoms)


def finish_kernel(moments, slots, first, second, places, out, charges):
    summed = moments[...]
    lane = lane_index((2, LANES))
    row = row_index((2, LANES))

    def pair(index):
        picked = jnp.where(lane - row == 2 * index, summed, 0.0)
        return jnp.broadcast_to(jnp.sum(picked, axis=1, keepdims=True), (2, LANES))

    rows = [pair(index) for index in range(9)]
    c_0, c_1, c_2 = solve(rows[:6])
    totals = c_0 * rows[6] + c_1 * rows[7] + c_2 * rows[8]
    balance = totals[0:1] / totals[1:2]
    sign = jnp.concatenate([jnp.ones((1, LANES), jnp.float32), -balance], axis=0)
    c_0, c_1, c_2 = c_0 * sign, c_1 * sign, c_2 * sign
    for cell in range(CELLS):
        q, z = cell // CZ, cell % CZ + 1
        mixed = c_0 * slots[q, z, 4:6, :] + c_1 * first[q, z] + c_2 * second[q, z]
        charges[cell : cell + 1, :] = jnp.sum(mixed, axis=0, keepdims=True)
    tiles = [jnp.zeros((8, LANES), jnp.float32) for _ in range(places.shape[1] // 8)]
    for cell in range(CELLS):
        line = spread(charges[cell : cell + 1, :])
        for at in range(len(tiles)):
            here = slice(8 * at, 8 * at + 8)
            moved = jnp.take_along_axis(line, places[1, here, :], axis=1)
            tiles[at] = jnp.where(places[0, here, :] == cell, moved, tiles[at])
    out[...] = jnp.concatenate(tiles, axis=0)[: out.shape[0]]


def finish(moments, slots, first, second, places, atoms_local):
    return pl.pallas_call(
        finish_kernel,
        out_shape=jax.ShapeDtypeStruct((atoms_local // LANES, LANES), jnp.float32),
        in_specs=[IN_VMEM] * 5,
        out_specs=IN_VMEM,
        scratch_shapes=[VMEM((CELLS, LANES), jnp.float32)],
        compiler_params=params(8),
    )(moments, slots, first, second, places)


def partner(block, axis, mask):
    count = lax.axis_size(axis)
    return lax.ppermute(block, axis, [(low, low ^ mask) for low in range(count)])


def shifted(block, along_x, across_y=0):
    count = lax.axis_size("gx")
    route = [(i, ((i + 4 * along_x) % count) ^ (2 * across_y)) for i in range(count)]
    return lax.ppermute(block, "gx", route)


def with_z_faces(edge, inner):
    other = partner(edge, "gx", 1)
    parts = [other[:, 0:1], edge[:, 1:2], inner, edge[:, 0:1], other[:, 1:2]]
    return jnp.concatenate(parts, axis=1)


def flat(columns):
    return columns.reshape((-1,) + columns.shape[-2:])


def x_faces(core, across_y=0):
    count = lax.axis_size("gx")
    flip = 2 * across_y
    odd = (lax.axis_index("gx") // 4) % 2 == 1
    if (count // 4) % 2:
        return shifted(core[2:], 1, across_y), shifted(core[:2], -1, across_y)
    route = [(i, ((i + (4 if (i // 4) % 2 else -4)) % count) ^ flip) for i in range(count)]
    second = lax.ppermute(jnp.where(odd, core[2:], core[:2]), "gx", route)
    route = [(i, i ^ 4 ^ flip) for i in range(count)]
    first = lax.ppermute(jnp.where(odd, core[:2], core[2:]), "gx", route)
    return first, second


def sorted_faces(first, second):
    odd = (lax.axis_index("gx") // 4) % 2 == 1
    if (lax.axis_size("gx") // 4) % 2:
        return first, second
    return jnp.where(odd, first, second), jnp.where(odd, second, first)


def exchange(edge, inner, on_core, on_faces, on_corners, forward=False):
    core = with_z_faces(edge, inner)
    first, second = x_faces(core)
    beyond = partner(core, "gx", 2)
    diagonal = None if forward else x_faces(core, 1)
    sums, spill, *more = on_core(flat(core))
    if forward:
        second, first, beyond, sums = lax.optimization_barrier((second, first, beyond, sums))
    else:
        second, first, sums = lax.optimization_barrier((second, first, sums))
    low, high = sorted_faces(first, second)
    if forward:
        corners = partner(jnp.concatenate([low, high], axis=0), "gx", 2)
    pieces = [flat(part) for part in (low, high, beyond)]
    sums, spill, *more = on_faces(pieces, sums, spill, *more)
    if not forward:
        first, second, sums = lax.optimization_barrier((*diagonal, sums))
        corners = jnp.concatenate(sorted_faces(first, second), axis=0)
    corners = flat(corners)
    return core, pieces, corners, on_corners(corners, sums, spill, core, *more)


def global_sum(values):
    count = lax.axis_size("gx")
    if count & (count - 1):
        return lax.psum(values, "gx")
    step = 1
    while step < count:
        if step >= 2 and 4 * step <= count:
            others = [partner(values, "gx", k * step) for k in (3, 2, 1)]
            values = (values + others[0]) + (others[1] + others[2])
            step *= 4
        else:
            values = values + partner(values, "gx", step)
            step *= 2
    return values


def local(cell_offsets, electronegativity, hardness, charge_widths, cell_counts, cell_atoms):
    edge, inner = prepare(
        cell_counts, cell_offsets, electronegativity, hardness, charge_widths, cell_atoms
    )
    stored = []

    def keep(tiles, *others):
        stored.append(tiles)
        return others

    def build_ends(corners, sums, spill, core, *own):
        (edge,) = keep(*build_corners(EDGES, corners, *own, sums, spill, flat(core)))
        (inner,) = keep(*build_corners(INNER, corners, *own, sums, spill, flat(core)))
        return by_column(edge), by_column(inner)

    def by_column(cells):
        return cells.reshape((QUADS, -1) + cells.shape[1:])

    slots, pieces, corners, ends = exchange(
        by_column(edge),
        by_column(inner),
        lambda core: keep(*build_core(core)),
        lambda faces, sums, spill, *own: keep(*build_faces(faces, *own, sums, spill)) + own,
        build_ends,
        forward=True,
    )
    info = flat(slots)

    def apply(edge, inner, on_corners):
        return exchange(
            edge,
            inner,
            lambda own: apply_core(info, own, stored[0]),
            lambda faces, sums, spill: apply_faces(pieces, faces, stored[1], sums, spill),
            on_corners,
        )

    def apply_ends(others, sums, spill, _):
        edge = apply_corners(corners, others, stored[2], sums, spill, info)
        inner = apply_corners(corners, others, stored[3], sums, spill, info)
        return by_column(edge), by_column(inner)

    first, _, _, ends = apply(*ends, apply_ends)
    second = with_z_faces(*ends)
    high = shifted(second[:2], -1)
    beyond = partner(second, "gx", 2)
    corner = shifted(second[:2], -1, 1)
    sums, spill, turned, line = apply_last_core(
        info, flat(second), stored[0], slots, first, second
    )
    high, beyond, sums = lax.optimization_barrier((high, beyond, sums))
    upper = [flat(high), flat(beyond)]
    sums, spill = apply_upper_faces(pieces[1:], upper, stored[1], sums, spill)
    corner, sums = lax.optimization_barrier((corner, sums))
    moments = apply_last(
        corners, flat(corner), stored[2], stored[3], sums, spill, turned, line
    )
    moments, cell_counts, cell_atoms = lax.optimization_barrier((moments, cell_counts, cell_atoms))
    atoms_local = cell_offsets.shape[1]
    places = inverted(cell_counts, cell_atoms, atoms_local)
    charges = finish(global_sum(moments), slots, first, second, places, atoms_local)
    return charges.reshape(-1)


def solution(mesh):
    placed = (
        P(None, ("grp", "gx")),
        P(("grp", "gx")),
        P(("grp", "gx")),
        P(("grp", "gx")),
        P(("grp", "gx")),
        P(("grp", "gx"), None),
    )
    return jax.shard_map(
        local, mesh=mesh, in_specs=placed, out_specs=P(("grp", "gx")), check_vma=False
    )
```

```python
import functools
import math

import jax
import jax.numpy as jnp
from jax import lax
from jax.experimental import pallas as pl
from jax.experimental.pallas import tpu as pltpu
from jax.sharding import PartitionSpec as P

CX = 2
CY = 2
CZ = 8
EZ = CZ + 2
CELLS = CX * CY * CZ
QUADS = CX * CY
LANES = 128
BLOCKS = 11
GROUPS = ((0, 1, 2, 3), (4, 5, 6, 7), (8, 9, 10))

COULOMB = 14.399645
ROOT_PI = math.sqrt(math.pi)
SCREEN = 1.0 / (math.sqrt(2.0) * 3.0)
EWALD_SELF = math.sqrt(2.0 / math.pi) / 3.0
SIDE = 12.0 * SCREEN
CUT_SQUARED = (12.0 * SCREEN) ** 2
CLOSEST_SQUARED = (0.5 * SCREEN) ** 2
PAIR_SCALE = COULOMB * SCREEN

VMEM = pltpu.VMEM
SMEM = pltpu.SMEM


def params(mib):
    return pltpu.CompilerParams(vmem_limit_bytes=mib * 2**20)


def lane_index(shape):
    return lax.broadcasted_iota(jnp.int32, shape, len(shape) - 1)


def row_index(shape):
    return lax.broadcasted_iota(jnp.int32, shape, len(shape) - 2)


def edge_place(slot):
    return slot // 2, (CZ - 1) * (1 - slot % 2)


def inner_place(slot):
    return slot // (CZ - 2), 1 + slot % (CZ - 2)


EDGES = 2 * QUADS
INNER = CELLS - EDGES
PLACES = {EDGES: edge_place, INNER: inner_place}
LAYERS = {EDGES: (0, CZ - 1), INNER: range(1, CZ - 1)}


def gather_cells(counted, atoms, table, others, out):
    place = PLACES[out.shape[0]]
    row = row_index((8, LANES))
    lane = lane_index((1, LANES))

    def pick(source, pointers):
        share = 8 // len(pointers)
        pointer = spread(pointers[-1])
        for k in range(len(pointers) - 2, -1, -1):
            pointer = jnp.where(row < share * (k + 1), pointers[k], pointer)
        high = pointer >> 7
        low = pointer & 127
        picked = jnp.zeros((8, LANES), jnp.float32)
        for chunk in range(source.shape[0]):
            part = jnp.take_along_axis(source[chunk], low, axis=1)
            picked = jnp.where(high == chunk, part, picked)
        return picked

    def four_cells(step, _):
        slots = [4 * step + k for k in range(4)]
        places = [place(slot) for slot in slots]
        counts = [counted[pl.ds(q * CZ + z, 1), :] for q, z in places]
        occupied = [lane < count for count in counts]
        pointers = [
            jnp.where(live, atoms[pl.ds(q * CZ + z, 1), :], 0)
            for (q, z), live in zip(places, occupied)
        ]
        pairs = [pick(table, pointers[:2]), pick(table, pointers[2:])]
        both = pick(others, pointers)
        for k, (slot, live) in enumerate(zip(slots, occupied)):
            q = places[k][0]
            at = 4 * (k % 2)
            picked = pairs[k // 2][at : at + 4]
            width = jnp.where(live, picked[3:4], 1.0)
            hard = both[2 * k + 1 : 2 * k + 2]
            diag = jnp.where(live, hard + COULOMB * (1.0 / (width * ROOT_PI) - EWALD_SELF), 1.0)
            negative = jnp.where(live, both[2 * k : 2 * k + 1], 0.0)
            out[slot, 0:1, :] = (picked[0:1] + (q // CY).astype(jnp.float32)) * SIDE
            out[slot, 1:2, :] = (picked[1:2] + (q % CY).astype(jnp.float32)) * SIDE
            out[slot, 2:3, :] = picked[2:3] * SIDE
            out[slot, 3:4, :] = (2.0 * SCREEN * SCREEN) * width * width
            out[slot, 4:5, :] = -negative / diag
            out[slot, 5:6, :] = jnp.where(live, 1.0 / diag, 0.0)
            out[slot, 6:7, :] = diag
            out[slot, 7:8, :] = counts[k].astype(jnp.float32)
        return 0

    lax.fori_loop(0, out.shape[0] // 4, four_cells, 0, unroll=2)


def prepare_kernel(
    counts_hbm, offsets, negativity, hardness, widths, atoms_hbm, edge, counted, atoms, table, others,
    counts, raw_offsets, raw_negativity, raw_hardness, raw_widths, sems,
):
    copies = [
        pltpu.make_async_copy(source, target, sems.at[index])
        for index, (source, target) in enumerate(
            [
                (counts_hbm, counts),
                (offsets, raw_offsets),
                (negativity, raw_negativity),
                (hardness, raw_hardness),
                (widths, raw_widths),
                (atoms_hbm, atoms),
            ]
        )
    ]
    for copy in copies:
        copy.start()
    for copy in copies:
        copy.wait()
    for chunk in range(table.shape[0]):
        here = slice(chunk * LANES, (chunk + 1) * LANES)
        for first in (0, 4):
            table[chunk, first : first + 3, :] = raw_offsets[:, here]
            table[chunk, first + 3 : first + 4, :] = raw_widths[chunk : chunk + 1, :]
        for first in (0, 2, 4, 6):
            others[chunk, first : first + 1, :] = raw_negativity[chunk : chunk + 1, :]
            others[chunk, first + 1 : first + 2, :] = raw_hardness[chunk : chunk + 1, :]
    for cell in range(CELLS):
        counted[cell : cell + 1, :] = jnp.full((1, LANES), counts[cell])
    gather_cells(counted, atoms, table, others, edge)


def prepare_rest_kernel(counted, atoms, table, others, inner):
    gather_cells(counted, atoms, table, others, inner)


def prepare(counts, offsets, negativity, hardness, widths, atoms):
    chunks = offsets.shape[1] // LANES
    plane = (chunks, LANES)
    tables = jax.ShapeDtypeStruct((chunks, 8, LANES), jnp.float32)
    lists = jax.ShapeDtypeStruct(atoms.shape, jnp.int32)
    edge, *rest = pl.pallas_call(
        prepare_kernel,
        out_shape=(
            jax.ShapeDtypeStruct((EDGES, 8, LANES), jnp.float32),
            lists,
            lists,
            tables,
            tables,
        ),
        in_specs=[pl.BlockSpec(memory_space=pltpu.HBM)] * 6,
        out_specs=(pl.BlockSpec(memory_space=VMEM),) * 5,
        scratch_shapes=[
            SMEM(counts.shape, jnp.int32),
            VMEM(offsets.shape, jnp.float32),
            VMEM(plane, jnp.float32),
            VMEM(plane, jnp.float32),
            VMEM(plane, jnp.float32),
            pltpu.SemaphoreType.DMA((6,)),
        ],
        compiler_params=params(8),
    )(
        *[
            pltpu.with_memory_space_constraint(array, pltpu.HBM)
            for array in (
                counts,
                offsets,
                negativity.reshape(plane),
                hardness.reshape(plane),
                widths.reshape(plane),
                atoms,
            )
        ]
    )
    inner = pl.pallas_call(
        prepare_rest_kernel,
        out_shape=jax.ShapeDtypeStruct((INNER, 8, LANES), jnp.float32),
        in_specs=[pl.BlockSpec(memory_space=VMEM)] * 4,
        out_specs=pl.BlockSpec(memory_space=VMEM),
        compiler_params=params(8),
        cost_estimate=pl.CostEstimate(flops=2**20, bytes_accessed=2**22, transcendentals=0),
    )(*rest)
    return edge, inner


def pack_column(
    info, cells, source, packed, spills, target, at, shift, layers=range(CZ), info_source=None
):
    lane = lane_index((8, LANES))
    row = row_index((8, LANES))
    for z in layers:
        base = source * EZ + z
        known = base if info_source is None else info_source * EZ + z
        low, mid, top = [spread(info[known + k, 7:8, :]).astype(jnp.int32) for k in range(3)]
        end = low + mid - LANES
        tiles = [cells[base + k] for k in range(3)]
        if shift is not None:
            for k in range(3):
                offset = jnp.where(row == 2, (k - 1) * SIDE, 0.0)
                for axis in range(2):
                    offset = jnp.where(row == axis, shift[axis] * SIDE, offset)
                tiles[k] = tiles[k] + offset
        second = jnp.take_along_axis(tiles[1], (lane - low) & 127, axis=1)
        third = jnp.take_along_axis(tiles[2], (lane - end) & 127, axis=1)
        packed[target * CZ + z, 0] = jnp.where(lane < low, tiles[0], second)
        packed[target * CZ + z, 1] = jnp.where(lane < end, second, third)
        spill = jnp.where(lane < end + top - LANES, third, 0.0)
        spills[target * CZ + z] = pltpu.roll(spill, at, 1) if at else spill


def pack_core(info, cells, packed, spills, build):
    for q in range(QUADS):
        pack_column(info, cells, q, packed, spills, q, 8 * q, (0, 0) if build else None)


def pack_faces(infos, pieces, packed, spills, build):
    for side in range(2):
        sign = 2 * side - 1
        for y in range(CY):
            shift = (sign * CX, 0) if build else None
            at = 32 + 8 * y
            pack_column(infos[side], pieces[side], y, packed, spills, 2 * side + y, at, shift)
        for x in range(CX):
            shift = (0, sign * CY) if build else None
            source = 2 * x + 1 - side
            target = 4 + 2 * x + side
            at = 48 + 8 * x
            pack_column(infos[2], pieces[2], source, packed, spills, target, at, shift)


def pack_corners(info, cells, packed, spills, build, layers):
    for side_x in range(2):
        for side_y in range(2):
            shift = ((2 * side_x - 1) * CX, (2 * side_y - 1) * CY) if build else None
            source = 2 * side_x + 1 - side_y
            target = 2 * side_x + side_y
            pack_column(info, cells, source, packed, spills, target, 64, shift, layers)


def pack_upper_faces(infos, pieces, packed, spills):
    for y in range(CY):
        pack_column(infos[0], pieces[0], y, packed, spills, 2 + y, 32 + 8 * y, None)
    for x in range(CX):
        pack_column(infos[1], pieces[1], 2 * x, packed, spills, 5 + 2 * x, 48 + 8 * x, None)


def pack_upper_corners(info, cells, packed, spills):
    for side_y in range(2):
        source = 1 - side_y
        pack_column(info, cells, source, packed, spills, 2 + side_y, 64, None, info_source=2 + source)


def upper_columns(q):
    columns = face_columns(q)
    return [columns[2 * k : 2 * k + 2] for k in range(2) if (q >> (1 - k)) & 1], 4 * (q == 1)


def core_columns(q):
    return [q ^ k for k in range(4)]


def face_columns(q):
    x, y = q >> 1, q & 1
    return [2 * x, 2 * x + 1, 4 + y, 6 + y]


def overflow_of(spills, columns, z):
    return sum(spills[column * CZ + z] for column in columns)


def spread(row):
    return jnp.broadcast_to(row, (8, LANES))


def couple(x_i, y_i, z_i, w_i, x_j, y_j, z_j, w_j):
    delta_x = x_j - x_i
    delta_y = y_j - y_i
    delta_z = z_j - z_i
    squared = delta_x * delta_x + delta_y * delta_y + delta_z * delta_z
    held = jnp.maximum(squared, CLOSEST_SQUARED)
    inverse = lax.rsqrt(held)
    distance = held * inverse
    scaled = distance * lax.rsqrt(w_i + w_j)
    value = (lax.erf(scaled) - lax.erf(distance)) * inverse
    return jnp.where(squared < CUT_SQUARED, value, 0.0)


def to_rows(sums, block):
    here = lane_index((8, LANES)) - row_index((8, LANES)) == 8 * block
    return jnp.where(here, jnp.sum(sums, axis=1, keepdims=True), 0.0)


def add_rows(cell, sums, rows):
    for index in range(2):
        total = jnp.zeros((8, LANES), jnp.float32)
        for block in range(BLOCKS):
            total = total + to_rows(sums[cell, block, index], block)
        rows.append(jnp.sum(total, axis=0, keepdims=True))


def finish_cell(slot, place, target, info, sums, out):
    q, z = place(slot)
    rows = []
    add_rows(slot, sums, rows)
    own = info.at[q * EZ + z + 1]
    scale = PAIR_SCALE / own[6:7, :]
    live = lane_index((1, LANES)) < own[7:8, :].astype(jnp.int32)
    out[target, 0:1, :] = jnp.where(live, rows[0] * scale, 0.0)
    out[target, 1:2, :] = jnp.where(live, rows[1] * scale, 0.0)


def build_cell(cell, slot, lines, turned, kernels, before, sums, below):
    own = None
    if below is not None:
        own = lane_index((8, LANES)) - row_index((8, LANES)) - below
    for group in GROUPS:
        sums_s, sums_t = start_sums(cell, before, group)
        mine = [[turned[cell, block, k] for k in range(4)] for block in group]
        for index, line in enumerate(lines):
            beside = [line(k) for k in range(6)]
            for at, block in enumerate(group):
                value = couple(*mine[at], *beside[:4])
                if own is not None and index < 2:
                    value = jnp.where(own == 8 * block - LANES * index, 0.0, value)
                kernels[slot, block, index] = value
                sums_s[at] = sums_s[at] + value * beside[4]
                sums_t[at] = sums_t[at] + value * beside[5]
        for at, block in enumerate(group):
            sums[slot, block, 0] = sums_s[at]
            sums[slot, block, 1] = sums_t[at]


def start_sums(cell, before, blocks):
    if before is None:
        zeros = [jnp.zeros((8, LANES), jnp.float32) for _ in blocks]
        return zeros, list(zeros)
    sums_s = [before[cell, block, 0] for block in blocks]
    return sums_s, [before[cell, block, 1] for block in blocks]


def lines_of(packed, columns, z):
    def line(column, half):
        return lambda k: spread(packed[column * CZ + z, half, k : k + 1, :])

    return [line(column, half) for column in columns for half in range(2)]


def rest_line(rest, cell):
    return lambda k: spread(rest[cell, k : k + 1, :])


def parts_of(value):
    high = value.astype(jnp.bfloat16).astype(jnp.float32)
    rest = value - high
    middle = rest.astype(jnp.bfloat16).astype(jnp.float32)
    return high, middle, rest - middle


def turn_cells(core, turned):
    chosen = row_index((24, 4 * LANES)) & 7
    ones = jnp.where(chosen == lane_index((24, 4 * LANES)) >> 7, 1.0, 0.0).astype(jnp.bfloat16)
    for cell in range(CELLS):
        here = core[(cell // CZ) * EZ + cell % CZ + 1]
        left = jnp.concatenate(parts_of(here), axis=0).T[: 8 * BLOCKS + 8].astype(jnp.bfloat16)
        wide = lax.dot_general(
            left, ones, (((1,), (0,)), ((), ())), preferred_element_type=jnp.float32
        )
        for block in range(BLOCKS):
            for k in range(4):
                turned[cell, block, k] = wide[8 * block : 8 * block + 8, k * LANES : (k + 1) * LANES]


def core_spills(spills, spill):
    for z in range(CZ):
        spill[z] = overflow_of(spills, range(QUADS), z)


def face_spills(spills, before, spill):
    for cell in range(CELLS):
        q, z = cell // CZ, cell % CZ
        spill[cell] = before[z] + overflow_of(spills, face_columns(q), z)


def corner_loop(start, stop, work, finish, sums):
    def one_cell(slot, _):
        finish(jnp.maximum(slot - 1, start))
        work(slot)
        return 0

    sums[start] = jnp.zeros(sums.shape[1:], jnp.float32)
    lax.fori_loop(start, stop, one_cell, 0, unroll=4)
    finish(stop - 1)


def corner_spills(spills, before, rest, place):
    for slot in range(rest.shape[0]):
        q, z = place(slot)
        rest[slot] = before[q * CZ + z] + spills[q * CZ + z]


def core_kernel(core, kernels, sums, spill, turned, packed, spills):
    turn_cells(core, turned)
    pack_core(core, core, packed, spills, True)
    core_spills(spills, spill)

    def one_cell(cell, _):
        q, z = cell // CZ, cell % CZ
        below = spread(core[q * EZ + z, 7:8, :]).astype(jnp.int32)
        lines = lines_of(packed, core_columns(q), z)
        build_cell(cell, cell, lines, turned, kernels, None, sums, below)
        return 0

    lax.fori_loop(0, CELLS, one_cell, 0, unroll=2)


def face_kernel(
    x_low, x_high, beyond, turned, before, spill_before, kernels, sums, spill, packed, spills
):
    pieces = [x_low, x_high, beyond]
    pack_faces(pieces, pieces, packed, spills, True)
    face_spills(spills, spill_before, spill)

    def one_cell(cell, _):
        lines = lines_of(packed, face_columns(cell // CZ), cell % CZ)
        build_cell(cell, cell, lines, turned, kernels, before, sums, None)
        return 0

    lax.fori_loop(0, CELLS, one_cell, 0, unroll=2)


def corner_kernel(
    corners, turned, before, spill_before, core, kernels, out, packed, spills, rest, sums
):
    slots = kernels.shape[0]
    place = PLACES[slots]
    pack_corners(corners, corners, packed, spills, True, LAYERS[slots])
    corner_spills(spills, spill_before, rest, place)

    def work(slot):
        q, z = place(slot)
        lines = lines_of(packed, [q], z) + [rest_line(rest, slot)]
        build_cell(q * CZ + z, slot, lines, turned, kernels, before, sums, None)

    def finish(slot):
        finish_cell(slot, place, slot, core, sums, out)

    corner_loop(0, slots, work, finish, sums)


IN_VMEM = pl.BlockSpec(memory_space=VMEM)
IN_SMEM = pl.BlockSpec(memory_space=SMEM)
PAIR = jax.ShapeDtypeStruct((CELLS, 2, LANES), jnp.float32)
SPILL = jax.ShapeDtypeStruct((CELLS, 8, LANES), jnp.float32)
SUMS = jax.ShapeDtypeStruct((CELLS, BLOCKS, 2, 8, LANES), jnp.float32)
TURNED = jax.ShapeDtypeStruct((CELLS, BLOCKS, 4, 8, LANES), jnp.float32)
CORE_SPILL = jax.ShapeDtypeStruct((CZ, 8, LANES), jnp.float32)
CORE_TILES, FACE_TILES, CORNER_TILES = 8, 8, 3


def held(tiles, cells=CELLS):
    return VMEM((cells, BLOCKS, tiles, 8, LANES), jnp.float32)


def pairs(cells):
    return jax.ShapeDtypeStruct((cells, 2, LANES), jnp.float32)


def call(kernel, outs, scratch, tiles, *arrays):
    work = CELLS * BLOCKS * tiles * 8 * LANES
    return pl.pallas_call(
        kernel,
        out_shape=outs,
        in_specs=[IN_SMEM if array.ndim == 1 else IN_VMEM for array in arrays],
        out_specs=jax.tree.map(lambda _: IN_VMEM, outs),
        scratch_shapes=scratch,
        compiler_params=params(8),
        cost_estimate=pl.CostEstimate(
            flops=30 * work, bytes_accessed=8 * work, transcendentals=4 * work
        ),
    )(*arrays)


def packs(columns):
    return [
        VMEM((columns * CZ, 2, 8, LANES), jnp.float32),
        VMEM((columns * CZ, 8, LANES), jnp.float32),
    ]


def build_core(core):
    outs = (held(CORE_TILES), SUMS, CORE_SPILL, TURNED)
    return call(core_kernel, outs, packs(4), CORE_TILES, core)


def build_faces(pieces, turned, before, spill):
    outs = (held(FACE_TILES), SUMS, SPILL)
    return call(face_kernel, outs, packs(8), FACE_TILES, *pieces, turned, before, spill)


def corner_scratch(cells):
    rest = VMEM((cells, 8, LANES), jnp.float32)
    return packs(4) + [rest, VMEM((cells, BLOCKS, 2, 8, LANES), jnp.float32)]


def build_corners(cells, corners, turned, before, spill, core):
    outs = (held(CORNER_TILES, cells), pairs(cells))
    arrays = [corners, turned, before, spill, core]
    return call(corner_kernel, outs, corner_scratch(cells), CORNER_TILES, *arrays)


def cell_sums(cell, slot, lines, stored, before, first=0):
    sums_s, sums_t = start_sums(cell, before, range(BLOCKS))
    for index, line in enumerate(lines):
        line_s, line_t = line(0), line(1)
        for block in range(BLOCKS):
            value = stored[slot, block, first + index]
            sums_s[block] = sums_s[block] + value * line_s
            sums_t[block] = sums_t[block] + value * line_t
    return sums_s, sums_t


def apply_cell(cell, slot, lines, stored, before, sums, first=0):
    sums_s, sums_t = cell_sums(cell, slot, lines, stored, before, first)
    for block in range(BLOCKS):
        sums[slot, block, 0] = sums_s[block]
        sums[slot, block, 1] = sums_t[block]


def widen(pieces, wides, scale=None):
    for piece, wide in zip(pieces, wides):
        wide[:, 0:2, :] = piece[...] if scale is None else scale * piece[...]


def apply_core_kernel(info, core, stored, sums, spill, wide, packed, spills):
    widen([core], [wide])
    pack_core(info, wide, packed, spills, False)
    core_spills(spills, spill)

    def one_cell(cell, _):
        lines = lines_of(packed, core_columns(cell // CZ), cell % CZ)
        apply_cell(cell, cell, lines, stored, None, sums)
        return 0

    lax.fori_loop(0, CELLS, one_cell, 0, unroll=4)


def apply_face_kernel(*refs):
    infos, pieces, (stored, before, spill_before, sums, spill), wides, (packed, spills) = split(
        refs, 3, 3, 5, 3, 2
    )
    widen(pieces, wides)
    pack_faces(infos, wides, packed, spills, False)
    face_spills(spills, spill_before, spill)

    def one_cell(cell, _):
        lines = lines_of(packed, face_columns(cell // CZ), cell % CZ)
        apply_cell(cell, cell, lines, stored, before, sums)
        return 0

    lax.fori_loop(0, CELLS, one_cell, 0, unroll=4)


def apply_corner_cells(stored, before, spill_before, core, out, packed, spills, rest, sums):
    slots = stored.shape[0]
    place = PLACES[slots]
    corner_spills(spills, spill_before, rest, place)

    def work(slot):
        q, z = place(slot)
        lines = lines_of(packed, [q], z) + [rest_line(rest, slot)]
        apply_cell(q * CZ + z, slot, lines, stored, before, sums)

    def finish(slot):
        finish_cell(slot, place, slot, core, sums, out)

    corner_loop(0, slots, work, finish, sums)


def upper_corner_cells(stored, before, spill_before, turned, packed, spills, rest, total):
    slots = stored.shape[0]
    place = PLACES[slots]
    for slot in range(slots):
        q, z = place(slot)
        tile = spill_before[q * CZ + z]
        rest[slot] = tile + spills[q * CZ + z] if q >= CY else tile

    def weigh(cell, sums, total):
        total_s, total_t = total
        for block in range(BLOCKS):
            total_s = total_s + sums[0][block] * turned[cell, block, 0]
            total_t = total_t + sums[1][block] * turned[cell, block, 1]
        return total_s, total_t

    def low(slot, total):
        q, z = place(slot)
        cell = q * CZ + z
        return weigh(cell, cell_sums(cell, slot, [rest_line(rest, slot)], stored, before, 2), total)

    def high(slot, total):
        q, z = place(slot)
        cell = q * CZ + z
        lines = lines_of(packed, [q], z) + [rest_line(rest, slot)]
        return weigh(cell, cell_sums(cell, slot, lines, stored, before), total)

    total = lax.fori_loop(0, slots // 2, low, total, unroll=4)
    return lax.fori_loop(slots // 2, slots, high, total, unroll=4)


def upper_face_kernel(
    info_high, info_beyond, high, beyond, stored, before, spill_before, sums, spill,
    wide_high, wide_beyond, packed, spills,
):
    wides = [wide_high, wide_beyond]
    widen([high, beyond], wides, 2.0)
    pack_upper_faces([info_high, info_beyond], wides, packed, spills)
    for cell in range(CELLS):
        q, z = cell // CZ, cell % CZ
        groups, _ = upper_columns(q)
        spill[cell] = sum([spills[c * CZ + z] for group in groups for c in group], spill_before[z])
    sums[0:CZ] = before[0:CZ]
    for q in range(1, QUADS):
        groups, first = upper_columns(q)
        columns = [column for group in groups for column in group]

        def one_cell(z, _, q=q, columns=columns, first=first):
            cell = q * CZ + z
            apply_cell(cell, cell, lines_of(packed, columns, z), stored, before, sums, first)
            return 0

        lax.fori_loop(0, CZ, one_cell, 0, unroll=4)


def apply_corner_kernel(
    info, corners, stored, before, spill_before, core, out, wide, packed, spills, rest, sums
):
    widen([corners], [wide])
    pack_corners(info, wide, packed, spills, False, LAYERS[stored.shape[0]])
    apply_corner_cells(
        stored, before, spill_before, core, out, packed, spills, rest, sums
    )


def split(refs, *sizes):
    parts = []
    for size in sizes:
        parts.append(refs[:size])
        refs = refs[size:]
    return parts


def turn_pairs(core, turned):
    row = row_index((8, 2 * LANES))
    chosen = ((row & 1) == lane_index((8, 2 * LANES)) >> 7) & (row < 6)
    ones = jnp.where(chosen, 1.0, 0.0).astype(jnp.bfloat16)
    for cell in range(CELLS):
        pair = core[(cell // CZ) * EZ + cell % CZ + 1]
        parts = jnp.concatenate(parts_of(pair) + (jnp.zeros_like(pair),), axis=0)
        left = parts.T[: 8 * BLOCKS + 8].astype(jnp.bfloat16)
        wide = lax.dot_general(
            left, ones, (((1,), (0,)), ((), ())), preferred_element_type=jnp.float32
        )
        for block in range(BLOCKS):
            for k in range(2):
                turned[cell, block, k] = wide[8 * block : 8 * block + 8, k * LANES : (k + 1) * LANES]


def pair_place(index):
    return lane_index((2, LANES)) - row_index((2, LANES)) == 2 * index


def last_core_kernel(
    info, core, stored, slots, first, second, sums, spill, turned, line, wide, packed, spills
):
    turn_pairs(core, turned)
    apply_core_kernel(info, core, stored, sums, spill, wide, packed, spills)
    d = slots[:, 1 : 1 + CZ, 6:7, :].reshape(CELLS, 1, LANES)
    v_0 = slots[:, 1 : 1 + CZ, 4:6, :].reshape(CELLS, 2, LANES)
    v_1 = first[:, 1 : 1 + CZ].reshape(v_0.shape)
    v_2 = second[:, 1 : 1 + CZ].reshape(v_0.shape)
    d_0 = d * v_0
    d_2 = d * v_2
    parts = [d_0 * v_0, d_0 * v_1, d * v_1 * v_1, d_2 * v_1, d_2 * v_2, None, v_0, v_1, v_2]
    found = jnp.zeros((2, LANES), jnp.float32)
    for index, part in enumerate(parts):
        if part is not None:
            total = jnp.sum(jnp.sum(part, axis=0), axis=1, keepdims=True)
            found = jnp.where(pair_place(index), total, found)
    line[...] = found


def apply_last_kernel(
    info, corners, edge, inner, before, spill_before, turned, line, moments,
    wide, packed, spills, edge_rest, inner_rest,
):
    widen([corners], [wide], 2.0)
    pack_upper_corners(info, wide, packed, spills)
    total = (jnp.zeros((8, LANES), jnp.float32), jnp.zeros((8, LANES), jnp.float32))
    for stored, rest in ((edge, edge_rest), (inner, inner_rest)):
        total = upper_corner_cells(
            stored, before, spill_before, turned, packed, spills, rest, total
        )
    last = [jnp.sum(part, axis=0, keepdims=True) for part in total]
    last = PAIR_SCALE * jnp.sum(jnp.concatenate(last, axis=0), axis=1, keepdims=True)
    found = jnp.where(pair_place(5), last, line[...])
    moments[...] = jnp.sum(found, axis=0, keepdims=True)


def wide(piece):
    return VMEM((piece.shape[0], 8, LANES), jnp.float32)


def apply_core(info, core, stored):
    stored = pltpu.with_memory_space_constraint(stored, VMEM)
    scratch = [wide(core)] + packs(4)
    return call(apply_core_kernel, (SUMS, CORE_SPILL), scratch, 2, info, core, stored)


def apply_faces(infos, pieces, stored, before, spill):
    stored = pltpu.with_memory_space_constraint(stored, VMEM)
    scratch = [wide(piece) for piece in pieces] + packs(8)
    return call(
        apply_face_kernel, (SUMS, SPILL), scratch, 2, *infos, *pieces, stored, before, spill
    )


def apply_upper_faces(infos, pieces, stored, before, spill):
    stored = pltpu.with_memory_space_constraint(stored, VMEM)
    scratch = [wide(piece) for piece in pieces] + packs(8)
    return call(
        upper_face_kernel, (SUMS, SPILL), scratch, 2, *infos, *pieces, stored, before, spill
    )


def apply_corners(info, corners, stored, before, spill, core):
    stored = pltpu.with_memory_space_constraint(stored, VMEM)
    cells = stored.shape[0]
    arrays = [info, corners, stored, before, spill, core]
    scratch = [wide(corners)] + corner_scratch(cells)
    return call(apply_corner_kernel, pairs(cells), scratch, 2, *arrays)


def apply_last_core(info, core, stored, slots, first, second):
    stored = pltpu.with_memory_space_constraint(stored, VMEM)
    outs = (SUMS, CORE_SPILL, SUMS, jax.ShapeDtypeStruct((2, LANES), jnp.float32))
    scratch = [wide(core)] + packs(4)
    return call(last_core_kernel, outs, scratch, 2, info, core, stored, slots, first, second)


def apply_last(info, corners, edge, inner, before, spill, turned, line):
    edge = pltpu.with_memory_space_constraint(edge, VMEM)
    inner = pltpu.with_memory_space_constraint(inner, VMEM)
    arrays = [info, corners, edge, inner, before, spill, turned, line]
    scratch = [wide(corners)] + packs(4)
    scratch += [VMEM((cells, 8, LANES), jnp.float32) for cells in (EDGES, INNER)]
    out = jax.ShapeDtypeStruct((1, LANES), jnp.float32)
    return call(apply_last_kernel, out, scratch, 2, *arrays)


def solve(g):
    tiny = 1e-6
    h = [g[k] + g[k + 1] for k in range(5)]
    ratio_1 = h[1] / h[0]
    ratio_2 = h[2] / h[0]
    pivot_1 = h[2] - ratio_1 * h[1]
    mixed = h[3] - ratio_1 * h[2]
    rest_1 = g[1] - ratio_1 * g[0]
    live_1 = pivot_1 > tiny * h[2]
    safe_1 = jnp.where(live_1, pivot_1, 1.0)
    ratio_3 = jnp.where(live_1, mixed / safe_1, 0.0)
    pivot_2 = h[4] - ratio_2 * h[2] - ratio_3 * mixed
    rest_2 = g[2] - ratio_2 * g[0] - ratio_3 * rest_1
    live_2 = live_1 & (pivot_2 > tiny * h[4])
    c_2 = jnp.where(live_2, rest_2 / jnp.where(live_2, pivot_2, 1.0), 0.0)
    c_1 = jnp.where(live_1, (rest_1 - mixed * c_2) / safe_1, 0.0)
    c_0 = (g[0] - h[1] * c_1 - h[2] * c_2) / h[0]
    return c_0, c_1, c_2


def invert(counts, atoms, places):
    rows = places.shape[1]
    row_low = row_index((LANES, LANES))
    row_high = row_index((rows, LANES))
    lane = lane_index((rows, LANES))

    def one_cell(cell, total):
        live = lane_index((1, LANES)) < counts[cell]
        pointer = jnp.where(live, atoms[pl.ds(cell, 1), :], -1)
        here = (pointer >> 7) == row_high
        cells = jnp.where(here, cell, 0).astype(jnp.float32)
        slots = jnp.where(here, lane, 0).astype(jnp.float32)
        parts = jnp.concatenate([cells, slots], axis=0).astype(jnp.bfloat16)
        lows = jnp.where((pointer & 127) == row_low, 1.0, 0.0).astype(jnp.bfloat16)
        return total + lax.dot_general(
            parts, lows, (((1,), (1,)), ((), ())), preferred_element_type=jnp.float32
        )

    total = jnp.zeros((2 * rows, LANES), jnp.float32)
    total = lax.fori_loop(0, CELLS, one_cell, total, unroll=8).astype(jnp.int32)
    places[0] = total[:rows]
    places[1] = total[rows:]


def inverted(counts, atoms, atoms_local):
    rows = (atoms_local // LANES + 15) // 16 * 16
    return call(invert, jax.ShapeDtypeStruct((2, rows, LANES), jnp.int32), [], 2, counts, atoms)


def finish_kernel(moments, slots, first, second, places, out, charges):
    summed = moments[...]
    lane = lane_index((2, LANES))
    row = row_index((2, LANES))

    def pair(index):
        picked = jnp.where(lane - row == 2 * index, summed, 0.0)
        return jnp.broadcast_to(jnp.sum(picked, axis=1, keepdims=True), (2, LANES))

    rows = [pair(index) for index in range(9)]
    c_0, c_1, c_2 = solve(rows[:6])
    totals = c_0 * rows[6] + c_1 * rows[7] + c_2 * rows[8]
    balance = totals[0:1] / totals[1:2]
    sign = jnp.concatenate([jnp.ones((1, LANES), jnp.float32), -balance], axis=0)
    c_0, c_1, c_2 = c_0 * sign, c_1 * sign, c_2 * sign
    for cell in range(CELLS):
        q, z = cell // CZ, cell % CZ + 1
        mixed = c_0 * slots[q, z, 4:6, :] + c_1 * first[q, z] + c_2 * second[q, z]
        charges[cell : cell + 1, :] = jnp.sum(mixed, axis=0, keepdims=True)
    tiles = [jnp.zeros((8, LANES), jnp.float32) for _ in range((out.shape[0] + 7) // 8)]
    for cell in range(CELLS):
        line = spread(charges[cell : cell + 1, :])
        for at in range(len(tiles)):
            here = slice(8 * at, 8 * at + 8)
            moved = jnp.take_along_axis(line, places[1, here, :], axis=1)
            tiles[at] = jnp.where(places[0, here, :] == cell, moved, tiles[at])
    out[...] = jnp.concatenate(tiles, axis=0)[: out.shape[0]]


def finish(moments, slots, first, second, places, atoms_local):
    return pl.pallas_call(
        finish_kernel,
        out_shape=jax.ShapeDtypeStruct((atoms_local // LANES, LANES), jnp.float32),
        in_specs=[IN_VMEM] * 5,
        out_specs=IN_VMEM,
        scratch_shapes=[VMEM((CELLS, LANES), jnp.float32)],
        compiler_params=params(8),
    )(moments, slots, first, second, places)


def partner(block, axis, mask):
    count = lax.axis_size(axis)
    return lax.ppermute(block, axis, [(low, low ^ mask) for low in range(count)])


def shifted(block, along_x, across_y=0):
    count = lax.axis_size("gx")
    route = [(i, ((i + 4 * along_x) % count) ^ (2 * across_y)) for i in range(count)]
    return lax.ppermute(block, "gx", route)


def with_z_faces(edge, inner):
    other = partner(edge, "gx", 1)
    parts = [other[:, 0:1], edge[:, 1:2], inner, edge[:, 0:1], other[:, 1:2]]
    return jnp.concatenate(parts, axis=1)


def flat(columns):
    return columns.reshape((-1,) + columns.shape[-2:])


def x_faces(core):
    count = lax.axis_size("gx")
    rows = count // 4
    odd = (lax.axis_index("gx") // 4) % 2 == 1
    if rows % 2:
        return shifted(core[2:], 1), shifted(core[:2], -1)
    route = [(i, (i + (4 if (i // 4) % 2 else -4)) % count) for i in range(count)]
    second = lax.ppermute(jnp.where(odd, core[2:], core[:2]), "gx", route)
    first = lax.ppermute(jnp.where(odd, core[:2], core[2:]), "gx", [(i, i ^ 4) for i in range(count)])
    return first, second


def sorted_faces(first, second):
    odd = (lax.axis_index("gx") // 4) % 2 == 1
    if (lax.axis_size("gx") // 4) % 2:
        return first, second
    return jnp.where(odd, first, second), jnp.where(odd, second, first)


def exchange(edge, inner, on_core, on_faces, on_corners, faces_last=False):
    core = with_z_faces(edge, inner)
    first, second = x_faces(core)
    beyond = partner(core, "gx", 2)
    sums, spill, *more = on_core(flat(core))
    if faces_last:
        second, first, beyond, sums = lax.optimization_barrier((second, first, beyond, sums))
    else:
        second, first, sums = lax.optimization_barrier((second, first, sums))
    low, high = sorted_faces(first, second)
    corners = partner(jnp.concatenate([low, high], axis=0), "gx", 2)
    pieces = [flat(part) for part in (low, high, beyond)]
    sums, spill, *more = on_faces(pieces, sums, spill, *more)
    corners = flat(corners)
    return core, pieces, corners, on_corners(corners, sums, spill, core, *more)


def global_sum(values):
    count = lax.axis_size("gx")
    if count & (count - 1):
        return lax.psum(values, "gx")
    step = 1
    while step < count:
        if step >= 2 and 4 * step <= count:
            others = [partner(values, "gx", k * step) for k in (1, 2, 3)]
            values = (values + others[0]) + (others[1] + others[2])
            step *= 4
        else:
            values = values + partner(values, "gx", step)
            step *= 2
    return values


def local(cell_offsets, electronegativity, hardness, charge_widths, cell_counts, cell_atoms):
    edge, inner = prepare(
        cell_counts, cell_offsets, electronegativity, hardness, charge_widths, cell_atoms
    )
    stored = []

    def keep(tiles, *others):
        stored.append(tiles)
        return others

    def build_ends(corners, sums, spill, core, *own):
        (edge,) = keep(*build_corners(EDGES, corners, *own, sums, spill, flat(core)))
        (inner,) = keep(*build_corners(INNER, corners, *own, sums, spill, flat(core)))
        return by_column(edge), by_column(inner)

    def by_column(cells):
        return cells.reshape((QUADS, -1) + cells.shape[1:])

    slots, pieces, corners, ends = exchange(
        by_column(edge),
        by_column(inner),
        lambda core: keep(*build_core(core)),
        lambda faces, sums, spill, *own: keep(*build_faces(faces, *own, sums, spill)) + own,
        build_ends,
        faces_last=True,
    )
    info = flat(slots)

    def apply(edge, inner, on_corners):
        return exchange(
            edge,
            inner,
            lambda own: apply_core(info, own, stored[0]),
            lambda faces, sums, spill: apply_faces(pieces, faces, stored[1], sums, spill),
            on_corners,
        )

    def apply_ends(others, sums, spill, _):
        edge = apply_corners(corners, others, stored[2], sums, spill, info)
        inner = apply_corners(corners, others, stored[3], sums, spill, info)
        return by_column(edge), by_column(inner)

    first, _, _, ends = apply(*ends, apply_ends)
    second = with_z_faces(*ends)
    high = shifted(second[:2], -1)
    beyond = partner(second, "gx", 2)
    corner = shifted(second[:2], -1, 1)
    sums, spill, turned, line = apply_last_core(
        info, flat(second), stored[0], slots, first, second
    )
    high, beyond, sums = lax.optimization_barrier((high, beyond, sums))
    upper = [flat(high), flat(beyond)]
    sums, spill = apply_upper_faces(pieces[1:], upper, stored[1], sums, spill)
    corner, sums = lax.optimization_barrier((corner, sums))
    moments = apply_last(
        corners, flat(corner), stored[2], stored[3], sums, spill, turned, line
    )
    moments, cell_counts, cell_atoms = lax.optimization_barrier((moments, cell_counts, cell_atoms))
    atoms_local = cell_offsets.shape[1]
    places = inverted(cell_counts, cell_atoms, atoms_local)
    charges = finish(global_sum(moments), slots, first, second, places, atoms_local)
    return charges.reshape(-1)


def solution(mesh):
    placed = (
        P(None, ("grp", "gx")),
        P(("grp", "gx")),
        P(("grp", "gx")),
        P(("grp", "gx")),
        P(("grp", "gx")),
        P(("grp", "gx"), None),
    )
    return jax.shard_map(
        local, mesh=mesh, in_specs=placed, out_specs=P(("grp", "gx")), check_vma=False
    )
```

```python
import functools
import math

import jax
import jax.numpy as jnp
from jax import lax
from jax.experimental import pallas as pl
from jax.experimental.pallas import tpu as pltpu
from jax.sharding import PartitionSpec as P

CX = 2
CY = 2
CZ = 8
EZ = CZ + 2
CELLS = CX * CY * CZ
QUADS = CX * CY
LANES = 128
BLOCKS = 11
GROUPS = ((0, 1, 2, 3), (4, 5, 6, 7), (8, 9, 10))

COULOMB = 14.399645
ROOT_PI = math.sqrt(math.pi)
SCREEN = 1.0 / (math.sqrt(2.0) * 3.0)
EWALD_SELF = math.sqrt(2.0 / math.pi) / 3.0
SIDE = 12.0 * SCREEN
CUT_SQUARED = (12.0 * SCREEN) ** 2
CLOSEST_SQUARED = (0.5 * SCREEN) ** 2
PAIR_SCALE = COULOMB * SCREEN

VMEM = pltpu.VMEM
SMEM = pltpu.SMEM


def params(mib):
    return pltpu.CompilerParams(vmem_limit_bytes=mib * 2**20)


def lane_index(shape):
    return lax.broadcasted_iota(jnp.int32, shape, len(shape) - 1)


def row_index(shape):
    return lax.broadcasted_iota(jnp.int32, shape, len(shape) - 2)


def edge_place(slot):
    return slot // 2, (CZ - 1) * (1 - slot % 2)


def inner_place(slot):
    return slot // (CZ - 2), 1 + slot % (CZ - 2)


EDGES = 2 * QUADS
INNER = CELLS - EDGES
PLACES = {EDGES: edge_place, INNER: inner_place}
LAYERS = {EDGES: (0, CZ - 1), INNER: range(1, CZ - 1)}


def gather_cells(counted, atoms, table, others, out):
    place = PLACES[out.shape[0]]
    row = row_index((8, LANES))
    lane = lane_index((1, LANES))

    def pick(source, pointers):
        share = 8 // len(pointers)
        pointer = spread(pointers[-1])
        for k in range(len(pointers) - 2, -1, -1):
            pointer = jnp.where(row < share * (k + 1), pointers[k], pointer)
        high = pointer >> 7
        low = pointer & 127
        picked = jnp.zeros((8, LANES), jnp.float32)
        for chunk in range(source.shape[0]):
            part = jnp.take_along_axis(source[chunk], low, axis=1)
            picked = jnp.where(high == chunk, part, picked)
        return picked

    def four_cells(step, _):
        slots = [4 * step + k for k in range(4)]
        places = [place(slot) for slot in slots]
        counts = [counted[pl.ds(q * CZ + z, 1), :] for q, z in places]
        occupied = [lane < count for count in counts]
        pointers = [
            jnp.where(live, atoms[pl.ds(q * CZ + z, 1), :], 0)
            for (q, z), live in zip(places, occupied)
        ]
        pairs = [pick(table, pointers[:2]), pick(table, pointers[2:])]
        both = pick(others, pointers)
        for k, (slot, live) in enumerate(zip(slots, occupied)):
            q = places[k][0]
            at = 4 * (k % 2)
            picked = pairs[k // 2][at : at + 4]
            width = jnp.where(live, picked[3:4], 1.0)
            hard = both[2 * k + 1 : 2 * k + 2]
            diag = jnp.where(live, hard + COULOMB * (1.0 / (width * ROOT_PI) - EWALD_SELF), 1.0)
            negative = jnp.where(live, both[2 * k : 2 * k + 1], 0.0)
            out[slot, 0:1, :] = (picked[0:1] + (q // CY).astype(jnp.float32)) * SIDE
            out[slot, 1:2, :] = (picked[1:2] + (q % CY).astype(jnp.float32)) * SIDE
            out[slot, 2:3, :] = picked[2:3] * SIDE
            out[slot, 3:4, :] = (2.0 * SCREEN * SCREEN) * width * width
            out[slot, 4:5, :] = -negative / diag
            out[slot, 5:6, :] = jnp.where(live, 1.0 / diag, 0.0)
            out[slot, 6:7, :] = diag
            out[slot, 7:8, :] = counts[k].astype(jnp.float32)
        return 0

    lax.fori_loop(0, out.shape[0] // 4, four_cells, 0, unroll=2)


def prepare_kernel(
    counts_hbm, offsets, negativity, hardness, widths, atoms_hbm, edge, counted, atoms, table, others,
    counts, raw_offsets, raw_negativity, raw_hardness, raw_widths, sems,
):
    copies = [
        pltpu.make_async_copy(source, target, sems.at[index])
        for index, (source, target) in enumerate(
            [
                (counts_hbm, counts),
                (offsets, raw_offsets),
                (negativity, raw_negativity),
                (hardness, raw_hardness),
                (widths, raw_widths),
                (atoms_hbm, atoms),
            ]
        )
    ]
    for copy in copies:
        copy.start()
    for copy in copies:
        copy.wait()
    for chunk in range(table.shape[0]):
        here = slice(chunk * LANES, (chunk + 1) * LANES)
        for first in (0, 4):
            table[chunk, first : first + 3, :] = raw_offsets[:, here]
            table[chunk, first + 3 : first + 4, :] = raw_widths[chunk : chunk + 1, :]
        for first in (0, 2, 4, 6):
            others[chunk, first : first + 1, :] = raw_negativity[chunk : chunk + 1, :]
            others[chunk, first + 1 : first + 2, :] = raw_hardness[chunk : chunk + 1, :]
    for cell in range(CELLS):
        counted[cell : cell + 1, :] = jnp.full((1, LANES), counts[cell])
    gather_cells(counted, atoms, table, others, edge)


def prepare_rest_kernel(counted, atoms, table, others, inner):
    gather_cells(counted, atoms, table, others, inner)


def prepare(counts, offsets, negativity, hardness, widths, atoms):
    chunks = offsets.shape[1] // LANES
    plane = (chunks, LANES)
    tables = jax.ShapeDtypeStruct((chunks, 8, LANES), jnp.float32)
    lists = jax.ShapeDtypeStruct(atoms.shape, jnp.int32)
    edge, *rest = pl.pallas_call(
        prepare_kernel,
        out_shape=(
            jax.ShapeDtypeStruct((EDGES, 8, LANES), jnp.float32),
            lists,
            lists,
            tables,
            tables,
        ),
        in_specs=[pl.BlockSpec(memory_space=pltpu.HBM)] * 6,
        out_specs=(pl.BlockSpec(memory_space=VMEM),) * 5,
        scratch_shapes=[
            SMEM(counts.shape, jnp.int32),
            VMEM(offsets.shape, jnp.float32),
            VMEM(plane, jnp.float32),
            VMEM(plane, jnp.float32),
            VMEM(plane, jnp.float32),
            pltpu.SemaphoreType.DMA((6,)),
        ],
        compiler_params=params(8),
    )(
        *[
            pltpu.with_memory_space_constraint(array, pltpu.HBM)
            for array in (
                counts,
                offsets,
                negativity.reshape(plane),
                hardness.reshape(plane),
                widths.reshape(plane),
                atoms,
            )
        ]
    )
    inner = pl.pallas_call(
        prepare_rest_kernel,
        out_shape=jax.ShapeDtypeStruct((INNER, 8, LANES), jnp.float32),
        in_specs=[pl.BlockSpec(memory_space=VMEM)] * 4,
        out_specs=pl.BlockSpec(memory_space=VMEM),
        compiler_params=params(8),
        cost_estimate=pl.CostEstimate(flops=2**20, bytes_accessed=2**22, transcendentals=0),
    )(*rest)
    return edge, inner


def pack_column(
    info, cells, source, packed, spills, target, at, shift, layers=range(CZ), info_source=None
):
    lane = lane_index((8, LANES))
    row = row_index((8, LANES))
    for z in layers:
        base = source * EZ + z
        known = base if info_source is None else info_source * EZ + z
        low, mid, top = [spread(info[known + k, 7:8, :]).astype(jnp.int32) for k in range(3)]
        end = low + mid - LANES
        tiles = [cells[base + k] for k in range(3)]
        if shift is not None:
            for k in range(3):
                offset = jnp.where(row == 2, (k - 1) * SIDE, 0.0)
                for axis in range(2):
                    offset = jnp.where(row == axis, shift[axis] * SIDE, offset)
                tiles[k] = tiles[k] + offset
        second = jnp.take_along_axis(tiles[1], (lane - low) & 127, axis=1)
        third = jnp.take_along_axis(tiles[2], (lane - end) & 127, axis=1)
        packed[target * CZ + z, 0] = jnp.where(lane < low, tiles[0], second)
        packed[target * CZ + z, 1] = jnp.where(lane < end, second, third)
        spill = jnp.where(lane < end + top - LANES, third, 0.0)
        spills[target * CZ + z] = pltpu.roll(spill, at, 1) if at else spill


def pack_core(info, cells, packed, spills, build):
    for q in range(QUADS):
        pack_column(info, cells, q, packed, spills, q, 8 * q, (0, 0) if build else None)


def pack_faces(infos, pieces, packed, spills, build):
    for side in range(2):
        sign = 2 * side - 1
        for y in range(CY):
            shift = (sign * CX, 0) if build else None
            at = 32 + 8 * y
            pack_column(infos[side], pieces[side], y, packed, spills, 2 * side + y, at, shift)
        for x in range(CX):
            shift = (0, sign * CY) if build else None
            source = 2 * x + 1 - side
            target = 4 + 2 * x + side
            at = 48 + 8 * x
            pack_column(infos[2], pieces[2], source, packed, spills, target, at, shift)


def pack_corners(info, cells, packed, spills, build, layers):
    for side_x in range(2):
        for side_y in range(2):
            shift = ((2 * side_x - 1) * CX, (2 * side_y - 1) * CY) if build else None
            source = 2 * side_x + 1 - side_y
            target = 2 * side_x + side_y
            pack_column(info, cells, source, packed, spills, target, 64, shift, layers)


def pack_upper_faces(infos, pieces, packed, spills):
    for y in range(CY):
        pack_column(infos[0], pieces[0], y, packed, spills, 2 + y, 32 + 8 * y, None)
    for x in range(CX):
        pack_column(infos[1], pieces[1], 2 * x, packed, spills, 5 + 2 * x, 48 + 8 * x, None)


def pack_upper_corners(info, cells, packed, spills):
    for side_y in range(2):
        source = 1 - side_y
        pack_column(info, cells, source, packed, spills, 2 + side_y, 64, None, info_source=2 + source)


def upper_columns(q):
    columns = face_columns(q)
    return [columns[2 * k : 2 * k + 2] for k in range(2) if (q >> (1 - k)) & 1], 4 * (q == 1)


def core_columns(q):
    return [q ^ k for k in range(4)]


def face_columns(q):
    x, y = q >> 1, q & 1
    return [2 * x, 2 * x + 1, 4 + y, 6 + y]


def overflow_of(spills, columns, z):
    return sum(spills[column * CZ + z] for column in columns)


def spread(row):
    return jnp.broadcast_to(row, (8, LANES))


def couple(x_i, y_i, z_i, w_i, x_j, y_j, z_j, w_j):
    delta_x = x_j - x_i
    delta_y = y_j - y_i
    delta_z = z_j - z_i
    squared = delta_x * delta_x + delta_y * delta_y + delta_z * delta_z
    held = jnp.maximum(squared, CLOSEST_SQUARED)
    inverse = lax.rsqrt(held)
    distance = held * inverse
    scaled = distance * lax.rsqrt(w_i + w_j)
    value = (lax.erf(scaled) - lax.erf(distance)) * inverse
    return jnp.where(squared < CUT_SQUARED, value, 0.0)


def to_rows(sums, block):
    here = lane_index((8, LANES)) - row_index((8, LANES)) == 8 * block
    return jnp.where(here, jnp.sum(sums, axis=1, keepdims=True), 0.0)


def add_rows(cell, sums, rows):
    for index in range(2):
        total = jnp.zeros((8, LANES), jnp.float32)
        for block in range(BLOCKS):
            total = total + to_rows(sums[cell, block, index], block)
        rows.append(jnp.sum(total, axis=0, keepdims=True))


def finish_cell(slot, place, target, info, sums, out):
    q, z = place(slot)
    rows = []
    add_rows(slot, sums, rows)
    own = info.at[q * EZ + z + 1]
    scale = PAIR_SCALE / own[6:7, :]
    live = lane_index((1, LANES)) < own[7:8, :].astype(jnp.int32)
    out[target, 0:1, :] = jnp.where(live, rows[0] * scale, 0.0)
    out[target, 1:2, :] = jnp.where(live, rows[1] * scale, 0.0)


def build_cell(cell, slot, lines, turned, kernels, before, sums, below):
    own = None
    if below is not None:
        own = lane_index((8, LANES)) - row_index((8, LANES)) - below
    for group in GROUPS:
        sums_s, sums_t = start_sums(cell, before, group)
        mine = [[turned[cell, block, k] for k in range(4)] for block in group]
        for index, line in enumerate(lines):
            beside = [line(k) for k in range(6)]
            for at, block in enumerate(group):
                value = couple(*mine[at], *beside[:4])
                if own is not None and index < 2:
                    value = jnp.where(own == 8 * block - LANES * index, 0.0, value)
                kernels[slot, block, index] = value
                sums_s[at] = sums_s[at] + value * beside[4]
                sums_t[at] = sums_t[at] + value * beside[5]
        for at, block in enumerate(group):
            sums[slot, block, 0] = sums_s[at]
            sums[slot, block, 1] = sums_t[at]


def start_sums(cell, before, blocks):
    if before is None:
        zeros = [jnp.zeros((8, LANES), jnp.float32) for _ in blocks]
        return zeros, list(zeros)
    sums_s = [before[cell, block, 0] for block in blocks]
    return sums_s, [before[cell, block, 1] for block in blocks]


def lines_of(packed, columns, z):
    def line(column, half):
        return lambda k: spread(packed[column * CZ + z, half, k : k + 1, :])

    return [line(column, half) for column in columns for half in range(2)]


def rest_line(rest, cell):
    return lambda k: spread(rest[cell, k : k + 1, :])


def parts_of(value):
    high = value.astype(jnp.bfloat16).astype(jnp.float32)
    rest = value - high
    middle = rest.astype(jnp.bfloat16).astype(jnp.float32)
    return high, middle, rest - middle


def turn_cells(core, turned):
    chosen = row_index((24, 4 * LANES)) & 7
    ones = jnp.where(chosen == lane_index((24, 4 * LANES)) >> 7, 1.0, 0.0).astype(jnp.bfloat16)
    for cell in range(CELLS):
        here = core[(cell // CZ) * EZ + cell % CZ + 1]
        left = jnp.concatenate(parts_of(here), axis=0).T[: 8 * BLOCKS + 8].astype(jnp.bfloat16)
        wide = lax.dot_general(
            left, ones, (((1,), (0,)), ((), ())), preferred_element_type=jnp.float32
        )
        for block in range(BLOCKS):
            for k in range(4):
                turned[cell, block, k] = wide[8 * block : 8 * block + 8, k * LANES : (k + 1) * LANES]


def core_spills(spills, spill):
    for z in range(CZ):
        spill[z] = overflow_of(spills, range(QUADS), z)


def face_spills(spills, before, spill):
    for cell in range(CELLS):
        q, z = cell // CZ, cell % CZ
        spill[cell] = before[z] + overflow_of(spills, face_columns(q), z)


def corner_loop(start, stop, work, finish, sums):
    def one_cell(slot, _):
        finish(jnp.maximum(slot - 1, start))
        work(slot)
        return 0

    sums[start] = jnp.zeros(sums.shape[1:], jnp.float32)
    lax.fori_loop(start, stop, one_cell, 0, unroll=4)
    finish(stop - 1)


def corner_spills(spills, before, rest, place):
    for slot in range(rest.shape[0]):
        q, z = place(slot)
        rest[slot] = before[q * CZ + z] + spills[q * CZ + z]


def core_kernel(core, kernels, sums, spill, turned, packed, spills):
    turn_cells(core, turned)
    pack_core(core, core, packed, spills, True)
    core_spills(spills, spill)

    def one_cell(cell, _):
        q, z = cell // CZ, cell % CZ
        below = spread(core[q * EZ + z, 7:8, :]).astype(jnp.int32)
        lines = lines_of(packed, core_columns(q), z)
        build_cell(cell, cell, lines, turned, kernels, None, sums, below)
        return 0

    lax.fori_loop(0, CELLS, one_cell, 0, unroll=4)


def face_kernel(
    x_low, x_high, beyond, turned, before, spill_before, kernels, sums, spill, packed, spills
):
    pieces = [x_low, x_high, beyond]
    pack_faces(pieces, pieces, packed, spills, True)
    face_spills(spills, spill_before, spill)

    def one_cell(cell, _):
        lines = lines_of(packed, face_columns(cell // CZ), cell % CZ)
        build_cell(cell, cell, lines, turned, kernels, before, sums, None)
        return 0

    lax.fori_loop(0, CELLS, one_cell, 0, unroll=4)


def corner_kernel(
    corners, turned, before, spill_before, core, kernels, out, packed, spills, rest, sums
):
    slots = kernels.shape[0]
    place = PLACES[slots]
    pack_corners(corners, corners, packed, spills, True, LAYERS[slots])
    corner_spills(spills, spill_before, rest, place)

    def work(slot):
        q, z = place(slot)
        lines = lines_of(packed, [q], z) + [rest_line(rest, slot)]
        build_cell(q * CZ + z, slot, lines, turned, kernels, before, sums, None)

    def finish(slot):
        finish_cell(slot, place, slot, core, sums, out)

    corner_loop(0, slots, work, finish, sums)


IN_VMEM = pl.BlockSpec(memory_space=VMEM)
IN_SMEM = pl.BlockSpec(memory_space=SMEM)
PAIR = jax.ShapeDtypeStruct((CELLS, 2, LANES), jnp.float32)
SPILL = jax.ShapeDtypeStruct((CELLS, 8, LANES), jnp.float32)
SUMS = jax.ShapeDtypeStruct((CELLS, BLOCKS, 2, 8, LANES), jnp.float32)
TURNED = jax.ShapeDtypeStruct((CELLS, BLOCKS, 4, 8, LANES), jnp.float32)
CORE_SPILL = jax.ShapeDtypeStruct((CZ, 8, LANES), jnp.float32)
CORE_TILES, FACE_TILES, CORNER_TILES = 8, 8, 3


def held(tiles, cells=CELLS):
    return VMEM((cells, BLOCKS, tiles, 8, LANES), jnp.float32)


def pairs(cells):
    return jax.ShapeDtypeStruct((cells, 2, LANES), jnp.float32)


def call(kernel, outs, scratch, tiles, *arrays):
    work = CELLS * BLOCKS * tiles * 8 * LANES
    return pl.pallas_call(
        kernel,
        out_shape=outs,
        in_specs=[IN_SMEM if array.ndim == 1 else IN_VMEM for array in arrays],
        out_specs=jax.tree.map(lambda _: IN_VMEM, outs),
        scratch_shapes=scratch,
        compiler_params=params(8),
        cost_estimate=pl.CostEstimate(
            flops=30 * work, bytes_accessed=8 * work, transcendentals=4 * work
        ),
    )(*arrays)


def packs(columns):
    return [
        VMEM((columns * CZ, 2, 8, LANES), jnp.float32),
        VMEM((columns * CZ, 8, LANES), jnp.float32),
    ]


def build_core(core):
    outs = (held(CORE_TILES), SUMS, CORE_SPILL, TURNED)
    return call(core_kernel, outs, packs(4), CORE_TILES, core)


def build_faces(pieces, turned, before, spill):
    outs = (held(FACE_TILES), SUMS, SPILL)
    return call(face_kernel, outs, packs(8), FACE_TILES, *pieces, turned, before, spill)


def corner_scratch(cells):
    rest = VMEM((cells, 8, LANES), jnp.float32)
    return packs(4) + [rest, VMEM((cells, BLOCKS, 2, 8, LANES), jnp.float32)]


def build_corners(cells, corners, turned, before, spill, core):
    outs = (held(CORNER_TILES, cells), pairs(cells))
    arrays = [corners, turned, before, spill, core]
    return call(corner_kernel, outs, corner_scratch(cells), CORNER_TILES, *arrays)


def cell_sums(cell, slot, lines, stored, before, first=0):
    sums_s, sums_t = start_sums(cell, before, range(BLOCKS))
    for index, line in enumerate(lines):
        line_s, line_t = line(0), line(1)
        for block in range(BLOCKS):
            value = stored[slot, block, first + index]
            sums_s[block] = sums_s[block] + value * line_s
            sums_t[block] = sums_t[block] + value * line_t
    return sums_s, sums_t


def apply_cell(cell, slot, lines, stored, before, sums, first=0):
    sums_s, sums_t = cell_sums(cell, slot, lines, stored, before, first)
    for block in range(BLOCKS):
        sums[slot, block, 0] = sums_s[block]
        sums[slot, block, 1] = sums_t[block]


def widen(pieces, wides, scale=None):
    for piece, wide in zip(pieces, wides):
        wide[:, 0:2, :] = piece[...] if scale is None else scale * piece[...]


def apply_core_kernel(info, core, stored, sums, spill, wide, packed, spills):
    widen([core], [wide])
    pack_core(info, wide, packed, spills, False)
    core_spills(spills, spill)

    def one_cell(cell, _):
        lines = lines_of(packed, core_columns(cell // CZ), cell % CZ)
        apply_cell(cell, cell, lines, stored, None, sums)
        return 0

    lax.fori_loop(0, CELLS, one_cell, 0, unroll=8)


def apply_face_kernel(*refs):
    infos, pieces, (stored, before, spill_before, sums, spill), wides, (packed, spills) = split(
        refs, 3, 3, 5, 3, 2
    )
    widen(pieces, wides)
    pack_faces(infos, wides, packed, spills, False)
    face_spills(spills, spill_before, spill)

    def one_cell(cell, _):
        lines = lines_of(packed, face_columns(cell // CZ), cell % CZ)
        apply_cell(cell, cell, lines, stored, before, sums)
        return 0

    lax.fori_loop(0, CELLS, one_cell, 0, unroll=8)


def apply_corner_cells(stored, before, spill_before, core, out, packed, spills, rest, sums):
    slots = stored.shape[0]
    place = PLACES[slots]
    corner_spills(spills, spill_before, rest, place)

    def work(slot):
        q, z = place(slot)
        lines = lines_of(packed, [q], z) + [rest_line(rest, slot)]
        apply_cell(q * CZ + z, slot, lines, stored, before, sums)

    def finish(slot):
        finish_cell(slot, place, slot, core, sums, out)

    corner_loop(0, slots, work, finish, sums)


def upper_corner_cells(stored, before, spill_before, turned, packed, spills, rest, total):
    slots = stored.shape[0]
    place = PLACES[slots]
    for slot in range(slots):
        q, z = place(slot)
        tile = spill_before[q * CZ + z]
        rest[slot] = tile + spills[q * CZ + z] if q >= CY else tile

    def weigh(cell, sums, total):
        total_s, total_t = total
        for block in range(BLOCKS):
            total_s = total_s + sums[0][block] * turned[cell, block, 0]
            total_t = total_t + sums[1][block] * turned[cell, block, 1]
        return total_s, total_t

    def low(slot, total):
        q, z = place(slot)
        cell = q * CZ + z
        return weigh(cell, cell_sums(cell, slot, [rest_line(rest, slot)], stored, before, 2), total)

    def high(slot, total):
        q, z = place(slot)
        cell = q * CZ + z
        lines = lines_of(packed, [q], z) + [rest_line(rest, slot)]
        return weigh(cell, cell_sums(cell, slot, lines, stored, before), total)

    total = lax.fori_loop(0, slots // 2, low, total, unroll=4)
    return lax.fori_loop(slots // 2, slots, high, total, unroll=4)


def upper_face_kernel(
    info_high, info_beyond, high, beyond, stored, before, spill_before, sums, spill,
    wide_high, wide_beyond, packed, spills,
):
    wides = [wide_high, wide_beyond]
    widen([high, beyond], wides, 2.0)
    pack_upper_faces([info_high, info_beyond], wides, packed, spills)
    for cell in range(CELLS):
        q, z = cell // CZ, cell % CZ
        groups, _ = upper_columns(q)
        spill[cell] = sum([spills[c * CZ + z] for group in groups for c in group], spill_before[z])
    sums[0:CZ] = before[0:CZ]
    for q in range(1, QUADS):
        groups, first = upper_columns(q)
        columns = [column for group in groups for column in group]

        def one_cell(z, _, q=q, columns=columns, first=first):
            cell = q * CZ + z
            apply_cell(cell, cell, lines_of(packed, columns, z), stored, before, sums, first)
            return 0

        lax.fori_loop(0, CZ, one_cell, 0, unroll=8)


def apply_corner_kernel(
    info, corners, stored, before, spill_before, core, out, wide, packed, spills, rest, sums
):
    widen([corners], [wide])
    pack_corners(info, wide, packed, spills, False, LAYERS[stored.shape[0]])
    apply_corner_cells(
        stored, before, spill_before, core, out, packed, spills, rest, sums
    )


def split(refs, *sizes):
    parts = []
    for size in sizes:
        parts.append(refs[:size])
        refs = refs[size:]
    return parts


def turn_pairs(core, turned):
    row = row_index((8, 2 * LANES))
    chosen = ((row & 1) == lane_index((8, 2 * LANES)) >> 7) & (row < 6)
    ones = jnp.where(chosen, 1.0, 0.0).astype(jnp.bfloat16)
    for cell in range(CELLS):
        pair = core[(cell // CZ) * EZ + cell % CZ + 1]
        parts = jnp.concatenate(parts_of(pair) + (jnp.zeros_like(pair),), axis=0)
        left = parts.T[: 8 * BLOCKS + 8].astype(jnp.bfloat16)
        wide = lax.dot_general(
            left, ones, (((1,), (0,)), ((), ())), preferred_element_type=jnp.float32
        )
        for block in range(BLOCKS):
            for k in range(2):
                turned[cell, block, k] = wide[8 * block : 8 * block + 8, k * LANES : (k + 1) * LANES]


def pair_place(index):
    return lane_index((2, LANES)) - row_index((2, LANES)) == 2 * index


def last_core_kernel(
    info, core, stored, slots, first, second, sums, spill, turned, line, wide, packed, spills
):
    turn_pairs(core, turned)
    apply_core_kernel(info, core, stored, sums, spill, wide, packed, spills)
    d = slots[:, 1 : 1 + CZ, 6:7, :].reshape(CELLS, 1, LANES)
    v_0 = slots[:, 1 : 1 + CZ, 4:6, :].reshape(CELLS, 2, LANES)
    v_1 = first[:, 1 : 1 + CZ].reshape(v_0.shape)
    v_2 = second[:, 1 : 1 + CZ].reshape(v_0.shape)
    d_0 = d * v_0
    d_2 = d * v_2
    parts = [d_0 * v_0, d_0 * v_1, d * v_1 * v_1, d_2 * v_1, d_2 * v_2, None, v_0, v_1, v_2]
    found = jnp.zeros((2, LANES), jnp.float32)
    for index, part in enumerate(parts):
        if part is not None:
            total = jnp.sum(jnp.sum(part, axis=0), axis=1, keepdims=True)
            found = jnp.where(pair_place(index), total, found)
    line[...] = found


def apply_last_kernel(
    info, corners, edge, inner, before, spill_before, turned, line, moments,
    wide, packed, spills, edge_rest, inner_rest,
):
    widen([corners], [wide], 2.0)
    pack_upper_corners(info, wide, packed, spills)
    total = (jnp.zeros((8, LANES), jnp.float32), jnp.zeros((8, LANES), jnp.float32))
    for stored, rest in ((edge, edge_rest), (inner, inner_rest)):
        total = upper_corner_cells(
            stored, before, spill_before, turned, packed, spills, rest, total
        )
    last = [jnp.sum(part, axis=0, keepdims=True) for part in total]
    last = PAIR_SCALE * jnp.sum(jnp.concatenate(last, axis=0), axis=1, keepdims=True)
    found = jnp.where(pair_place(5), last, line[...])
    moments[...] = jnp.sum(found, axis=0, keepdims=True)


def wide(piece):
    return VMEM((piece.shape[0], 8, LANES), jnp.float32)


def apply_core(info, core, stored):
    stored = pltpu.with_memory_space_constraint(stored, VMEM)
    scratch = [wide(core)] + packs(4)
    return call(apply_core_kernel, (SUMS, CORE_SPILL), scratch, 2, info, core, stored)


def apply_faces(infos, pieces, stored, before, spill):
    stored = pltpu.with_memory_space_constraint(stored, VMEM)
    scratch = [wide(piece) for piece in pieces] + packs(8)
    return call(
        apply_face_kernel, (SUMS, SPILL), scratch, 2, *infos, *pieces, stored, before, spill
    )


def apply_upper_faces(infos, pieces, stored, before, spill):
    stored = pltpu.with_memory_space_constraint(stored, VMEM)
    scratch = [wide(piece) for piece in pieces] + packs(8)
    return call(
        upper_face_kernel, (SUMS, SPILL), scratch, 2, *infos, *pieces, stored, before, spill
    )


def apply_corners(info, corners, stored, before, spill, core):
    stored = pltpu.with_memory_space_constraint(stored, VMEM)
    cells = stored.shape[0]
    arrays = [info, corners, stored, before, spill, core]
    scratch = [wide(corners)] + corner_scratch(cells)
    return call(apply_corner_kernel, pairs(cells), scratch, 2, *arrays)


def apply_last_core(info, core, stored, slots, first, second):
    stored = pltpu.with_memory_space_constraint(stored, VMEM)
    outs = (SUMS, CORE_SPILL, SUMS, jax.ShapeDtypeStruct((2, LANES), jnp.float32))
    scratch = [wide(core)] + packs(4)
    return call(last_core_kernel, outs, scratch, 2, info, core, stored, slots, first, second)


def apply_last(info, corners, edge, inner, before, spill, turned, line):
    edge = pltpu.with_memory_space_constraint(edge, VMEM)
    inner = pltpu.with_memory_space_constraint(inner, VMEM)
    arrays = [info, corners, edge, inner, before, spill, turned, line]
    scratch = [wide(corners)] + packs(4)
    scratch += [VMEM((cells, 8, LANES), jnp.float32) for cells in (EDGES, INNER)]
    out = jax.ShapeDtypeStruct((1, LANES), jnp.float32)
    return call(apply_last_kernel, out, scratch, 2, *arrays)


def solve(g):
    tiny = 1e-6
    h = [g[k] + g[k + 1] for k in range(5)]
    ratio_1 = h[1] / h[0]
    ratio_2 = h[2] / h[0]
    pivot_1 = h[2] - ratio_1 * h[1]
    mixed = h[3] - ratio_1 * h[2]
    rest_1 = g[1] - ratio_1 * g[0]
    live_1 = pivot_1 > tiny * h[2]
    safe_1 = jnp.where(live_1, pivot_1, 1.0)
    ratio_3 = jnp.where(live_1, mixed / safe_1, 0.0)
    pivot_2 = h[4] - ratio_2 * h[2] - ratio_3 * mixed
    rest_2 = g[2] - ratio_2 * g[0] - ratio_3 * rest_1
    live_2 = live_1 & (pivot_2 > tiny * h[4])
    c_2 = jnp.where(live_2, rest_2 / jnp.where(live_2, pivot_2, 1.0), 0.0)
    c_1 = jnp.where(live_1, (rest_1 - mixed * c_2) / safe_1, 0.0)
    c_0 = (g[0] - h[1] * c_1 - h[2] * c_2) / h[0]
    return c_0, c_1, c_2


def invert(counts, atoms, places):
    rows = places.shape[1]
    row_low = row_index((LANES, LANES))
    row_high = row_index((rows, LANES))
    lane = lane_index((rows, LANES))

    def one_cell(cell, total):
        live = lane_index((1, LANES)) < counts[cell]
        pointer = jnp.where(live, atoms[pl.ds(cell, 1), :], -1)
        here = (pointer >> 7) == row_high
        cells = jnp.where(here, cell, 0).astype(jnp.float32)
        slots = jnp.where(here, lane, 0).astype(jnp.float32)
        parts = jnp.concatenate([cells, slots], axis=0).astype(jnp.bfloat16)
        lows = jnp.where((pointer & 127) == row_low, 1.0, 0.0).astype(jnp.bfloat16)
        return total + lax.dot_general(
            parts, lows, (((1,), (1,)), ((), ())), preferred_element_type=jnp.float32
        )

    total = jnp.zeros((2 * rows, LANES), jnp.float32)
    total = lax.fori_loop(0, CELLS, one_cell, total, unroll=8).astype(jnp.int32)
    places[0] = total[:rows]
    places[1] = total[rows:]


def inverted(counts, atoms, atoms_local):
    rows = (atoms_local // LANES + 15) // 16 * 16
    return call(invert, jax.ShapeDtypeStruct((2, rows, LANES), jnp.int32), [], 2, counts, atoms)


def finish_kernel(moments, slots, first, second, places, out, charges):
    summed = moments[...]
    lane = lane_index((2, LANES))
    row = row_index((2, LANES))

    def pair(index):
        picked = jnp.where(lane - row == 2 * index, summed, 0.0)
        return jnp.broadcast_to(jnp.sum(picked, axis=1, keepdims=True), (2, LANES))

    rows = [pair(index) for index in range(9)]
    c_0, c_1, c_2 = solve(rows[:6])
    totals = c_0 * rows[6] + c_1 * rows[7] + c_2 * rows[8]
    balance = totals[0:1] / totals[1:2]
    sign = jnp.concatenate([jnp.ones((1, LANES), jnp.float32), -balance], axis=0)
    c_0, c_1, c_2 = c_0 * sign, c_1 * sign, c_2 * sign
    for cell in range(CELLS):
        q, z = cell // CZ, cell % CZ + 1
        mixed = c_0 * slots[q, z, 4:6, :] + c_1 * first[q, z] + c_2 * second[q, z]
        charges[cell : cell + 1, :] = jnp.sum(mixed, axis=0, keepdims=True)
    tiles = [jnp.zeros((8, LANES), jnp.float32) for _ in range((out.shape[0] + 7) // 8)]
    for cell in range(CELLS):
        line = spread(charges[cell : cell + 1, :])
        for at in range(len(tiles)):
            here = slice(8 * at, 8 * at + 8)
            moved = jnp.take_along_axis(line, places[1, here, :], axis=1)
            tiles[at] = jnp.where(places[0, here, :] == cell, moved, tiles[at])
    out[...] = jnp.concatenate(tiles, axis=0)[: out.shape[0]]


def finish(moments, slots, first, second, places, atoms_local):
    return pl.pallas_call(
        finish_kernel,
        out_shape=jax.ShapeDtypeStruct((atoms_local // LANES, LANES), jnp.float32),
        in_specs=[IN_VMEM] * 5,
        out_specs=IN_VMEM,
        scratch_shapes=[VMEM((CELLS, LANES), jnp.float32)],
        compiler_params=params(8),
    )(moments, slots, first, second, places)


def partner(block, axis, mask):
    count = lax.axis_size(axis)
    return lax.ppermute(block, axis, [(low, low ^ mask) for low in range(count)])


def shifted(block, along_x, across_y=0):
    count = lax.axis_size("gx")
    route = [(i, ((i + 4 * along_x) % count) ^ (2 * across_y)) for i in range(count)]
    return lax.ppermute(block, "gx", route)


def with_z_faces(edge, inner):
    other = partner(edge, "gx", 1)
    parts = [other[:, 0:1], edge[:, 1:2], inner, edge[:, 0:1], other[:, 1:2]]
    return jnp.concatenate(parts, axis=1)


def flat(columns):
    return columns.reshape((-1,) + columns.shape[-2:])


def x_faces(core):
    count = lax.axis_size("gx")
    rows = count // 4
    odd = (lax.axis_index("gx") // 4) % 2 == 1
    if rows % 2:
        return shifted(core[2:], 1), shifted(core[:2], -1)
    route = [(i, (i + (4 if (i // 4) % 2 else -4)) % count) for i in range(count)]
    second = lax.ppermute(jnp.where(odd, core[2:], core[:2]), "gx", route)
    first = lax.ppermute(jnp.where(odd, core[:2], core[2:]), "gx", [(i, i ^ 4) for i in range(count)])
    return first, second


def sorted_faces(first, second):
    odd = (lax.axis_index("gx") // 4) % 2 == 1
    if (lax.axis_size("gx") // 4) % 2:
        return first, second
    return jnp.where(odd, first, second), jnp.where(odd, second, first)


def exchange(edge, inner, on_core, on_faces, on_corners, faces_last=False):
    core = with_z_faces(edge, inner)
    first, second = x_faces(core)
    beyond = partner(core, "gx", 2)
    sums, spill, *more = on_core(flat(core))
    if faces_last:
        second, first, beyond, sums = lax.optimization_barrier((second, first, beyond, sums))
    else:
        second, first, sums = lax.optimization_barrier((second, first, sums))
    low, high = sorted_faces(first, second)
    corners = partner(jnp.concatenate([low, high], axis=0), "gx", 2)
    pieces = [flat(part) for part in (low, high, beyond)]
    sums, spill, *more = on_faces(pieces, sums, spill, *more)
    corners = flat(corners)
    return core, pieces, corners, on_corners(corners, sums, spill, core, *more)


def global_sum(values):
    count = lax.axis_size("gx")
    if count & (count - 1):
        return lax.psum(values, "gx")
    step = 1
    while step < count:
        if step >= 2 and 4 * step <= count:
            others = [partner(values, "gx", k * step) for k in (1, 2, 3)]
            values = (values + others[0]) + (others[1] + others[2])
            step *= 4
        else:
            values = values + partner(values, "gx", step)
            step *= 2
    return values


def local(cell_offsets, electronegativity, hardness, charge_widths, cell_counts, cell_atoms):
    edge, inner = prepare(
        cell_counts, cell_offsets, electronegativity, hardness, charge_widths, cell_atoms
    )
    stored = []

    def keep(tiles, *others):
        stored.append(tiles)
        return others

    def build_ends(corners, sums, spill, core, *own):
        (edge,) = keep(*build_corners(EDGES, corners, *own, sums, spill, flat(core)))
        (inner,) = keep(*build_corners(INNER, corners, *own, sums, spill, flat(core)))
        return by_column(edge), by_column(inner)

    def by_column(cells):
        return cells.reshape((QUADS, -1) + cells.shape[1:])

    slots, pieces, corners, ends = exchange(
        by_column(edge),
        by_column(inner),
        lambda core: keep(*build_core(core)),
        lambda faces, sums, spill, *own: keep(*build_faces(faces, *own, sums, spill)) + own,
        build_ends,
        faces_last=True,
    )
    info = flat(slots)

    def apply(edge, inner, on_corners):
        return exchange(
            edge,
            inner,
            lambda own: apply_core(info, own, stored[0]),
            lambda faces, sums, spill: apply_faces(pieces, faces, stored[1], sums, spill),
            on_corners,
        )

    def apply_ends(others, sums, spill, _):
        edge = apply_corners(corners, others, stored[2], sums, spill, info)
        inner = apply_corners(corners, others, stored[3], sums, spill, info)
        return by_column(edge), by_column(inner)

    first, _, _, ends = apply(*ends, apply_ends)
    second = with_z_faces(*ends)
    high = shifted(second[:2], -1)
    beyond = partner(second, "gx", 2)
    corner = shifted(second[:2], -1, 1)
    sums, spill, turned, line = apply_last_core(
        info, flat(second), stored[0], slots, first, second
    )
    high, beyond, sums = lax.optimization_barrier((high, beyond, sums))
    upper = [flat(high), flat(beyond)]
    sums, spill = apply_upper_faces(pieces[1:], upper, stored[1], sums, spill)
    corner, sums = lax.optimization_barrier((corner, sums))
    moments = apply_last(
        corners, flat(corner), stored[2], stored[3], sums, spill, turned, line
    )
    moments, cell_counts, cell_atoms = lax.optimization_barrier((moments, cell_counts, cell_atoms))
    atoms_local = cell_offsets.shape[1]
    places = inverted(cell_counts, cell_atoms, atoms_local)
    charges = finish(global_sum(moments), slots, first, second, places, atoms_local)
    return charges.reshape(-1)


def solution(mesh):
    placed = (
        P(None, ("grp", "gx")),
        P(("grp", "gx")),
        P(("grp", "gx")),
        P(("grp", "gx")),
        P(("grp", "gx")),
        P(("grp", "gx"), None),
    )
    return jax.shard_map(
        local, mesh=mesh, in_specs=placed, out_specs=P(("grp", "gx")), check_vma=False
    )
```

```python
import functools
import math

import jax
import jax.numpy as jnp
from jax import lax
from jax.experimental import pallas as pl
from jax.experimental.pallas import tpu as pltpu
from jax.sharding import PartitionSpec as P

CX = 2
CY = 2
CZ = 8
EZ = CZ + 2
CELLS = CX * CY * CZ
QUADS = CX * CY
LANES = 128
BLOCKS = 11
GROUPS = ((0, 1, 2, 3), (4, 5, 6, 7), (8, 9, 10))

COULOMB = 14.399645
ROOT_PI = math.sqrt(math.pi)
SCREEN = 1.0 / (math.sqrt(2.0) * 3.0)
EWALD_SELF = math.sqrt(2.0 / math.pi) / 3.0
SIDE = 12.0 * SCREEN
CUT_SQUARED = (12.0 * SCREEN) ** 2
CLOSEST_SQUARED = (0.5 * SCREEN) ** 2
PAIR_SCALE = COULOMB * SCREEN

VMEM = pltpu.VMEM
SMEM = pltpu.SMEM


def params(mib):
    return pltpu.CompilerParams(vmem_limit_bytes=mib * 2**20)


def lane_index(shape):
    return lax.broadcasted_iota(jnp.int32, shape, len(shape) - 1)


def row_index(shape):
    return lax.broadcasted_iota(jnp.int32, shape, len(shape) - 2)


def edge_place(slot):
    return slot // 2, (CZ - 1) * (1 - slot % 2)


def inner_place(slot):
    return slot // (CZ - 2), 1 + slot % (CZ - 2)


EDGES = 2 * QUADS
INNER = CELLS - EDGES
PLACES = {EDGES: edge_place, INNER: inner_place}
LAYERS = {EDGES: (0, CZ - 1), INNER: range(1, CZ - 1)}


def gather_cells(counted, atoms, table, others, out):
    place = PLACES[out.shape[0]]
    row = row_index((8, LANES))
    lane = lane_index((1, LANES))

    def pick(source, pointers):
        share = 8 // len(pointers)
        pointer = spread(pointers[-1])
        for k in range(len(pointers) - 2, -1, -1):
            pointer = jnp.where(row < share * (k + 1), pointers[k], pointer)
        high = pointer >> 7
        low = pointer & 127
        picked = jnp.zeros((8, LANES), jnp.float32)
        for chunk in range(source.shape[0]):
            part = jnp.take_along_axis(source[chunk], low, axis=1)
            picked = jnp.where(high == chunk, part, picked)
        return picked

    def four_cells(step, _):
        slots = [4 * step + k for k in range(4)]
        places = [place(slot) for slot in slots]
        counts = [counted[pl.ds(q * CZ + z, 1), :] for q, z in places]
        occupied = [lane < count for count in counts]
        pointers = [
            jnp.where(live, atoms[pl.ds(q * CZ + z, 1), :], 0)
            for (q, z), live in zip(places, occupied)
        ]
        pairs = [pick(table, pointers[:2]), pick(table, pointers[2:])]
        both = pick(others, pointers)
        for k, (slot, live) in enumerate(zip(slots, occupied)):
            q = places[k][0]
            at = 4 * (k % 2)
            picked = pairs[k // 2][at : at + 4]
            width = jnp.where(live, picked[3:4], 1.0)
            hard = both[2 * k + 1 : 2 * k + 2]
            diag = jnp.where(live, hard + COULOMB * (1.0 / (width * ROOT_PI) - EWALD_SELF), 1.0)
            negative = jnp.where(live, both[2 * k : 2 * k + 1], 0.0)
            out[slot, 0:1, :] = (picked[0:1] + (q // CY).astype(jnp.float32)) * SIDE
            out[slot, 1:2, :] = (picked[1:2] + (q % CY).astype(jnp.float32)) * SIDE
            out[slot, 2:3, :] = picked[2:3] * SIDE
            out[slot, 3:4, :] = (2.0 * SCREEN * SCREEN) * width * width
            out[slot, 4:5, :] = -negative / diag
            out[slot, 5:6, :] = jnp.where(live, 1.0 / diag, 0.0)
            out[slot, 6:7, :] = diag
            out[slot, 7:8, :] = counts[k].astype(jnp.float32)
        return 0

    lax.fori_loop(0, out.shape[0] // 4, four_cells, 0, unroll=2)


def prepare_kernel(
    counts_hbm, offsets, negativity, hardness, widths, atoms_hbm, edge, counted, atoms, table, others,
    counts, raw_offsets, raw_negativity, raw_hardness, raw_widths, sems,
):
    copies = [
        pltpu.make_async_copy(source, target, sems.at[index])
        for index, (source, target) in enumerate(
            [
                (counts_hbm, counts),
                (offsets, raw_offsets),
                (negativity, raw_negativity),
                (hardness, raw_hardness),
                (widths, raw_widths),
                (atoms_hbm, atoms),
            ]
        )
    ]
    for copy in copies:
        copy.start()
    for copy in copies:
        copy.wait()
    for chunk in range(table.shape[0]):
        here = slice(chunk * LANES, (chunk + 1) * LANES)
        for first in (0, 4):
            table[chunk, first : first + 3, :] = raw_offsets[:, here]
            table[chunk, first + 3 : first + 4, :] = raw_widths[chunk : chunk + 1, :]
        for first in (0, 2, 4, 6):
            others[chunk, first : first + 1, :] = raw_negativity[chunk : chunk + 1, :]
            others[chunk, first + 1 : first + 2, :] = raw_hardness[chunk : chunk + 1, :]
    for cell in range(CELLS):
        counted[cell : cell + 1, :] = jnp.full((1, LANES), counts[cell])
    gather_cells(counted, atoms, table, others, edge)


def prepare_rest_kernel(counted, atoms, table, others, inner):
    gather_cells(counted, atoms, table, others, inner)


def prepare(counts, offsets, negativity, hardness, widths, atoms):
    chunks = offsets.shape[1] // LANES
    plane = (chunks, LANES)
    tables = jax.ShapeDtypeStruct((chunks, 8, LANES), jnp.float32)
    lists = jax.ShapeDtypeStruct(atoms.shape, jnp.int32)
    edge, *rest = pl.pallas_call(
        prepare_kernel,
        out_shape=(
            jax.ShapeDtypeStruct((EDGES, 8, LANES), jnp.float32),
            lists,
            lists,
            tables,
            tables,
        ),
        in_specs=[pl.BlockSpec(memory_space=pltpu.HBM)] * 6,
        out_specs=(pl.BlockSpec(memory_space=VMEM),) * 5,
        scratch_shapes=[
            SMEM(counts.shape, jnp.int32),
            VMEM(offsets.shape, jnp.float32),
            VMEM(plane, jnp.float32),
            VMEM(plane, jnp.float32),
            VMEM(plane, jnp.float32),
            pltpu.SemaphoreType.DMA((6,)),
        ],
        compiler_params=params(8),
    )(
        *[
            pltpu.with_memory_space_constraint(array, pltpu.HBM)
            for array in (
                counts,
                offsets,
                negativity.reshape(plane),
                hardness.reshape(plane),
                widths.reshape(plane),
                atoms,
            )
        ]
    )
    inner = pl.pallas_call(
        prepare_rest_kernel,
        out_shape=jax.ShapeDtypeStruct((INNER, 8, LANES), jnp.float32),
        in_specs=[pl.BlockSpec(memory_space=VMEM)] * 4,
        out_specs=pl.BlockSpec(memory_space=VMEM),
        compiler_params=params(8),
        cost_estimate=pl.CostEstimate(flops=2**20, bytes_accessed=2**22, transcendentals=0),
    )(*rest)
    return edge, inner


def pack_column(
    info, cells, source, packed, spills, target, at, shift, layers=range(CZ), info_source=None
):
    lane = lane_index((8, LANES))
    row = row_index((8, LANES))
    for z in layers:
        base = source * EZ + z
        known = base if info_source is None else info_source * EZ + z
        low, mid, top = [spread(info[known + k, 7:8, :]).astype(jnp.int32) for k in range(3)]
        end = low + mid - LANES
        tiles = [cells[base + k] for k in range(3)]
        if shift is not None:
            for k in range(3):
                offset = jnp.where(row == 2, (k - 1) * SIDE, 0.0)
                for axis in range(2):
                    offset = jnp.where(row == axis, shift[axis] * SIDE, offset)
                tiles[k] = tiles[k] + offset
        second = jnp.take_along_axis(tiles[1], (lane - low) & 127, axis=1)
        third = jnp.take_along_axis(tiles[2], (lane - end) & 127, axis=1)
        packed[target * CZ + z, 0] = jnp.where(lane < low, tiles[0], second)
        packed[target * CZ + z, 1] = jnp.where(lane < end, second, third)
        spill = jnp.where(lane < end + top - LANES, third, 0.0)
        spills[target * CZ + z] = pltpu.roll(spill, at, 1) if at else spill


def pack_core(info, cells, packed, spills, build):
    for q in range(QUADS):
        pack_column(info, cells, q, packed, spills, q, 8 * q, (0, 0) if build else None)


def pack_faces(infos, pieces, packed, spills, build):
    for side in range(2):
        sign = 2 * side - 1
        for y in range(CY):
            shift = (sign * CX, 0) if build else None
            at = 32 + 8 * y
            pack_column(infos[side], pieces[side], y, packed, spills, 2 * side + y, at, shift)
        for x in range(CX):
            shift = (0, sign * CY) if build else None
            source = 2 * x + 1 - side
            target = 4 + 2 * x + side
            at = 48 + 8 * x
            pack_column(infos[2], pieces[2], source, packed, spills, target, at, shift)


def pack_corners(info, cells, packed, spills, build, layers):
    for side_x in range(2):
        for side_y in range(2):
            shift = ((2 * side_x - 1) * CX, (2 * side_y - 1) * CY) if build else None
            source = 2 * side_x + 1 - side_y
            target = 2 * side_x + side_y
            pack_column(info, cells, source, packed, spills, target, 64, shift, layers)


def pack_upper_faces(infos, pieces, packed, spills):
    for y in range(CY):
        pack_column(infos[0], pieces[0], y, packed, spills, 2 + y, 32 + 8 * y, None)
    for x in range(CX):
        pack_column(infos[1], pieces[1], 2 * x, packed, spills, 5 + 2 * x, 48 + 8 * x, None)


def pack_upper_corners(info, cells, packed, spills):
    for side_y in range(2):
        source = 1 - side_y
        pack_column(info, cells, source, packed, spills, 2 + side_y, 64, None, info_source=2 + source)


def upper_columns(q):
    columns = face_columns(q)
    return [columns[2 * k : 2 * k + 2] for k in range(2) if (q >> (1 - k)) & 1], 4 * (q == 1)


def core_columns(q):
    return [q ^ k for k in range(4)]


def face_columns(q):
    x, y = q >> 1, q & 1
    return [2 * x, 2 * x + 1, 4 + y, 6 + y]


def overflow_of(spills, columns, z):
    return sum(spills[column * CZ + z] for column in columns)


def spread(row):
    return jnp.broadcast_to(row, (8, LANES))


def couple(x_i, y_i, z_i, w_i, x_j, y_j, z_j, w_j):
    delta_x = x_j - x_i
    delta_y = y_j - y_i
    delta_z = z_j - z_i
    squared = delta_x * delta_x + delta_y * delta_y + delta_z * delta_z
    held = jnp.maximum(squared, CLOSEST_SQUARED)
    inverse = lax.rsqrt(held)
    distance = held * inverse
    scaled = distance * lax.rsqrt(w_i + w_j)
    value = (lax.erf(scaled) - lax.erf(distance)) * inverse
    return jnp.where(squared < CUT_SQUARED, value, 0.0)


def to_rows(sums, block):
    here = lane_index((8, LANES)) - row_index((8, LANES)) == 8 * block
    return jnp.where(here, jnp.sum(sums, axis=1, keepdims=True), 0.0)


def add_rows(cell, sums, rows):
    for index in range(2):
        total = jnp.zeros((8, LANES), jnp.float32)
        for block in range(BLOCKS):
            total = total + to_rows(sums[cell, block, index], block)
        rows.append(jnp.sum(total, axis=0, keepdims=True))


def finish_cell(slot, place, target, info, sums, out):
    q, z = place(slot)
    rows = []
    add_rows(slot, sums, rows)
    own = info.at[q * EZ + z + 1]
    scale = PAIR_SCALE / own[6:7, :]
    live = lane_index((1, LANES)) < own[7:8, :].astype(jnp.int32)
    out[target, 0:1, :] = jnp.where(live, rows[0] * scale, 0.0)
    out[target, 1:2, :] = jnp.where(live, rows[1] * scale, 0.0)


def build_cell(cell, slot, lines, turned, kernels, before, sums, below):
    own = None
    if below is not None:
        own = lane_index((8, LANES)) - row_index((8, LANES)) - below
    for group in GROUPS:
        sums_s, sums_t = start_sums(cell, before, group)
        mine = [[turned[cell, block, k] for k in range(4)] for block in group]
        for index, line in enumerate(lines):
            beside = [line(k) for k in range(6)]
            for at, block in enumerate(group):
                value = couple(*mine[at], *beside[:4])
                if own is not None and index < 2:
                    value = jnp.where(own == 8 * block - LANES * index, 0.0, value)
                kernels[slot, block, index] = value
                sums_s[at] = sums_s[at] + value * beside[4]
                sums_t[at] = sums_t[at] + value * beside[5]
        for at, block in enumerate(group):
            sums[slot, block, 0] = sums_s[at]
            sums[slot, block, 1] = sums_t[at]


def start_sums(cell, before, blocks):
    if before is None:
        zeros = [jnp.zeros((8, LANES), jnp.float32) for _ in blocks]
        return zeros, list(zeros)
    sums_s = [before[cell, block, 0] for block in blocks]
    return sums_s, [before[cell, block, 1] for block in blocks]


def lines_of(packed, columns, z):
    def line(column, half):
        return lambda k: spread(packed[column * CZ + z, half, k : k + 1, :])

    return [line(column, half) for column in columns for half in range(2)]


def rest_line(rest, cell):
    return lambda k: spread(rest[cell, k : k + 1, :])


def parts_of(value):
    high = value.astype(jnp.bfloat16).astype(jnp.float32)
    rest = value - high
    middle = rest.astype(jnp.bfloat16).astype(jnp.float32)
    return high, middle, rest - middle


def turn_cells(core, turned):
    chosen = row_index((24, 4 * LANES)) & 7
    ones = jnp.where(chosen == lane_index((24, 4 * LANES)) >> 7, 1.0, 0.0).astype(jnp.bfloat16)
    for cell in range(CELLS):
        here = core[(cell // CZ) * EZ + cell % CZ + 1]
        left = jnp.concatenate(parts_of(here), axis=0).T[: 8 * BLOCKS + 8].astype(jnp.bfloat16)
        wide = lax.dot_general(
            left, ones, (((1,), (0,)), ((), ())), preferred_element_type=jnp.float32
        )
        for block in range(BLOCKS):
            for k in range(4):
                turned[cell, block, k] = wide[8 * block : 8 * block + 8, k * LANES : (k + 1) * LANES]


def core_spills(spills, spill):
    for z in range(CZ):
        spill[z] = overflow_of(spills, range(QUADS), z)


def face_spills(spills, before, spill):
    for cell in range(CELLS):
        q, z = cell // CZ, cell % CZ
        spill[cell] = before[z] + overflow_of(spills, face_columns(q), z)


def corner_loop(start, stop, work, finish, sums):
    def one_cell(slot, _):
        finish(jnp.maximum(slot - 1, start))
        work(slot)
        return 0

    sums[start] = jnp.zeros(sums.shape[1:], jnp.float32)
    lax.fori_loop(start, stop, one_cell, 0, unroll=4)
    finish(stop - 1)


def corner_spills(spills, before, rest, place):
    for slot in range(rest.shape[0]):
        q, z = place(slot)
        rest[slot] = before[q * CZ + z] + spills[q * CZ + z]


def core_kernel(core, kernels, sums, spill, turned, packed, spills):
    turn_cells(core, turned)
    pack_core(core, core, packed, spills, True)
    core_spills(spills, spill)

    def one_cell(cell, _):
        q, z = cell // CZ, cell % CZ
        below = spread(core[q * EZ + z, 7:8, :]).astype(jnp.int32)
        lines = lines_of(packed, core_columns(q), z)
        build_cell(cell, cell, lines, turned, kernels, None, sums, below)
        return 0

    lax.fori_loop(0, CELLS, one_cell, 0, unroll=4)


def face_kernel(
    x_low, x_high, beyond, turned, before, spill_before, kernels, sums, spill, packed, spills
):
    pieces = [x_low, x_high, beyond]
    pack_faces(pieces, pieces, packed, spills, True)
    face_spills(spills, spill_before, spill)

    def one_cell(cell, _):
        lines = lines_of(packed, face_columns(cell // CZ), cell % CZ)
        build_cell(cell, cell, lines, turned, kernels, before, sums, None)
        return 0

    lax.fori_loop(0, CELLS, one_cell, 0, unroll=4)


def corner_kernel(
    corners, turned, before, spill_before, core, kernels, out, packed, spills, rest, sums
):
    slots = kernels.shape[0]
    place = PLACES[slots]
    pack_corners(corners, corners, packed, spills, True, LAYERS[slots])
    corner_spills(spills, spill_before, rest, place)

    def work(slot):
        q, z = place(slot)
        lines = lines_of(packed, [q], z) + [rest_line(rest, slot)]
        build_cell(q * CZ + z, slot, lines, turned, kernels, before, sums, None)

    def finish(slot):
        finish_cell(slot, place, slot, core, sums, out)

    corner_loop(0, slots, work, finish, sums)


IN_VMEM = pl.BlockSpec(memory_space=VMEM)
IN_SMEM = pl.BlockSpec(memory_space=SMEM)
PAIR = jax.ShapeDtypeStruct((CELLS, 2, LANES), jnp.float32)
SPILL = jax.ShapeDtypeStruct((CELLS, 8, LANES), jnp.float32)
SUMS = jax.ShapeDtypeStruct((CELLS, BLOCKS, 2, 8, LANES), jnp.float32)
TURNED = jax.ShapeDtypeStruct((CELLS, BLOCKS, 4, 8, LANES), jnp.float32)
CORE_SPILL = jax.ShapeDtypeStruct((CZ, 8, LANES), jnp.float32)
CORE_TILES, FACE_TILES, CORNER_TILES = 8, 8, 3


def held(tiles, cells=CELLS):
    return VMEM((cells, BLOCKS, tiles, 8, LANES), jnp.float32)


def pairs(cells):
    return jax.ShapeDtypeStruct((cells, 2, LANES), jnp.float32)


def call(kernel, outs, scratch, tiles, *arrays):
    work = CELLS * BLOCKS * tiles * 8 * LANES
    return pl.pallas_call(
        kernel,
        out_shape=outs,
        in_specs=[IN_SMEM if array.ndim == 1 else IN_VMEM for array in arrays],
        out_specs=jax.tree.map(lambda _: IN_VMEM, outs),
        scratch_shapes=scratch,
        compiler_params=params(8),
        cost_estimate=pl.CostEstimate(
            flops=30 * work, bytes_accessed=8 * work, transcendentals=4 * work
        ),
    )(*arrays)


def packs(columns):
    return [
        VMEM((columns * CZ, 2, 8, LANES), jnp.float32),
        VMEM((columns * CZ, 8, LANES), jnp.float32),
    ]


def build_core(core):
    outs = (held(CORE_TILES), SUMS, CORE_SPILL, TURNED)
    return call(core_kernel, outs, packs(4), CORE_TILES, core)


def build_faces(pieces, turned, before, spill):
    outs = (held(FACE_TILES), SUMS, SPILL)
    return call(face_kernel, outs, packs(8), FACE_TILES, *pieces, turned, before, spill)


def corner_scratch(cells):
    rest = VMEM((cells, 8, LANES), jnp.float32)
    return packs(4) + [rest, VMEM((cells, BLOCKS, 2, 8, LANES), jnp.float32)]


def build_corners(cells, corners, turned, before, spill, core):
    outs = (held(CORNER_TILES, cells), pairs(cells))
    arrays = [corners, turned, before, spill, core]
    return call(corner_kernel, outs, corner_scratch(cells), CORNER_TILES, *arrays)


def cell_sums(cell, slot, lines, stored, before, first=0):
    sums_s, sums_t = start_sums(cell, before, range(BLOCKS))
    for index, line in enumerate(lines):
        line_s, line_t = line(0), line(1)
        for block in range(BLOCKS):
            value = stored[slot, block, first + index]
            sums_s[block] = sums_s[block] + value * line_s
            sums_t[block] = sums_t[block] + value * line_t
    return sums_s, sums_t


def apply_cell(cell, slot, lines, stored, before, sums, first=0):
    sums_s, sums_t = cell_sums(cell, slot, lines, stored, before, first)
    for block in range(BLOCKS):
        sums[slot, block, 0] = sums_s[block]
        sums[slot, block, 1] = sums_t[block]


def widen(pieces, wides, scale=None):
    for piece, wide in zip(pieces, wides):
        wide[:, 0:2, :] = piece[...] if scale is None else scale * piece[...]


def apply_core_kernel(info, core, stored, sums, spill, wide, packed, spills):
    widen([core], [wide])
    pack_core(info, wide, packed, spills, False)
    core_spills(spills, spill)

    def one_cell(cell, _):
        lines = lines_of(packed, core_columns(cell // CZ), cell % CZ)
        apply_cell(cell, cell, lines, stored, None, sums)
        return 0

    lax.fori_loop(0, CELLS, one_cell, 0, unroll=8)


def apply_face_kernel(*refs):
    infos, pieces, (stored, before, spill_before, sums, spill), wides, (packed, spills) = split(
        refs, 3, 3, 5, 3, 2
    )
    widen(pieces, wides)
    pack_faces(infos, wides, packed, spills, False)
    face_spills(spills, spill_before, spill)

    def one_cell(cell, _):
        lines = lines_of(packed, face_columns(cell // CZ), cell % CZ)
        apply_cell(cell, cell, lines, stored, before, sums)
        return 0

    lax.fori_loop(0, CELLS, one_cell, 0, unroll=8)


def apply_corner_cells(stored, before, spill_before, core, out, packed, spills, rest, sums):
    slots = stored.shape[0]
    place = PLACES[slots]
    corner_spills(spills, spill_before, rest, place)

    def work(slot):
        q, z = place(slot)
        lines = lines_of(packed, [q], z) + [rest_line(rest, slot)]
        apply_cell(q * CZ + z, slot, lines, stored, before, sums)

    def finish(slot):
        finish_cell(slot, place, slot, core, sums, out)

    corner_loop(0, slots, work, finish, sums)


def upper_corner_cells(stored, before, spill_before, turned, packed, spills, rest, total):
    slots = stored.shape[0]
    place = PLACES[slots]
    for slot in range(slots):
        q, z = place(slot)
        tile = spill_before[q * CZ + z]
        rest[slot] = tile + spills[q * CZ + z] if q >= CY else tile

    def weigh(cell, sums, total):
        total_s, total_t = total
        for block in range(BLOCKS):
            total_s = total_s + sums[0][block] * turned[cell, block, 0]
            total_t = total_t + sums[1][block] * turned[cell, block, 1]
        return total_s, total_t

    def low(slot, total):
        q, z = place(slot)
        cell = q * CZ + z
        return weigh(cell, cell_sums(cell, slot, [rest_line(rest, slot)], stored, before, 2), total)

    def high(slot, total):
        q, z = place(slot)
        cell = q * CZ + z
        lines = lines_of(packed, [q], z) + [rest_line(rest, slot)]
        return weigh(cell, cell_sums(cell, slot, lines, stored, before), total)

    total = lax.fori_loop(0, slots // 2, low, total, unroll=4)
    return lax.fori_loop(slots // 2, slots, high, total, unroll=4)


def upper_face_kernel(
    info_high, info_beyond, high, beyond, stored, before, spill_before, sums, spill,
    wide_high, wide_beyond, packed, spills,
):
    wides = [wide_high, wide_beyond]
    widen([high, beyond], wides, 2.0)
    pack_upper_faces([info_high, info_beyond], wides, packed, spills)
    for cell in range(CELLS):
        q, z = cell // CZ, cell % CZ
        groups, _ = upper_columns(q)
        spill[cell] = sum([spills[c * CZ + z] for group in groups for c in group], spill_before[z])
    sums[0:CZ] = before[0:CZ]
    for q in range(1, QUADS):
        groups, first = upper_columns(q)
        columns = [column for group in groups for column in group]

        def one_cell(z, _, q=q, columns=columns, first=first):
            cell = q * CZ + z
            apply_cell(cell, cell, lines_of(packed, columns, z), stored, before, sums, first)
            return 0

        lax.fori_loop(0, CZ, one_cell, 0, unroll=8)


def apply_corner_kernel(
    info, corners, stored, before, spill_before, core, out, wide, packed, spills, rest, sums
):
    widen([corners], [wide])
    pack_corners(info, wide, packed, spills, False, LAYERS[stored.shape[0]])
    apply_corner_cells(
        stored, before, spill_before, core, out, packed, spills, rest, sums
    )


def split(refs, *sizes):
    parts = []
    for size in sizes:
        parts.append(refs[:size])
        refs = refs[size:]
    return parts


def turn_pairs(core, turned):
    row = row_index((8, 2 * LANES))
    chosen = ((row & 1) == lane_index((8, 2 * LANES)) >> 7) & (row < 6)
    ones = jnp.where(chosen, 1.0, 0.0).astype(jnp.bfloat16)
    for cell in range(CELLS):
        pair = core[(cell // CZ) * EZ + cell % CZ + 1]
        parts = jnp.concatenate(parts_of(pair) + (jnp.zeros_like(pair),), axis=0)
        left = parts.T[: 8 * BLOCKS + 8].astype(jnp.bfloat16)
        wide = lax.dot_general(
            left, ones, (((1,), (0,)), ((), ())), preferred_element_type=jnp.float32
        )
        for block in range(BLOCKS):
            for k in range(2):
                turned[cell, block, k] = wide[8 * block : 8 * block + 8, k * LANES : (k + 1) * LANES]


def pair_place(index):
    return lane_index((2, LANES)) - row_index((2, LANES)) == 2 * index


def last_core_kernel(
    info, core, stored, slots, first, second, sums, spill, turned, line, wide, packed, spills
):
    turn_pairs(core, turned)
    apply_core_kernel(info, core, stored, sums, spill, wide, packed, spills)
    d = slots[:, 1 : 1 + CZ, 6:7, :].reshape(CELLS, 1, LANES)
    v_0 = slots[:, 1 : 1 + CZ, 4:6, :].reshape(CELLS, 2, LANES)
    v_1 = first[:, 1 : 1 + CZ].reshape(v_0.shape)
    v_2 = second[:, 1 : 1 + CZ].reshape(v_0.shape)
    d_0 = d * v_0
    d_2 = d * v_2
    parts = [d_0 * v_0, d_0 * v_1, d * v_1 * v_1, d_2 * v_1, d_2 * v_2, None, v_0, v_1, v_2]
    found = jnp.zeros((2, LANES), jnp.float32)
    for index, part in enumerate(parts):
        if part is not None:
            total = jnp.sum(jnp.sum(part, axis=0), axis=1, keepdims=True)
            found = jnp.where(pair_place(index), total, found)
    line[...] = found


def apply_last_kernel(
    info, corners, edge, inner, before, spill_before, turned, line, moments,
    wide, packed, spills, edge_rest, inner_rest,
):
    widen([corners], [wide], 2.0)
    pack_upper_corners(info, wide, packed, spills)
    total = (jnp.zeros((8, LANES), jnp.float32), jnp.zeros((8, LANES), jnp.float32))
    for stored, rest in ((edge, edge_rest), (inner, inner_rest)):
        total = upper_corner_cells(
            stored, before, spill_before, turned, packed, spills, rest, total
        )
    last = [jnp.sum(part, axis=0, keepdims=True) for part in total]
    last = PAIR_SCALE * jnp.sum(jnp.concatenate(last, axis=0), axis=1, keepdims=True)
    found = jnp.where(pair_place(5), last, line[...])
    moments[...] = jnp.sum(found, axis=0, keepdims=True)


def wide(piece):
    return VMEM((piece.shape[0], 8, LANES), jnp.float32)


def apply_core(info, core, stored):
    stored = pltpu.with_memory_space_constraint(stored, VMEM)
    scratch = [wide(core)] + packs(4)
    return call(apply_core_kernel, (SUMS, CORE_SPILL), scratch, 2, info, core, stored)


def apply_faces(infos, pieces, stored, before, spill):
    stored = pltpu.with_memory_space_constraint(stored, VMEM)
    scratch = [wide(piece) for piece in pieces] + packs(8)
    return call(
        apply_face_kernel, (SUMS, SPILL), scratch, 2, *infos, *pieces, stored, before, spill
    )


def apply_upper_faces(infos, pieces, stored, before, spill):
    stored = pltpu.with_memory_space_constraint(stored, VMEM)
    scratch = [wide(piece) for piece in pieces] + packs(8)
    return call(
        upper_face_kernel, (SUMS, SPILL), scratch, 2, *infos, *pieces, stored, before, spill
    )


def apply_corners(info, corners, stored, before, spill, core):
    stored = pltpu.with_memory_space_constraint(stored, VMEM)
    cells = stored.shape[0]
    arrays = [info, corners, stored, before, spill, core]
    scratch = [wide(corners)] + corner_scratch(cells)
    return call(apply_corner_kernel, pairs(cells), scratch, 2, *arrays)


def apply_last_core(info, core, stored, slots, first, second):
    stored = pltpu.with_memory_space_constraint(stored, VMEM)
    outs = (SUMS, CORE_SPILL, SUMS, jax.ShapeDtypeStruct((2, LANES), jnp.float32))
    scratch = [wide(core)] + packs(4)
    return call(last_core_kernel, outs, scratch, 2, info, core, stored, slots, first, second)


def apply_last(info, corners, edge, inner, before, spill, turned, line):
    edge = pltpu.with_memory_space_constraint(edge, VMEM)
    inner = pltpu.with_memory_space_constraint(inner, VMEM)
    arrays = [info, corners, edge, inner, before, spill, turned, line]
    scratch = [wide(corners)] + packs(4)
    scratch += [VMEM((cells, 8, LANES), jnp.float32) for cells in (EDGES, INNER)]
    out = jax.ShapeDtypeStruct((1, LANES), jnp.float32)
    return call(apply_last_kernel, out, scratch, 2, *arrays)


def solve(g):
    tiny = 1e-6
    h = [g[k] + g[k + 1] for k in range(5)]
    ratio_1 = h[1] / h[0]
    ratio_2 = h[2] / h[0]
    pivot_1 = h[2] - ratio_1 * h[1]
    mixed = h[3] - ratio_1 * h[2]
    rest_1 = g[1] - ratio_1 * g[0]
    live_1 = pivot_1 > tiny * h[2]
    safe_1 = jnp.where(live_1, pivot_1, 1.0)
    ratio_3 = jnp.where(live_1, mixed / safe_1, 0.0)
    pivot_2 = h[4] - ratio_2 * h[2] - ratio_3 * mixed
    rest_2 = g[2] - ratio_2 * g[0] - ratio_3 * rest_1
    live_2 = live_1 & (pivot_2 > tiny * h[4])
    c_2 = jnp.where(live_2, rest_2 / jnp.where(live_2, pivot_2, 1.0), 0.0)
    c_1 = jnp.where(live_1, (rest_1 - mixed * c_2) / safe_1, 0.0)
    c_0 = (g[0] - h[1] * c_1 - h[2] * c_2) / h[0]
    return c_0, c_1, c_2


def invert(counts, atoms, places):
    rows = places.shape[1]
    row_low = row_index((LANES, LANES))
    row_high = row_index((rows, LANES))
    lane = lane_index((rows, LANES))

    def one_cell(cell, total):
        live = lane_index((1, LANES)) < counts[cell]
        pointer = jnp.where(live, atoms[pl.ds(cell, 1), :], -1)
        here = (pointer >> 7) == row_high
        cells = jnp.where(here, cell, 0).astype(jnp.float32)
        slots = jnp.where(here, lane, 0).astype(jnp.float32)
        parts = jnp.concatenate([cells, slots], axis=0).astype(jnp.bfloat16)
        lows = jnp.where((pointer & 127) == row_low, 1.0, 0.0).astype(jnp.bfloat16)
        return total + lax.dot_general(
            parts, lows, (((1,), (1,)), ((), ())), preferred_element_type=jnp.float32
        )

    total = jnp.zeros((2 * rows, LANES), jnp.float32)
    total = lax.fori_loop(0, CELLS, one_cell, total, unroll=8).astype(jnp.int32)
    places[0] = total[:rows]
    places[1] = total[rows:]


def inverted(counts, atoms, atoms_local):
    rows = (atoms_local // LANES + 15) // 16 * 16
    return call(invert, jax.ShapeDtypeStruct((2, rows, LANES), jnp.int32), [], 2, counts, atoms)


def finish_kernel(moments, slots, first, second, places, out, charges):
    summed = moments[...]
    lane = lane_index((2, LANES))
    row = row_index((2, LANES))

    def pair(index):
        picked = jnp.where(lane - row == 2 * index, summed, 0.0)
        return jnp.broadcast_to(jnp.sum(picked, axis=1, keepdims=True), (2, LANES))

    rows = [pair(index) for index in range(9)]
    c_0, c_1, c_2 = solve(rows[:6])
    totals = c_0 * rows[6] + c_1 * rows[7] + c_2 * rows[8]
    balance = totals[0:1] / totals[1:2]
    sign = jnp.concatenate([jnp.ones((1, LANES), jnp.float32), -balance], axis=0)
    c_0, c_1, c_2 = c_0 * sign, c_1 * sign, c_2 * sign
    for cell in range(CELLS):
        q, z = cell // CZ, cell % CZ + 1
        mixed = c_0 * slots[q, z, 4:6, :] + c_1 * first[q, z] + c_2 * second[q, z]
        charges[cell : cell + 1, :] = jnp.sum(mixed, axis=0, keepdims=True)
    tiles = [jnp.zeros((8, LANES), jnp.float32) for _ in range((out.shape[0] + 7) // 8)]
    for cell in range(CELLS):
        line = spread(charges[cell : cell + 1, :])
        for at in range(len(tiles)):
            here = slice(8 * at, 8 * at + 8)
            moved = jnp.take_along_axis(line, places[1, here, :], axis=1)
            tiles[at] = jnp.where(places[0, here, :] == cell, moved, tiles[at])
    out[...] = jnp.concatenate(tiles, axis=0)[: out.shape[0]]


def finish(moments, slots, first, second, places, atoms_local):
    return pl.pallas_call(
        finish_kernel,
        out_shape=jax.ShapeDtypeStruct((atoms_local // LANES, LANES), jnp.float32),
        in_specs=[IN_VMEM] * 5,
        out_specs=IN_VMEM,
        scratch_shapes=[VMEM((CELLS, LANES), jnp.float32)],
        compiler_params=params(8),
    )(moments, slots, first, second, places)


def partner(block, axis, mask):
    count = lax.axis_size(axis)
    return lax.ppermute(block, axis, [(low, low ^ mask) for low in range(count)])


def shifted(block, along_x, across_y=0):
    count = lax.axis_size("gx")
    route = [(i, ((i + 4 * along_x) % count) ^ (2 * across_y)) for i in range(count)]
    return lax.ppermute(block, "gx", route)


def with_z_faces(edge, inner):
    other = partner(edge, "gx", 1)
    parts = [other[:, 0:1], edge[:, 1:2], inner, edge[:, 0:1], other[:, 1:2]]
    return jnp.concatenate(parts, axis=1)


def flat(columns):
    return columns.reshape((-1,) + columns.shape[-2:])


def x_faces(core):
    count = lax.axis_size("gx")
    rows = count // 4
    odd = (lax.axis_index("gx") // 4) % 2 == 1
    if rows % 2:
        return shifted(core[2:], 1), shifted(core[:2], -1)
    route = [(i, (i + (4 if (i // 4) % 2 else -4)) % count) for i in range(count)]
    second = lax.ppermute(jnp.where(odd, core[2:], core[:2]), "gx", route)
    first = lax.ppermute(jnp.where(odd, core[:2], core[2:]), "gx", [(i, i ^ 4) for i in range(count)])
    return first, second


def sorted_faces(first, second):
    odd = (lax.axis_index("gx") // 4) % 2 == 1
    if (lax.axis_size("gx") // 4) % 2:
        return first, second
    return jnp.where(odd, first, second), jnp.where(odd, second, first)


def exchange(edge, inner, on_core, on_faces, on_corners, faces_last=False):
    core = with_z_faces(edge, inner)
    first, second = x_faces(core)
    beyond = partner(core, "gx", 2)
    sums, spill, *more = on_core(flat(core))
    if faces_last:
        second, first, beyond, sums = lax.optimization_barrier((second, first, beyond, sums))
    else:
        first, second, sums = lax.optimization_barrier((first, second, sums))
    low, high = sorted_faces(first, second)
    corners = partner(jnp.concatenate([low, high], axis=0), "gx", 2)
    pieces = [flat(part) for part in (low, high, beyond)]
    sums, spill, *more = on_faces(pieces, sums, spill, *more)
    corners = flat(corners)
    return core, pieces, corners, on_corners(corners, sums, spill, core, *more)


def global_sum(values):
    count = lax.axis_size("gx")
    if count & (count - 1):
        return lax.psum(values, "gx")
    step = 1
    while step < count:
        if step >= 2 and 4 * step <= count:
            others = [partner(values, "gx", k * step) for k in (1, 2, 3)]
            values = (values + others[0]) + (others[1] + others[2])
            step *= 4
        else:
            values = values + partner(values, "gx", step)
            step *= 2
    return values


def local(cell_offsets, electronegativity, hardness, charge_widths, cell_counts, cell_atoms):
    edge, inner = prepare(
        cell_counts, cell_offsets, electronegativity, hardness, charge_widths, cell_atoms
    )
    stored = []

    def keep(tiles, *others):
        stored.append(tiles)
        return others

    def build_ends(corners, sums, spill, core, *own):
        (edge,) = keep(*build_corners(EDGES, corners, *own, sums, spill, flat(core)))
        (inner,) = keep(*build_corners(INNER, corners, *own, sums, spill, flat(core)))
        return by_column(edge), by_column(inner)

    def by_column(cells):
        return cells.reshape((QUADS, -1) + cells.shape[1:])

    slots, pieces, corners, ends = exchange(
        by_column(edge),
        by_column(inner),
        lambda core: keep(*build_core(core)),
        lambda faces, sums, spill, *own: keep(*build_faces(faces, *own, sums, spill)) + own,
        build_ends,
        faces_last=True,
    )
    info = flat(slots)

    def apply(edge, inner, on_corners):
        return exchange(
            edge,
            inner,
            lambda own: apply_core(info, own, stored[0]),
            lambda faces, sums, spill: apply_faces(pieces, faces, stored[1], sums, spill),
            on_corners,
        )

    def apply_ends(others, sums, spill, _):
        edge = apply_corners(corners, others, stored[2], sums, spill, info)
        inner = apply_corners(corners, others, stored[3], sums, spill, info)
        return by_column(edge), by_column(inner)

    first, _, _, ends = apply(*ends, apply_ends)
    second = with_z_faces(*ends)
    high = shifted(second[:2], -1)
    beyond = partner(second, "gx", 2)
    corner = shifted(second[:2], -1, 1)
    sums, spill, turned, line = apply_last_core(
        info, flat(second), stored[0], slots, first, second
    )
    high, beyond, sums = lax.optimization_barrier((high, beyond, sums))
    upper = [flat(high), flat(beyond)]
    sums, spill = apply_upper_faces(pieces[1:], upper, stored[1], sums, spill)
    corner, sums = lax.optimization_barrier((corner, sums))
    moments = apply_last(
        corners, flat(corner), stored[2], stored[3], sums, spill, turned, line
    )
    moments, cell_counts, cell_atoms = lax.optimization_barrier((moments, cell_counts, cell_atoms))
    atoms_local = cell_offsets.shape[1]
    places = inverted(cell_counts, cell_atoms, atoms_local)
    charges = finish(global_sum(moments), slots, first, second, places, atoms_local)
    return charges.reshape(-1)


def solution(mesh):
    placed = (
        P(None, ("grp", "gx")),
        P(("grp", "gx")),
        P(("grp", "gx")),
        P(("grp", "gx")),
        P(("grp", "gx")),
        P(("grp", "gx"), None),
    )
    return jax.shard_map(
        local, mesh=mesh, in_specs=placed, out_specs=P(("grp", "gx")), check_vma=False
    )
```
